32 devices in a mesh: seq: 32 (over z, y, x, core).
Axes of the slice: x: 2, y: 2, z: 4, core: 2. Of those that a mesh axis runs over, the one named last changes fastest.
Arguments:
- tokens_in: bfloat16 [8192, 1024], P('seq'), may hold values from -6 to 6
- cotangent: bfloat16 [8192, 1024], P('seq'), may hold values from -6 to 6
- pad_mask: int32 [8192], P('seq'), may hold values 0 or 1
- doc_lengths: int32 [7], replicated, may hold values from 64 to 7745, as said below
- masters: float32 [480, 32, 1024], P('seq')
- moment_one: float32 [480, 32, 1024], P('seq'), may hold values from -16 to 16
- moment_two: float32 [480, 32, 1024], P('seq'), may hold values from 0.4096 to 6.5536
- block_slot: int32 [416], replicated, may hold values from 0 to 479, as said below
- vectors: float32 [11, 1024], replicated
- vector_one: float32 [11, 1024], replicated, may hold values from -28 to 28
- vector_two: float32 [11, 1024], replicated, may hold values from 0.8192 to 16.384
Outputs:
- layer_out: bfloat16 [8192, 1024], P('seq')
- input_grad: float32 [8192, 1024], P('seq')
- new_moment_one: float32 [480, 32, 1024], P('seq')
- new_moment_two: float32 [480, 32, 1024], P('seq')
- new_masters: float32 [480, 32, 1024], P('seq')
- new_vector_one: float32 [11, 1024], replicated
- new_vector_two: float32 [11, 1024], replicated
- new_vectors: float32 [11, 1024], replicated
The draws below stay inside these ranges and needn't reach their ends.
Inputs may be any that keep to these rules, and one draw needn't show every extreme that they name: `doc_lengths`: the 7 documents fill all 8192 tokens; the fourth begins among the first 256 tokens, ends among the last 256 and has exactly 7745 tokens; every other one has 64 tokens or more. `block_slot`: distinct slot numbers; all 15 slots of some device are named.
All inputs are finite; a program needn't handle non-finite values. No bound on the sum of `pad_mask` on one device may be relied on, other than what follows from the above.
Results may differ from the reference program's by a relative error of at most 0.01.
Values may be sent and summed in bfloat16 or wider, within the bound.
A program may use at most 384 MiB of HBM per device.

```python
import math
import jax
import jax.numpy as jnp
from jax import lax

EMBED_SIZE = 1024
FF = 4096
TOK_DEV = 256
TOKENS = 8192
BLOCK_ROWS = 32
ROWS_ALL = 13312
BLOCKS = 416
SLOTS = 15
SLOTS_ALL = 480
MIN_DOC = 64
NVEC = 11
STEP = 10


def slot_map(key):
    first_key, second_key, third_key = jax.random.split(jax.random.fold_in(key, 101), 3)
    device_total = SLOTS_ALL // SLOTS
    full_device = jax.random.randint(first_key, (), 0, device_total)
    slot_ids = jnp.arange(SLOTS_ALL, dtype=jnp.int32)
    ranks = jax.random.permutation(second_key, SLOTS_ALL).astype(jnp.int32)
    scores = jnp.where(slot_ids // SLOTS == full_device, slot_ids - SLOTS_ALL, ranks)
    order = jnp.argsort(scores, stable=True).astype(jnp.int32)
    block_order = jax.random.permutation(third_key, BLOCKS).astype(jnp.int32)
    return jnp.zeros((BLOCKS,), jnp.int32).at[block_order].set(order[:BLOCKS])


def draw_block_slot(key, part):
    return slot_map(key)


def draw_masters(key, part):
    blocks = slot_map(key)
    key = jax.random.fold_in(key, 3)
    owner_block = jnp.full((SLOTS_ALL,), -1, jnp.int32).at[blocks].set(jnp.arange(BLOCKS, dtype=jnp.int32))
    first_row = owner_block * BLOCK_ROWS
    base = 1.0 / math.sqrt(EMBED_SIZE)
    scale = jnp.where(first_row < 0, base, jnp.where(first_row < EMBED_SIZE, 2.5 * base, jnp.where(first_row < 3 * EMBED_SIZE, base, jnp.where(first_row < 4 * EMBED_SIZE, 5.0 * base, jnp.where(first_row < 5 * EMBED_SIZE + FF, base, 1.0 / math.sqrt(FF))))))
    values = jax.random.truncated_normal(key, -4.0, 4.0, (SLOTS_ALL, BLOCK_ROWS, EMBED_SIZE), jnp.float32)
    return values * scale[:, None, None]


def split_three(key, total):
    first_key, second_key = jax.random.split(key)
    part_one = jax.random.randint(first_key, (), MIN_DOC, total - 2 * MIN_DOC + 1)
    part_two = jax.random.randint(second_key, (), MIN_DOC, total - part_one - MIN_DOC + 1)
    return (part_one, part_two, total - part_one - part_two)


def draw_doc_lengths(key, part):
    key = jax.random.fold_in(key, 11)
    learnable_entry_labels = jax.random.split(key, 4)
    head_total = jax.random.randint(learnable_entry_labels[0], (), 3 * MIN_DOC, TOK_DEV)
    tail_total = TOK_DEV - 1 + 3 * MIN_DOC - head_total
    head_one, head_two, head_three = split_three(learnable_entry_labels[2], head_total)
    tail_one, tail_two, tail_three = split_three(learnable_entry_labels[3], tail_total)
    middle = TOKENS - head_total - tail_total
    return jnp.stack([head_one, head_two, head_three, middle, tail_one, tail_two, tail_three]).astype(jnp.int32)


def draw_vectors(key, part):
    key = jax.random.fold_in(key, 5)
    learnable_entry_labels = jax.random.split(key, 7)
    fast_share = 0.5
    layernorm_scale_lines = jax.random.uniform(learnable_entry_labels[0], (2, EMBED_SIZE), jnp.float32, 0.6, 1.4)
    layernorm_offset_lines = jax.random.uniform(learnable_entry_labels[1], (2, EMBED_SIZE), jnp.float32, -0.3, 0.3)
    prior_step_blend_factors = jax.random.uniform(learnable_entry_labels[2], (4, EMBED_SIZE), jnp.float32, 0.15, 0.9)
    extra_blend_factor = jax.random.uniform(learnable_entry_labels[6], (1, EMBED_SIZE), jnp.float32, 0.15, 0.9)
    fast = jax.random.uniform(learnable_entry_labels[3], (EMBED_SIZE,), jnp.float32) < fast_share
    fast_rate = jax.random.uniform(learnable_entry_labels[4], (EMBED_SIZE,), jnp.float32, 1.0 / 50.0, 1.0 / 30.0)
    slow_rate = jnp.exp(jax.random.uniform(learnable_entry_labels[5], (EMBED_SIZE,), jnp.float32, math.log(0.02 / TOKENS), math.log(2.3 / TOKENS)))
    feature_fade_speed = jnp.log(jnp.where(fast, fast_rate, slow_rate))
    current_item_reward = jax.random.uniform(jax.random.fold_in(learnable_entry_labels[5], 9), (EMBED_SIZE,), jnp.float32, -1.0, 1.0)
    return jnp.stack([layernorm_scale_lines[0], layernorm_offset_lines[0], prior_step_blend_factors[0], prior_step_blend_factors[1], prior_step_blend_factors[2], feature_fade_speed, current_item_reward, layernorm_scale_lines[1], layernorm_offset_lines[1], prior_step_blend_factors[3], extra_blend_factor[0]])


def place_ends(entries, stream_key, smallest, top_value):
    longest = entries.shape.index(max(entries.shape))
    spots = []
    for shift in (0, 1):
        where = [jax.random.randint(jax.random.fold_in(stream_key, axis), (), 0, length) for axis, length in enumerate(entries.shape)]
        where[longest] = (where[longest] + shift) % entries.shape[longest]
        spots.append(tuple(where))
    return entries.at[spots[0]].set(smallest).at[spots[1]].set(top_value)


def block_levels(stream_key, dims, cuts, low, high):
    loudness = 1.0
    for position, shards_of in cuts:
        draws = jax.random.uniform(jax.random.fold_in(jax.random.fold_in(stream_key, 6), position), (shards_of,), jnp.float32, low / len(cuts), high / len(cuts))
        loudness = loudness * jnp.repeat(jnp.exp(draws), dims[position] // shards_of).reshape((-1,) + (1,) * (len(dims) - 1 - position))
    return loudness


def bell_draw(stream_key, extent, spread, reach, cuts=(), held_as=jnp.bfloat16):
    values = spread * jax.random.normal(stream_key, extent, jnp.float32)
    if cuts:
        values = values * block_levels(stream_key, extent, cuts, -0.22, 0.18)
    return jnp.clip(values, -reach, reach).astype(held_as)


def setup_inputs(seed: int = 0) -> dict:
    key_list = jax.random.split(jax.random.key(seed), 12)
    return {
        "tokens_in": bell_draw(key_list[0], (TOKENS, EMBED_SIZE), 1.0, 6.0, ((0, 32),)),
        "cotangent": bell_draw(key_list[1], (TOKENS, EMBED_SIZE), 1.0, 6.0, ((0, 32),)),
        "pad_mask": place_ends((jax.random.randint(key_list[2], (TOKENS,), 0, 8) < 7).astype(jnp.int32), jax.random.fold_in(key_list[2], 1), 0, 1),
        "doc_lengths": draw_doc_lengths(jax.random.fold_in(key_list[11], 71), 0),
        "masters": draw_masters(jax.random.fold_in(key_list[11], 71), 0),
        "moment_one": bell_draw(key_list[5], (SLOTS_ALL, BLOCK_ROWS, EMBED_SIZE), (0.033 * TOKENS ** 0.5), 16.0, ((0, 32),), jnp.float32),
        "moment_two": jnp.clip(jnp.exp(math.log(6.5536) - 2.7725887 * jax.random.uniform(key_list[6], (SLOTS_ALL, BLOCK_ROWS, EMBED_SIZE), jnp.float32) ** block_levels(key_list[6], (SLOTS_ALL, BLOCK_ROWS, EMBED_SIZE), ((0, 32),), -0.2, 0.2)), 0.4096, 6.5536),
        "block_slot": draw_block_slot(jax.random.fold_in(key_list[11], 71), 0),
        "vectors": draw_vectors(jax.random.fold_in(key_list[11], 71), 0),
        "vector_one": bell_draw(key_list[9], (NVEC, EMBED_SIZE), (0.05 * TOKENS ** 0.5), 28.0, (), jnp.float32),
        "vector_two": jnp.clip(jnp.exp(jax.random.uniform(key_list[10], (NVEC, EMBED_SIZE), jnp.float32, math.log(0.8192), math.log(16.384))), 0.8192, 16.384),
    }


NEGATIVE = -1e+30
NORM_EPS = 1e-05
BETA_ONE = 0.9
BETA_TWO = 0.999
ADAM_EPS = 1e-08
MATRIX_RATE = 0.05
WEIGHT_DECAY = 0.01
VECTOR_RATE = (0.25, 0.25, 0.25, 0.25, 0.25, 2.0, 0.25, 0.25, 0.25, 0.25, 0.25)

@jax.custom_vjp
def low(v):
    return lax.optimization_barrier(v.astype(jnp.bfloat16)).astype(jnp.float32)

@jax.custom_vjp
def low_back(v):
    return v

def low_keep(v):
    return (low(v), None)

def low_pass(kept, grad):
    return (grad,)

def back_keep(v):
    return (v, None)

def back_low(kept, grad):
    return (low(grad),)
low.defvjp(low_keep, low_pass)
low_back.defvjp(back_keep, back_low)

def product(left_side, right_side):
    return jnp.dot(left_side, right_side, precision=lax.Precision.HIGHEST, preferred_element_type=jnp.float32)

def product_back(left_side, right_side):
    return lax.dot_general(left_side, right_side, (((1,), (1,)), ((), ())), precision=lax.Precision.HIGHEST, preferred_element_type=jnp.float32)

def norm_rows(values, gain_row, bias_row):
    mean_row = lax.optimization_barrier(jnp.mean(values, axis=-1, keepdims=True))
    centered = values - mean_row
    variance = lax.optimization_barrier(jnp.mean(centered * centered, axis=-1, keepdims=True))
    return centered * lax.rsqrt(variance + NORM_EPS) * gain_row + bias_row

def shifted_norm(block_rows, prior_row, start_block, gain_row, bias_row):
    normed = norm_rows(block_rows, gain_row, bias_row)
    prior = norm_rows(prior_row[None, :], gain_row, bias_row)
    previous = jnp.concatenate([prior, normed[:-1]], axis=0) * (1.0 - start_block)[:, None]
    return (normed, previous)

def mix_pair(mix_row, normed, previous):
    return mix_row * normed + (1.0 - mix_row) * previous

def wkv_all(key_rows, value_rows, starts, decay_rate, time_first):
    features = key_rows.shape[1]

    def token_step(carry_state, pieces):
        num_state, den_state, max_state = carry_state
        key_now, value_now, start_now = pieces
        keep_state = 1.0 - start_now
        num_state = num_state * keep_state
        den_state = den_state * keep_state
        max_state = jnp.where(start_now > 0.5, NEGATIVE, max_state)
        top_log = jnp.maximum(max_state, time_first + key_now)
        old_weight = jnp.exp(max_state - top_log)
        new_weight = jnp.exp(time_first + key_now - top_log)
        result = (old_weight * num_state + new_weight * value_now) / (old_weight * den_state + new_weight)
        next_max = jnp.maximum(max_state - decay_rate, key_now)
        old_decayed = jnp.exp(max_state - decay_rate - next_max)
        new_entry = jnp.exp(key_now - next_max)
        next_state = (old_decayed * num_state + new_entry * value_now, old_decayed * den_state + new_entry, next_max)
        return (next_state, result)

    def block_step(carry_state, pieces):
        return lax.scan(token_step, carry_state, pieces)
    block_size = math.gcd(key_rows.shape[0], 128)
    block_count = key_rows.shape[0] // block_size
    pieces = (key_rows.reshape(block_count, block_size, features), value_rows.reshape(block_count, block_size, features), starts.reshape(block_count, block_size, 1))
    initial = (jnp.zeros((features,), jnp.float32), jnp.zeros((features,), jnp.float32), jnp.full((features,), NEGATIVE, jnp.float32))
    _, weighted = lax.scan(jax.checkpoint(block_step), initial, pieces)
    return weighted.reshape(key_rows.shape)

def layer(inputs, weight_rows, vectors, starts):
    weights = low(weight_rows)
    key_w = weights[:EMBED_SIZE]
    value_w = weights[EMBED_SIZE:2 * EMBED_SIZE]
    recept_w = weights[2 * EMBED_SIZE:3 * EMBED_SIZE]
    output_w = weights[3 * EMBED_SIZE:4 * EMBED_SIZE]
    chan_recept_w = weights[4 * EMBED_SIZE:5 * EMBED_SIZE]
    chan_key_w = weights[5 * EMBED_SIZE:5 * EMBED_SIZE + FF]
    chan_value_w = weights[5 * EMBED_SIZE + FF:]
    block_size = math.gcd(TOKENS, 4096)
    block_count = TOKENS // block_size

    def blocked(values):
        return values.reshape((block_count, block_size) + values.shape[1:])

    def priors(values):
        lasts = values[block_size - 1::block_size]
        return jnp.concatenate([jnp.zeros((1, EMBED_SIZE), jnp.float32), lasts[:-1]], axis=0)

    def section_keys(pieces):
        block_rows, prior_row, start_block = pieces
        normed, previous = shifted_norm(block_rows, prior_row, start_block, vectors[0], vectors[1])
        in_key = low(mix_pair(vectors[2], normed, previous))
        in_value = low(mix_pair(vectors[3], normed, previous))
        return (low_back(product(in_key, key_w)), low_back(product(in_value, value_w)))
    key_rows, value_rows = lax.map(jax.checkpoint(section_keys), (blocked(inputs), priors(inputs), blocked(starts)))
    weighted = wkv_all(key_rows.reshape(TOKENS, EMBED_SIZE), value_rows.reshape(TOKENS, EMBED_SIZE), starts, jnp.exp(vectors[5]), vectors[6])

    def section_mix(pieces):
        block_rows, prior_row, start_block, weighted_block = pieces
        normed, previous = shifted_norm(block_rows, prior_row, start_block, vectors[0], vectors[1])
        in_recept = low(mix_pair(vectors[4], normed, previous))
        receptance = low_back(product(in_recept, recept_w))
        mixed = low(jax.nn.sigmoid(receptance) * weighted_block)
        return block_rows + low_back(product(mixed, output_w))
    resid = lax.map(jax.checkpoint(section_mix), (blocked(inputs), priors(inputs), blocked(starts), blocked(weighted))).reshape(TOKENS, EMBED_SIZE)

    def section_chan(pieces):
        block_rows, prior_row, start_block = pieces
        normed, previous = shifted_norm(block_rows, prior_row, start_block, vectors[7], vectors[8])
        chan_in_key = low(mix_pair(vectors[9], normed, previous))
        chan_in_recept = low(mix_pair(vectors[10], normed, previous))
        hidden_pre = low_back(product_back(chan_in_key, chan_key_w))
        squared = low(jnp.square(jax.nn.relu(hidden_pre)))
        chan_value = low_back(product(squared, chan_value_w))
        chan_gate = low_back(product(chan_in_recept, chan_recept_w))
        return block_rows + jax.nn.sigmoid(chan_gate) * chan_value
    return lax.map(jax.checkpoint(section_chan), (blocked(resid), priors(resid), blocked(starts))).reshape(TOKENS, EMBED_SIZE)

def adam_update(weight, first_moment, second_moment, gradient, step_rate, feature_fade_speed):
    first_moment = BETA_ONE * first_moment + (1.0 - BETA_ONE) * gradient
    second_moment = BETA_TWO * second_moment + (1.0 - BETA_TWO) * gradient * gradient
    first_fixed = first_moment / (1.0 - BETA_ONE ** STEP)
    second_fixed = second_moment / (1.0 - BETA_TWO ** STEP)
    weight = weight - step_rate * (first_fixed / (jnp.sqrt(second_fixed) + ADAM_EPS) + feature_fade_speed * weight)
    return (first_moment, second_moment, weight)

def reference(tokens_in, cotangent, pad_mask, doc_lengths, masters, moment_one, moment_two, block_slot, vectors, vector_one, vector_two):
    offsets = (jnp.cumsum(doc_lengths) - doc_lengths).astype(jnp.int32)
    starts = jnp.zeros((TOKENS,), jnp.float32).at[offsets].set(1.0)
    weight_rows = masters[block_slot].reshape(ROWS_ALL, EMBED_SIZE)
    inputs = tokens_in.astype(jnp.float32)
    out_value, pullback = jax.vjp(lambda first_arg, second_arg, third_arg: layer(first_arg, second_arg, third_arg, starts), inputs, weight_rows, vectors)
    out_grad = cotangent.astype(jnp.float32) * pad_mask.astype(jnp.float32)[:, None]
    input_grad, row_grad, vector_grad = pullback(out_grad)
    slot_grad = jnp.zeros(masters.shape, jnp.float32).at[block_slot].set(row_grad.reshape(BLOCKS, BLOCK_ROWS, EMBED_SIZE))
    new_one, new_two, new_master = adam_update(masters, moment_one, moment_two, slot_grad, MATRIX_RATE, WEIGHT_DECAY)
    vector_rates = jnp.array(VECTOR_RATE, jnp.float32)[:, None]
    vector_first, vector_second, vector_next = adam_update(vectors, vector_one, vector_two, vector_grad, vector_rates, 0.0)
    return (out_value.astype(jnp.bfloat16), input_grad, new_one, new_two, new_master, vector_first, vector_second, vector_next)
```

```python
import functools
import math

import jax
import jax.numpy as jnp
from jax import lax
from jax.experimental import pallas as pl
from jax.experimental.pallas import tpu as pltpu
from jax.sharding import PartitionSpec as P

EMBED_SIZE = 1024
FF = 4096
BLOCK_ROWS = 32
ROWS_ALL = 13312
BLOCKS = 416
STEP = 10
GRID_DEVICES = 32
MESH = pl.DeviceIdType.MESH

def grid_place():
    me = lax.axis_index("seq")
    return me, lax.rem(me, 2), lax.rem(me // 2, 2), lax.rem(me // 4, 2), me // 8

def spans(slots):
    third = -(-slots // 3)
    cuts = [0, third, min(2 * third, slots), slots]
    return [(cuts[i], cuts[i + 1] - cuts[i]) for i in range(3)]

def gather_kernel(slots, own_ref, out_ref, *scratch):
    send_sem, recv_sem, sib_send, sib_recv, own_sem = scratch
    me, core, x, y, z = grid_place()
    sib = me + 1 - 2 * core
    x_peer = me + 2 - 4 * x
    y_peer = me + 4 - 8 * y
    up = me + 8
    down = me - 8
    bar = pltpu.get_barrier_semaphore()
    pl.semaphore_signal(bar, inc=1, device_id=(sib,), device_id_type=MESH)
    pl.semaphore_signal(bar, inc=1, device_id=(x_peer,), device_id_type=MESH)
    pl.semaphore_signal(bar, inc=1, device_id=(y_peer,), device_id_type=MESH)
    @pl.when(z < 3)
    def _():
        pl.semaphore_signal(bar, inc=1, device_id=(up,), device_id_type=MESH)
    @pl.when(z > 0)
    def _():
        pl.semaphore_signal(bar, inc=1, device_id=(down,), device_id_type=MESH)
    pl.semaphore_wait(bar, 4 + jnp.where((z > 0) & (z < 3), 1, 0))
    span = spans(slots)
    targets = (x_peer, y_peer, up, down)

    def chip(cx, cy, cz):
        return (cz * 2 + cy) * 2 + cx

    def view(cx, cy, cz, color, c=None):
        dev = chip(cx, cy, cz) * 2 + (core if c is None else c)
        lo, n = span[color]
        return out_ref.at[dev, pl.ds(lo, n)]

    def send(cx, cy, cz, color, way, own=False):
        lo, n = span[color]
        src = own_ref.at[pl.ds(lo, n)] if own else view(cx, cy, cz, color)
        idx = chip(cx, cy, cz)
        return pltpu.make_async_remote_copy(src_ref=src, dst_ref=view(cx, cy, cz, color),
            send_sem=send_sem.at[idx, color, way], recv_sem=recv_sem.at[idx, color],
            device_id=(targets[way],), device_id_type=MESH)

    def send_sib(cx, cy, cz, color, own=False):
        lo, n = span[color]
        src = own_ref.at[pl.ds(lo, n)] if own else view(cx, cy, cz, color)
        idx = chip(cx, cy, cz)
        return pltpu.make_async_remote_copy(src_ref=src, dst_ref=view(cx, cy, cz, color),
            send_sem=sib_send.at[idx, color], recv_sem=sib_recv.at[idx, color],
            device_id=(sib,), device_id_type=MESH)

    x2, y2 = 1 - x, 1 - y
    pending = []

    def go(copy, cond=None):
        if cond is None:
            copy.start()
        else:
            @pl.when(cond)
            def _():
                copy.start()
        pending.append((copy, cond))

    zup, zdown = z < 3, z > 0
    own_copies = []
    for color in range(3):
        lo, n = span[color]
        cp = pltpu.make_async_copy(own_ref.at[pl.ds(lo, n)], view(x, y, z, color), own_sem.at[color])
        cp.start()
        own_copies.append(cp)
    order = {0: (0, 2, 1), 1: (1, 2, 0)}
    for color in (0, 1, 2):
        go(send(x, y, z, color, 2, True), zup)
        go(send(x, y, z, color, 3, True), zdown)
    for color, way in ((0, 0), (1, 1), (2, 0), (2, 1), (0, 1), (1, 0)):
        go(send(x, y, z, color, way, True))
    for color in range(3):
        go(send_sib(x, y, z, color, True))

    def arrive(cx, cy, cz, color):
        send(cx, cy, cz, color, 0).wait_recv()

    def sibling(cx, cy, cz, color):
        go(send_sib(cx, cy, cz, color))

    is0, is1 = core == 0, core == 1
    px = jnp.where(is0, x2, x)
    py = jnp.where(is0, y, y2)
    qx = jnp.where(is0, x, x2)
    qy = jnp.where(is0, y2, y)
    first = lambda cx, cy, cz: (go(send(cx, cy, cz, 2, 0), is0), go(send(cx, cy, cz, 2, 1), is1))
    last = lambda cx, cy, cz: (go(send(cx, cy, cz, 2, 1), is0), go(send(cx, cy, cz, 2, 0), is1))

    arrive(x2, y, z, 0)
    go(send(x2, y, z, 0, 2), zup)
    go(send(x2, y, z, 0, 3), zdown)
    go(send(x2, y, z, 0, 1))
    sibling(x2, y, z, 0)
    arrive(x, y2, z, 1)
    go(send(x, y2, z, 1, 2), zup)
    go(send(x, y2, z, 1, 3), zdown)
    go(send(x, y2, z, 1, 0))
    sibling(x, y2, z, 1)
    arrive(px, py, z, 2)
    last(px, py, z)
    sibling(px, py, z, 2)

    for dist in (1, 2, 3):
        sides = []
        for sign, fwd, guard_f in ((1, 3, zdown), (-1, 2, zup)):
            q = z + sign * dist
            have = (q >= 0) & (q < 4)
            sides.append((q, fwd, have, guard_f))
        for which in ("c", "a", "b", "a2", "b2"):
            for q, fwd, have, gf in sides:
                @pl.when(have)
                def _(q=q, fwd=fwd, gf=gf, which=which):
                    if which == "c":
                        arrive(x, y, q, 2)
                        cp = send(x, y, q, 2, fwd)
                        pl.when(gf)(lambda: cp.start())
                        for w in (0, 1):
                            send(x, y, q, 2, w).start()
                        send_sib(x, y, q, 2).start()
                    else:
                        color = 0 if which[0] == "a" else 1
                        cx, cy = {"a": (x, y), "b": (x, y), "a2": (x2, y), "b2": (x, y2)}[which]
                        arrive(cx, cy, q, color)
                        cp = send(cx, cy, q, color, fwd)
                        pl.when(gf)(lambda: cp.start())
                        send(cx, cy, q, color, 1 if color == 0 else 0).start()
                        send_sib(cx, cy, q, color).start()
        for q, fwd, have, gf in sides:
            @pl.when(have)
            def _(q=q):
                arrive(px, py, q, 2)
                pl.when(is0)(lambda: send(px, py, q, 2, 1).start())
                pl.when(is1)(lambda: send(px, py, q, 2, 0).start())
                send_sib(px, py, q, 2).start()
        if dist == 1:
            tail_list = [(z, None)]
        else:
            tail_list = []
        def terminal(q):
            for cx, cy, color in ((x, y2, 0), (x2, y2, 0), (x2, y, 1), (x2, y2, 1), (qx, qy, 2), (x2, y2, 2)):
                arrive(cx, cy, q, color)
                send_sib(cx, cy, q, color).start()
        if dist == 1:
            terminal(z)
        else:
            for sign in (1, -1):
                q = z + sign * (dist - 1)
                pl.when((q >= 0) & (q < 4))(lambda q=q: terminal(q))
        if dist == 3:
            for sign in (1, -1):
                q = z + sign * 3
                pl.when((q >= 0) & (q < 4))(lambda q=q: terminal(q))
    for cp in own_copies:
        cp.wait()
    for color in range(3):
        pl.when(zup)(lambda color=color: send(x, y, z, color, 2).wait_send())
        pl.when(zdown)(lambda color=color: send(x, y, z, color, 3).wait_send())
        for w in (0, 1):
            send(x, y, z, color, w).wait_send()
    for cx, cy, color, w in ((x2, y, 0, 1), (x, y2, 1, 0)):
        pl.when(zup)(lambda: send(cx, cy, z, color, 2).wait_send())
        pl.when(zdown)(lambda: send(cx, cy, z, color, 3).wait_send())
        send(cx, cy, z, color, w).wait_send()
    pl.when(is0)(lambda: send(px, py, z, 2, 1).wait_send())
    pl.when(is1)(lambda: send(px, py, z, 2, 0).wait_send())
    for dist in (1, 2, 3):
        for sign, fwd, gf in ((1, 3, zdown), (-1, 2, zup)):
            q = z + sign * dist
            @pl.when((q >= 0) & (q < 4))
            def _(q=q, fwd=fwd, gf=gf):
                for cx, cy, color in ((x, y, 2), (x, y, 0), (x, y, 1), (x2, y, 0), (x, y2, 1)):
                    pl.when(gf)(lambda: send(cx, cy, q, color, fwd).wait_send())
                    ways = (0, 1) if color == 2 else ((1,) if color == 0 else (0,))
                    for w in ways:
                        send(cx, cy, q, color, w).wait_send()
                pl.when(is0)(lambda: send(px, py, q, 2, 1).wait_send())
                pl.when(is1)(lambda: send(px, py, q, 2, 0).wait_send())
    for cz in range(4):
        for cy in range(2):
            for cx in range(2):
                for color in range(3):
                    cp = send_sib(cx, cy, cz, color)
                    cp.wait_send()
                    cp.wait_recv()

def gather_blocks(owned, cid=1):
    slots = owned.shape[0]
    return pl.pallas_call(
        functools.partial(gather_kernel, slots),
        out_shape=jax.ShapeDtypeStruct((32,) + owned.shape, owned.dtype),
        in_specs=[pl.BlockSpec(memory_space=pl.ANY)],
        out_specs=pl.BlockSpec(memory_space=pl.ANY),
        scratch_shapes=[
            pltpu.SemaphoreType.DMA((16, 3, 4)),
            pltpu.SemaphoreType.DMA((16, 3)),
            pltpu.SemaphoreType.DMA((16, 3)),
            pltpu.SemaphoreType.DMA((16, 3)),
            pltpu.SemaphoreType.DMA((3,)),
        ],
        compiler_params=pltpu.CompilerParams(collective_id=cid, has_side_effects=True),
        name="gather_blocks",
    )(owned)

def scatter_kernel(slots, part_ref, out_ref, acc, sib, xin, yin, zin, load_sem, sib_send, sib_recv, send_sem, xsem, ysem, zsem):
    me, core, x, y, z = grid_place()
    sibling = me + 1 - 2 * core
    x_peer = me + 2 - 4 * x
    y_peer = me + 4 - 8 * y
    up, down = me + 8, me - 8
    zup, zdown = z < 3, z > 0
    bar = pltpu.get_barrier_semaphore()
    for peer in (sibling, x_peer, y_peer):
        pl.semaphore_signal(bar, inc=1, device_id=(peer,), device_id_type=MESH)
    @pl.when(zup)
    def _():
        pl.semaphore_signal(bar, inc=1, device_id=(up,), device_id_type=MESH)
    @pl.when(zdown)
    def _():
        pl.semaphore_signal(bar, inc=1, device_id=(down,), device_id_type=MESH)
    span = spans(slots)
    x2, y2 = 1 - x, 1 - y
    is0, is1 = core == 0, core == 1
    px, py = jnp.where(is0, x2, x), jnp.where(is0, y, y2)
    qx, qy = jnp.where(is0, x, x2), jnp.where(is0, y2, y)

    def load(chip):
        return pltpu.make_async_copy(part_ref.at[2 * chip + core], acc.at[chip], load_sem.at[chip])

    def give(chip):
        return pltpu.make_async_remote_copy(src_ref=part_ref.at[2 * chip + 1 - core], dst_ref=sib.at[chip],
            send_sem=sib_send.at[chip], recv_sem=sib_recv.at[chip], device_id=(sibling,), device_id_type=MESH)

    levels = []
    for dist in (3, 2, 1):
        for sign in (1, -1):
            q = z + sign * dist
            levels.append((dist, sign, q, (q >= 0) & (q < 4)))
    for _, _, q, have in levels:
        @pl.when(have)
        def _(q=q):
            for i in range(4):
                load(4 * q + i).start()
    for i in range(4):
        load(4 * z + i).start()
    pl.semaphore_wait(bar, 4 + jnp.where(zup & zdown, 1, 0))
    for _, _, q, have in levels:
        @pl.when(have)
        def _(q=q):
            for i in range(4):
                give(4 * q + i).start()
    for i in range(4):
        give(4 * z + i).start()

    def ready(q):
        for i in range(4):
            chip = 4 * q + i
            load(chip).wait()
            give(chip).wait_recv()
            def step(s, _, chip=chip):
                total = acc[chip, s].astype(jnp.float32) + sib[chip, s].astype(jnp.float32)
                acc[chip, s] = total.astype(acc.dtype)
                return 0
            lax.fori_loop(0, slots, step, 0)

    def chip_of(cx, cy, cz):
        return (cz * 2 + cy) * 2 + cx

    def out_copy(cx, cy, cz, color, target, buf, index, sem):
        lo, n = span[color]
        chip = chip_of(cx, cy, cz)
        return pltpu.make_async_remote_copy(src_ref=acc.at[chip, pl.ds(lo, n)], dst_ref=buf.at[index, pl.ds(0, n)],
            send_sem=send_sem.at[chip, color], recv_sem=sem.at[index], device_id=(target,), device_id_type=MESH)

    def arrived(buf, index, sem, color):
        lo, n = span[color]
        pltpu.make_async_remote_copy(src_ref=acc.at[0, pl.ds(lo, n)], dst_ref=buf.at[index, pl.ds(0, n)],
            send_sem=send_sem.at[0, color], recv_sem=sem.at[index], device_id=(sibling,), device_id_type=MESH).wait_recv()

    def add(cx, cy, cz, color, pieces):
        lo, n = span[color]
        chip = chip_of(cx, cy, cz)
        for buf, index, sem in pieces:
            arrived(buf, index, sem, color)
        def step(s, _):
            total = acc[chip, lo + s].astype(jnp.float32)
            for buf, index, _sem in pieces:
                total = total + buf[index, s].astype(jnp.float32)
            acc[chip, lo + s] = total.astype(acc.dtype)
            return 0
        lax.fori_loop(0, n, step, 0)

    def X(i): return (xin, i, xsem)
    def Y(i): return (yin, i, ysem)
    def Z(i): return (zin, i, zsem)

    def terminal(q):
        for i, cx in enumerate((x, x2)):
            out_copy(cx, y2, q, 0, y_peer, yin, 2 * q + i, ysem).start()
        for i, cy in enumerate((y, y2)):
            out_copy(x2, cy, q, 1, x_peer, xin, 2 * q + i, xsem).start()
        @pl.when(is0)
        def _():
            for i, cx in enumerate((x, x2)):
                out_copy(cx, y2, q, 2, y_peer, yin, 8 + 2 * q + i, ysem).start()
        @pl.when(is1)
        def _():
            for i, cy in enumerate((y, y2)):
                out_copy(x2, cy, q, 2, x_peer, xin, 8 + 2 * q + i, xsem).start()

    def plane_two(q):
        @pl.when(is0)
        def _():
            add(x2, y, q, 2, [Y(8 + 2 * q + 1)])
            out_copy(x2, y, q, 2, x_peer, xin, 8 + 2 * q, xsem).start()
        @pl.when(is1)
        def _():
            add(x, y2, q, 2, [X(8 + 2 * q + 1)])
            out_copy(x, y2, q, 2, y_peer, yin, 8 + 2 * q, ysem).start()

    def column(q, sign, dist):
        target = up if sign == 1 else down
        more = zdown if sign == 1 else zup
        at_target = dist == 1
        base_out = (20 if (at_target and sign == 1) else 5 * q)
        kinds = (
            (0, x, y, 2, [X(8 + 2 * q), Y(8 + 2 * q)]),
            (1, x, y, 0, [Y(2 * q)]),
            (2, x, y, 1, [X(2 * q)]),
            (3, x2, y, 0, [Y(2 * q + 1)]),
            (4, x, y2, 1, [X(2 * q + 1)]),
        )
        for k, cx, cy, color, pieces in (kinds[1], kinds[2], kinds[3], kinds[4], kinds[0]):
            @pl.when(more)
            def _():
                add(cx, cy, q, color, pieces + [Z(5 * q + k)])
            @pl.when(jnp.logical_not(more))
            def _():
                add(cx, cy, q, color, pieces)
            out_copy(cx, cy, q, color, target, zin, base_out + k, zsem).start()

    def run(dist, work):
        for d, sign, q, have in levels:
            if d == dist:
                pl.when(have)(functools.partial(work, q, sign, dist))

    def begin(q, sign, dist):
        ready(q)
        terminal(q)

    def middle(q, sign, dist):
        plane_two(q)
    run(3, begin)
    run(3, middle)
    run(2, begin)
    run(3, column)
    run(2, middle)
    run(1, begin)
    run(2, column)
    run(1, middle)
    ready(z)
    terminal(z)
    run(1, column)
    plane_two(z)

    def own(k, cx, cy, color, pieces):
        @pl.when(zup & zdown)
        def _():
            add(cx, cy, z, color, pieces + [Z(5 * z + k), Z(20 + k)])
        @pl.when(zup & jnp.logical_not(zdown))
        def _():
            add(cx, cy, z, color, pieces + [Z(5 * z + k)])
        @pl.when(zdown & jnp.logical_not(zup))
        def _():
            add(cx, cy, z, color, pieces + [Z(20 + k)])
    own(3, x2, y, 0, [Y(2 * z + 1)])
    out_copy(x2, y, z, 0, x_peer, xin, 16, xsem).start()
    own(4, x, y2, 1, [X(2 * z + 1)])
    out_copy(x, y2, z, 1, y_peer, yin, 16, ysem).start()
    own(0, x, y, 2, [X(8 + 2 * z), Y(8 + 2 * z)])
    own(1, x, y, 0, [Y(2 * z), X(16)])
    own(2, x, y, 1, [X(2 * z), Y(16)])
    pltpu.sync_copy(acc.at[chip_of(x, y, z)], out_ref)
    for chip in range(16):
        give(chip).wait_send()
        for color in range(3):
            @pl.when(chip != chip_of(x, y, z))
            def _():
                lo, n = span[color]
                pltpu.make_async_remote_copy(src_ref=acc.at[chip, pl.ds(lo, n)], dst_ref=xin.at[0, pl.ds(0, n)],
                    send_sem=send_sem.at[chip, color], recv_sem=xsem.at[0], device_id=(sibling,), device_id_type=MESH).wait_send()

def scatter_blocks(part, cid=2):
    _, slots, rows, feats = part.shape
    most = max(n for _, n in spans(slots))
    chunk = (most, rows, feats)
    dt = part.dtype
    return pl.pallas_call(
        functools.partial(scatter_kernel, slots),
        out_shape=jax.ShapeDtypeStruct(part.shape[1:], dt),
        in_specs=[pl.BlockSpec(memory_space=pl.ANY)],
        out_specs=pl.BlockSpec(memory_space=pl.ANY),
        scratch_shapes=[
            pltpu.VMEM((16, slots, rows, feats), dt),
            pltpu.VMEM((16, slots, rows, feats), dt),
            pltpu.VMEM((17,) + chunk, dt),
            pltpu.VMEM((17,) + chunk, dt),
            pltpu.VMEM((25,) + chunk, dt),
            pltpu.SemaphoreType.DMA((16,)),
            pltpu.SemaphoreType.DMA((16,)),
            pltpu.SemaphoreType.DMA((16,)),
            pltpu.SemaphoreType.DMA((16, 3)),
            pltpu.SemaphoreType.DMA((17,)),
            pltpu.SemaphoreType.DMA((17,)),
            pltpu.SemaphoreType.DMA((25,)),
        ],
        compiler_params=pltpu.CompilerParams(collective_id=cid, has_side_effects=True, vmem_limit_bytes=58 * 2**20),
        name="scatter_blocks",
    )(part)


def exchange_kernel(devices, own_ref, out_ref, send_sem, recv_sem, own_sem):
    me = lax.axis_index("seq")
    bar = pltpu.get_barrier_semaphore()
    for o in range(1, devices):
        pl.semaphore_signal(bar, inc=1, device_id=(lax.rem(me + o, devices),), device_id_type=MESH)
    pl.semaphore_wait(bar, devices - 1)
    keep = pltpu.make_async_copy(own_ref, out_ref.at[me], own_sem)
    keep.start()

    def copy(o, place, peer):
        return pltpu.make_async_remote_copy(
            src_ref=own_ref,
            dst_ref=out_ref.at[place],
            send_sem=send_sem.at[o],
            recv_sem=recv_sem.at[o],
            device_id=(peer,),
            device_id_type=MESH,
        )

    for o in range(1, devices):
        copy(o, me, lax.rem(me + o, devices)).start()
    for o in range(1, devices):
        peer = lax.rem(me - o + devices, devices)
        copy(o, peer, peer).wait()
    keep.wait()


def exchange_rows(rows, cid):
    devices = lax.axis_size("seq")
    if devices != GRID_DEVICES:
        return lax.all_gather(rows[None], "seq", axis=0, tiled=True)
    return pl.pallas_call(
        functools.partial(exchange_kernel, devices),
        out_shape=jax.ShapeDtypeStruct((devices,) + rows.shape, rows.dtype),
        in_specs=[pl.BlockSpec(memory_space=pltpu.VMEM)],
        out_specs=pl.BlockSpec(memory_space=pltpu.VMEM),
        scratch_shapes=[
            pltpu.SemaphoreType.DMA((devices,)),
            pltpu.SemaphoreType.DMA((devices,)),
            pltpu.SemaphoreType.DMA,
        ],
        compiler_params=pltpu.CompilerParams(collective_id=cid, has_side_effects=True),
        name="exchange_rows",
    )(rows)


NEGATIVE = -1e30
NORM_EPS = 1e-05
BETA_ONE = 0.9
BETA_TWO = 0.999
ADAM_EPS = 1e-08
MATRIX_RATE = 0.05
WEIGHT_DECAY = 0.01
VECTOR_RATE = (0.25, 0.25, 0.25, 0.25, 0.25, 2.0, 0.25, 0.25, 0.25, 0.25, 0.25)


def shifted(block, axis, distance):
    devices = range(lax.axis_size(axis))
    route = [(i - distance, i) for i in devices if i - distance in devices]
    return lax.ppermute(block, axis, route)


def product(left_side, right_side):
    return jnp.dot(left_side, right_side, preferred_element_type=jnp.float32)


def product_back(left_side, right_side):
    return lax.dot_general(
        left_side, right_side, (((1,), (1,)), ((), ())), preferred_element_type=jnp.float32
    )


def product_left(left_side, right_side):
    return lax.dot_general(
        left_side, right_side, (((0,), (0,)), ((), ())), preferred_element_type=jnp.float32
    )


def norm_forward(values, gain_row, bias_row):
    mean_row = jnp.mean(values, axis=1, keepdims=True)
    centered = values - mean_row
    inverse = lax.rsqrt(jnp.mean(centered * centered, axis=1, keepdims=True) + NORM_EPS)
    unit_rows = centered * inverse
    return (unit_rows * gain_row + bias_row, unit_rows, inverse)


def norm_backward(grad_out, unit_rows, inverse, gain_row):
    scaled = grad_out * gain_row
    inner = (
        scaled
        - jnp.mean(scaled, axis=1, keepdims=True)
        - unit_rows * jnp.mean(scaled * unit_rows, axis=1, keepdims=True)
    )
    return (inner * inverse, jnp.sum(grad_out * unit_rows, axis=0), jnp.sum(grad_out, axis=0))


def split_rows(gathered, block_slot):
    weight_rows = gathered[block_slot].reshape(ROWS_ALL, EMBED_SIZE)
    return (
        weight_rows[:EMBED_SIZE],
        weight_rows[EMBED_SIZE : 2 * EMBED_SIZE],
        weight_rows[2 * EMBED_SIZE : 3 * EMBED_SIZE],
        weight_rows[3 * EMBED_SIZE : 4 * EMBED_SIZE],
        weight_rows[4 * EMBED_SIZE : 5 * EMBED_SIZE],
        weight_rows[5 * EMBED_SIZE : 5 * EMBED_SIZE + FF],
        weight_rows[5 * EMBED_SIZE + FF :],
    )


def local_pass(key_rows, value_rows, starts, decay_rate, time_first):
    tokens, features = key_rows.shape
    block_size = math.gcd(tokens, 128)
    block_count = tokens // block_size
    position = jnp.arange(block_size, dtype=jnp.float32)
    causal = (position[None, :] < position[:, None]).astype(jnp.float32)

    def block_step(carry_state, pieces):
        num_state, den_state, max_state = carry_state
        key_block, value_block, start_block = pieces
        doc_index = jnp.cumsum(start_block)
        same_doc = (doc_index[:, None] == doc_index[None, :]).astype(jnp.float32) * causal
        carried = (doc_index == 0.0)[:, None]
        top_key = jnp.max(key_block, axis=0)
        weight_in = jnp.exp(
            key_block - top_key - (block_size - 1.0 - position)[:, None] * decay_rate
        )
        partial_value = jnp.dot(
            same_doc,
            jnp.concatenate([weight_in * value_block, weight_in], axis=1),
            precision=lax.Precision.HIGHEST,
            preferred_element_type=jnp.float32,
        )
        inner_log = top_key + (block_size - position)[:, None] * decay_rate
        carry_log = jnp.where(carried, max_state - position[:, None] * decay_rate, NEGATIVE)
        own_log = time_first + key_block
        top_log = jnp.maximum(jnp.maximum(inner_log, carry_log), own_log)
        inner_weight = jnp.exp(inner_log - top_log)
        carry_weight = jnp.exp(carry_log - top_log)
        own_weight = jnp.exp(own_log - top_log)
        numerator = (
            inner_weight * partial_value[:, :features]
            + carry_weight * num_state
            + own_weight * value_block
        )
        denominator = (
            inner_weight * partial_value[:, features:] + carry_weight * den_state + own_weight
        )
        last_doc = (doc_index == doc_index[block_size - 1]).astype(jnp.float32)[:, None]
        end_log = jnp.where(
            doc_index[block_size - 1] == 0.0, max_state - block_size * decay_rate, NEGATIVE
        )
        new_max = jnp.maximum(top_key, end_log)
        inner_scale = jnp.exp(top_key - new_max)
        carry_scale = jnp.exp(end_log - new_max)
        new_num = (
            inner_scale * jnp.sum(last_doc * weight_in * value_block, axis=0)
            + carry_scale * num_state
        )
        new_den = inner_scale * jnp.sum(last_doc * weight_in, axis=0) + carry_scale * den_state
        return ((new_num, new_den, new_max), (numerator, denominator, top_log))

    zeros_row = jnp.zeros((features,), jnp.float32)
    initial = (zeros_row, zeros_row, jnp.full((features,), NEGATIVE, jnp.float32))
    pieces = (
        key_rows.reshape(block_count, block_size, features),
        value_rows.reshape(block_count, block_size, features),
        starts.reshape(block_count, block_size),
    )
    summary, (numerator, denominator, top_log) = lax.scan(block_step, initial, pieces)
    return (
        numerator.reshape(tokens, features),
        denominator.reshape(tokens, features),
        top_log.reshape(tokens, features),
        summary,
    )


def with_state(
    numerator, denominator, top_log, state_num, state_den, state_max, carried_dev, decay_rate
):
    steps = jnp.arange(numerator.shape[0], dtype=jnp.float32)[:, None]
    carry_log = jnp.where(carried_dev, state_max - steps * decay_rate, NEGATIVE)
    joint_max = jnp.maximum(top_log, carry_log)
    local_weight = jnp.exp(top_log - joint_max)
    carry_weight = jnp.exp(carry_log - joint_max)
    return (local_weight * numerator + carry_weight * state_num) / (
        local_weight * denominator + carry_weight * state_den
    )


def adam_update(weight, first_moment, second_moment, gradient, step_rate, feature_fade_speed):
    first_moment = BETA_ONE * first_moment + (1.0 - BETA_ONE) * gradient
    second_moment = BETA_TWO * second_moment + (1.0 - BETA_TWO) * gradient * gradient
    first_fixed = first_moment / (1.0 - BETA_ONE**STEP)
    second_fixed = second_moment / (1.0 - BETA_TWO**STEP)
    weight = weight - step_rate * (
        first_fixed / (jnp.sqrt(second_fixed) + ADAM_EPS) + feature_fade_speed * weight
    )
    return (first_moment, second_moment, weight)


def body(
    tokens_in,
    cotangent,
    pad_mask,
    doc_lengths,
    masters,
    moment_one,
    moment_two,
    block_slot,
    vectors,
    vector_one,
    vector_two,
):
    tokens = tokens_in.shape[0]
    features = tokens_in.shape[1]
    devices = lax.axis_size("seq")
    device_place = lax.axis_index("seq")
    offsets = jnp.cumsum(doc_lengths) - doc_lengths
    positions = device_place * tokens + jnp.arange(tokens, dtype=jnp.int32)
    starts = jnp.sum((positions[:, None] == offsets[None, :]).astype(jnp.float32), axis=1)
    keep_rows = (1.0 - starts)[:, None]
    carried_dev = (jnp.cumsum(starts) == 0.0)[:, None]
    zeros_row = jnp.zeros((features,), jnp.float32)
    owned_rows = masters.astype(jnp.bfloat16)
    if devices == GRID_DEVICES:
        gathered = gather_blocks(owned_rows).reshape(-1, BLOCK_ROWS, EMBED_SIZE)
    else:
        gathered = lax.all_gather(owned_rows, "seq", axis=0, tiled=True)
    forward_rows = split_rows(gathered, block_slot)
    key_w, value_w, recept_w, output_w, chan_recept_w, chan_key_w, chan_value_w = forward_rows
    inputs = tokens_in.astype(jnp.float32)
    normed, unit_one, inverse_one = norm_forward(inputs, vectors[0], vectors[1])
    rim_one = shifted(normed[tokens - 1 :], "seq", 1)
    previous = jnp.concatenate([rim_one, normed[:-1]], axis=0) * keep_rows
    in_key = (vectors[2] * normed + (1.0 - vectors[2]) * previous).astype(jnp.bfloat16)
    in_value = (vectors[3] * normed + (1.0 - vectors[3]) * previous).astype(jnp.bfloat16)
    in_recept = (vectors[4] * normed + (1.0 - vectors[4]) * previous).astype(jnp.bfloat16)
    key_rows = product(in_key, key_w)
    value_rows = product(in_value, value_w)
    receptance = product(in_recept, recept_w)
    decay_rate = jnp.exp(vectors[5])
    time_first = vectors[6]
    local_out, head_back = jax.vjp(
        lambda key_arg, value_arg, rate_arg, first_arg: local_pass(
            key_arg, value_arg, starts, rate_arg, first_arg
        ),
        key_rows,
        value_rows,
        decay_rate,
        time_first,
    )
    numerator, denominator, top_log, summary = local_out
    sum_num, sum_den, sum_max = summary
    reset_flag = jnp.max(starts)[None]
    count_row = jnp.full((1,), float(tokens), jnp.float32)
    empty_state = (
        zeros_row,
        zeros_row,
        jnp.full((features,), NEGATIVE, jnp.float32),
        jnp.zeros((1,), jnp.float32),
        jnp.zeros((1,), jnp.float32),
    )

    def merge_state(early, later):
        early_num, early_den, early_max, early_count, early_reset = early
        later_num, later_den, later_max, later_count, later_reset = later
        aged_max = early_max - later_count * decay_rate
        joint_max = jnp.maximum(aged_max, later_max)
        old_weight = jnp.exp(aged_max - joint_max)
        new_weight = jnp.exp(later_max - joint_max)
        restart = later_reset > 0.5
        return (
            jnp.where(restart, later_num, old_weight * early_num + new_weight * later_num),
            jnp.where(restart, later_den, old_weight * early_den + new_weight * later_den),
            jnp.where(restart, later_max, joint_max),
            early_count + later_count,
            jnp.maximum(early_reset, later_reset),
        )

    all_rows = exchange_rows(jnp.stack([sum_num, sum_den, sum_max]), 3)
    offset_rows = offsets // tokens
    has_start = jnp.sum(
        (offset_rows[None, :] == jnp.arange(devices)[:, None]).astype(jnp.float32), axis=1
    )
    summaries = (
        all_rows[:, 0],
        all_rows[:, 1],
        all_rows[:, 2],
        jnp.full((devices, 1), float(tokens), jnp.float32),
        jnp.minimum(has_start, 1.0)[:, None],
    )
    running = lax.associative_scan(merge_state, summaries)
    below_index = jnp.maximum(device_place - 1, 0)
    incoming = tuple(
        (
            jnp.where(
                device_place > 0,
                lax.dynamic_index_in_dim(column, below_index, 0, keepdims=False),
                blank_item,
            )
            for column, blank_item in zip(running, empty_state)
        )
    )
    in_num, in_den, in_max = (incoming[0], incoming[1], incoming[2])
    weighted, tail_back = jax.vjp(
        lambda numer_arg, denom_arg, top_arg, state_num, state_den, rate_arg: with_state(
            numer_arg, denom_arg, top_arg, state_num, state_den, in_max, carried_dev, rate_arg
        ),
        numerator,
        denominator,
        top_log,
        in_num,
        in_den,
        decay_rate,
    )
    gate_one = jax.nn.sigmoid(receptance)
    mixed = (gate_one * weighted).astype(jnp.bfloat16)
    resid = inputs + product(mixed, output_w)
    normed_two, unit_two, inverse_two = norm_forward(resid, vectors[7], vectors[8])
    rim_two = shifted(normed_two[tokens - 1 :], "seq", 1)
    previous_two = jnp.concatenate([rim_two, normed_two[:-1]], axis=0) * keep_rows
    chan_in_key = (vectors[9] * normed_two + (1.0 - vectors[9]) * previous_two).astype(jnp.bfloat16)
    chan_in_recept = (vectors[10] * normed_two + (1.0 - vectors[10]) * previous_two).astype(
        jnp.bfloat16
    )
    hidden_pre = product_back(chan_in_key, chan_key_w)
    squared = jnp.square(jax.nn.relu(hidden_pre)).astype(jnp.bfloat16)
    chan_value = product(squared, chan_value_w)
    gate_two = jax.nn.sigmoid(product(chan_in_recept, chan_recept_w))
    layer_out = (resid + gate_two * chan_value).astype(jnp.bfloat16)
    (
        key_back,
        value_back,
        recept_back,
        output_back,
        chan_recept_back,
        chan_key_back,
        chan_value_back,
    ) = forward_rows
    out_grad = cotangent.astype(jnp.float32) * pad_mask.astype(jnp.float32)[:, None]
    grad_chan_value = (out_grad * gate_two).astype(jnp.bfloat16)
    grad_chan_gate = (out_grad * chan_value * gate_two * (1.0 - gate_two)).astype(jnp.bfloat16)
    grad_squared = product_back(grad_chan_value, chan_value_back)
    grad_hidden = (grad_squared * 2.0 * jax.nn.relu(hidden_pre)).astype(jnp.bfloat16)
    grad_chan_value_w = product_left(squared, grad_chan_value)
    grad_chan_key_w = product_left(grad_hidden, chan_in_key)
    grad_chan_recept_w = product_left(chan_in_recept, grad_chan_gate)
    grad_chan_in_key = product(grad_hidden, chan_key_back)
    grad_chan_in_recept = product_back(grad_chan_gate, chan_recept_back)
    grad_normed_two = vectors[9] * grad_chan_in_key + vectors[10] * grad_chan_in_recept
    grad_previous_two = (1.0 - vectors[9]) * grad_chan_in_key + (
        1.0 - vectors[10]
    ) * grad_chan_in_recept
    spread_two = normed_two - previous_two
    grad_chan_mix_key = jnp.sum(grad_chan_in_key * spread_two, axis=0)
    grad_chan_mix_recept = jnp.sum(grad_chan_in_recept * spread_two, axis=0)
    carried_two = grad_previous_two * keep_rows
    back_rim_two = shifted(carried_two[:1], "seq", -1)
    grad_normed_two = grad_normed_two + jnp.concatenate([carried_two[1:], back_rim_two], axis=0)
    grad_from_two, grad_gain_two, grad_bias_two = norm_backward(
        grad_normed_two, unit_two, inverse_two, vectors[7]
    )
    grad_resid = out_grad + grad_from_two
    grad_attn = grad_resid.astype(jnp.bfloat16)
    grad_output_w = product_left(mixed, grad_attn)
    grad_mixed = product_back(grad_attn, output_back)
    grad_weighted = grad_mixed * gate_one
    grad_recept = (grad_mixed * weighted * gate_one * (1.0 - gate_one)).astype(jnp.bfloat16)
    grad_numer, grad_denom, grad_top, grad_in_num, grad_in_den, grad_rate_tail = tail_back(
        grad_weighted
    )
    lift_scale = jnp.where(in_max > -1e29, jnp.exp(-in_max), 0.0)
    direct_num = grad_in_num * lift_scale
    direct_den = grad_in_den * lift_scale
    multiplier = (1.0 - reset_flag) * jnp.exp(-float(tokens) * decay_rate)
    blank_grad = (zeros_row, zeros_row, jnp.ones((features,), jnp.float32))

    def merge_grad(early, later):
        return (later[0] + later[2] * early[0], later[1] + later[2] * early[1], later[2] * early[2])

    back_rows = exchange_rows(jnp.stack([direct_num, direct_den, multiplier]), 4)
    terms_back = (back_rows[:, 0], back_rows[:, 1], back_rows[:, 2])
    running_back = lax.associative_scan(merge_grad, tuple((column[::-1] for column in terms_back)))
    above_index = jnp.maximum(devices - 2 - device_place, 0)
    onward = tuple(
        (
            jnp.where(
                device_place < devices - 1,
                lax.dynamic_index_in_dim(column, above_index, 0, keepdims=False),
                blank_item,
            )
            for column, blank_item in zip(running_back, blank_grad)
        )
    )
    end_scale = jnp.exp(sum_max)
    out_num = onward[0] * end_scale
    out_den = onward[1] * end_scale
    out_max = (onward[0] * sum_num + onward[1] * sum_den) * end_scale
    grad_key_rows, grad_value_rows, grad_rate_head, grad_first = head_back(
        (grad_numer, grad_denom, grad_top, (out_num, out_den, out_max))
    )
    state_scale = jnp.exp(in_max)
    grad_rate_cross = (
        -float(tokens) * multiplier * (onward[0] * in_num + onward[1] * in_den) * state_scale
    )
    grad_decay = (grad_rate_tail + grad_rate_head + grad_rate_cross) * decay_rate
    grad_key_low = grad_key_rows.astype(jnp.bfloat16)
    grad_value_low = grad_value_rows.astype(jnp.bfloat16)
    grad_key_w = product_left(in_key, grad_key_low)
    grad_value_w = product_left(in_value, grad_value_low)
    grad_recept_w = product_left(in_recept, grad_recept)
    grad_in_key = product_back(grad_key_low, key_back)
    grad_in_value = product_back(grad_value_low, value_back)
    grad_in_recept = product_back(grad_recept, recept_back)
    grad_normed = (
        vectors[2] * grad_in_key + vectors[3] * grad_in_value + vectors[4] * grad_in_recept
    )
    grad_previous = (
        (1.0 - vectors[2]) * grad_in_key
        + (1.0 - vectors[3]) * grad_in_value
        + (1.0 - vectors[4]) * grad_in_recept
    )
    spread_one = normed - previous
    grad_mix_key = jnp.sum(grad_in_key * spread_one, axis=0)
    grad_mix_value = jnp.sum(grad_in_value * spread_one, axis=0)
    grad_mix_recept = jnp.sum(grad_in_recept * spread_one, axis=0)
    carried_one = grad_previous * keep_rows
    back_rim_one = shifted(carried_one[:1], "seq", -1)
    grad_normed = grad_normed + jnp.concatenate([carried_one[1:], back_rim_one], axis=0)
    grad_from_one, grad_gain_one, grad_bias_one = norm_backward(
        grad_normed, unit_one, inverse_one, vectors[0]
    )
    input_grad = grad_resid + grad_from_one
    row_grad = jnp.concatenate(
        [
            grad_key_w,
            grad_value_w,
            grad_recept_w,
            grad_output_w,
            grad_chan_recept_w,
            grad_chan_key_w,
            grad_chan_value_w,
        ],
        axis=0,
    )
    slot_total = masters.shape[0] * devices
    slot_block = (
        jnp.full((slot_total,), BLOCKS, jnp.int32)
        .at[block_slot]
        .set(jnp.arange(BLOCKS, dtype=jnp.int32))
    )
    named = (slot_block < BLOCKS)[:, None, None]
    low_grad = row_grad.astype(jnp.bfloat16).reshape(BLOCKS, BLOCK_ROWS, EMBED_SIZE)
    slot_grad = jnp.where(named, low_grad[jnp.minimum(slot_block, BLOCKS - 1)], 0.0)
    if devices == GRID_DEVICES:
        owner_grad = scatter_blocks(slot_grad.reshape((devices,) + masters.shape))
        owner_grad = owner_grad.astype(jnp.float32)
    else:
        owner_grad = lax.psum_scatter(
            slot_grad.astype(jnp.float32), "seq", scatter_dimension=0, tiled=True
        )
    stacked = jnp.stack(
        [
            grad_gain_one,
            grad_bias_one,
            grad_mix_key,
            grad_mix_value,
            grad_mix_recept,
            grad_decay,
            grad_first,
            grad_gain_two,
            grad_bias_two,
            grad_chan_mix_key,
            grad_chan_mix_recept,
        ]
    )
    vector_grad = lax.psum(stacked, "seq")
    new_one, new_two, new_master = adam_update(
        masters, moment_one, moment_two, owner_grad, MATRIX_RATE, WEIGHT_DECAY
    )
    vector_rates = jnp.array(VECTOR_RATE, jnp.float32)[:, None]
    vector_first, vector_second, vector_next = adam_update(
        vectors, vector_one, vector_two, vector_grad, vector_rates, 0.0
    )
    return (
        layer_out,
        input_grad,
        new_one,
        new_two,
        new_master,
        vector_first,
        vector_second,
        vector_next,
    )


def solution(mesh):
    placed = (
        P("seq", None),
        P("seq", None),
        P("seq"),
        P(),
        P("seq", None, None),
        P("seq", None, None),
        P("seq", None, None),
        P(),
        P(),
        P(),
        P(),
    )
    return jax.shard_map(
        body,
        mesh=mesh,
        in_specs=placed,
        out_specs=(
            P("seq", None),
            P("seq", None),
            P("seq", None, None),
            P("seq", None, None),
            P("seq", None, None),
            P(),
            P(),
            P(),
        ),
        check_vma=False,
    )
```

```python
import functools

import jax
import jax.numpy as jnp
from jax import lax
from jax.experimental import pallas as pl
from jax.experimental.pallas import tpu as pltpu
from jax.sharding import PartitionSpec as P

EMBED_SIZE = 1024
FF = 4096
BLOCK_ROWS = 32
ROWS_ALL = 13312
BLOCKS = 416
STEP = 10
GRID_DEVICES = 32
MESH = pl.DeviceIdType.MESH


NEGATIVE = -1e30
NORM_EPS = 1e-05
BETA_ONE = 0.9
BETA_TWO = 0.999
ADAM_EPS = 1e-08
MATRIX_RATE = 0.05
WEIGHT_DECAY = 0.01
VECTOR_RATE = (0.25, 0.25, 0.25, 0.25, 0.25, 2.0, 0.25, 0.25, 0.25, 0.25, 0.25)


def shifted(block, axis, distance):
    devices = range(lax.axis_size(axis))
    route = [(i - distance, i) for i in devices if i - distance in devices]
    return lax.ppermute(block, axis, route)


def product_back(left_side, right_side):
    return lax.dot_general(
        left_side, right_side, (((1,), (1,)), ((), ())), preferred_element_type=jnp.float32
    )


def product_left(left_side, right_side):
    return lax.dot_general(
        left_side, right_side, (((0,), (0,)), ((), ())), preferred_element_type=jnp.float32
    )


def adam_update(weight, first_moment, second_moment, gradient, step_rate, feature_fade_speed):
    first_moment = BETA_ONE * first_moment + (1.0 - BETA_ONE) * gradient
    second_moment = BETA_TWO * second_moment + (1.0 - BETA_TWO) * gradient * gradient
    first_fixed = first_moment / (1.0 - BETA_ONE**STEP)
    second_fixed = second_moment / (1.0 - BETA_TWO**STEP)
    weight = weight - step_rate * (
        first_fixed / (jnp.sqrt(second_fixed) + ADAM_EPS) + feature_fade_speed * weight
    )
    return (first_moment, second_moment, weight)


def grid_place():
    me = lax.axis_index("seq")
    return me, lax.rem(me, 2), lax.rem(me // 2, 2), lax.rem(me // 4, 2), me // 8

def spans(slots):
    side = 4 * slots // 15
    cuts = [0, side, 2 * side, slots]
    return [(cuts[i], cuts[i + 1] - cuts[i]) for i in range(3)]

def gather_kernel(slots, own_ref, x_ref, grad_ref, out_ref, after_ref, after_grad_ref, before_ref, *scratch):
    send_sem, recv_sem, sib_send, sib_recv, own_sem, halo_send, halo_recv = scratch
    me, core, x, y, z = grid_place()
    sib = me + 1 - 2 * core
    x_peer = me + 2 - 4 * x
    y_peer = me + 4 - 8 * y
    up = me + 8
    down = me - 8
    bar = pltpu.get_barrier_semaphore()
    pl.semaphore_signal(bar, inc=1, device_id=(sib,), device_id_type=MESH)
    pl.semaphore_signal(bar, inc=1, device_id=(x_peer,), device_id_type=MESH)
    pl.semaphore_signal(bar, inc=1, device_id=(y_peer,), device_id_type=MESH)
    @pl.when(z < 3)
    def _():
        pl.semaphore_signal(bar, inc=1, device_id=(up,), device_id_type=MESH)
    @pl.when(z > 0)
    def _():
        pl.semaphore_signal(bar, inc=1, device_id=(down,), device_id_type=MESH)
    more, less = me < GRID_DEVICES - 1, me > 0

    @pl.when(more)
    def _():
        pl.semaphore_signal(bar, inc=1, device_id=(me + 1,), device_id_type=MESH)

    @pl.when(less)
    def _():
        pl.semaphore_signal(bar, inc=1, device_id=(me - 1,), device_id_type=MESH)

    halos = jnp.where(more, 1, 0) + jnp.where(less, 1, 0)
    pl.semaphore_wait(bar, 4 + jnp.where((z > 0) & (z < 3), 1, 0) + halos)
    tokens = x_ref.shape[0]

    def halo_copy(k):
        src, dst, peer = (
            (x_ref.at[pl.ds(0, 16)], after_ref, me - 1),
            (grad_ref.at[pl.ds(0, 16)], after_grad_ref, me - 1),
            (x_ref.at[pl.ds(tokens - 16, 16)], before_ref, me + 1),
        )[k]
        return pltpu.make_async_remote_copy(src_ref=src, dst_ref=dst, send_sem=halo_send.at[k],
            recv_sem=halo_recv.at[k], device_id=(peer,), device_id_type=MESH)
    span = spans(slots)
    targets = (x_peer, y_peer, up, down)

    def chip(cx, cy, cz):
        return (cz * 2 + cy) * 2 + cx

    def view(cx, cy, cz, color, c=None):
        dev = chip(cx, cy, cz) * 2 + (core if c is None else c)
        lo, n = span[color]
        return out_ref.at[dev, pl.ds(lo, n)]

    def send(cx, cy, cz, color, way, own=False):
        lo, n = span[color]
        src = own_ref.at[pl.ds(lo, n)] if own else view(cx, cy, cz, color)
        idx = chip(cx, cy, cz)
        return pltpu.make_async_remote_copy(src_ref=src, dst_ref=view(cx, cy, cz, color),
            send_sem=send_sem.at[idx, color, way], recv_sem=recv_sem.at[idx, color],
            device_id=(targets[way],), device_id_type=MESH)

    def send_sib(cx, cy, cz, color, own=False):
        lo, n = span[color]
        src = own_ref.at[pl.ds(lo, n)] if own else view(cx, cy, cz, color)
        idx = chip(cx, cy, cz)
        return pltpu.make_async_remote_copy(src_ref=src, dst_ref=view(cx, cy, cz, color),
            send_sem=sib_send.at[idx, color], recv_sem=sib_recv.at[idx, color],
            device_id=(sib,), device_id_type=MESH)

    x2, y2 = 1 - x, 1 - y
    pending = []

    def go(copy, cond=None):
        if cond is None:
            copy.start()
        else:
            @pl.when(cond)
            def _():
                copy.start()
        pending.append((copy, cond))

    zup, zdown = z < 3, z > 0
    own_copies = []
    for color in range(3):
        lo, n = span[color]
        cp = pltpu.make_async_copy(own_ref.at[pl.ds(lo, n)], view(x, y, z, color), own_sem.at[color])
        cp.start()
        own_copies.append(cp)
    order = {0: (0, 2, 1), 1: (1, 2, 0)}
    for color in (0, 1, 2):
        go(send(x, y, z, color, 2, True), zup)
        go(send(x, y, z, color, 3, True), zdown)
    for color, way in ((0, 0), (1, 1), (2, 0), (2, 1), (0, 1), (1, 0)):
        go(send(x, y, z, color, way, True))
    for color in range(3):
        go(send_sib(x, y, z, color, True))

    def arrive(cx, cy, cz, color):
        send(cx, cy, cz, color, 0).wait_recv()

    def sibling(cx, cy, cz, color):
        go(send_sib(cx, cy, cz, color))

    is0, is1 = core == 0, core == 1
    px = jnp.where(is0, x2, x)
    py = jnp.where(is0, y, y2)
    qx = jnp.where(is0, x, x2)
    qy = jnp.where(is0, y2, y)
    first = lambda cx, cy, cz: (go(send(cx, cy, cz, 2, 0), is0), go(send(cx, cy, cz, 2, 1), is1))
    last = lambda cx, cy, cz: (go(send(cx, cy, cz, 2, 1), is0), go(send(cx, cy, cz, 2, 0), is1))

    arrive(x2, y, z, 0)
    go(send(x2, y, z, 0, 2), zup)
    go(send(x2, y, z, 0, 3), zdown)
    go(send(x2, y, z, 0, 1))
    sibling(x2, y, z, 0)
    arrive(x, y2, z, 1)
    go(send(x, y2, z, 1, 2), zup)
    go(send(x, y2, z, 1, 3), zdown)
    go(send(x, y2, z, 1, 0))
    sibling(x, y2, z, 1)
    arrive(px, py, z, 2)
    last(px, py, z)
    sibling(px, py, z, 2)

    for dist in (1, 2, 3):
        sides = []
        for sign, fwd, guard_f in ((1, 3, zdown), (-1, 2, zup)):
            q = z + sign * dist
            have = (q >= 0) & (q < 4)
            sides.append((q, fwd, have, guard_f))
        for which in ("c", "a", "b", "a2", "b2"):
            for q, fwd, have, gf in sides:
                @pl.when(have)
                def _(q=q, fwd=fwd, gf=gf, which=which):
                    if which == "c":
                        arrive(x, y, q, 2)
                        cp = send(x, y, q, 2, fwd)
                        pl.when(gf)(lambda: cp.start())
                        for w in (0, 1):
                            send(x, y, q, 2, w).start()
                        send_sib(x, y, q, 2).start()
                    else:
                        color = 0 if which[0] == "a" else 1
                        cx, cy = {"a": (x, y), "b": (x, y), "a2": (x2, y), "b2": (x, y2)}[which]
                        arrive(cx, cy, q, color)
                        cp = send(cx, cy, q, color, fwd)
                        pl.when(gf)(lambda: cp.start())
                        send(cx, cy, q, color, 1 if color == 0 else 0).start()
                        send_sib(cx, cy, q, color).start()
        for q, fwd, have, gf in sides:
            @pl.when(have)
            def _(q=q):
                arrive(px, py, q, 2)
                pl.when(is0)(lambda: send(px, py, q, 2, 1).start())
                pl.when(is1)(lambda: send(px, py, q, 2, 0).start())
                send_sib(px, py, q, 2).start()
        if dist == 1:
            tail_list = [(z, None)]
        else:
            tail_list = []
        def terminal(q):
            for cx, cy, color in ((x, y2, 0), (x2, y2, 0), (x2, y, 1), (x2, y2, 1), (qx, qy, 2), (x2, y2, 2)):
                arrive(cx, cy, q, color)
                send_sib(cx, cy, q, color).start()
        if dist == 1:
            terminal(z)
        else:
            for sign in (1, -1):
                q = z + sign * (dist - 1)
                pl.when((q >= 0) & (q < 4))(lambda q=q: terminal(q))
        if dist == 3:
            for sign in (1, -1):
                q = z + sign * 3
                pl.when((q >= 0) & (q < 4))(lambda q=q: terminal(q))
    @pl.when(less)
    def _():
        for k in (0, 1):
            halo_copy(k).start()

    @pl.when(more)
    def _():
        halo_copy(2).start()

    @pl.when(less)
    def _():
        for k in (0, 1):
            halo_copy(k).wait_send()
        halo_copy(2).wait_recv()

    @pl.when(more)
    def _():
        halo_copy(2).wait_send()
        for k in (0, 1):
            halo_copy(k).wait_recv()

    for cp in own_copies:
        cp.wait()
    for color in range(3):
        pl.when(zup)(lambda color=color: send(x, y, z, color, 2).wait_send())
        pl.when(zdown)(lambda color=color: send(x, y, z, color, 3).wait_send())
        for w in (0, 1):
            send(x, y, z, color, w).wait_send()
    for cx, cy, color, w in ((x2, y, 0, 1), (x, y2, 1, 0)):
        pl.when(zup)(lambda: send(cx, cy, z, color, 2).wait_send())
        pl.when(zdown)(lambda: send(cx, cy, z, color, 3).wait_send())
        send(cx, cy, z, color, w).wait_send()
    pl.when(is0)(lambda: send(px, py, z, 2, 1).wait_send())
    pl.when(is1)(lambda: send(px, py, z, 2, 0).wait_send())
    for dist in (1, 2, 3):
        for sign, fwd, gf in ((1, 3, zdown), (-1, 2, zup)):
            q = z + sign * dist
            @pl.when((q >= 0) & (q < 4))
            def _(q=q, fwd=fwd, gf=gf):
                for cx, cy, color in ((x, y, 2), (x, y, 0), (x, y, 1), (x2, y, 0), (x, y2, 1)):
                    pl.when(gf)(lambda: send(cx, cy, q, color, fwd).wait_send())
                    ways = (0, 1) if color == 2 else ((1,) if color == 0 else (0,))
                    for w in ways:
                        send(cx, cy, q, color, w).wait_send()
                pl.when(is0)(lambda: send(px, py, q, 2, 1).wait_send())
                pl.when(is1)(lambda: send(px, py, q, 2, 0).wait_send())
    for cz in range(4):
        for cy in range(2):
            for cx in range(2):
                for color in range(3):
                    cp = send_sib(cx, cy, cz, color)
                    cp.wait_send()
                    cp.wait_recv()

def gather_blocks(owned, tokens_in, out_grad, cid=1):
    slots = owned.shape[0]
    anywhere = pl.BlockSpec(memory_space=pl.ANY)
    halo = jax.ShapeDtypeStruct((16,) + tokens_in.shape[1:], tokens_in.dtype)
    return pl.pallas_call(
        functools.partial(gather_kernel, slots),
        out_shape=(jax.ShapeDtypeStruct((GRID_DEVICES,) + owned.shape, owned.dtype), halo, halo, halo),
        in_specs=[anywhere] * 3,
        out_specs=(anywhere,) * 4,
        scratch_shapes=[
            pltpu.SemaphoreType.DMA((16, 3, 4)),
            pltpu.SemaphoreType.DMA((16, 3)),
            pltpu.SemaphoreType.DMA((16, 3)),
            pltpu.SemaphoreType.DMA((16, 3)),
            pltpu.SemaphoreType.DMA((3,)),
            pltpu.SemaphoreType.DMA((3,)),
            pltpu.SemaphoreType.DMA((3,)),
        ],
        compiler_params=pltpu.CompilerParams(collective_id=cid, has_side_effects=True),
        name="gather_blocks",
    )(owned, tokens_in, out_grad)


def scatter_kernel(
    slots, part_ref, rows_ref, out_ref, total_ref, acc, sib, xin, yin, zin, sums,
    load_sem, sib_send, sib_recv, send_sem, xsem, ysem, zsem, row_send, row_recv,
):
    me, core, x, y, z = grid_place()
    sibling = me + 1 - 2 * core
    x_peer = me + 2 - 4 * x
    y_peer = me + 4 - 8 * y
    up, down = me + 8, me - 8
    zup, zdown = z < 3, z > 0
    bar = pltpu.get_barrier_semaphore()
    for peer in (sibling, x_peer, y_peer):
        pl.semaphore_signal(bar, inc=1, device_id=(peer,), device_id_type=MESH)
    @pl.when(zup)
    def _():
        pl.semaphore_signal(bar, inc=1, device_id=(up,), device_id_type=MESH)
    @pl.when(zdown)
    def _():
        pl.semaphore_signal(bar, inc=1, device_id=(down,), device_id_type=MESH)
    far = me + 16 - 32 * (z // 2)
    pl.semaphore_signal(bar, inc=1, device_id=(far,), device_id_type=MESH)
    row_peers = (sibling, x_peer, y_peer, me + 8 - 16 * lax.rem(z, 2), far)
    sums[0] = rows_ref[...]
    span = spans(slots)
    x2, y2 = 1 - x, 1 - y
    is0, is1 = core == 0, core == 1

    def row_copy(k):
        return pltpu.make_async_remote_copy(src_ref=sums.at[2 * k], dst_ref=sums.at[2 * k + 1],
            send_sem=row_send.at[k], recv_sem=row_recv.at[k], device_id=(row_peers[k],), device_id_type=MESH)

    def row_step(k):
        row_copy(k).wait()
        sums[2 * k + 2] = sums[2 * k] + sums[2 * k + 1]
        if k < 4:
            row_copy(k + 1).start()

    def load(chip):
        return pltpu.make_async_copy(part_ref.at[2 * chip + core], acc.at[chip], load_sem.at[chip])

    def give(chip):
        return pltpu.make_async_remote_copy(src_ref=part_ref.at[2 * chip + 1 - core], dst_ref=sib.at[chip],
            send_sem=sib_send.at[chip], recv_sem=sib_recv.at[chip], device_id=(sibling,), device_id_type=MESH)

    levels = []
    for dist in (3, 2, 1):
        for sign in (1, -1):
            q = z + sign * dist
            levels.append((dist, sign, q, (q >= 0) & (q < 4)))

    def run(dist, work):
        for d, sign, q, have in levels:
            if d == dist:
                pl.when(have)(functools.partial(work, q))

    def run_signed(dist, work):
        for d, sign, q, have in levels:
            if d == dist:
                pl.when(have)(functools.partial(work, q, sign, dist))

    def begin_loads(q):
        for i in plane_order():
            load(4 * q + i).start()

    def begin_gives(q):
        for i in plane_order():
            give(4 * q + i).start()

    def plane_order():
        return (2 * y2 + x2, 2 * y + x2, 2 * y2 + x, 2 * y + x)

    run(3, begin_loads)
    run(2, begin_loads)
    run(1, begin_loads)
    begin_loads(z)
    pl.semaphore_wait(bar, 5 + jnp.where(zup & zdown, 1, 0))
    row_copy(0).start()
    run(3, begin_gives)
    run(2, begin_gives)

    def ready(cx, cy, q):
        chip = chip_of(cx, cy, q)
        load(chip).wait()
        give(chip).wait_recv()

        def step(s, _):
            total = acc[chip, s].astype(jnp.float32) + sib[chip, s].astype(jnp.float32)
            acc[chip, s] = total.astype(acc.dtype)
            return 0

        lax.fori_loop(0, slots, step, 0)

    def chip_of(cx, cy, cz):
        return (cz * 2 + cy) * 2 + cx

    def out_copy(cx, cy, cz, color, target, buf, index, sem):
        lo, n = span[color]
        chip = chip_of(cx, cy, cz)
        return pltpu.make_async_remote_copy(src_ref=acc.at[chip, pl.ds(lo, n)], dst_ref=buf.at[index, pl.ds(0, n)],
            send_sem=send_sem.at[chip, color], recv_sem=sem.at[index], device_id=(target,), device_id_type=MESH)

    def arrived(buf, index, sem, color):
        lo, n = span[color]
        pltpu.make_async_remote_copy(src_ref=acc.at[0, pl.ds(lo, n)], dst_ref=buf.at[index, pl.ds(0, n)],
            send_sem=send_sem.at[0, color], recv_sem=sem.at[index], device_id=(sibling,), device_id_type=MESH).wait_recv()

    def add(cx, cy, cz, color, pieces):
        lo, n = span[color]
        chip = chip_of(cx, cy, cz)
        for buf, index, sem in pieces:
            arrived(buf, index, sem, color)
        def step(s, _):
            total = acc[chip, lo + s].astype(jnp.float32)
            for buf, index, _sem in pieces:
                total = total + buf[index, s].astype(jnp.float32)
            acc[chip, lo + s] = total.astype(acc.dtype)
            return 0
        lax.fori_loop(0, n, step, 0)

    def X(i): return (xin, i, xsem)
    def Y(i): return (yin, i, ysem)
    def Z(i): return (zin, i, zsem)

    def term_x(q, color, i):
        cy = (y, y2)[i]
        out_copy(x2, cy, q, color, x_peer, xin, (8 if color == 2 else 0) + 2 * q + i, xsem).start()

    def term_y(q, color, i):
        cx = (x, x2)[i]
        out_copy(cx, y2, q, color, y_peer, yin, (8 if color == 2 else 0) + 2 * q + i, ysem).start()

    def term_a(q):
        ready(x2, y2, q)
        term_x(q, 1, 1)
        term_y(q, 0, 1)

    def term_c(q):

        @pl.when(is0)
        def _():
            term_y(q, 2, 1)
            term_y(q, 2, 0)

        @pl.when(is1)
        def _():
            term_x(q, 2, 1)
            term_x(q, 2, 0)

        ready(x, y, q)

    def term_b(q):
        ready(x2, y, q)
        term_x(q, 1, 0)
        ready(x, y2, q)
        term_y(q, 0, 0)

    def plane_two(q):
        @pl.when(is0)
        def _():
            add(x2, y, q, 2, [Y(8 + 2 * q + 1)])
            out_copy(x2, y, q, 2, x_peer, xin, 8 + 2 * q, xsem).start()
        @pl.when(is1)
        def _():
            add(x, y2, q, 2, [X(8 + 2 * q + 1)])
            out_copy(x, y2, q, 2, y_peer, yin, 8 + 2 * q, ysem).start()

    def column(part, q, sign, dist):
        target = up if sign == 1 else down
        more = zdown if sign == 1 else zup
        at_target = dist == 1
        base_out = (20 if (at_target and sign == 1) else 5 * q)
        kinds = (
            (0, x, y, 2, [X(8 + 2 * q), Y(8 + 2 * q)]),
            (1, x, y, 0, [Y(2 * q)]),
            (2, x, y, 1, [X(2 * q)]),
            (3, x2, y, 0, [Y(2 * q + 1)]),
            (4, x, y2, 1, [X(2 * q + 1)]),
        )
        for k, cx, cy, color, pieces in ((kinds[4], kinds[3], kinds[2], kinds[1]), (kinds[0],))[part]:
            @pl.when(more)
            def _():
                add(cx, cy, q, color, pieces + [Z(5 * q + k)])
            @pl.when(jnp.logical_not(more))
            def _():
                add(cx, cy, q, color, pieces)
            out_copy(cx, cy, q, color, target, zin, base_out + k, zsem).start()

    planes = functools.partial(column, 0)
    last = functools.partial(column, 1)
    run(3, term_a)
    run(3, term_b)
    run(3, term_c)
    row_step(0)
    run_signed(3, planes)
    run(2, term_a)
    run(2, term_b)
    run(2, term_c)
    run(3, plane_two)
    run(1, begin_gives)
    run_signed(3, last)
    run(1, term_a)
    run(1, term_b)
    run(1, term_c)
    row_step(1)
    run_signed(2, planes)
    begin_gives(z)
    run(2, plane_two)
    term_a(z)
    term_b(z)
    term_c(z)
    run_signed(2, last)
    row_step(2)
    run_signed(1, planes)
    run(1, plane_two)
    run_signed(1, last)
    row_step(3)
    plane_two(z)
    row_step(4)
    total_ref[...] = sums[10]

    def own(k, cx, cy, color, pieces):
        @pl.when(zup & zdown)
        def _():
            add(cx, cy, z, color, pieces + [Z(5 * z + k), Z(20 + k)])
        @pl.when(zup & jnp.logical_not(zdown))
        def _():
            add(cx, cy, z, color, pieces + [Z(5 * z + k)])
        @pl.when(zdown & jnp.logical_not(zup))
        def _():
            add(cx, cy, z, color, pieces + [Z(20 + k)])
    own(3, x2, y, 0, [Y(2 * z + 1)])
    out_copy(x2, y, z, 0, x_peer, xin, 16, xsem).start()
    own(4, x, y2, 1, [X(2 * z + 1)])
    out_copy(x, y2, z, 1, y_peer, yin, 16, ysem).start()
    own(0, x, y, 2, [X(8 + 2 * z), Y(8 + 2 * z)])
    own(1, x, y, 0, [Y(2 * z), X(16)])
    own(2, x, y, 1, [X(2 * z), Y(16)])
    pltpu.sync_copy(acc.at[chip_of(x, y, z)], out_ref)
    for chip in range(16):
        give(chip).wait_send()
        for color in range(3):
            @pl.when(chip != chip_of(x, y, z))
            def _():
                lo, n = span[color]
                pltpu.make_async_remote_copy(src_ref=acc.at[chip, pl.ds(lo, n)], dst_ref=xin.at[0, pl.ds(0, n)],
                    send_sem=send_sem.at[chip, color], recv_sem=xsem.at[0], device_id=(sibling,), device_id_type=MESH).wait_send()

def scatter_blocks(part, rows, cid=2):
    _, slots, height, feats = part.shape
    most = max(n for _, n in spans(slots))
    chunk = (most, height, feats)
    dt = part.dtype
    return pl.pallas_call(
        functools.partial(scatter_kernel, slots),
        out_shape=(
            jax.ShapeDtypeStruct(part.shape[1:], dt),
            jax.ShapeDtypeStruct(rows.shape, rows.dtype),
        ),
        in_specs=[pl.BlockSpec(memory_space=pl.ANY), pl.BlockSpec(memory_space=pltpu.VMEM)],
        out_specs=(pl.BlockSpec(memory_space=pl.ANY), pl.BlockSpec(memory_space=pltpu.VMEM)),
        scratch_shapes=[
            pltpu.VMEM((16, slots, height, feats), dt),
            pltpu.VMEM((16, slots, height, feats), dt),
            pltpu.VMEM((17,) + chunk, dt),
            pltpu.VMEM((17,) + chunk, dt),
            pltpu.VMEM((25,) + chunk, dt),
            pltpu.VMEM((11,) + rows.shape, rows.dtype),
            pltpu.SemaphoreType.DMA((16,)),
            pltpu.SemaphoreType.DMA((16,)),
            pltpu.SemaphoreType.DMA((16,)),
            pltpu.SemaphoreType.DMA((16, 3)),
            pltpu.SemaphoreType.DMA((17,)),
            pltpu.SemaphoreType.DMA((17,)),
            pltpu.SemaphoreType.DMA((25,)),
            pltpu.SemaphoreType.DMA((5,)),
            pltpu.SemaphoreType.DMA((5,)),
        ],
        compiler_params=pltpu.CompilerParams(collective_id=cid, has_side_effects=True, vmem_limit_bytes=58 * 2**20),
        name="scatter_blocks",
    )(part, rows)


ROW_TILE = 16
CHUNKS = 8
LANES = 128
VMEM_BYTES = 60 * 2**20


def rows_at(index, size=ROW_TILE):
    return pl.ds(pl.multiple_of(index * size, size), size)


def fetch_blocks(slot_ref, pool_ref, store_ref, sem, first_block, place, count):
    def step(b, carry):
        pltpu.make_async_copy(
            pool_ref.at[slot_ref[first_block + b]], store_ref.at[place + b], sem
        ).start()
        return carry

    lax.fori_loop(0, count, step, 0)


def await_blocks(pool_ref, store_ref, sem, place, count):
    pltpu.make_async_copy(
        pool_ref.at[pl.ds(0, count)], store_ref.at[pl.ds(place, count)], sem
    ).wait()


def times_weight(left_ref, store_ref, place, count, write, width=256):
    features = store_ref.shape[2]

    def step(n, carry):
        cols = pl.ds(pl.multiple_of(n * width, width), width)
        right = store_ref[place : place + count, :, cols].reshape(count * BLOCK_ROWS, width)
        write(cols, jnp.dot(left_ref[...], right, preferred_element_type=jnp.float32))
        return carry

    lax.fori_loop(0, features // width, step, 0)


def times_weight_back(left_ref, store_ref, place, count, write, width=256):
    blocks = width // BLOCK_ROWS

    def step(n, carry):
        cols = pl.ds(pl.multiple_of(n * width, width), width)
        right = store_ref[pl.ds(place + n * blocks, blocks)].reshape(width, store_ref.shape[2])
        write(cols, product_back(left_ref[...], right))
        return carry

    lax.fori_loop(0, count // blocks, step, 0)


def weight_gradient(left_ref, right_ref, own, slot_ref, grad_ref, stage, sems, first_block, width=256):
    blocks = width // BLOCK_ROWS
    steps = left_ref.shape[1] // width

    def drain(slot):
        pltpu.make_async_copy(stage.at[slot], grad_ref.at[pl.ds(0, blocks)], sems.at[slot]).wait()

    def step(n, carry):
        slot = lax.rem(n, 2)

        @pl.when(n >= 2)
        def _():
            drain(slot)

        cols = pl.ds(pl.multiple_of(n * width, width), width)
        piece = product_left(left_ref[0:own, cols], right_ref[0:own])
        stage[slot] = piece.astype(stage.dtype).reshape(stage.shape[1:])

        def put(b, inner):
            pltpu.make_async_copy(
                stage.at[slot, b],
                grad_ref.at[slot_ref[first_block + n * blocks + b]],
                sems.at[slot],
            ).start()
            return inner

        return lax.fori_loop(0, blocks, put, carry)

    lax.fori_loop(0, steps, step, 0)
    drain(0)
    drain(1)


def unit_norm(values):
    centered = values - jnp.mean(values, axis=1, keepdims=True)
    inverse = lax.rsqrt(jnp.mean(centered * centered, axis=1, keepdims=True) + NORM_EPS)
    return centered * inverse, inverse


def merge(first, second):
    top = jnp.maximum(first[2], second[2])
    one, two = jnp.exp(first[2] - top), jnp.exp(second[2] - top)
    return (one * first[0] + two * second[0], one * first[1] + two * second[1], top)


def aged(state, distance, alive, rate):
    return (state[0], state[1], jnp.where(alive > 0.5, state[2] - distance * rate, NEGATIVE))


def reset(state, start):
    cut = start > 0.5
    return (
        jnp.where(cut, 0.0, state[0]),
        jnp.where(cut, 0.0, state[1]),
        jnp.where(cut, NEGATIVE, state[2]),
    )


def advance(state, key, value, rate):
    older = state[2] - rate
    top = jnp.maximum(older, key)
    old, new = jnp.exp(older - top), jnp.exp(key - top)
    return (old * state[0] + new * value, old * state[1] + new, top)


def shift_in(ext, own):
    ext[0:8] = jnp.concatenate([ext[own + 10 : own + 11], ext[own : own + 7]], axis=0)


def halo_previous(ext, own, features):
    return jnp.concatenate(
        [
            ext[own + 7 : own + 8],
            ext[own + 8 : own + 9],
            ext[own + 11 : own + 12],
            jnp.zeros((ROW_TILE - 3, features), jnp.float32),
        ],
        axis=0,
    )


def normed_pair(ext, marks_ref, j):
    here = ext[pl.ds(pl.multiple_of(j * ROW_TILE + 8, 8), ROW_TILE)]
    before = ext[rows_at(j)] * marks_ref[rows_at(j), 1:2]
    return here, before


def over_tiles(tiles, work, halo):
    def step(j, carry):
        work(j)
        return carry

    lax.fori_loop(0, tiles - 1, step, 0)
    halo(tiles - 1)


def take_step(wide, first, length):
    at = pl.ds(first, CHUNKS, stride=length)
    return jnp.concatenate([wide[k, at] for k in range(wide.shape[0])], axis=1)


def put_step(wide, first, length, tile):
    at = pl.ds(first, CHUNKS, stride=length)
    lanes = wide.shape[2]
    for k in range(wide.shape[0]):
        wide[k, at] = tile[:, k * lanes : (k + 1) * lanes]


def take_rows(wide, at):
    return jnp.concatenate([wide[k, at] for k in range(wide.shape[0])], axis=1)


def put_rows(wide, at, tile):
    lanes = wide.shape[2]
    for k in range(wide.shape[0]):
        wide[k, at] = tile[:, k * lanes : (k + 1) * lanes]


def none_between(offsets, low, high):
    hit = None
    for offset in offsets:
        inside = (low <= offset) & (offset <= high)
        hit = inside if hit is None else hit | inside
    return jnp.where(hit, 0.0, 1.0)


def write_marks(doc_ref, marks_ref, chunk_ref, link_ref, flag_ref, own, devices):
    rows = marks_ref.shape[0]
    length = own // CHUNKS
    total = own * devices
    me = lax.axis_index("seq")
    first = me * own
    offsets = [jnp.int32(0)]
    for k in range(doc_ref.shape[0] - 1):
        offsets.append(offsets[-1] + doc_ref[k])
    row = lax.broadcasted_iota(jnp.int32, (rows, 1), 0)
    chunk, step = lax.rem(row, CHUNKS), row // CHUNKS
    extra = jnp.where(row < own + 2, row, own - 1 - (row - (own + 2)) - own)
    place = first + jnp.where(row < own, chunk * length + step, extra)
    inside = (place >= 0) & (place < total)
    keep = jnp.where(inside, none_between(offsets, place, place), 0.0)
    begin = first + chunk * length
    marks_ref[:, 0:1] = 1.0 - keep
    marks_ref[:, 1:2] = keep
    marks_ref[:, 2:3] = jnp.where(row < own, none_between(offsets, begin, place), 1.0)
    marks_ref[:, 3:4] = jnp.where(row < own, none_between(offsets, place + 1, begin + length - 1), 1.0)
    chunk = lax.broadcasted_iota(jnp.int32, (CHUNKS, 1), 0)
    begin = first + chunk * length
    end = begin + length - 1
    chunk_ref[:, 0:1] = none_between(offsets, begin, end)
    chunk_ref[:, 1:2] = jnp.where(first > 0, none_between(offsets, first - 1, begin - 1), 0.0)
    chunk_ref[:, 2:3] = none_between(offsets, begin, end - 1)
    chunk_ref[:, 3:4] = (1 + chunk * length).astype(jnp.float32)
    chunk_ref[:, 4:5] = jnp.where(first + own < total, none_between(offsets, end + 1, first + own), 0.0)
    chunk_ref[:, 5:6] = (1 + (CHUNKS - 1 - chunk) * length).astype(jnp.float32)
    count = link_ref.shape[0]
    group = devices // count
    span = own * group
    here = me // group
    other = lax.broadcasted_iota(jnp.int32, (count, 1), 0)
    link_ref[:, 0:1] = jnp.where(other < here, none_between(offsets, span * (other + 1) - 1, span * here - 2), 0.0)
    link_ref[:, 1:2] = (span * (here - 1 - other)).astype(jnp.float32)
    link_ref[:, 2:3] = jnp.where(other > here, none_between(offsets, span * (here + 1) + 1, span * other), 0.0)
    link_ref[:, 3:4] = (span * (other - here - 1)).astype(jnp.float32)
    pair = span * here + jnp.zeros((1, 1), jnp.int32)
    flag_ref[:, 0:1] = none_between(offsets, pair + own - 1, pair + 2 * own - 2)
    flag_ref[:, 1:2] = none_between(offsets, pair - 1, pair + own - 2)
    flag_ref[:, 2:3] = none_between(offsets, pair + 1, pair + own)
    flag_ref[:, 3:4] = none_between(offsets, pair + own + 1, pair + 2 * own)


def open_kernel(
    devices,
    slot_ref, doc_ref, tokens_ref, grads_ref, after_ref, after_grad_ref, before_ref, vec_ref, pool_ref,
    x_ref, grad_ref, marks_ref, chunk_ref, link_ref, flag_ref,
    key_ref, value_ref, recept_ref, num_ref, den_ref, max_ref, in_key, in_value, in_recept, prefix_ref, summary_ref,
    ext, wide, wide_grad, store, sem,
):
    rows, features = x_ref.shape
    own = rows - ROW_TILE
    tiles = rows // ROW_TILE
    length = own // CHUNKS
    per = EMBED_SIZE // BLOCK_ROWS
    for m in range(3):
        fetch_blocks(slot_ref, pool_ref, store, sem.at[m], m * per, m * per, per)
    write_marks(doc_ref, marks_ref, chunk_ref, link_ref, flag_ref, own, devices)
    me = lax.axis_index("seq")

    def widen(j, carry):
        put_rows(wide, rows_at(j), tokens_ref[rows_at(j)].astype(jnp.float32))
        put_rows(wide_grad, rows_at(j), grads_ref[rows_at(j)].astype(jnp.float32))
        return carry

    lax.fori_loop(0, tiles - 1, widen, 0)

    def norm(j, tile):
        x_ref[rows_at(j)] = tile.astype(jnp.bfloat16)
        unit, _ = unit_norm(tile)
        ext[pl.ds(pl.multiple_of(j * ROW_TILE + 8, 8), ROW_TILE)] = unit * vec_ref[0:1] + vec_ref[1:2]

    def arrange(j, carry):
        norm(j, jnp.concatenate([take_step(wide, 2 * j + k, length) for k in range(2)], axis=0))
        pair = [take_step(wide_grad, 2 * j + k, length) for k in range(2)]
        grad_ref[rows_at(j)] = jnp.concatenate(pair, axis=0).astype(jnp.bfloat16)
        return carry

    lax.fori_loop(0, tiles - 1, arrange, 0)
    more, less = me < devices - 1, me > 0
    later = jnp.where(more, after_ref[...].astype(jnp.float32), 0.0)[0:2]
    earlier = jnp.where(less, before_ref[...].astype(jnp.float32), 0.0)
    blank_rows = jnp.zeros((ROW_TILE - 4, features), jnp.float32)
    norm(
        tiles - 1,
        jnp.concatenate([later, earlier[ROW_TILE - 1 :], earlier[ROW_TILE - 2 : ROW_TILE - 1], blank_rows], axis=0),
    )
    later_grad = jnp.where(more, after_grad_ref[...].astype(jnp.float32), 0.0)[0:2]
    grad_ref[own:rows] = jnp.concatenate([later_grad, blank_rows, blank_rows[:2]], axis=0).astype(jnp.bfloat16)
    shift_in(ext, own)

    def mix(j, here, before):
        for row, ref in ((2, in_key), (3, in_value), (4, in_recept)):
            weight = vec_ref[row : row + 1]
            ref[rows_at(j)] = (weight * here + (1.0 - weight) * before).astype(jnp.bfloat16)

    def halo(j):
        here = ext[own + 8 : own + 8 + ROW_TILE]
        before = halo_previous(ext, own, features) * marks_ref[own:rows, 1:2]
        mix(j, here, before)

    over_tiles(tiles, lambda j: mix(j, *normed_pair(ext, marks_ref, j)), halo)
    for m, (left, out) in enumerate(((in_key, key_ref), (in_value, value_ref), (in_recept, recept_ref))):
        await_blocks(pool_ref, store, sem.at[m], m * per, per)

        def write(cols, piece, out=out):
            out[:, cols] = piece

        times_weight(left, store, m * per, per, write)
    rate = jnp.exp(vec_ref[5:6])

    def token(i, state, key, value):
        state = reset(state, marks_ref[rows_at(i, CHUNKS), 0:1])
        num_ref[rows_at(i, CHUNKS)], den_ref[rows_at(i, CHUNKS)], max_ref[rows_at(i, CHUNKS)] = state
        return advance(state, key, value, rate)

    def step(i, state):
        return token(i, state, key_ref[rows_at(i, CHUNKS)], value_ref[rows_at(i, CHUNKS)])

    blank = jnp.zeros((CHUNKS, features), jnp.float32)
    state = lax.fori_loop(0, length - 1, step, (blank, blank, blank + NEGATIVE))
    late = tuple(item[CHUNKS - 1 :] for item in state)
    ends = step(length - 1, state)
    prior = (value_ref[own + 2 : own + 3], jnp.ones((1, features), jnp.float32), key_ref[own + 2 : own + 3])
    for c in range(CHUNKS):
        for k in range(3):
            prefix_ref[k, c : c + 1] = prior[k]
        if c < CHUNKS - 1:
            old = aged(prior, float(length), chunk_ref[c : c + 1, 0:1], rate)
            prior = merge(tuple(item[c : c + 1] for item in ends), old)
    last = merge(late, aged(prior, float(length - 1), chunk_ref[CHUNKS - 1 :, 2:3], rate))
    summary_ref[...] = jnp.concatenate(last, axis=0)


def open_pass(devices, slots, doc_lengths, tokens_in, out_grad, halo, vectors, pool):
    own, features = tokens_in.shape
    rows = own + ROW_TILE
    count = devices // 2 if devices == GRID_DEVICES else devices
    full = jax.ShapeDtypeStruct((rows, features), jnp.float32)
    part = jax.ShapeDtypeStruct((own, features), jnp.float32)
    low = jax.ShapeDtypeStruct((rows, features), jnp.bfloat16)
    small = lambda *shape: jax.ShapeDtypeStruct(shape, jnp.float32)
    vmem = pl.BlockSpec(memory_space=pltpu.VMEM)
    smem = pl.BlockSpec(memory_space=pltpu.SMEM)
    return pl.pallas_call(
        functools.partial(open_kernel, devices),
        out_shape=(
            low, low, small(rows, 4), small(CHUNKS, 6), small(count, 4), small(1, 4),
            full, full, full, part, part, part, low, low, low, small(3, CHUNKS, features), small(3, features),
        ),
        in_specs=[smem] * 2 + [vmem] * 6 + [pl.BlockSpec(memory_space=pl.ANY)],
        out_specs=(vmem,) * 17,
        scratch_shapes=[
            pltpu.VMEM((rows + 8, features), jnp.float32),
            pltpu.VMEM((features // LANES, own, LANES), jnp.float32),
            pltpu.VMEM((features // LANES, own, LANES), jnp.float32),
            pltpu.VMEM((3 * EMBED_SIZE // BLOCK_ROWS, BLOCK_ROWS, features), jnp.bfloat16),
            pltpu.SemaphoreType.DMA((3,)),
        ],
        compiler_params=pltpu.CompilerParams(vmem_limit_bytes=VMEM_BYTES),
        name="open_pass",
    )(slots, doc_lengths, tokens_in, out_grad, *halo, vectors, pool)


def middle_kernel(
    slot_ref, x_ref, grad_ref, vec_ref, marks_ref, chunk_ref, incoming_ref, prefix_ref,
    key_ref, value_ref, recept_ref, num_ref, den_ref, max_ref, pool_ref,
    layer_ref, resid_grad, wkv, gw, full_num, full_den, full_max, own_share, back_num, back_den, back_max,
    recept_grad, suffix_ref, summary_ref, sums_ref, slot_grad,
    mixed, ext, unit, inverse, low_key, low_recept, hidden, squared, value_acc, gate, gcv, gcg, hidden_grad,
    attn_grad, top_log, wide, store, stage, sem, stage_sem,
):
    rows, features = x_ref.shape
    own = rows - ROW_TILE
    tiles = rows // ROW_TILE
    length = own // CHUNKS
    per = EMBED_SIZE // BLOCK_ROWS
    ff = FF // BLOCK_ROWS
    at_out, at_recept, at_key, at_value = 0, per, 2 * per, 2 * per + ff
    fetch_blocks(slot_ref, pool_ref, store, sem.at[0], 3 * per, at_out, per)
    fetch_blocks(slot_ref, pool_ref, store, sem.at[1], 5 * per, at_key, ff)
    fetch_blocks(slot_ref, pool_ref, store, sem.at[2], 5 * per + ff, at_value, ff)
    fetch_blocks(slot_ref, pool_ref, store, sem.at[3], 4 * per, at_recept, per)
    rate = jnp.exp(vec_ref[5:6])
    bonus = vec_ref[6:7]
    incoming = tuple(incoming_ref[k : k + 1] for k in range(3))
    carry = merge(
        tuple(prefix_ref[k] for k in range(3)),
        aged(tuple(jnp.broadcast_to(v, (CHUNKS, features)) for v in incoming), chunk_ref[:, 3:4], chunk_ref[:, 1:2], rate),
    )

    def attend(j, size, state, key, value, recept):
        own_log = bonus + key
        top = jnp.maximum(state[2], own_log)
        old, new = jnp.exp(state[2] - top), jnp.exp(own_log - top)
        scale = 1.0 / (old * state[1] + new)
        out = (old * state[0] + new * value) * scale
        wkv[rows_at(j, size)] = out
        own_share[rows_at(j, size)] = new * scale
        top_log[rows_at(j, size)] = top
        value_acc[rows_at(j, size)] = scale
        ext[rows_at(j, size)] = jax.nn.sigmoid(recept) * out

    def attend_step(i, state_carry):
        at = rows_at(i, CHUNKS)
        alive = marks_ref[at, 2:3]
        distance = jnp.float32(i) if isinstance(i, int) else i.astype(jnp.float32)
        state = merge((num_ref[at], den_ref[at], max_ref[at]), aged(carry, distance, alive, rate))
        full_num[at], full_den[at], full_max[at] = state
        attend(i, CHUNKS, state, key_ref[at], value_ref[at], recept_ref[at])
        return state_carry

    lax.fori_loop(0, length, attend_step, 0)

    def row(ref, r):
        return ref[r : r + 1]

    end = advance(
        (row(full_num, own - 1), row(full_den, own - 1), row(full_max, own - 1)),
        row(key_ref, own - 1), row(value_ref, own - 1), rate,
    )
    halo_one = reset(end, marks_ref[own : own + 1, 0:1])
    halo_two = reset(
        advance(halo_one, row(key_ref, own), row(value_ref, own), rate), marks_ref[own + 1 : own + 2, 0:1]
    )
    halo_zero = reset(incoming, marks_ref[own + 2 : own + 3, 0:1])
    rest = jnp.zeros((ROW_TILE - 3, features), jnp.float32)
    halo_state = tuple(
        jnp.concatenate([halo_one[k], halo_two[k], halo_zero[k], rest + (NEGATIVE if k == 2 else 0.0)], axis=0)
        for k in range(3)
    )
    attend(tiles - 1, ROW_TILE, halo_state, key_ref[own:rows], value_ref[own:rows], recept_ref[own:rows])

    def pack(j, c):
        mixed[rows_at(j)] = ext[rows_at(j)].astype(jnp.bfloat16)
        back_num[rows_at(j)] = value_acc[rows_at(j)]
        return c

    lax.fori_loop(0, tiles, pack, 0)
    await_blocks(pool_ref, store, sem.at[0], at_out, per)

    def write_resid(cols, piece):
        unit[:, cols] = x_ref[:, cols].astype(jnp.float32) + piece

    times_weight(mixed, store, at_out, per, write_resid)

    def norm(j, c):
        resid = unit[rows_at(j)]
        resid_grad[rows_at(j)] = resid
        out, inv = unit_norm(resid)
        unit[rows_at(j)] = out
        inverse[rows_at(j)] = inv
        ext[pl.ds(pl.multiple_of(j * ROW_TILE + 8, 8), ROW_TILE)] = out * vec_ref[7:8] + vec_ref[8:9]
        return c

    lax.fori_loop(0, tiles, norm, 0)
    shift_in(ext, own)

    def mix(j, here, before):
        for r, ref in ((9, low_key), (10, low_recept)):
            weight = vec_ref[r : r + 1]
            ref[rows_at(j)] = (weight * here + (1.0 - weight) * before).astype(jnp.bfloat16)

    def halo_pair():
        here = ext[own + 8 : own + 8 + ROW_TILE]
        return here, halo_previous(ext, own, features) * marks_ref[own:rows, 1:2]

    over_tiles(tiles, lambda j: mix(j, *normed_pair(ext, marks_ref, j)), lambda j: mix(j, *halo_pair()))

    await_blocks(pool_ref, store, sem.at[1], at_key, ff)

    def write_hidden(cols, piece):
        up = jnp.maximum(piece, 0.0)
        hidden[:, cols] = up
        squared[:, cols] = (up * up).astype(jnp.bfloat16)

    times_weight_back(low_key, store, at_key, ff, write_hidden)
    await_blocks(pool_ref, store, sem.at[2], at_value, ff)

    def write_value(cols, piece):
        value_acc[:, cols] = piece

    times_weight(squared, store, at_value, ff, write_value)
    await_blocks(pool_ref, store, sem.at[3], at_recept, per)

    def write_gate(cols, piece):
        gate[:, cols] = piece

    times_weight(low_recept, store, at_recept, per, write_gate)

    def finish(j, c):
        at = rows_at(j)
        opened = jax.nn.sigmoid(gate[at])
        value = value_acc[at]
        out = resid_grad[at] + opened * value

        @pl.when(j < tiles - 1)
        def _():
            for k in range(2):
                put_step(wide, 2 * j + k, length, out[8 * k : 8 * k + 8])

        grad = grad_ref[at].astype(jnp.float32) * opened
        gcv[at] = grad.astype(jnp.bfloat16)
        gcg[at] = (grad * value * (1.0 - opened)).astype(jnp.bfloat16)
        return c

    lax.fori_loop(0, tiles, finish, 0)

    def emit(j, c):
        layer_ref[rows_at(j)] = take_rows(wide, rows_at(j)).astype(jnp.bfloat16)
        return c

    lax.fori_loop(0, tiles - 1, emit, 0)

    def write_hidden_grad(cols, piece):
        hidden_grad[:, cols] = (piece * (2.0 * hidden[:, cols])).astype(jnp.bfloat16)

    times_weight_back(gcv, store, at_value, ff, write_hidden_grad)
    weight_gradient(squared, gcv, own, slot_ref, slot_grad, stage, stage_sem, 5 * per + ff)
    weight_gradient(hidden_grad, low_key, own, slot_ref, slot_grad, stage, stage_sem, 5 * per)
    weight_gradient(low_recept, gcg, own, slot_ref, slot_grad, stage, stage_sem, 4 * per)
    times_weight(hidden_grad, store, at_key, ff, write_value)
    times_weight_back(gcg, store, at_recept, per, write_gate)
    carried = hidden.at[:, 0:features]
    mix_key, mix_recept = vec_ref[9:10], vec_ref[10:11]

    def carry_over(j, c):
        at = rows_at(j)
        carried[at] = marks_ref[at, 1:2] * ((1.0 - mix_key) * value_acc[at] + (1.0 - mix_recept) * gate[at])
        return c

    lax.fori_loop(0, tiles, carry_over, 0)
    halo_next = jnp.concatenate(
        [carried[own + 1 : own + 2], jnp.zeros((ROW_TILE - 1, features), jnp.float32)], axis=0
    )
    carried[own : own + 8] = jnp.concatenate([carried[1:8], carried[own : own + 1]], axis=0)

    def norm_back(j, following):
        at = rows_at(j)
        grad = mix_key * value_acc[at] + mix_recept * gate[at] + following
        scaled = grad * vec_ref[7:8]
        inner = (
            scaled
            - jnp.mean(scaled, axis=1, keepdims=True)
            - unit[at] * jnp.mean(scaled * unit[at], axis=1, keepdims=True)
        )
        total = grad_ref[at].astype(jnp.float32) + inner * inverse[at]
        resid_grad[at] = total
        attn_grad[at] = total.astype(jnp.bfloat16)
        return grad

    def fold(piece):
        return piece[:8] + piece[8:]

    def back_step(j, sums):
        at = rows_at(j)
        grad = norm_back(j, carried[pl.ds(pl.multiple_of(j * ROW_TILE + 8, 8), ROW_TILE)])
        here, before = normed_pair(ext, marks_ref, j)
        spread = here - before
        return (
            sums[0] + fold(grad * unit[at]),
            sums[1] + fold(grad),
            sums[2] + fold(value_acc[at] * spread),
            sums[3] + fold(gate[at] * spread),
        )

    blank = jnp.zeros((CHUNKS, features), jnp.float32)
    sums = lax.fori_loop(0, tiles - 1, back_step, (blank,) * 4)
    for k in range(4):
        sums_ref[k : k + 1] = jnp.sum(sums[k], axis=0, keepdims=True)
    norm_back(tiles - 1, halo_next)

    weight_gradient(mixed, attn_grad, own, slot_ref, slot_grad, stage, stage_sem, 3 * per)
    times_weight_back(attn_grad, store, at_out, per, write_gate)

    def gate_back(j, c):
        at = rows_at(j)
        opened = jax.nn.sigmoid(recept_ref[at])
        grad = gate[at] * opened
        gw[at] = grad
        recept_grad[at] = (grad * wkv[at] * (1.0 - opened)).astype(jnp.bfloat16)
        ext[at] = grad * back_num[at]
        return c

    lax.fori_loop(0, tiles, gate_back, 0)

    def back_token(state, share, out, top, start):
        older = state[2] - rate
        high = jnp.maximum(older, -top)
        old, new = jnp.exp(older - high), jnp.exp(-top - high)
        return reset((old * state[0] + new * share, old * state[1] - new * share * out, high), start)

    def back_scan(n, state):
        i = length - 1 - n
        at = rows_at(i, CHUNKS)
        back_num[at], back_den[at], back_max[at] = state
        return back_token(state, ext[at], wkv[at], top_log[at], marks_ref[at, 0:1])

    heads = lax.fori_loop(0, length, back_scan, (blank, blank, blank + NEGATIVE))
    for ref in (back_num, back_den, back_max):
        ref[own:rows] = jnp.zeros((ROW_TILE, features), jnp.float32)
    nothing = jnp.zeros((1, features), jnp.float32)
    after = back_token(
        (nothing, nothing, nothing + NEGATIVE),
        row(ext, own), row(wkv, own), row(top_log, own), marks_ref[own : own + 1, 0:1],
    )
    for c in range(CHUNKS - 1, -1, -1):
        for k in range(3):
            suffix_ref[k, c : c + 1] = after[k]
        if c > 0:
            old = aged(after, float(length), chunk_ref[c : c + 1, 0:1], rate)
            after = merge(tuple(item[c : c + 1] for item in heads), old)
    first = (row(back_num, 0), row(back_den, 0), row(back_max, 0))
    last = merge(first, aged(after, float(length - 1), marks_ref[0:1, 3:4], rate))
    summary_ref[...] = jnp.concatenate(last, axis=0)


def middle_pass(slots, x_rows, grad_rows, vectors, marks, chunk_marks, incoming, opened, pool):
    key, value, recept, num, den, top, prefix = opened
    rows, features = x_rows.shape
    own = rows - ROW_TILE
    full = jax.ShapeDtypeStruct((rows, features), jnp.float32)
    part = jax.ShapeDtypeStruct((own, features), jnp.float32)
    low = jax.ShapeDtypeStruct((rows, features), jnp.bfloat16)
    vmem = pl.BlockSpec(memory_space=pltpu.VMEM)
    anywhere = pl.BlockSpec(memory_space=pl.ANY)
    f32 = lambda *shape: pltpu.VMEM(shape, jnp.float32)
    b16 = lambda *shape: pltpu.VMEM(shape, jnp.bfloat16)
    return pl.pallas_call(
        middle_kernel,
        out_shape=(
            jax.ShapeDtypeStruct((own, features), jnp.bfloat16),
            full, full, full, part, part, part, full, full, full, full, low,
            jax.ShapeDtypeStruct((3, CHUNKS, features), jnp.float32),
            jax.ShapeDtypeStruct((3, features), jnp.float32),
            jax.ShapeDtypeStruct((4, features), jnp.float32),
            jax.ShapeDtypeStruct(pool.shape, jnp.bfloat16),
        ),
        in_specs=[pl.BlockSpec(memory_space=pltpu.SMEM)] + [vmem] * 13 + [anywhere],
        out_specs=(vmem,) * 15 + (anywhere,),
        scratch_shapes=[
            b16(rows, features),
            f32(rows + 8, features),
            f32(rows, features),
            f32(rows, 1),
            b16(rows, features),
            b16(rows, features),
            f32(rows, FF),
            b16(rows, FF),
            f32(rows, features),
            f32(rows, features),
            b16(rows, features),
            b16(rows, features),
            b16(rows, FF),
            b16(rows, features),
            f32(rows, features),
            f32(features // LANES, own, LANES),
            b16((2 * EMBED_SIZE + 2 * FF) // BLOCK_ROWS, BLOCK_ROWS, features),
            b16(2, 256 // BLOCK_ROWS, BLOCK_ROWS, features),
            pltpu.SemaphoreType.DMA((4,)),
            pltpu.SemaphoreType.DMA((2,)),
        ],
        compiler_params=pltpu.CompilerParams(vmem_limit_bytes=VMEM_BYTES),
        name="middle_pass",
    )(slots, x_rows, grad_rows, vectors, marks, chunk_marks, incoming, prefix, key, value, recept, num, den, top, pool)


def close_kernel(
    slot_ref, x_ref, vec_ref, marks_ref, chunk_ref, incoming_ref, suffix_ref, key_ref, value_ref,
    in_key, in_value, in_recept, resid_grad, wkv, gw, full_num, full_den, full_max, own_share,
    back_num, back_den, back_max, recept_grad, sums_two_ref, pool_ref, grads_in,
    input_ref, sums_ref, slot_grad,
    ext, unit, inverse, key_wide, value_wide, key_grad, value_grad, grad_key_in, grad_value_in, grad_recept_in,
    carried, wide, store, stage, sem, stage_sem,
):
    rows, features = x_ref.shape
    own = rows - ROW_TILE
    tiles = rows // ROW_TILE
    length = own // CHUNKS
    per = EMBED_SIZE // BLOCK_ROWS
    for m in range(3):
        fetch_blocks(slot_ref, pool_ref, store, sem.at[m], m * per, m * per, per)
    rate = jnp.exp(vec_ref[5:6])
    incoming = tuple(incoming_ref[k : k + 1] for k in range(3))
    carry = merge(
        tuple(suffix_ref[k] for k in range(3)),
        aged(tuple(jnp.broadcast_to(v, (CHUNKS, features)) for v in incoming), chunk_ref[:, 5:6], chunk_ref[:, 4:5], rate),
    )

    def spread_back(state, key, value, share, grad, out):
        direct = share * grad
        bonus_grad = direct * (value - out)
        lift = jnp.exp(key + state[2])
        return bonus_grad + lift * (state[0] * value + state[1]), direct + lift * state[0], bonus_grad

    def token(i, sums):
        at = rows_at(i, CHUNKS)
        distance = (length - 1 - i).astype(jnp.float32)
        state = merge((back_num[at], back_den[at], back_max[at]), aged(carry, distance, marks_ref[at, 3:4], rate))
        key_g, value_g, bonus_grad = spread_back(state, key_ref[at], value_ref[at], own_share[at], gw[at], wkv[at])
        key_wide[at] = key_g
        value_wide[at] = value_g
        fade = jnp.exp(state[2] + full_max[at] - rate) * (state[0] * full_num[at] + state[1] * full_den[at])
        return sums[0] + fade, sums[1] + bonus_grad

    blank = jnp.zeros((CHUNKS, features), jnp.float32)
    fade, bonus_sum = lax.fori_loop(0, length, token, (blank, blank))
    sums_ref[5:6] = -rate * jnp.sum(fade, axis=0, keepdims=True)
    sums_ref[6:7] = jnp.sum(bonus_sum, axis=0, keepdims=True)
    halo = tuple(
        jnp.concatenate([incoming[k], jnp.zeros((ROW_TILE - 1, features), jnp.float32) + (NEGATIVE if k == 2 else 0.0)], axis=0)
        for k in range(3)
    )
    key_g, value_g, _ = spread_back(
        halo, key_ref[own:rows], value_ref[own:rows], own_share[own:rows], gw[own:rows], wkv[own:rows]
    )
    key_wide[own:rows] = key_g
    value_wide[own:rows] = value_g

    def pack(j, c):
        at = rows_at(j)
        key_grad[at] = key_wide[at].astype(jnp.bfloat16)
        value_grad[at] = value_wide[at].astype(jnp.bfloat16)
        return c

    lax.fori_loop(0, tiles, pack, 0)
    weight_gradient(in_recept, recept_grad, own, slot_ref, slot_grad, stage, stage_sem, 2 * per)
    weight_gradient(in_key, key_grad, own, slot_ref, slot_grad, stage, stage_sem, 0)
    weight_gradient(in_value, value_grad, own, slot_ref, slot_grad, stage, stage_sem, per)
    for m, (left, out) in enumerate(((key_grad, grad_key_in), (value_grad, grad_value_in), (recept_grad, grad_recept_in))):
        await_blocks(pool_ref, store, sem.at[m], m * per, per)

        def write(cols, piece, out=out):
            out[:, cols] = piece

        times_weight_back(left, store, m * per, per, write)

    def norm(j, c):
        out, inv = unit_norm(x_ref[rows_at(j)].astype(jnp.float32))
        unit[rows_at(j)] = out
        inverse[rows_at(j)] = inv
        ext[pl.ds(pl.multiple_of(j * ROW_TILE + 8, 8), ROW_TILE)] = out * vec_ref[0:1] + vec_ref[1:2]
        return c

    lax.fori_loop(0, tiles, norm, 0)
    shift_in(ext, own)
    mixes = tuple(vec_ref[k : k + 1] for k in (2, 3, 4))

    def carry_over(j, c):
        at = rows_at(j)
        total = (1.0 - mixes[0]) * grad_key_in[at] + (1.0 - mixes[1]) * grad_value_in[at] + (1.0 - mixes[2]) * grad_recept_in[at]
        carried[at] = marks_ref[at, 1:2] * total
        return c

    lax.fori_loop(0, tiles, carry_over, 0)
    carried[own : own + 8] = jnp.concatenate([carried[1:8], carried[own : own + 1]], axis=0)

    def fold(piece):
        return piece[:8] + piece[8:]

    def back_step(j, sums):
        at = rows_at(j)
        grads = (grad_key_in[at], grad_value_in[at], grad_recept_in[at])
        grad = carried[pl.ds(pl.multiple_of(j * ROW_TILE + 8, 8), ROW_TILE)]
        for weight, piece in zip(mixes, grads):
            grad = grad + weight * piece
        scaled = grad * vec_ref[0:1]
        inner = (
            scaled
            - jnp.mean(scaled, axis=1, keepdims=True)
            - unit[at] * jnp.mean(scaled * unit[at], axis=1, keepdims=True)
        )
        out = resid_grad[at] + inner * inverse[at]
        for k in range(2):
            put_step(wide, 2 * j + k, length, out[8 * k : 8 * k + 8])
        here, before = normed_pair(ext, marks_ref, j)
        spread = here - before
        return (sums[0] + fold(grad * unit[at]), sums[1] + fold(grad)) + tuple(
            s + fold(piece * spread) for s, piece in zip(sums[2:], grads)
        )

    sums = lax.fori_loop(0, tiles - 1, back_step, (blank,) * 5)
    for k in range(5):
        sums_ref[k : k + 1] = jnp.sum(sums[k], axis=0, keepdims=True)
    sums_ref[7:] = sums_two_ref[...]

    def emit(j, c):
        input_ref[rows_at(j)] = take_rows(wide, rows_at(j))
        return c

    lax.fori_loop(0, tiles - 1, emit, 0)


def close_pass(slots, x_rows, vectors, marks, chunk_marks, incoming, suffix, key, value, lows, kept, pool, slot_grad):
    rows, features = x_rows.shape
    own = rows - ROW_TILE
    vmem = pl.BlockSpec(memory_space=pltpu.VMEM)
    anywhere = pl.BlockSpec(memory_space=pl.ANY)
    f32 = lambda *shape: pltpu.VMEM(shape, jnp.float32)
    b16 = lambda *shape: pltpu.VMEM(shape, jnp.bfloat16)
    operands = (slots, x_rows, vectors, marks, chunk_marks, incoming, suffix, key, value) + lows + kept + (pool, slot_grad)
    return pl.pallas_call(
        close_kernel,
        out_shape=(
            jax.ShapeDtypeStruct((own, features), jnp.float32),
            jax.ShapeDtypeStruct(vectors.shape, jnp.float32),
            jax.ShapeDtypeStruct(pool.shape, jnp.bfloat16),
        ),
        in_specs=[pl.BlockSpec(memory_space=pltpu.SMEM)] + [vmem] * (len(operands) - 3) + [anywhere] * 2,
        out_specs=(vmem, vmem, anywhere),
        input_output_aliases={len(operands) - 1: 2},
        scratch_shapes=[
            f32(rows + 8, features),
            f32(rows, features),
            f32(rows, 1),
            f32(rows, features),
            f32(rows, features),
            b16(rows, features),
            b16(rows, features),
            f32(rows, features),
            f32(rows, features),
            f32(rows, features),
            f32(rows, features),
            f32(features // LANES, own, LANES),
            b16(3 * EMBED_SIZE // BLOCK_ROWS, BLOCK_ROWS, features),
            b16(2, 256 // BLOCK_ROWS, BLOCK_ROWS, features),
            pltpu.SemaphoreType.DMA((3,)),
            pltpu.SemaphoreType.DMA((2,)),
        ],
        compiler_params=pltpu.CompilerParams(vmem_limit_bytes=VMEM_BYTES),
        name="close_pass",
    )(*operands)


def chain_kernel(forward, tokens, own_ref, vec_ref, link_ref, flag_ref, out_ref, near, chips, joint, send_sem, recv_sem):
    me, core, _, _, _ = grid_place()
    chip = me // 2
    count = GRID_DEVICES // 2
    sign = 1 if forward else -1
    before = chip if forward else count - 1 - chip
    sibling = me + 1 - 2 * core
    chips[...] = jnp.zeros_like(chips)
    bar = pltpu.get_barrier_semaphore()
    pl.semaphore_signal(bar, inc=1, device_id=(sibling,), device_id_type=MESH)
    for o in range(1, count):
        @pl.when(o <= before)
        def _():
            pl.semaphore_signal(bar, inc=1, device_id=(me - 2 * sign * o,), device_id_type=MESH)
    pl.semaphore_wait(bar, count - before)
    swap = pltpu.make_async_remote_copy(
        src_ref=own_ref, dst_ref=near, send_sem=send_sem.at[0], recv_sem=recv_sem.at[0],
        device_id=(sibling,), device_id_type=MESH,
    )
    swap.start()
    rate = jnp.exp(vec_ref[5:6])
    at = 0 if forward else 2
    swap.wait()
    mine = tuple(own_ref[k : k + 1] for k in range(3))
    other = tuple(near[k : k + 1] for k in range(3))
    second = (core == 1) if forward else (core == 0)
    one = tuple(jnp.where(second, b, a) for a, b in zip(mine, other))
    two = tuple(jnp.where(second, a, b) for a, b in zip(mine, other))
    joint[...] = jnp.concatenate(merge(two, aged(one, float(tokens), flag_ref[0:1, at : at + 1], rate)), axis=0)

    def copy(o, place, peer):
        return pltpu.make_async_remote_copy(
            src_ref=joint, dst_ref=chips.at[place], send_sem=send_sem.at[o], recv_sem=recv_sem.at[o],
            device_id=(peer,), device_id_type=MESH,
        )

    for o in range(1, count):
        @pl.when(o < count - before)
        def _():
            copy(o, chip, me + 2 * sign * o).start()
    for o in range(1, count):
        @pl.when(o <= before)
        def _():
            copy(o, chip - sign * o, sibling).wait_recv()
    logs = jnp.where(link_ref[:, at : at + 1] > 0.5, chips[:, 2] - link_ref[:, at + 1 : at + 2] * rate, NEGATIVE)
    top = jnp.max(logs, axis=0, keepdims=True)
    weight = jnp.exp(logs - top)
    prior = (
        jnp.sum(weight * chips[:, 0], axis=0, keepdims=True),
        jnp.sum(weight * chips[:, 1], axis=0, keepdims=True),
        top,
    )
    beside = merge(one, aged(prior, float(tokens), flag_ref[0:1, at + 1 : at + 2], rate))
    out_ref[...] = jnp.concatenate([jnp.where(second, b, a) for a, b in zip(prior, beside)], axis=0)
    for o in range(1, count):
        @pl.when(o < count - before)
        def _():
            copy(o, chip, me + 2 * sign * o).wait_send()


def chain_state(rows, vectors, links, flags, forward, tokens, cid):
    devices = lax.axis_size("seq")
    if devices != GRID_DEVICES:
        every = lax.all_gather(rows[None], "seq", axis=0, tiled=True)
        at = 0 if forward else 2
        aged_logs = every[:, 2] - links[:, at + 1 : at + 2] * jnp.exp(vectors[5])
        logs = jnp.where(links[:, at : at + 1] > 0.5, aged_logs, NEGATIVE)
        top = jnp.max(logs, axis=0)
        weight = jnp.exp(logs - top)
        return jnp.stack([jnp.sum(weight * every[:, 0], axis=0), jnp.sum(weight * every[:, 1], axis=0), top])
    count = devices // 2
    vmem = pl.BlockSpec(memory_space=pltpu.VMEM)
    return pl.pallas_call(
        functools.partial(chain_kernel, forward, tokens),
        out_shape=jax.ShapeDtypeStruct(rows.shape, jnp.float32),
        in_specs=[vmem] * 4,
        out_specs=vmem,
        scratch_shapes=[
            pltpu.VMEM(rows.shape, jnp.float32),
            pltpu.VMEM((count,) + rows.shape, jnp.float32),
            pltpu.VMEM(rows.shape, jnp.float32),
            pltpu.SemaphoreType.DMA((count,)),
            pltpu.SemaphoreType.DMA((count,)),
        ],
        compiler_params=pltpu.CompilerParams(collective_id=cid, has_side_effects=True),
        name="chain_forward" if forward else "chain_backward",
    )(rows, vectors, links, flags)


def body(
    tokens_in,
    cotangent,
    pad_mask,
    doc_lengths,
    masters,
    moment_one,
    moment_two,
    block_slot,
    vectors,
    vector_one,
    vector_two,
):
    tokens, features = tokens_in.shape
    devices = lax.axis_size("seq")
    device_place = lax.axis_index("seq")
    owned_rows = masters.astype(jnp.bfloat16)
    out_grad = cotangent * pad_mask.astype(cotangent.dtype)[:, None]
    if devices == GRID_DEVICES:
        gathered, *halo = gather_blocks(owned_rows, tokens_in, out_grad)
        gathered = gathered.reshape(-1, BLOCK_ROWS, features)
    else:
        gathered = lax.all_gather(owned_rows, "seq", axis=0, tiled=True)
        halo = [
            shifted(tokens_in[:ROW_TILE], "seq", -1),
            shifted(out_grad[:ROW_TILE], "seq", -1),
            shifted(tokens_in[tokens - ROW_TILE :], "seq", 1),
        ]
    (
        x_rows, grad_rows, marks, chunk_marks, links, flags,
        key, value, recept, num, den, top, in_key, in_value, in_recept, prefix, summary,
    ) = open_pass(devices, block_slot, doc_lengths, tokens_in, out_grad, halo, vectors, gathered)
    incoming = chain_state(summary, vectors, links, flags, True, tokens, 3)
    (
        layer_out, resid_grad, wkv, gw, full_num, full_den, full_max, own_share, back_num, back_den, back_max,
        recept_grad, suffix, back_summary, sums_two, slot_grad,
    ) = middle_pass(
        block_slot, x_rows, grad_rows, vectors, marks, chunk_marks, incoming,
        (key, value, recept, num, den, top, prefix), gathered,
    )
    back_incoming = chain_state(back_summary, vectors, links, flags, False, tokens, 4)
    input_grad, stacked, slot_grad = close_pass(
        block_slot, x_rows, vectors, marks, chunk_marks, back_incoming, suffix, key, value,
        (in_key, in_value, in_recept),
        (resid_grad, wkv, gw, full_num, full_den, full_max, own_share, back_num, back_den, back_max, recept_grad, sums_two),
        gathered, slot_grad,
    )
    own_slots = device_place * masters.shape[0] + jnp.arange(masters.shape[0], dtype=jnp.int32)
    named = jnp.any(own_slots[:, None] == block_slot[None, :], axis=1)
    if devices == GRID_DEVICES:
        owner_grad, vector_grad = scatter_blocks(slot_grad.reshape((devices,) + masters.shape), stacked)
        owner_grad = owner_grad.astype(jnp.float32)
    else:
        owner_grad = lax.psum_scatter(
            slot_grad.astype(jnp.float32), "seq", scatter_dimension=0, tiled=True
        )
        vector_grad = lax.psum(stacked, "seq")
    owner_grad = jnp.where(named[:, None, None], owner_grad, 0.0)
    new_one, new_two, new_master = adam_update(
        masters, moment_one, moment_two, owner_grad, MATRIX_RATE, WEIGHT_DECAY
    )
    vector_rates = jnp.array(VECTOR_RATE, jnp.float32)[:, None]
    vector_first, vector_second, vector_next = adam_update(
        vectors, vector_one, vector_two, vector_grad, vector_rates, 0.0
    )
    return (
        layer_out,
        input_grad,
        new_one,
        new_two,
        new_master,
        vector_first,
        vector_second,
        vector_next,
    )


def solution(mesh):
    placed = (
        P("seq", None),
        P("seq", None),
        P("seq"),
        P(),
        P("seq", None, None),
        P("seq", None, None),
        P("seq", None, None),
        P(),
        P(),
        P(),
        P(),
    )
    return jax.shard_map(
        body,
        mesh=mesh,
        in_specs=placed,
        out_specs=(
            P("seq", None),
            P("seq", None),
            P("seq", None, None),
            P("seq", None, None),
            P("seq", None, None),
            P(),
            P(),
            P(),
        ),
        check_vma=False,
    )
```

```python
import functools

import jax
import jax.numpy as jnp
from jax import lax
from jax.experimental import pallas as pl
from jax.experimental.pallas import tpu as pltpu
from jax.sharding import PartitionSpec as P

EMBED_SIZE = 1024
FF = 4096
BLOCK_ROWS = 32
ROWS_ALL = 13312
BLOCKS = 416
STEP = 10
GRID_DEVICES = 32
MESH = pl.DeviceIdType.MESH


NEGATIVE = -1e30
NORM_EPS = 1e-05
BETA_ONE = 0.9
BETA_TWO = 0.999
ADAM_EPS = 1e-08
MATRIX_RATE = 0.05
WEIGHT_DECAY = 0.01
VECTOR_RATE = (0.25, 0.25, 0.25, 0.25, 0.25, 2.0, 0.25, 0.25, 0.25, 0.25, 0.25)


def shifted(block, axis, distance):
    devices = range(lax.axis_size(axis))
    route = [(i - distance, i) for i in devices if i - distance in devices]
    return lax.ppermute(block, axis, route)


def product_back(left_side, right_side):
    return lax.dot_general(
        left_side, right_side, (((1,), (1,)), ((), ())), preferred_element_type=jnp.float32
    )


def product_left(left_side, right_side):
    return lax.dot_general(
        left_side, right_side, (((0,), (0,)), ((), ())), preferred_element_type=jnp.float32
    )


def adam_update(weight, first_moment, second_moment, gradient, step_rate, feature_fade_speed):
    first_moment = BETA_ONE * first_moment + (1.0 - BETA_ONE) * gradient
    second_moment = BETA_TWO * second_moment + (1.0 - BETA_TWO) * gradient * gradient
    first_fixed = first_moment / (1.0 - BETA_ONE**STEP)
    second_fixed = second_moment / (1.0 - BETA_TWO**STEP)
    weight = weight - step_rate * (
        first_fixed / (jnp.sqrt(second_fixed) + ADAM_EPS) + feature_fade_speed * weight
    )
    return (first_moment, second_moment, weight)


def grid_place():
    me = lax.axis_index("seq")
    return me, lax.rem(me, 2), lax.rem(me // 2, 2), lax.rem(me // 4, 2), me // 8

def spans(slots):
    side = 4 * slots // 15
    cuts = [0, side, 2 * side, slots]
    return [(cuts[i], cuts[i + 1] - cuts[i]) for i in range(3)]

def gather_kernel(slots, own_ref, x_ref, grad_ref, out_ref, after_ref, after_grad_ref, before_ref, *scratch):
    send_sem, recv_sem, sib_send, sib_recv, own_sem, halo_send, halo_recv = scratch
    me, core, x, y, z = grid_place()
    sib = me + 1 - 2 * core
    x_peer = me + 2 - 4 * x
    y_peer = me + 4 - 8 * y
    up = me + 8
    down = me - 8
    bar = pltpu.get_barrier_semaphore()
    pl.semaphore_signal(bar, inc=1, device_id=(sib,), device_id_type=MESH)
    pl.semaphore_signal(bar, inc=1, device_id=(x_peer,), device_id_type=MESH)
    pl.semaphore_signal(bar, inc=1, device_id=(y_peer,), device_id_type=MESH)
    @pl.when(z < 3)
    def _():
        pl.semaphore_signal(bar, inc=1, device_id=(up,), device_id_type=MESH)
    @pl.when(z > 0)
    def _():
        pl.semaphore_signal(bar, inc=1, device_id=(down,), device_id_type=MESH)
    more, less = me < GRID_DEVICES - 1, me > 0

    @pl.when(more)
    def _():
        pl.semaphore_signal(bar, inc=1, device_id=(me + 1,), device_id_type=MESH)

    @pl.when(less)
    def _():
        pl.semaphore_signal(bar, inc=1, device_id=(me - 1,), device_id_type=MESH)

    halos = jnp.where(more, 1, 0) + jnp.where(less, 1, 0)
    pl.semaphore_wait(bar, 4 + jnp.where((z > 0) & (z < 3), 1, 0) + halos)
    tokens = x_ref.shape[0]

    def halo_copy(k):
        src, dst, peer = (
            (x_ref.at[pl.ds(0, 16)], after_ref, me - 1),
            (grad_ref.at[pl.ds(0, 16)], after_grad_ref, me - 1),
            (x_ref.at[pl.ds(tokens - 16, 16)], before_ref, me + 1),
        )[k]
        return pltpu.make_async_remote_copy(src_ref=src, dst_ref=dst, send_sem=halo_send.at[k],
            recv_sem=halo_recv.at[k], device_id=(peer,), device_id_type=MESH)
    span = spans(slots)
    targets = (x_peer, y_peer, up, down)

    def chip(cx, cy, cz):
        return (cz * 2 + cy) * 2 + cx

    def view(cx, cy, cz, color, c=None):
        dev = chip(cx, cy, cz) * 2 + (core if c is None else c)
        lo, n = span[color]
        return out_ref.at[dev, pl.ds(lo, n)]

    def send(cx, cy, cz, color, way, own=False):
        lo, n = span[color]
        src = own_ref.at[pl.ds(lo, n)] if own else view(cx, cy, cz, color)
        idx = chip(cx, cy, cz)
        return pltpu.make_async_remote_copy(src_ref=src, dst_ref=view(cx, cy, cz, color),
            send_sem=send_sem.at[idx, color, way], recv_sem=recv_sem.at[idx, color],
            device_id=(targets[way],), device_id_type=MESH)

    def send_sib(cx, cy, cz, color, own=False):
        lo, n = span[color]
        src = own_ref.at[pl.ds(lo, n)] if own else view(cx, cy, cz, color)
        idx = chip(cx, cy, cz)
        return pltpu.make_async_remote_copy(src_ref=src, dst_ref=view(cx, cy, cz, color),
            send_sem=sib_send.at[idx, color], recv_sem=sib_recv.at[idx, color],
            device_id=(sib,), device_id_type=MESH)

    x2, y2 = 1 - x, 1 - y
    pending = []

    def go(copy, cond=None):
        if cond is None:
            copy.start()
        else:
            @pl.when(cond)
            def _():
                copy.start()
        pending.append((copy, cond))

    zup, zdown = z < 3, z > 0
    own_copies = []
    for color in range(3):
        lo, n = span[color]
        cp = pltpu.make_async_copy(own_ref.at[pl.ds(lo, n)], view(x, y, z, color), own_sem.at[color])
        cp.start()
        own_copies.append(cp)
    order = {0: (0, 2, 1), 1: (1, 2, 0)}
    for color in (0, 1, 2):
        go(send(x, y, z, color, 2, True), zup)
        go(send(x, y, z, color, 3, True), zdown)
    for color, way in ((0, 0), (1, 1), (2, 0), (2, 1), (0, 1), (1, 0)):
        go(send(x, y, z, color, way, True))
    for color in range(3):
        go(send_sib(x, y, z, color, True))

    def arrive(cx, cy, cz, color):
        send(cx, cy, cz, color, 0).wait_recv()

    def sibling(cx, cy, cz, color):
        go(send_sib(cx, cy, cz, color))

    is0, is1 = core == 0, core == 1
    px = jnp.where(is0, x2, x)
    py = jnp.where(is0, y, y2)
    qx = jnp.where(is0, x, x2)
    qy = jnp.where(is0, y2, y)
    first = lambda cx, cy, cz: (go(send(cx, cy, cz, 2, 0), is0), go(send(cx, cy, cz, 2, 1), is1))
    last = lambda cx, cy, cz: (go(send(cx, cy, cz, 2, 1), is0), go(send(cx, cy, cz, 2, 0), is1))

    arrive(x2, y, z, 0)
    go(send(x2, y, z, 0, 2), zup)
    go(send(x2, y, z, 0, 3), zdown)
    go(send(x2, y, z, 0, 1))
    sibling(x2, y, z, 0)
    arrive(x, y2, z, 1)
    go(send(x, y2, z, 1, 2), zup)
    go(send(x, y2, z, 1, 3), zdown)
    go(send(x, y2, z, 1, 0))
    sibling(x, y2, z, 1)
    arrive(px, py, z, 2)
    last(px, py, z)
    sibling(px, py, z, 2)

    for dist in (1, 2, 3):
        sides = []
        for sign, fwd, guard_f in ((1, 3, zdown), (-1, 2, zup)):
            q = z + sign * dist
            have = (q >= 0) & (q < 4)
            sides.append((q, fwd, have, guard_f))
        for which in ("c", "a", "b", "a2", "b2"):
            for q, fwd, have, gf in sides:
                @pl.when(have)
                def _(q=q, fwd=fwd, gf=gf, which=which):
                    if which == "c":
                        arrive(x, y, q, 2)
                        cp = send(x, y, q, 2, fwd)
                        pl.when(gf)(lambda: cp.start())
                        for w in (0, 1):
                            send(x, y, q, 2, w).start()
                        send_sib(x, y, q, 2).start()
                    else:
                        color = 0 if which[0] == "a" else 1
                        cx, cy = {"a": (x, y), "b": (x, y), "a2": (x2, y), "b2": (x, y2)}[which]
                        arrive(cx, cy, q, color)
                        cp = send(cx, cy, q, color, fwd)
                        pl.when(gf)(lambda: cp.start())
                        send(cx, cy, q, color, 1 if color == 0 else 0).start()
                        send_sib(cx, cy, q, color).start()
        for q, fwd, have, gf in sides:
            @pl.when(have)
            def _(q=q):
                arrive(px, py, q, 2)
                pl.when(is0)(lambda: send(px, py, q, 2, 1).start())
                pl.when(is1)(lambda: send(px, py, q, 2, 0).start())
                send_sib(px, py, q, 2).start()
        if dist == 1:
            tail_list = [(z, None)]
        else:
            tail_list = []
        def terminal(q):
            for cx, cy, color in ((x, y2, 0), (x2, y2, 0), (x2, y, 1), (x2, y2, 1), (qx, qy, 2), (x2, y2, 2)):
                arrive(cx, cy, q, color)
                send_sib(cx, cy, q, color).start()
        if dist == 1:
            terminal(z)
        else:
            for sign in (1, -1):
                q = z + sign * (dist - 1)
                pl.when((q >= 0) & (q < 4))(lambda q=q: terminal(q))
        if dist == 3:
            for sign in (1, -1):
                q = z + sign * 3
                pl.when((q >= 0) & (q < 4))(lambda q=q: terminal(q))
    @pl.when(less)
    def _():
        for k in (0, 1):
            halo_copy(k).start()

    @pl.when(more)
    def _():
        halo_copy(2).start()

    @pl.when(less)
    def _():
        for k in (0, 1):
            halo_copy(k).wait_send()
        halo_copy(2).wait_recv()

    @pl.when(more)
    def _():
        halo_copy(2).wait_send()
        for k in (0, 1):
            halo_copy(k).wait_recv()

    for cp in own_copies:
        cp.wait()
    for color in range(3):
        pl.when(zup)(lambda color=color: send(x, y, z, color, 2).wait_send())
        pl.when(zdown)(lambda color=color: send(x, y, z, color, 3).wait_send())
        for w in (0, 1):
            send(x, y, z, color, w).wait_send()
    for cx, cy, color, w in ((x2, y, 0, 1), (x, y2, 1, 0)):
        pl.when(zup)(lambda: send(cx, cy, z, color, 2).wait_send())
        pl.when(zdown)(lambda: send(cx, cy, z, color, 3).wait_send())
        send(cx, cy, z, color, w).wait_send()
    pl.when(is0)(lambda: send(px, py, z, 2, 1).wait_send())
    pl.when(is1)(lambda: send(px, py, z, 2, 0).wait_send())
    for dist in (1, 2, 3):
        for sign, fwd, gf in ((1, 3, zdown), (-1, 2, zup)):
            q = z + sign * dist
            @pl.when((q >= 0) & (q < 4))
            def _(q=q, fwd=fwd, gf=gf):
                for cx, cy, color in ((x, y, 2), (x, y, 0), (x, y, 1), (x2, y, 0), (x, y2, 1)):
                    pl.when(gf)(lambda: send(cx, cy, q, color, fwd).wait_send())
                    ways = (0, 1) if color == 2 else ((1,) if color == 0 else (0,))
                    for w in ways:
                        send(cx, cy, q, color, w).wait_send()
                pl.when(is0)(lambda: send(px, py, q, 2, 1).wait_send())
                pl.when(is1)(lambda: send(px, py, q, 2, 0).wait_send())
    for cz in range(4):
        for cy in range(2):
            for cx in range(2):
                for color in range(3):
                    cp = send_sib(cx, cy, cz, color)
                    cp.wait_send()
                    cp.wait_recv()

def gather_blocks(owned, tokens_in, out_grad, cid=1):
    slots = owned.shape[0]
    anywhere = pl.BlockSpec(memory_space=pl.ANY)
    halo = jax.ShapeDtypeStruct((16,) + tokens_in.shape[1:], tokens_in.dtype)
    return pl.pallas_call(
        functools.partial(gather_kernel, slots),
        out_shape=(jax.ShapeDtypeStruct((GRID_DEVICES,) + owned.shape, owned.dtype), halo, halo, halo),
        in_specs=[anywhere] * 3,
        out_specs=(anywhere,) * 4,
        scratch_shapes=[
            pltpu.SemaphoreType.DMA((16, 3, 4)),
            pltpu.SemaphoreType.DMA((16, 3)),
            pltpu.SemaphoreType.DMA((16, 3)),
            pltpu.SemaphoreType.DMA((16, 3)),
            pltpu.SemaphoreType.DMA((3,)),
            pltpu.SemaphoreType.DMA((3,)),
            pltpu.SemaphoreType.DMA((3,)),
        ],
        compiler_params=pltpu.CompilerParams(collective_id=cid, has_side_effects=True),
        name="gather_blocks",
    )(owned, tokens_in, out_grad)


def scatter_kernel(
    slots, part_ref, rows_ref, out_ref, total_ref, acc, sib, xin, yin, zin, sums,
    load_sem, sib_send, sib_recv, send_sem, xsem, ysem, zsem, row_send, row_recv,
):
    me, core, x, y, z = grid_place()
    sibling = me + 1 - 2 * core
    x_peer = me + 2 - 4 * x
    y_peer = me + 4 - 8 * y
    up, down = me + 8, me - 8
    zup, zdown = z < 3, z > 0
    bar = pltpu.get_barrier_semaphore()
    for peer in (sibling, x_peer, y_peer):
        pl.semaphore_signal(bar, inc=1, device_id=(peer,), device_id_type=MESH)
    @pl.when(zup)
    def _():
        pl.semaphore_signal(bar, inc=1, device_id=(up,), device_id_type=MESH)
    @pl.when(zdown)
    def _():
        pl.semaphore_signal(bar, inc=1, device_id=(down,), device_id_type=MESH)
    far = me + 16 - 32 * (z // 2)
    pl.semaphore_signal(bar, inc=1, device_id=(far,), device_id_type=MESH)
    row_peers = (sibling, x_peer, y_peer, me + 8 - 16 * lax.rem(z, 2), far)
    sums[0] = rows_ref[...]
    span = spans(slots)
    x2, y2 = 1 - x, 1 - y
    is0, is1 = core == 0, core == 1

    def row_copy(k):
        return pltpu.make_async_remote_copy(src_ref=sums.at[2 * k], dst_ref=sums.at[2 * k + 1],
            send_sem=row_send.at[k], recv_sem=row_recv.at[k], device_id=(row_peers[k],), device_id_type=MESH)

    def row_step(k):
        row_copy(k).wait()
        sums[2 * k + 2] = sums[2 * k] + sums[2 * k + 1]
        if k < 4:
            row_copy(k + 1).start()

    def load(chip):
        return pltpu.make_async_copy(part_ref.at[2 * chip + core], acc.at[chip], load_sem.at[chip])

    def give(chip):
        return pltpu.make_async_remote_copy(src_ref=part_ref.at[2 * chip + 1 - core], dst_ref=sib.at[chip],
            send_sem=sib_send.at[chip], recv_sem=sib_recv.at[chip], device_id=(sibling,), device_id_type=MESH)

    levels = []
    for dist in (3, 2, 1):
        for sign in (1, -1):
            q = z + sign * dist
            levels.append((dist, sign, q, (q >= 0) & (q < 4)))

    def run(dist, work):
        for d, sign, q, have in levels:
            if d == dist:
                pl.when(have)(functools.partial(work, q))

    def run_signed(dist, work):
        for d, sign, q, have in levels:
            if d == dist:
                pl.when(have)(functools.partial(work, q, sign, dist))

    def begin_loads(q):
        for i in plane_order():
            load(4 * q + i).start()

    def begin_gives(q):
        for i in plane_order():
            give(4 * q + i).start()

    def plane_order():
        return (2 * y2 + x2, 2 * y + x2, 2 * y2 + x, 2 * y + x)

    run(3, begin_loads)
    run(2, begin_loads)
    run(1, begin_loads)
    begin_loads(z)
    pl.semaphore_wait(bar, 5 + jnp.where(zup & zdown, 1, 0))
    row_copy(0).start()
    run(3, begin_gives)
    run(2, begin_gives)

    def ready(cx, cy, q):
        chip = chip_of(cx, cy, q)
        load(chip).wait()
        give(chip).wait_recv()

        def step(s, _):
            total = acc[chip, s].astype(jnp.float32) + sib[chip, s].astype(jnp.float32)
            acc[chip, s] = total.astype(acc.dtype)
            return 0

        lax.fori_loop(0, slots, step, 0)

    def chip_of(cx, cy, cz):
        return (cz * 2 + cy) * 2 + cx

    def out_copy(cx, cy, cz, color, target, buf, index, sem):
        lo, n = span[color]
        chip = chip_of(cx, cy, cz)
        return pltpu.make_async_remote_copy(src_ref=acc.at[chip, pl.ds(lo, n)], dst_ref=buf.at[index, pl.ds(0, n)],
            send_sem=send_sem.at[chip, color], recv_sem=sem.at[index], device_id=(target,), device_id_type=MESH)

    def arrived(buf, index, sem, color):
        lo, n = span[color]
        pltpu.make_async_remote_copy(src_ref=acc.at[0, pl.ds(lo, n)], dst_ref=buf.at[index, pl.ds(0, n)],
            send_sem=send_sem.at[0, color], recv_sem=sem.at[index], device_id=(sibling,), device_id_type=MESH).wait_recv()

    def add(cx, cy, cz, color, pieces):
        lo, n = span[color]
        chip = chip_of(cx, cy, cz)
        for buf, index, sem in pieces:
            arrived(buf, index, sem, color)
        def step(s, _):
            total = acc[chip, lo + s].astype(jnp.float32)
            for buf, index, _sem in pieces:
                total = total + buf[index, s].astype(jnp.float32)
            acc[chip, lo + s] = total.astype(acc.dtype)
            return 0
        lax.fori_loop(0, n, step, 0)

    def X(i): return (xin, i, xsem)
    def Y(i): return (yin, i, ysem)
    def Z(i): return (zin, i, zsem)

    def term_x(q, color, i):
        cy = (y, y2)[i]
        out_copy(x2, cy, q, color, x_peer, xin, (8 if color == 2 else 0) + 2 * q + i, xsem).start()

    def term_y(q, color, i):
        cx = (x, x2)[i]
        out_copy(cx, y2, q, color, y_peer, yin, (8 if color == 2 else 0) + 2 * q + i, ysem).start()

    def term_a(q):
        ready(x2, y2, q)
        term_x(q, 1, 1)
        term_y(q, 0, 1)

    def term_c(q):

        @pl.when(is0)
        def _():
            term_y(q, 2, 1)
            term_y(q, 2, 0)

        @pl.when(is1)
        def _():
            term_x(q, 2, 1)
            term_x(q, 2, 0)

        ready(x, y, q)

    def term_b(q):
        ready(x2, y, q)
        term_x(q, 1, 0)
        ready(x, y2, q)
        term_y(q, 0, 0)

    def plane_two(q):
        @pl.when(is0)
        def _():
            add(x2, y, q, 2, [Y(8 + 2 * q + 1)])
            out_copy(x2, y, q, 2, x_peer, xin, 8 + 2 * q, xsem).start()
        @pl.when(is1)
        def _():
            add(x, y2, q, 2, [X(8 + 2 * q + 1)])
            out_copy(x, y2, q, 2, y_peer, yin, 8 + 2 * q, ysem).start()

    def column(part, q, sign, dist):
        target = up if sign == 1 else down
        more = zdown if sign == 1 else zup
        at_target = dist == 1
        base_out = (20 if (at_target and sign == 1) else 5 * q)
        kinds = (
            (0, x, y, 2, [X(8 + 2 * q), Y(8 + 2 * q)]),
            (1, x, y, 0, [Y(2 * q)]),
            (2, x, y, 1, [X(2 * q)]),
            (3, x2, y, 0, [Y(2 * q + 1)]),
            (4, x, y2, 1, [X(2 * q + 1)]),
        )
        for k, cx, cy, color, pieces in ((kinds[4], kinds[3], kinds[2], kinds[1]), (kinds[0],))[part]:
            @pl.when(more)
            def _():
                add(cx, cy, q, color, pieces + [Z(5 * q + k)])
            @pl.when(jnp.logical_not(more))
            def _():
                add(cx, cy, q, color, pieces)
            out_copy(cx, cy, q, color, target, zin, base_out + k, zsem).start()

    planes = functools.partial(column, 0)
    last = functools.partial(column, 1)
    run(3, term_a)
    run(3, term_b)
    run(3, term_c)
    row_step(0)
    run_signed(3, planes)
    run(2, term_a)
    run(2, term_b)
    run(2, term_c)
    run(3, plane_two)
    run(1, begin_gives)
    run_signed(3, last)
    run(1, term_a)
    run(1, term_b)
    run(1, term_c)
    row_step(1)
    run_signed(2, planes)
    begin_gives(z)
    run(2, plane_two)
    term_a(z)
    term_b(z)
    term_c(z)
    run_signed(2, last)
    row_step(2)
    run_signed(1, planes)
    run(1, plane_two)
    run_signed(1, last)
    row_step(3)
    plane_two(z)
    row_step(4)
    total_ref[...] = sums[10]

    def own(k, cx, cy, color, pieces):
        @pl.when(zup & zdown)
        def _():
            add(cx, cy, z, color, pieces + [Z(5 * z + k), Z(20 + k)])
        @pl.when(zup & jnp.logical_not(zdown))
        def _():
            add(cx, cy, z, color, pieces + [Z(5 * z + k)])
        @pl.when(zdown & jnp.logical_not(zup))
        def _():
            add(cx, cy, z, color, pieces + [Z(20 + k)])
    own(3, x2, y, 0, [Y(2 * z + 1)])
    out_copy(x2, y, z, 0, x_peer, xin, 16, xsem).start()
    own(4, x, y2, 1, [X(2 * z + 1)])
    out_copy(x, y2, z, 1, y_peer, yin, 16, ysem).start()
    own(0, x, y, 2, [X(8 + 2 * z), Y(8 + 2 * z)])
    own(1, x, y, 0, [Y(2 * z), X(16)])
    own(2, x, y, 1, [X(2 * z), Y(16)])
    pltpu.sync_copy(acc.at[chip_of(x, y, z)], out_ref)
    for chip in range(16):
        give(chip).wait_send()
        for color in range(3):
            @pl.when(chip != chip_of(x, y, z))
            def _():
                lo, n = span[color]
                pltpu.make_async_remote_copy(src_ref=acc.at[chip, pl.ds(lo, n)], dst_ref=xin.at[0, pl.ds(0, n)],
                    send_sem=send_sem.at[chip, color], recv_sem=xsem.at[0], device_id=(sibling,), device_id_type=MESH).wait_send()

def scatter_blocks(part, rows, cid=2):
    _, slots, height, feats = part.shape
    most = max(n for _, n in spans(slots))
    chunk = (most, height, feats)
    dt = part.dtype
    return pl.pallas_call(
        functools.partial(scatter_kernel, slots),
        out_shape=(
            jax.ShapeDtypeStruct(part.shape[1:], dt),
            jax.ShapeDtypeStruct(rows.shape, rows.dtype),
        ),
        in_specs=[pl.BlockSpec(memory_space=pl.ANY), pl.BlockSpec(memory_space=pltpu.VMEM)],
        out_specs=(pl.BlockSpec(memory_space=pl.ANY), pl.BlockSpec(memory_space=pltpu.VMEM)),
        scratch_shapes=[
            pltpu.VMEM((16, slots, height, feats), dt),
            pltpu.VMEM((16, slots, height, feats), dt),
            pltpu.VMEM((17,) + chunk, dt),
            pltpu.VMEM((17,) + chunk, dt),
            pltpu.VMEM((25,) + chunk, dt),
            pltpu.VMEM((11,) + rows.shape, rows.dtype),
            pltpu.SemaphoreType.DMA((16,)),
            pltpu.SemaphoreType.DMA((16,)),
            pltpu.SemaphoreType.DMA((16,)),
            pltpu.SemaphoreType.DMA((16, 3)),
            pltpu.SemaphoreType.DMA((17,)),
            pltpu.SemaphoreType.DMA((17,)),
            pltpu.SemaphoreType.DMA((25,)),
            pltpu.SemaphoreType.DMA((5,)),
            pltpu.SemaphoreType.DMA((5,)),
        ],
        compiler_params=pltpu.CompilerParams(collective_id=cid, has_side_effects=True, vmem_limit_bytes=58 * 2**20),
        name="scatter_blocks",
    )(part, rows)


ROW_TILE = 16
BIG_TILE = 64
CHUNKS = 8
LANES = 128
VMEM_BYTES = 60 * 2**20


def rows_at(index, size=ROW_TILE):
    return pl.ds(pl.multiple_of(index * size, size), size)


def fetch_blocks(slot_ref, pool_ref, store_ref, sem, first_block, place, count):
    def step(b, carry):
        for k in range(4):
            pltpu.make_async_copy(
                pool_ref.at[slot_ref[first_block + 4 * b + k]], store_ref.at[place + 4 * b + k], sem
            ).start()
        return carry

    lax.fori_loop(0, count // 4, step, 0)


def await_blocks(pool_ref, store_ref, sem, place, count):
    pltpu.make_async_copy(
        pool_ref.at[pl.ds(0, count)], store_ref.at[pl.ds(place, count)], sem
    ).wait()


def times_weight(left_ref, store_ref, place, count, write, width=512):
    features = store_ref.shape[2]

    def step(n, carry):
        cols = pl.ds(pl.multiple_of(n * width, width), width)
        right = store_ref[place : place + count, :, cols].reshape(count * BLOCK_ROWS, width)
        write(cols, jnp.dot(left_ref[...], right, preferred_element_type=jnp.float32))
        return carry

    lax.fori_loop(0, features // width, step, 0)


def times_weight_back(left_ref, store_ref, place, count, write, width=1024):
    blocks = width // BLOCK_ROWS

    def step(n, carry):
        cols = pl.ds(pl.multiple_of(n * width, width), width)
        right = store_ref[pl.ds(place + n * blocks, blocks)].reshape(width, store_ref.shape[2])
        write(cols, product_back(left_ref[...], right))
        return carry

    lax.fori_loop(0, count // blocks, step, 0)


def weight_gradient(left_ref, right_ref, own, slot_ref, grad_ref, store_ref, sem, first_block, place, width=1024):
    blocks = width // BLOCK_ROWS
    steps = left_ref.shape[1] // width

    def step(n, carry):
        cols = pl.ds(pl.multiple_of(n * width, width), width)
        piece = product_left(left_ref[0:own, cols], right_ref[0:own])
        at = place + n * blocks
        store_ref[pl.ds(at, blocks)] = piece.astype(store_ref.dtype).reshape(blocks, *store_ref.shape[1:])

        def put(b, inner):
            for k in range(4):
                pltpu.make_async_copy(
                    store_ref.at[at + 4 * b + k],
                    grad_ref.at[slot_ref[first_block + n * blocks + 4 * b + k]],
                    sem,
                ).start()
            return inner

        return lax.fori_loop(0, blocks // 4, put, carry)

    lax.fori_loop(0, steps, step, 0)


def await_gradient(store_ref, grad_ref, sem, place, count):
    pltpu.make_async_copy(
        store_ref.at[pl.ds(place, count)], grad_ref.at[pl.ds(0, count)], sem
    ).wait()


def for_rows(rows, work, sums=()):
    own = rows - ROW_TILE

    def step(j, carry):
        out = work(pl.multiple_of(j * BIG_TILE, BIG_TILE), BIG_TILE, *carry)
        return carry if out is None else out

    sums = lax.fori_loop(0, own // BIG_TILE, step, sums)
    return sums


def fold(piece):
    return jnp.sum(piece.reshape(-1, CHUNKS, piece.shape[1]), axis=0)


def unit_norm(values):
    centered = values - jnp.mean(values, axis=1, keepdims=True)
    inverse = lax.rsqrt(jnp.mean(centered * centered, axis=1, keepdims=True) + NORM_EPS)
    return centered * inverse, inverse


def merge(first, second):
    top = jnp.maximum(first[2], second[2])
    one, two = jnp.exp(first[2] - top), jnp.exp(second[2] - top)
    return (one * first[0] + two * second[0], one * first[1] + two * second[1], top)


def aged(state, distance, alive, rate):
    return (state[0], state[1], jnp.where(alive > 0.5, state[2] - distance * rate, NEGATIVE))


def reset(state, start):
    cut = start > 0.5
    return (
        jnp.where(cut, 0.0, state[0]),
        jnp.where(cut, 0.0, state[1]),
        jnp.where(cut, NEGATIVE, state[2]),
    )


def advance(state, key, value, rate):
    older = state[2] - rate
    top = jnp.maximum(older, key)
    old, new = jnp.exp(older - top), jnp.exp(key - top)
    return (old * state[0] + new * value, old * state[1] + new, top)


def shift_in(ext, own):
    ext[0:8] = jnp.concatenate([ext[own + 10 : own + 11], ext[own : own + 7]], axis=0)


def halo_previous(ext, own, features):
    return jnp.concatenate(
        [
            ext[own + 7 : own + 8],
            ext[own + 8 : own + 9],
            ext[own + 11 : own + 12],
            jnp.zeros((ROW_TILE - 3, features), jnp.float32),
        ],
        axis=0,
    )


def normed_pair(ext, marks_ref, first, size):
    here = ext[pl.ds(pl.multiple_of(first + 8, 8), size)]
    before = ext[pl.ds(first, size)] * marks_ref[pl.ds(first, size), 1:2]
    return here, before


def take_step(wide, first, length):
    at = pl.ds(first, CHUNKS, stride=length)
    return jnp.concatenate([wide[k, at] for k in range(wide.shape[0])], axis=1)


def put_step(wide, first, length, tile):
    at = pl.ds(first, CHUNKS, stride=length)
    lanes = wide.shape[2]
    for k in range(wide.shape[0]):
        wide[k, at] = tile[:, k * lanes : (k + 1) * lanes]


def take_rows(wide, at):
    return jnp.concatenate([wide[k, at] for k in range(wide.shape[0])], axis=1)


def put_rows(wide, at, tile):
    lanes = wide.shape[2]
    for k in range(wide.shape[0]):
        wide[k, at] = tile[:, k * lanes : (k + 1) * lanes]


def none_between(offsets, low, high):
    hit = None
    for offset in offsets:
        inside = (low <= offset) & (offset <= high)
        hit = inside if hit is None else hit | inside
    return jnp.where(hit, 0.0, 1.0)


def write_marks(doc_ref, marks_ref, chunk_ref, link_ref, flag_ref, own, devices):
    rows = marks_ref.shape[0]
    length = own // CHUNKS
    total = own * devices
    me = lax.axis_index("seq")
    first = me * own
    offsets = [jnp.int32(0)]
    for k in range(doc_ref.shape[0] - 1):
        offsets.append(offsets[-1] + doc_ref[k])
    row = lax.broadcasted_iota(jnp.int32, (rows, 1), 0)
    chunk, step = lax.rem(row, CHUNKS), row // CHUNKS
    extra = jnp.where(row < own + 2, row, own - 1 - (row - (own + 2)) - own)
    place = first + jnp.where(row < own, chunk * length + step, extra)
    inside = (place >= 0) & (place < total)
    keep = jnp.where(inside, none_between(offsets, place, place), 0.0)
    begin = first + chunk * length
    marks_ref[:, 0:1] = 1.0 - keep
    marks_ref[:, 1:2] = keep
    marks_ref[:, 2:3] = jnp.where(row < own, none_between(offsets, begin, place), 1.0)
    marks_ref[:, 3:4] = jnp.where(row < own, none_between(offsets, place + 1, begin + length - 1), 1.0)
    chunk = lax.broadcasted_iota(jnp.int32, (CHUNKS, 1), 0)
    begin = first + chunk * length
    end = begin + length - 1
    chunk_ref[:, 0:1] = none_between(offsets, begin, end)
    chunk_ref[:, 1:2] = jnp.where(first > 0, none_between(offsets, first - 1, begin - 1), 0.0)
    chunk_ref[:, 2:3] = none_between(offsets, begin, end - 1)
    chunk_ref[:, 3:4] = (1 + chunk * length).astype(jnp.float32)
    chunk_ref[:, 4:5] = jnp.where(first + own < total, none_between(offsets, end + 1, first + own), 0.0)
    chunk_ref[:, 5:6] = (1 + (CHUNKS - 1 - chunk) * length).astype(jnp.float32)
    count = link_ref.shape[0]
    group = devices // count
    span = own * group
    here = me // group
    other = lax.broadcasted_iota(jnp.int32, (count, 1), 0)
    link_ref[:, 0:1] = jnp.where(other < here, none_between(offsets, span * (other + 1) - 1, span * here - 2), 0.0)
    link_ref[:, 1:2] = (span * (here - 1 - other)).astype(jnp.float32)
    link_ref[:, 2:3] = jnp.where(other > here, none_between(offsets, span * (here + 1) + 1, span * other), 0.0)
    link_ref[:, 3:4] = (span * (other - here - 1)).astype(jnp.float32)
    pair = span * here + jnp.zeros((1, 1), jnp.int32)
    flag_ref[:, 0:1] = none_between(offsets, pair + own - 1, pair + 2 * own - 2)
    flag_ref[:, 1:2] = none_between(offsets, pair - 1, pair + own - 2)
    flag_ref[:, 2:3] = none_between(offsets, pair + 1, pair + own)
    flag_ref[:, 3:4] = none_between(offsets, pair + own + 1, pair + 2 * own)


def open_kernel(
    devices,
    slot_ref, doc_ref, tokens_ref, grads_ref, after_ref, after_grad_ref, before_ref, vec_ref, pool_ref,
    x_ref, grad_ref, marks_ref, chunk_ref, link_ref, flag_ref,
    key_ref, value_ref, recept_ref, num_ref, den_ref, max_ref, in_key, in_value, in_recept, prefix_ref, summary_ref,
    ext, wide, wide_grad, store, sem,
):
    rows, features = x_ref.shape
    own = rows - ROW_TILE
    tiles = rows // ROW_TILE
    length = own // CHUNKS
    per = EMBED_SIZE // BLOCK_ROWS
    for m in range(3):
        fetch_blocks(slot_ref, pool_ref, store, sem.at[m], m * per, m * per, per)
    write_marks(doc_ref, marks_ref, chunk_ref, link_ref, flag_ref, own, devices)
    me = lax.axis_index("seq")

    def widen(first, size):
        at = pl.ds(first, size)
        put_rows(wide, at, tokens_ref[at].astype(jnp.float32))
        put_rows(wide_grad, at, grads_ref[at].astype(jnp.float32))

    for_rows(rows, widen)

    def norm(first, size, tile):
        x_ref[pl.ds(first, size)] = tile.astype(jnp.bfloat16)
        unit, _ = unit_norm(tile)
        ext[pl.ds(pl.multiple_of(first + 8, 8), size)] = unit * vec_ref[0:1] + vec_ref[1:2]

    def arrange(first, size):
        steps = [first // CHUNKS + k for k in range(size // CHUNKS)]
        norm(first, size, jnp.concatenate([take_step(wide, i, length) for i in steps], axis=0))
        tile = jnp.concatenate([take_step(wide_grad, i, length) for i in steps], axis=0)
        grad_ref[pl.ds(first, size)] = tile.astype(jnp.bfloat16)

    for_rows(rows, arrange)
    more, less = me < devices - 1, me > 0
    later = jnp.where(more, after_ref[...].astype(jnp.float32), 0.0)[0:2]
    earlier = jnp.where(less, before_ref[...].astype(jnp.float32), 0.0)
    blank_rows = jnp.zeros((ROW_TILE - 4, features), jnp.float32)
    norm(
        own,
        ROW_TILE,
        jnp.concatenate([later, earlier[ROW_TILE - 1 :], earlier[ROW_TILE - 2 : ROW_TILE - 1], blank_rows], axis=0),
    )
    later_grad = jnp.where(more, after_grad_ref[...].astype(jnp.float32), 0.0)[0:2]
    grad_ref[own:rows] = jnp.concatenate([later_grad, blank_rows, blank_rows[:2]], axis=0).astype(jnp.bfloat16)
    shift_in(ext, own)

    def mix(first, size, here, before):
        for row, ref in ((2, in_key), (3, in_value), (4, in_recept)):
            weight = vec_ref[row : row + 1]
            ref[pl.ds(first, size)] = (weight * here + (1.0 - weight) * before).astype(jnp.bfloat16)

    for_rows(rows, lambda first, size: mix(first, size, *normed_pair(ext, marks_ref, first, size)))
    mix(own, ROW_TILE, ext[own + 8 : own + 8 + ROW_TILE], halo_previous(ext, own, features) * marks_ref[own:rows, 1:2])
    for m, (left, out) in enumerate(((in_key, key_ref), (in_value, value_ref), (in_recept, recept_ref))):
        await_blocks(pool_ref, store, sem.at[m], m * per, per)

        def write(cols, piece, out=out):
            out[:, cols] = piece

        times_weight(left, store, m * per, per, write)
    rate = jnp.exp(vec_ref[5:6])

    def token(i, state, key, value):
        state = reset(state, marks_ref[rows_at(i, CHUNKS), 0:1])
        num_ref[rows_at(i, CHUNKS)], den_ref[rows_at(i, CHUNKS)], max_ref[rows_at(i, CHUNKS)] = state
        return advance(state, key, value, rate)

    def step(i, state):
        return token(i, state, key_ref[rows_at(i, CHUNKS)], value_ref[rows_at(i, CHUNKS)])

    blank = jnp.zeros((CHUNKS, features), jnp.float32)
    state = lax.fori_loop(0, length - 1, step, (blank, blank, blank + NEGATIVE))
    late = tuple(item[CHUNKS - 1 :] for item in state)
    ends = step(length - 1, state)
    prior = (value_ref[own + 2 : own + 3], jnp.ones((1, features), jnp.float32), key_ref[own + 2 : own + 3])
    for c in range(CHUNKS):
        for k in range(3):
            prefix_ref[k, c : c + 1] = prior[k]
        if c < CHUNKS - 1:
            old = aged(prior, float(length), chunk_ref[c : c + 1, 0:1], rate)
            prior = merge(tuple(item[c : c + 1] for item in ends), old)
    last = merge(late, aged(prior, float(length - 1), chunk_ref[CHUNKS - 1 :, 2:3], rate))
    summary_ref[...] = jnp.concatenate(last, axis=0)


def open_pass(devices, slots, doc_lengths, tokens_in, out_grad, halo, vectors, pool):
    own, features = tokens_in.shape
    rows = own + ROW_TILE
    count = devices // 2 if devices == GRID_DEVICES else devices
    full = jax.ShapeDtypeStruct((rows, features), jnp.float32)
    part = jax.ShapeDtypeStruct((own, features), jnp.float32)
    low = jax.ShapeDtypeStruct((rows, features), jnp.bfloat16)
    small = lambda *shape: jax.ShapeDtypeStruct(shape, jnp.float32)
    vmem = pl.BlockSpec(memory_space=pltpu.VMEM)
    smem = pl.BlockSpec(memory_space=pltpu.SMEM)
    return pl.pallas_call(
        functools.partial(open_kernel, devices),
        out_shape=(
            low, low, small(rows, 4), small(CHUNKS, 6), small(count, 4), small(1, 4),
            full, full, full, part, part, part, low, low, low, small(3, CHUNKS, features), small(3, features),
        ),
        in_specs=[smem] * 2 + [vmem] * 6 + [pl.BlockSpec(memory_space=pl.ANY)],
        out_specs=(vmem,) * 17,
        scratch_shapes=[
            pltpu.VMEM((rows + 8, features), jnp.float32),
            pltpu.VMEM((features // LANES, own, LANES), jnp.float32),
            pltpu.VMEM((features // LANES, own, LANES), jnp.float32),
            pltpu.VMEM((3 * EMBED_SIZE // BLOCK_ROWS, BLOCK_ROWS, features), jnp.bfloat16),
            pltpu.SemaphoreType.DMA((3,)),
        ],
        compiler_params=pltpu.CompilerParams(vmem_limit_bytes=VMEM_BYTES),
        name="open_pass",
    )(slots, doc_lengths, tokens_in, out_grad, *halo, vectors, pool)


def middle_kernel(
    slot_ref, x_ref, grad_ref, vec_ref, marks_ref, chunk_ref, incoming_ref, prefix_ref,
    key_ref, value_ref, recept_ref, num_ref, den_ref, max_ref, pool_ref,
    layer_ref, resid_grad, wkv, gw, own_share, recept_grad, suffix_ref, summary_ref, sums_ref,
    full_out, back_out, slot_grad,
    full_num, full_den, full_max, mixed, ext, unit, inverse, low_key, low_recept, hidden, squared, value_acc, gate, gcv, gcg, hidden_grad,
    attn_grad, top_log, wide, store, sem, out_sem, state_sem,
):
    rows, features = x_ref.shape
    own = rows - ROW_TILE
    tiles = rows // ROW_TILE
    length = own // CHUNKS
    per = EMBED_SIZE // BLOCK_ROWS
    ff = FF // BLOCK_ROWS
    at_out, at_recept, at_key, at_value = 0, per, 2 * per, 2 * per + ff
    fetch_blocks(slot_ref, pool_ref, store, sem.at[0], 3 * per, at_out, per)
    fetch_blocks(slot_ref, pool_ref, store, sem.at[1], 5 * per, at_key, ff)
    fetch_blocks(slot_ref, pool_ref, store, sem.at[2], 5 * per + ff, at_value, ff)
    fetch_blocks(slot_ref, pool_ref, store, sem.at[3], 4 * per, at_recept, per)
    rate = jnp.exp(vec_ref[5:6])
    bonus = vec_ref[6:7]
    incoming = tuple(incoming_ref[k : k + 1] for k in range(3))
    carry = merge(
        tuple(prefix_ref[k] for k in range(3)),
        aged(tuple(jnp.broadcast_to(v, (CHUNKS, features)) for v in incoming), chunk_ref[:, 3:4], chunk_ref[:, 1:2], rate),
    )

    def attend(j, size, state, key, value, recept):
        own_log = bonus + key
        top = jnp.maximum(state[2], own_log)
        old, new = jnp.exp(state[2] - top), jnp.exp(own_log - top)
        scale = 1.0 / (old * state[1] + new)
        out = (old * state[0] + new * value) * scale
        wkv[rows_at(j, size)] = out
        own_share[rows_at(j, size)] = new * scale
        top_log[rows_at(j, size)] = top
        value_acc[rows_at(j, size)] = scale
        ext[rows_at(j, size)] = jax.nn.sigmoid(recept) * out

    def attend_step(i, state_carry):
        at = rows_at(i, CHUNKS)
        alive = marks_ref[at, 2:3]
        distance = jnp.float32(i) if isinstance(i, int) else i.astype(jnp.float32)
        state = merge((num_ref[at], den_ref[at], max_ref[at]), aged(carry, distance, alive, rate))
        full_num[at], full_den[at], full_max[at] = state
        attend(i, CHUNKS, state, key_ref[at], value_ref[at], recept_ref[at])
        return state_carry

    lax.fori_loop(0, length, attend_step, 0)

    def row(ref, r):
        return ref[r : r + 1]

    def state_copy(k, target):
        return pltpu.make_async_copy((full_num, full_den, full_max)[k], target.at[k], state_sem.at[k])

    for k in range(3):
        state_copy(k, full_out).start()
    end = advance(
        (row(full_num, own - 1), row(full_den, own - 1), row(full_max, own - 1)),
        row(key_ref, own - 1), row(value_ref, own - 1), rate,
    )
    halo_one = reset(end, marks_ref[own : own + 1, 0:1])
    halo_two = reset(
        advance(halo_one, row(key_ref, own), row(value_ref, own), rate), marks_ref[own + 1 : own + 2, 0:1]
    )
    halo_zero = reset(incoming, marks_ref[own + 2 : own + 3, 0:1])
    rest = jnp.zeros((ROW_TILE - 3, features), jnp.float32)
    halo_state = tuple(
        jnp.concatenate([halo_one[k], halo_two[k], halo_zero[k], rest + (NEGATIVE if k == 2 else 0.0)], axis=0)
        for k in range(3)
    )
    attend(tiles - 1, ROW_TILE, halo_state, key_ref[own:rows], value_ref[own:rows], recept_ref[own:rows])

    def pack(first, size):
        at = pl.ds(first, size)
        mixed[at] = ext[at].astype(jnp.bfloat16)
        gw[at] = value_acc[at]

    for_rows(rows, pack)
    pack(own, ROW_TILE)
    await_blocks(pool_ref, store, sem.at[0], at_out, per)

    def write_resid(cols, piece):
        unit[:, cols] = x_ref[:, cols].astype(jnp.float32) + piece

    times_weight(mixed, store, at_out, per, write_resid)

    def norm(first, size):
        at = pl.ds(first, size)
        resid = unit[at]
        resid_grad[at] = resid
        out, inv = unit_norm(resid)
        unit[at] = out
        inverse[at] = inv
        ext[pl.ds(pl.multiple_of(first + 8, 8), size)] = out * vec_ref[7:8] + vec_ref[8:9]

    for_rows(rows, norm)
    norm(own, ROW_TILE)
    shift_in(ext, own)

    def mix(first, size, here, before):
        for r, ref in ((9, low_key), (10, low_recept)):
            weight = vec_ref[r : r + 1]
            ref[pl.ds(first, size)] = (weight * here + (1.0 - weight) * before).astype(jnp.bfloat16)

    for_rows(rows, lambda first, size: mix(first, size, *normed_pair(ext, marks_ref, first, size)))
    mix(own, ROW_TILE, ext[own + 8 : own + 8 + ROW_TILE], halo_previous(ext, own, features) * marks_ref[own:rows, 1:2])

    await_blocks(pool_ref, store, sem.at[1], at_key, ff)

    def write_hidden(cols, piece):
        up = jnp.maximum(piece, 0.0)
        hidden[:, cols] = up
        squared[:, cols] = (up * up).astype(jnp.bfloat16)

    times_weight_back(low_key, store, at_key, ff, write_hidden)
    await_blocks(pool_ref, store, sem.at[2], at_value, ff)

    def write_value(cols, piece):
        value_acc[:, cols] = piece

    times_weight(squared, store, at_value, ff, write_value)
    await_blocks(pool_ref, store, sem.at[3], at_recept, per)

    def write_gate(cols, piece):
        gate[:, cols] = piece

    times_weight(low_recept, store, at_recept, per, write_gate)

    def finish(first, size):
        at = pl.ds(first, size)
        opened = jax.nn.sigmoid(gate[at])
        value = value_acc[at]
        grad = grad_ref[at].astype(jnp.float32) * opened
        gcv[at] = grad.astype(jnp.bfloat16)
        gcg[at] = (grad * value * (1.0 - opened)).astype(jnp.bfloat16)
        return resid_grad[at] + opened * value

    def finish_own(first, size):
        out = finish(first, size)
        for k in range(size // CHUNKS):
            put_step(wide, first // CHUNKS + k, length, out[CHUNKS * k : CHUNKS * (k + 1)])

    for_rows(rows, finish_own)
    finish(own, ROW_TILE)

    def emit(first, size):
        layer_ref[pl.ds(first, size)] = take_rows(wide, pl.ds(first, size)).astype(jnp.bfloat16)

    for_rows(rows, emit)

    def write_hidden_grad(cols, piece):
        hidden_grad[:, cols] = (piece * (2.0 * hidden[:, cols])).astype(jnp.bfloat16)

    times_weight_back(gcv, store, at_value, ff, write_hidden_grad)
    weight_gradient(squared, gcv, own, slot_ref, slot_grad, store, out_sem.at[2], 5 * per + ff, at_value)
    times_weight(hidden_grad, store, at_key, ff, write_value)
    weight_gradient(hidden_grad, low_key, own, slot_ref, slot_grad, store, out_sem.at[1], 5 * per, at_key)
    times_weight_back(gcg, store, at_recept, per, write_gate)
    weight_gradient(low_recept, gcg, own, slot_ref, slot_grad, store, out_sem.at[3], 4 * per, at_recept)
    carried = hidden.at[:, 0:features]
    mix_key, mix_recept = vec_ref[9:10], vec_ref[10:11]

    def carry_over(first, size):
        at = pl.ds(first, size)
        carried[at] = marks_ref[at, 1:2] * ((1.0 - mix_key) * value_acc[at] + (1.0 - mix_recept) * gate[at])

    for_rows(rows, carry_over)
    carry_over(own, ROW_TILE)
    halo_next = jnp.concatenate(
        [carried[own + 1 : own + 2], jnp.zeros((ROW_TILE - 1, features), jnp.float32)], axis=0
    )
    carried[own : own + 8] = jnp.concatenate([carried[1:8], carried[own : own + 1]], axis=0)

    def norm_back(first, size, following):
        at = pl.ds(first, size)
        grad = mix_key * value_acc[at] + mix_recept * gate[at] + following
        scaled = grad * vec_ref[7:8]
        inner = (
            scaled
            - jnp.mean(scaled, axis=1, keepdims=True)
            - unit[at] * jnp.mean(scaled * unit[at], axis=1, keepdims=True)
        )
        total = grad_ref[at].astype(jnp.float32) + inner * inverse[at]
        resid_grad[at] = total
        attn_grad[at] = total.astype(jnp.bfloat16)
        return grad

    def back_step(first, size, *sums):
        at = pl.ds(first, size)
        grad = norm_back(first, size, carried[pl.ds(pl.multiple_of(first + 8, 8), size)])
        here, before = normed_pair(ext, marks_ref, first, size)
        spread = here - before
        return (
            sums[0] + fold(grad * unit[at]),
            sums[1] + fold(grad),
            sums[2] + fold(value_acc[at] * spread),
            sums[3] + fold(gate[at] * spread),
        )

    blank = jnp.zeros((CHUNKS, features), jnp.float32)
    sums = for_rows(rows, back_step, (blank,) * 4)
    for k in range(4):
        sums_ref[k : k + 1] = jnp.sum(sums[k], axis=0, keepdims=True)
    norm_back(own, ROW_TILE, halo_next)

    times_weight_back(attn_grad, store, at_out, per, write_gate)
    weight_gradient(mixed, attn_grad, own, slot_ref, slot_grad, store, out_sem.at[0], 3 * per, at_out)

    def gate_back(first, size):
        at = pl.ds(first, size)
        opened = jax.nn.sigmoid(recept_ref[at])
        grad = gate[at] * opened
        ext[at] = grad * gw[at]
        gw[at] = grad
        recept_grad[at] = (grad * wkv[at] * (1.0 - opened)).astype(jnp.bfloat16)

    for_rows(rows, gate_back)
    gate_back(own, ROW_TILE)

    def back_token(state, share, out, top, start):
        older = state[2] - rate
        high = jnp.maximum(older, -top)
        old, new = jnp.exp(older - high), jnp.exp(-top - high)
        return reset((old * state[0] + new * share, old * state[1] - new * share * out, high), start)

    for k in range(3):
        state_copy(k, full_out).wait()
    back_num, back_den, back_max = full_num, full_den, full_max

    def back_scan(n, state):
        i = length - 1 - n
        at = rows_at(i, CHUNKS)
        back_num[at], back_den[at], back_max[at] = state
        return back_token(state, ext[at], wkv[at], top_log[at], marks_ref[at, 0:1])

    heads = lax.fori_loop(0, length, back_scan, (blank, blank, blank + NEGATIVE))
    for k in range(3):
        state_copy(k, back_out).start()
    nothing = jnp.zeros((1, features), jnp.float32)
    after = back_token(
        (nothing, nothing, nothing + NEGATIVE),
        row(ext, own), row(wkv, own), row(top_log, own), marks_ref[own : own + 1, 0:1],
    )
    for c in range(CHUNKS - 1, -1, -1):
        for k in range(3):
            suffix_ref[k, c : c + 1] = after[k]
        if c > 0:
            old = aged(after, float(length), chunk_ref[c : c + 1, 0:1], rate)
            after = merge(tuple(item[c : c + 1] for item in heads), old)
    first = (row(back_num, 0), row(back_den, 0), row(back_max, 0))
    last = merge(first, aged(after, float(length - 1), marks_ref[0:1, 3:4], rate))
    summary_ref[...] = jnp.concatenate(last, axis=0)
    for k, (place, count) in enumerate(((at_out, per), (at_key, ff), (at_value, ff), (at_recept, per))):
        await_gradient(store, slot_grad, out_sem.at[k], place, count)
    for k in range(3):
        state_copy(k, back_out).wait()


def middle_pass(slots, x_rows, grad_rows, vectors, marks, chunk_marks, incoming, opened, pool):
    key, value, recept, num, den, top, prefix = opened
    rows, features = x_rows.shape
    own = rows - ROW_TILE
    full = jax.ShapeDtypeStruct((rows, features), jnp.float32)
    part = jax.ShapeDtypeStruct((own, features), jnp.float32)
    low = jax.ShapeDtypeStruct((rows, features), jnp.bfloat16)
    vmem = pl.BlockSpec(memory_space=pltpu.VMEM)
    anywhere = pl.BlockSpec(memory_space=pl.ANY)
    f32 = lambda *shape: pltpu.VMEM(shape, jnp.float32)
    b16 = lambda *shape: pltpu.VMEM(shape, jnp.bfloat16)
    return pl.pallas_call(
        middle_kernel,
        out_shape=(
            jax.ShapeDtypeStruct((own, features), jnp.bfloat16),
            full, full, full, full, low,
            jax.ShapeDtypeStruct((3, CHUNKS, features), jnp.float32),
            jax.ShapeDtypeStruct((3, features), jnp.float32),
            jax.ShapeDtypeStruct((4, features), jnp.float32),
            jax.ShapeDtypeStruct((3, own, features), jnp.float32),
            jax.ShapeDtypeStruct((3, own, features), jnp.float32),
            jax.ShapeDtypeStruct(pool.shape, jnp.bfloat16),
        ),
        in_specs=[pl.BlockSpec(memory_space=pltpu.SMEM)] + [vmem] * 13 + [anywhere],
        out_specs=(vmem,) * 9 + (anywhere,) * 3,
        scratch_shapes=[
            f32(own, features),
            f32(own, features),
            f32(own, features),
            b16(rows, features),
            f32(rows + 8, features),
            f32(rows, features),
            f32(rows, 1),
            b16(rows, features),
            b16(rows, features),
            f32(rows, FF),
            b16(rows, FF),
            f32(rows, features),
            f32(rows, features),
            b16(rows, features),
            b16(rows, features),
            b16(rows, FF),
            b16(rows, features),
            f32(rows, features),
            f32(features // LANES, own, LANES),
            b16((2 * EMBED_SIZE + 2 * FF) // BLOCK_ROWS, BLOCK_ROWS, features),
            pltpu.SemaphoreType.DMA((4,)),
            pltpu.SemaphoreType.DMA((4,)),
            pltpu.SemaphoreType.DMA((3,)),
        ],
        compiler_params=pltpu.CompilerParams(vmem_limit_bytes=VMEM_BYTES),
        name="middle_pass",
    )(slots, x_rows, grad_rows, vectors, marks, chunk_marks, incoming, prefix, key, value, recept, num, den, top, pool)


def close_kernel(
    slot_ref, x_ref, vec_ref, marks_ref, chunk_ref, incoming_ref, suffix_ref, key_ref, value_ref,
    in_key, in_value, in_recept, resid_grad, wkv, gw, own_share, recept_grad, sums_two_ref, full_ref, back_ref,
    pool_ref, grads_in,
    input_ref, sums_ref, slot_grad,
    ext, unit, inverse, key_wide, value_wide, key_grad, value_grad, grad_key_in, grad_value_in, grad_recept_in,
    carried, wide, store, sem, out_sem,
):
    rows, features = x_ref.shape
    own = rows - ROW_TILE
    tiles = rows // ROW_TILE
    length = own // CHUNKS
    per = EMBED_SIZE // BLOCK_ROWS
    for m in range(3):
        fetch_blocks(slot_ref, pool_ref, store, sem.at[m], m * per, m * per, per)
    rate = jnp.exp(vec_ref[5:6])
    incoming = tuple(incoming_ref[k : k + 1] for k in range(3))
    carry = merge(
        tuple(suffix_ref[k] for k in range(3)),
        aged(tuple(jnp.broadcast_to(v, (CHUNKS, features)) for v in incoming), chunk_ref[:, 5:6], chunk_ref[:, 4:5], rate),
    )

    def spread_back(state, key, value, share, grad, out):
        direct = share * grad
        bonus_grad = direct * (value - out)
        lift = jnp.exp(key + state[2])
        return bonus_grad + lift * (state[0] * value + state[1]), direct + lift * state[0], bonus_grad

    def token(i, sums):
        at = rows_at(i, CHUNKS)
        distance = (length - 1 - i).astype(jnp.float32)
        state = merge(tuple(back_ref[k, at] for k in range(3)), aged(carry, distance, marks_ref[at, 3:4], rate))
        key_g, value_g, bonus_grad = spread_back(state, key_ref[at], value_ref[at], own_share[at], gw[at], wkv[at])
        key_wide[at] = key_g
        value_wide[at] = value_g
        fade = jnp.exp(state[2] + full_ref[2, at] - rate) * (state[0] * full_ref[0, at] + state[1] * full_ref[1, at])
        return sums[0] + fade, sums[1] + bonus_grad

    blank = jnp.zeros((CHUNKS, features), jnp.float32)
    fade, bonus_sum = lax.fori_loop(0, length, token, (blank, blank))
    sums_ref[5:6] = -rate * jnp.sum(fade, axis=0, keepdims=True)
    sums_ref[6:7] = jnp.sum(bonus_sum, axis=0, keepdims=True)
    halo = tuple(
        jnp.concatenate([incoming[k], jnp.zeros((ROW_TILE - 1, features), jnp.float32) + (NEGATIVE if k == 2 else 0.0)], axis=0)
        for k in range(3)
    )
    key_g, value_g, _ = spread_back(
        halo, key_ref[own:rows], value_ref[own:rows], own_share[own:rows], gw[own:rows], wkv[own:rows]
    )
    key_wide[own:rows] = key_g
    value_wide[own:rows] = value_g

    def pack(first, size):
        at = pl.ds(first, size)
        key_grad[at] = key_wide[at].astype(jnp.bfloat16)
        value_grad[at] = value_wide[at].astype(jnp.bfloat16)

    for_rows(rows, pack)
    pack(own, ROW_TILE)
    products = (
        (key_grad, grad_key_in, in_key),
        (value_grad, grad_value_in, in_value),
        (recept_grad, grad_recept_in, in_recept),
    )
    for m, (left, out, inputs) in enumerate(products):
        await_blocks(pool_ref, store, sem.at[m], m * per, per)

        def write(cols, piece, out=out):
            out[:, cols] = piece

        times_weight_back(left, store, m * per, per, write)
        weight_gradient(inputs, left, own, slot_ref, slot_grad, store, out_sem.at[m], m * per, m * per)

    def norm(first, size):
        at = pl.ds(first, size)
        out, inv = unit_norm(x_ref[at].astype(jnp.float32))
        unit[at] = out
        inverse[at] = inv
        ext[pl.ds(pl.multiple_of(first + 8, 8), size)] = out * vec_ref[0:1] + vec_ref[1:2]

    for_rows(rows, norm)
    norm(own, ROW_TILE)
    shift_in(ext, own)
    mixes = tuple(vec_ref[k : k + 1] for k in (2, 3, 4))

    def carry_over(first, size):
        at = pl.ds(first, size)
        total = (1.0 - mixes[0]) * grad_key_in[at] + (1.0 - mixes[1]) * grad_value_in[at] + (1.0 - mixes[2]) * grad_recept_in[at]
        carried[at] = marks_ref[at, 1:2] * total

    for_rows(rows, carry_over)
    carry_over(own, ROW_TILE)
    carried[own : own + 8] = jnp.concatenate([carried[1:8], carried[own : own + 1]], axis=0)

    def back_step(first, size, *sums):
        at = pl.ds(first, size)
        grads = (grad_key_in[at], grad_value_in[at], grad_recept_in[at])
        grad = carried[pl.ds(pl.multiple_of(first + 8, 8), size)]
        for weight, piece in zip(mixes, grads):
            grad = grad + weight * piece
        scaled = grad * vec_ref[0:1]
        inner = (
            scaled
            - jnp.mean(scaled, axis=1, keepdims=True)
            - unit[at] * jnp.mean(scaled * unit[at], axis=1, keepdims=True)
        )
        out = resid_grad[at] + inner * inverse[at]
        for k in range(size // CHUNKS):
            put_step(wide, first // CHUNKS + k, length, out[CHUNKS * k : CHUNKS * (k + 1)])
        here, before = normed_pair(ext, marks_ref, first, size)
        spread = here - before
        return (sums[0] + fold(grad * unit[at]), sums[1] + fold(grad)) + tuple(
            s + fold(piece * spread) for s, piece in zip(sums[2:], grads)
        )

    sums = for_rows(rows, back_step, (blank,) * 5)
    for k in range(5):
        sums_ref[k : k + 1] = jnp.sum(sums[k], axis=0, keepdims=True)
    sums_ref[7:] = sums_two_ref[...]

    def emit(first, size):
        input_ref[pl.ds(first, size)] = take_rows(wide, pl.ds(first, size))

    for_rows(rows, emit)
    for m in range(3):
        await_gradient(store, slot_grad, out_sem.at[m], m * per, per)


def close_pass(slots, x_rows, vectors, marks, chunk_marks, incoming, suffix, key, value, lows, kept, pool, slot_grad):
    rows, features = x_rows.shape
    own = rows - ROW_TILE
    vmem = pl.BlockSpec(memory_space=pltpu.VMEM)
    anywhere = pl.BlockSpec(memory_space=pl.ANY)
    f32 = lambda *shape: pltpu.VMEM(shape, jnp.float32)
    b16 = lambda *shape: pltpu.VMEM(shape, jnp.bfloat16)
    operands = (slots, x_rows, vectors, marks, chunk_marks, incoming, suffix, key, value) + lows + kept + (pool, slot_grad)
    return pl.pallas_call(
        close_kernel,
        out_shape=(
            jax.ShapeDtypeStruct((own, features), jnp.float32),
            jax.ShapeDtypeStruct(vectors.shape, jnp.float32),
            jax.ShapeDtypeStruct(pool.shape, jnp.bfloat16),
        ),
        in_specs=[pl.BlockSpec(memory_space=pltpu.SMEM)] + [vmem] * (len(operands) - 3) + [anywhere] * 2,
        out_specs=(vmem, vmem, anywhere),
        input_output_aliases={len(operands) - 1: 2},
        scratch_shapes=[
            f32(rows + 8, features),
            f32(rows, features),
            f32(rows, 1),
            f32(rows, features),
            f32(rows, features),
            b16(rows, features),
            b16(rows, features),
            f32(rows, features),
            f32(rows, features),
            f32(rows, features),
            f32(rows, features),
            f32(features // LANES, own, LANES),
            b16(3 * EMBED_SIZE // BLOCK_ROWS, BLOCK_ROWS, features),
            pltpu.SemaphoreType.DMA((3,)),
            pltpu.SemaphoreType.DMA((3,)),
        ],
        compiler_params=pltpu.CompilerParams(vmem_limit_bytes=VMEM_BYTES),
        name="close_pass",
    )(*operands)


def chain_kernel(forward, tokens, own_ref, vec_ref, link_ref, flag_ref, out_ref, near, chips, joint, send_sem, recv_sem):
    me, core, _, _, _ = grid_place()
    chip = me // 2
    count = GRID_DEVICES // 2
    sign = 1 if forward else -1
    before = chip if forward else count - 1 - chip
    sibling = me + 1 - 2 * core
    chips[...] = jnp.zeros_like(chips)
    bar = pltpu.get_barrier_semaphore()
    pl.semaphore_signal(bar, inc=1, device_id=(sibling,), device_id_type=MESH)
    for o in range(1, count):
        @pl.when(o <= before)
        def _():
            pl.semaphore_signal(bar, inc=1, device_id=(me - 2 * sign * o,), device_id_type=MESH)
    pl.semaphore_wait(bar, count - before)
    swap = pltpu.make_async_remote_copy(
        src_ref=own_ref, dst_ref=near, send_sem=send_sem.at[0], recv_sem=recv_sem.at[0],
        device_id=(sibling,), device_id_type=MESH,
    )
    swap.start()
    rate = jnp.exp(vec_ref[5:6])
    at = 0 if forward else 2
    swap.wait()
    mine = tuple(own_ref[k : k + 1] for k in range(3))
    other = tuple(near[k : k + 1] for k in range(3))
    second = (core == 1) if forward else (core == 0)
    one = tuple(jnp.where(second, b, a) for a, b in zip(mine, other))
    two = tuple(jnp.where(second, a, b) for a, b in zip(mine, other))
    joint[...] = jnp.concatenate(merge(two, aged(one, float(tokens), flag_ref[0:1, at : at + 1], rate)), axis=0)

    def copy(o, place, peer):
        return pltpu.make_async_remote_copy(
            src_ref=joint, dst_ref=chips.at[place], send_sem=send_sem.at[o], recv_sem=recv_sem.at[o],
            device_id=(peer,), device_id_type=MESH,
        )

    for o in range(1, count):
        @pl.when(o < count - before)
        def _():
            copy(o, chip, me + 2 * sign * o).start()
    for o in range(1, count):
        @pl.when(o <= before)
        def _():
            copy(o, chip - sign * o, sibling).wait_recv()
    logs = jnp.where(link_ref[:, at : at + 1] > 0.5, chips[:, 2] - link_ref[:, at + 1 : at + 2] * rate, NEGATIVE)
    top = jnp.max(logs, axis=0, keepdims=True)
    weight = jnp.exp(logs - top)
    prior = (
        jnp.sum(weight * chips[:, 0], axis=0, keepdims=True),
        jnp.sum(weight * chips[:, 1], axis=0, keepdims=True),
        top,
    )
    beside = merge(one, aged(prior, float(tokens), flag_ref[0:1, at + 1 : at + 2], rate))
    out_ref[...] = jnp.concatenate([jnp.where(second, b, a) for a, b in zip(prior, beside)], axis=0)
    for o in range(1, count):
        @pl.when(o < count - before)
        def _():
            copy(o, chip, me + 2 * sign * o).wait_send()


def chain_state(rows, vectors, links, flags, forward, tokens, cid):
    devices = lax.axis_size("seq")
    if devices != GRID_DEVICES:
        every = lax.all_gather(rows[None], "seq", axis=0, tiled=True)
        at = 0 if forward else 2
        aged_logs = every[:, 2] - links[:, at + 1 : at + 2] * jnp.exp(vectors[5])
        logs = jnp.where(links[:, at : at + 1] > 0.5, aged_logs, NEGATIVE)
        top = jnp.max(logs, axis=0)
        weight = jnp.exp(logs - top)
        return jnp.stack([jnp.sum(weight * every[:, 0], axis=0), jnp.sum(weight * every[:, 1], axis=0), top])
    count = devices // 2
    vmem = pl.BlockSpec(memory_space=pltpu.VMEM)
    return pl.pallas_call(
        functools.partial(chain_kernel, forward, tokens),
        out_shape=jax.ShapeDtypeStruct(rows.shape, jnp.float32),
        in_specs=[vmem] * 4,
        out_specs=vmem,
        scratch_shapes=[
            pltpu.VMEM(rows.shape, jnp.float32),
            pltpu.VMEM((count,) + rows.shape, jnp.float32),
            pltpu.VMEM(rows.shape, jnp.float32),
            pltpu.SemaphoreType.DMA((count,)),
            pltpu.SemaphoreType.DMA((count,)),
        ],
        compiler_params=pltpu.CompilerParams(collective_id=cid, has_side_effects=True),
        name="chain_forward" if forward else "chain_backward",
    )(rows, vectors, links, flags)


def body(
    tokens_in,
    cotangent,
    pad_mask,
    doc_lengths,
    masters,
    moment_one,
    moment_two,
    block_slot,
    vectors,
    vector_one,
    vector_two,
):
    tokens, features = tokens_in.shape
    devices = lax.axis_size("seq")
    device_place = lax.axis_index("seq")
    owned_rows = masters.astype(jnp.bfloat16)
    out_grad = cotangent * pad_mask.astype(cotangent.dtype)[:, None]
    if devices == GRID_DEVICES:
        gathered, *halo = gather_blocks(owned_rows, tokens_in, out_grad)
        gathered = gathered.reshape(-1, BLOCK_ROWS, features)
    else:
        gathered = lax.all_gather(owned_rows, "seq", axis=0, tiled=True)
        halo = [
            shifted(tokens_in[:ROW_TILE], "seq", -1),
            shifted(out_grad[:ROW_TILE], "seq", -1),
            shifted(tokens_in[tokens - ROW_TILE :], "seq", 1),
        ]
    (
        x_rows, grad_rows, marks, chunk_marks, links, flags,
        key, value, recept, num, den, top, in_key, in_value, in_recept, prefix, summary,
    ) = open_pass(devices, block_slot, doc_lengths, tokens_in, out_grad, halo, vectors, gathered)
    incoming = chain_state(summary, vectors, links, flags, True, tokens, 3)
    (
        layer_out, resid_grad, wkv, gw, own_share, recept_grad, suffix, back_summary, sums_two,
        full_state, back_state, slot_grad,
    ) = middle_pass(
        block_slot, x_rows, grad_rows, vectors, marks, chunk_marks, incoming,
        (key, value, recept, num, den, top, prefix), gathered,
    )
    back_incoming = chain_state(back_summary, vectors, links, flags, False, tokens, 4)
    input_grad, stacked, slot_grad = close_pass(
        block_slot, x_rows, vectors, marks, chunk_marks, back_incoming, suffix, key, value,
        (in_key, in_value, in_recept),
        (resid_grad, wkv, gw, own_share, recept_grad, sums_two, full_state, back_state),
        gathered, slot_grad,
    )
    own_slots = device_place * masters.shape[0] + jnp.arange(masters.shape[0], dtype=jnp.int32)
    named = jnp.any(own_slots[:, None] == block_slot[None, :], axis=1)
    if devices == GRID_DEVICES:
        owner_grad, vector_grad = scatter_blocks(slot_grad.reshape((devices,) + masters.shape), stacked)
        owner_grad = owner_grad.astype(jnp.float32)
    else:
        owner_grad = lax.psum_scatter(
            slot_grad.astype(jnp.float32), "seq", scatter_dimension=0, tiled=True
        )
        vector_grad = lax.psum(stacked, "seq")
    owner_grad = jnp.where(named[:, None, None], owner_grad, 0.0)
    new_one, new_two, new_master = adam_update(
        masters, moment_one, moment_two, owner_grad, MATRIX_RATE, WEIGHT_DECAY
    )
    vector_rates = jnp.array(VECTOR_RATE, jnp.float32)[:, None]
    vector_first, vector_second, vector_next = adam_update(
        vectors, vector_one, vector_two, vector_grad, vector_rates, 0.0
    )
    return (
        layer_out,
        input_grad,
        new_one,
        new_two,
        new_master,
        vector_first,
        vector_second,
        vector_next,
    )


def solution(mesh):
    placed = (
        P("seq", None),
        P("seq", None),
        P("seq"),
        P(),
        P("seq", None, None),
        P("seq", None, None),
        P("seq", None, None),
        P(),
        P(),
        P(),
        P(),
    )
    return jax.shard_map(
        body,
        mesh=mesh,
        in_specs=placed,
        out_specs=(
            P("seq", None),
            P("seq", None),
            P("seq", None, None),
            P("seq", None, None),
            P("seq", None, None),
            P(),
            P(),
            P(),
        ),
        check_vma=False,
    )
```

```python
import functools

import jax
import jax.numpy as jnp
from jax import lax
from jax.experimental import pallas as pl
from jax.experimental.pallas import tpu as pltpu
from jax.sharding import PartitionSpec as P

EMBED_SIZE = 1024
FF = 4096
BLOCK_ROWS = 32
ROWS_ALL = 13312
BLOCKS = 416
STEP = 10
GRID_DEVICES = 32
MESH = pl.DeviceIdType.MESH


NEGATIVE = -1e30
NORM_EPS = 1e-05
BETA_ONE = 0.9
BETA_TWO = 0.999
ADAM_EPS = 1e-08
MATRIX_RATE = 0.05
WEIGHT_DECAY = 0.01
VECTOR_RATE = (0.25, 0.25, 0.25, 0.25, 0.25, 2.0, 0.25, 0.25, 0.25, 0.25, 0.25)


def shifted(block, axis, distance):
    devices = range(lax.axis_size(axis))
    route = [(i - distance, i) for i in devices if i - distance in devices]
    return lax.ppermute(block, axis, route)


def product_back(left_side, right_side):
    return lax.dot_general(
        left_side, right_side, (((1,), (1,)), ((), ())), preferred_element_type=jnp.float32
    )


def product_left(left_side, right_side):
    return lax.dot_general(
        left_side, right_side, (((0,), (0,)), ((), ())), preferred_element_type=jnp.float32
    )


def adam_update(weight, first_moment, second_moment, gradient, step_rate, feature_fade_speed):
    first_moment = BETA_ONE * first_moment + (1.0 - BETA_ONE) * gradient
    second_moment = BETA_TWO * second_moment + (1.0 - BETA_TWO) * gradient * gradient
    first_fixed = first_moment / (1.0 - BETA_ONE**STEP)
    second_fixed = second_moment / (1.0 - BETA_TWO**STEP)
    weight = weight - step_rate * (
        first_fixed / (jnp.sqrt(second_fixed) + ADAM_EPS) + feature_fade_speed * weight
    )
    return (first_moment, second_moment, weight)


def grid_place():
    me = lax.axis_index("seq")
    return me, lax.rem(me, 2), lax.rem(me // 2, 2), lax.rem(me // 4, 2), me // 8

def spans(slots):
    side = 4 * slots // 15
    cuts = [0, side, 2 * side, slots]
    return [(cuts[i], cuts[i + 1] - cuts[i]) for i in range(3)]

def gather_kernel(
    slots, doc_ref, master_ref, tokens_ref, cot_ref, pad_ref, vec_ref,
    out_ref, x_ref, grad_ref, marks_ref, chunk_ref, link_ref, flag_ref, in_key, in_value, in_recept,
    column, ext, wide, wide_grad, own_ref, head_grad, after_ref, after_grad_ref, before_ref,
    *scratch,
):
    send_sem, recv_sem, sib_send, sib_recv, own_sem, halo_send, halo_recv = scratch
    me, core, x, y, z = grid_place()
    sib = me + 1 - 2 * core
    x_peer = me + 2 - 4 * x
    y_peer = me + 4 - 8 * y
    up = me + 8
    down = me - 8
    bar = pltpu.get_barrier_semaphore()
    pl.semaphore_signal(bar, inc=1, device_id=(sib,), device_id_type=MESH)
    pl.semaphore_signal(bar, inc=1, device_id=(x_peer,), device_id_type=MESH)
    pl.semaphore_signal(bar, inc=1, device_id=(y_peer,), device_id_type=MESH)
    @pl.when(z < 3)
    def _():
        pl.semaphore_signal(bar, inc=1, device_id=(up,), device_id_type=MESH)
    @pl.when(z > 0)
    def _():
        pl.semaphore_signal(bar, inc=1, device_id=(down,), device_id_type=MESH)
    more, less = me < GRID_DEVICES - 1, me > 0

    @pl.when(more)
    def _():
        pl.semaphore_signal(bar, inc=1, device_id=(me + 1,), device_id_type=MESH)

    @pl.when(less)
    def _():
        pl.semaphore_signal(bar, inc=1, device_id=(me - 1,), device_id_type=MESH)

    def lower(s, carry):
        own_ref[s] = master_ref[s].astype(own_ref.dtype)
        return carry

    lax.fori_loop(0, slots, lower, 0)
    mask_column(pad_ref, column)
    head_grad[...] = (cot_ref[0:ROW_TILE].astype(jnp.float32) * column[0:ROW_TILE]).astype(jnp.bfloat16)
    halos = jnp.where(more, 1, 0) + jnp.where(less, 1, 0)
    pl.semaphore_wait(bar, 4 + jnp.where((z > 0) & (z < 3), 1, 0) + halos)
    tokens = tokens_ref.shape[0]

    def halo_copy(k):
        src, dst, peer = (
            (tokens_ref.at[pl.ds(0, ROW_TILE)], after_ref, me - 1),
            (head_grad, after_grad_ref, me - 1),
            (tokens_ref.at[pl.ds(tokens - ROW_TILE, ROW_TILE)], before_ref, me + 1),
        )[k]
        return pltpu.make_async_remote_copy(src_ref=src, dst_ref=dst, send_sem=halo_send.at[k],
            recv_sem=halo_recv.at[k], device_id=(peer,), device_id_type=MESH)
    span = spans(slots)
    targets = (x_peer, y_peer, up, down)

    def chip(cx, cy, cz):
        return (cz * 2 + cy) * 2 + cx

    def view(cx, cy, cz, color, c=None):
        dev = chip(cx, cy, cz) * 2 + (core if c is None else c)
        lo, n = span[color]
        return out_ref.at[dev, pl.ds(lo, n)]

    def send(cx, cy, cz, color, way, own=False):
        lo, n = span[color]
        src = own_ref.at[pl.ds(lo, n)] if own else view(cx, cy, cz, color)
        idx = chip(cx, cy, cz)
        return pltpu.make_async_remote_copy(src_ref=src, dst_ref=view(cx, cy, cz, color),
            send_sem=send_sem.at[idx, color, way], recv_sem=recv_sem.at[idx, color],
            device_id=(targets[way],), device_id_type=MESH)

    def send_sib(cx, cy, cz, color, own=False):
        lo, n = span[color]
        src = own_ref.at[pl.ds(lo, n)] if own else view(cx, cy, cz, color)
        idx = chip(cx, cy, cz)
        return pltpu.make_async_remote_copy(src_ref=src, dst_ref=view(cx, cy, cz, color),
            send_sem=sib_send.at[idx, color], recv_sem=sib_recv.at[idx, color],
            device_id=(sib,), device_id_type=MESH)

    x2, y2 = 1 - x, 1 - y
    pending = []

    def go(copy, cond=None):
        if cond is None:
            copy.start()
        else:
            @pl.when(cond)
            def _():
                copy.start()
        pending.append((copy, cond))

    zup, zdown = z < 3, z > 0
    own_copies = []
    for color in range(3):
        lo, n = span[color]
        cp = pltpu.make_async_copy(own_ref.at[pl.ds(lo, n)], view(x, y, z, color), own_sem.at[color])
        cp.start()
        own_copies.append(cp)
    order = {0: (0, 2, 1), 1: (1, 2, 0)}
    for color in (0, 1, 2):
        go(send(x, y, z, color, 2, True), zup)
        go(send(x, y, z, color, 3, True), zdown)
    for color, way in ((0, 0), (1, 1), (2, 0), (2, 1), (0, 1), (1, 0)):
        go(send(x, y, z, color, way, True))
    for color in range(3):
        go(send_sib(x, y, z, color, True))

    @pl.when(less)
    def _():
        for k in (0, 1):
            halo_copy(k).start()

    @pl.when(more)
    def _():
        halo_copy(2).start()

    marks = (marks_ref, chunk_ref, link_ref, flag_ref)
    prepare_own(
        GRID_DEVICES, doc_ref, tokens_ref, cot_ref, column, vec_ref, x_ref, grad_ref, marks, ext, wide, wide_grad
    )

    def arrive(cx, cy, cz, color):
        send(cx, cy, cz, color, 0).wait_recv()

    def sibling(cx, cy, cz, color):
        go(send_sib(cx, cy, cz, color))

    is0, is1 = core == 0, core == 1
    px = jnp.where(is0, x2, x)
    py = jnp.where(is0, y, y2)
    qx = jnp.where(is0, x, x2)
    qy = jnp.where(is0, y2, y)
    first = lambda cx, cy, cz: (go(send(cx, cy, cz, 2, 0), is0), go(send(cx, cy, cz, 2, 1), is1))
    last = lambda cx, cy, cz: (go(send(cx, cy, cz, 2, 1), is0), go(send(cx, cy, cz, 2, 0), is1))

    arrive(x2, y, z, 0)
    go(send(x2, y, z, 0, 2), zup)
    go(send(x2, y, z, 0, 3), zdown)
    go(send(x2, y, z, 0, 1))
    sibling(x2, y, z, 0)
    arrive(x, y2, z, 1)
    go(send(x, y2, z, 1, 2), zup)
    go(send(x, y2, z, 1, 3), zdown)
    go(send(x, y2, z, 1, 0))
    sibling(x, y2, z, 1)
    arrive(px, py, z, 2)
    last(px, py, z)
    sibling(px, py, z, 2)

    def wait_halo():
        @pl.when(less)
        def _():
            for k in (0, 1):
                halo_copy(k).wait_send()
            halo_copy(2).wait_recv()

        @pl.when(more)
        def _():
            halo_copy(2).wait_send()
            for k in (0, 1):
                halo_copy(k).wait_recv()

    for dist in (1, 2, 3):
        sides = []
        for sign, fwd, guard_f in ((1, 3, zdown), (-1, 2, zup)):
            q = z + sign * dist
            have = (q >= 0) & (q < 4)
            sides.append((q, fwd, have, guard_f))
        for which in ("c", "a", "b", "a2", "b2"):
            for q, fwd, have, gf in sides:
                @pl.when(have)
                def _(q=q, fwd=fwd, gf=gf, which=which):
                    if which == "c":
                        arrive(x, y, q, 2)
                        cp = send(x, y, q, 2, fwd)
                        pl.when(gf)(lambda: cp.start())
                        for w in (0, 1):
                            send(x, y, q, 2, w).start()
                        send_sib(x, y, q, 2).start()
                    else:
                        color = 0 if which[0] == "a" else 1
                        cx, cy = {"a": (x, y), "b": (x, y), "a2": (x2, y), "b2": (x, y2)}[which]
                        arrive(cx, cy, q, color)
                        cp = send(cx, cy, q, color, fwd)
                        pl.when(gf)(lambda: cp.start())
                        send(cx, cy, q, color, 1 if color == 0 else 0).start()
                        send_sib(cx, cy, q, color).start()
        for q, fwd, have, gf in sides:
            @pl.when(have)
            def _(q=q):
                arrive(px, py, q, 2)
                pl.when(is0)(lambda: send(px, py, q, 2, 1).start())
                pl.when(is1)(lambda: send(px, py, q, 2, 0).start())
                send_sib(px, py, q, 2).start()
        if dist == 1:
            tail_list = [(z, None)]
        else:
            tail_list = []
        if dist == 1:
            wait_halo()
            lows = (in_key, in_value, in_recept)
            prepare_halo(
                GRID_DEVICES, after_ref, after_grad_ref, before_ref, vec_ref, x_ref, grad_ref, marks_ref, lows, ext
            )
        def terminal(q):
            for cx, cy, color in ((x, y2, 0), (x2, y2, 0), (x2, y, 1), (x2, y2, 1), (qx, qy, 2), (x2, y2, 2)):
                arrive(cx, cy, q, color)
                send_sib(cx, cy, q, color).start()
        if dist == 1:
            terminal(z)
        else:
            for sign in (1, -1):
                q = z + sign * (dist - 1)
                pl.when((q >= 0) & (q < 4))(lambda q=q: terminal(q))
        if dist == 3:
            for sign in (1, -1):
                q = z + sign * 3
                pl.when((q >= 0) & (q < 4))(lambda q=q: terminal(q))
    for cp in own_copies:
        cp.wait()
    for color in range(3):
        pl.when(zup)(lambda color=color: send(x, y, z, color, 2).wait_send())
        pl.when(zdown)(lambda color=color: send(x, y, z, color, 3).wait_send())
        for w in (0, 1):
            send(x, y, z, color, w).wait_send()
    for cx, cy, color, w in ((x2, y, 0, 1), (x, y2, 1, 0)):
        pl.when(zup)(lambda: send(cx, cy, z, color, 2).wait_send())
        pl.when(zdown)(lambda: send(cx, cy, z, color, 3).wait_send())
        send(cx, cy, z, color, w).wait_send()
    pl.when(is0)(lambda: send(px, py, z, 2, 1).wait_send())
    pl.when(is1)(lambda: send(px, py, z, 2, 0).wait_send())
    for dist in (1, 2, 3):
        for sign, fwd, gf in ((1, 3, zdown), (-1, 2, zup)):
            q = z + sign * dist
            @pl.when((q >= 0) & (q < 4))
            def _(q=q, fwd=fwd, gf=gf):
                for cx, cy, color in ((x, y, 2), (x, y, 0), (x, y, 1), (x2, y, 0), (x, y2, 1)):
                    pl.when(gf)(lambda: send(cx, cy, q, color, fwd).wait_send())
                    ways = (0, 1) if color == 2 else ((1,) if color == 0 else (0,))
                    for w in ways:
                        send(cx, cy, q, color, w).wait_send()
                pl.when(is0)(lambda: send(px, py, q, 2, 1).wait_send())
                pl.when(is1)(lambda: send(px, py, q, 2, 0).wait_send())
    for cz in range(4):
        for cy in range(2):
            for cx in range(2):
                for color in range(3):
                    cp = send_sib(cx, cy, cz, color)
                    cp.wait_send()
                    cp.wait_recv()

def gather_blocks(masters, doc_lengths, tokens_in, cotangent, pad_rows, vectors, cid=1):
    slots = masters.shape[0]
    shapes, scratch = prepared_shapes(GRID_DEVICES, *tokens_in.shape)
    anywhere = pl.BlockSpec(memory_space=pl.ANY)
    vmem = pl.BlockSpec(memory_space=pltpu.VMEM)
    halo = pltpu.VMEM((ROW_TILE,) + tokens_in.shape[1:], jnp.bfloat16)
    return pl.pallas_call(
        functools.partial(gather_kernel, slots),
        out_shape=(jax.ShapeDtypeStruct((GRID_DEVICES,) + masters.shape, jnp.bfloat16),) + shapes,
        in_specs=[pl.BlockSpec(memory_space=pltpu.SMEM)] + [vmem] * 5,
        out_specs=(anywhere,) + (vmem,) * len(shapes),
        scratch_shapes=scratch + [
            pltpu.VMEM(masters.shape, jnp.bfloat16),
            halo, halo, halo, halo,
            pltpu.SemaphoreType.DMA((16, 3, 4)),
            pltpu.SemaphoreType.DMA((16, 3)),
            pltpu.SemaphoreType.DMA((16, 3)),
            pltpu.SemaphoreType.DMA((16, 3)),
            pltpu.SemaphoreType.DMA((3,)),
            pltpu.SemaphoreType.DMA((3,)),
            pltpu.SemaphoreType.DMA((3,)),
        ],
        compiler_params=pltpu.CompilerParams(collective_id=cid, has_side_effects=True, vmem_limit_bytes=VMEM_BYTES),
        name="gather_blocks",
    )(doc_lengths, masters, tokens_in, cotangent, pad_rows, vectors)


def scatter_kernel(
    slots, part_ref, rows_ref, out_ref, total_ref, acc, sib, xin, yin, zin, sums,
    load_sem, sib_send, sib_recv, send_sem, xsem, ysem, zsem, row_send, row_recv,
):
    me, core, x, y, z = grid_place()
    sibling = me + 1 - 2 * core
    x_peer = me + 2 - 4 * x
    y_peer = me + 4 - 8 * y
    up, down = me + 8, me - 8
    zup, zdown = z < 3, z > 0
    bar = pltpu.get_barrier_semaphore()
    for peer in (sibling, x_peer, y_peer):
        pl.semaphore_signal(bar, inc=1, device_id=(peer,), device_id_type=MESH)
    @pl.when(zup)
    def _():
        pl.semaphore_signal(bar, inc=1, device_id=(up,), device_id_type=MESH)
    @pl.when(zdown)
    def _():
        pl.semaphore_signal(bar, inc=1, device_id=(down,), device_id_type=MESH)
    far = me + 16 - 32 * (z // 2)
    pl.semaphore_signal(bar, inc=1, device_id=(far,), device_id_type=MESH)
    row_peers = (sibling, x_peer, y_peer, me + 8 - 16 * lax.rem(z, 2), far)
    sums[0] = rows_ref[...]
    span = spans(slots)
    x2, y2 = 1 - x, 1 - y
    is0, is1 = core == 0, core == 1

    def row_copy(k):
        return pltpu.make_async_remote_copy(src_ref=sums.at[2 * k], dst_ref=sums.at[2 * k + 1],
            send_sem=row_send.at[k], recv_sem=row_recv.at[k], device_id=(row_peers[k],), device_id_type=MESH)

    def row_step(k):
        row_copy(k).wait()
        sums[2 * k + 2] = sums[2 * k] + sums[2 * k + 1]
        if k < 4:
            row_copy(k + 1).start()

    def load(chip):
        return pltpu.make_async_copy(part_ref.at[2 * chip + core], acc.at[chip], load_sem.at[chip])

    def give(chip):
        return pltpu.make_async_remote_copy(src_ref=part_ref.at[2 * chip + 1 - core], dst_ref=sib.at[chip],
            send_sem=sib_send.at[chip], recv_sem=sib_recv.at[chip], device_id=(sibling,), device_id_type=MESH)

    levels = []
    for dist in (3, 2, 1):
        for sign in (1, -1):
            q = z + sign * dist
            levels.append((dist, sign, q, (q >= 0) & (q < 4)))

    def run(dist, work):
        for d, sign, q, have in levels:
            if d == dist:
                pl.when(have)(functools.partial(work, q))

    def run_signed(dist, work):
        for d, sign, q, have in levels:
            if d == dist:
                pl.when(have)(functools.partial(work, q, sign, dist))

    def begin_loads(q):
        for i in plane_order():
            load(4 * q + i).start()

    def begin_gives(q):
        for i in plane_order():
            give(4 * q + i).start()

    def plane_order():
        return (2 * y2 + x2, 2 * y + x2, 2 * y2 + x, 2 * y + x)

    run(3, begin_loads)
    run(2, begin_loads)
    run(1, begin_loads)
    begin_loads(z)
    pl.semaphore_wait(bar, 5 + jnp.where(zup & zdown, 1, 0))
    row_copy(0).start()
    run(3, begin_gives)
    run(2, begin_gives)

    def ready(cx, cy, q):
        chip = chip_of(cx, cy, q)
        load(chip).wait()
        give(chip).wait_recv()

        def step(s, _):
            total = acc[chip, s].astype(jnp.float32) + sib[chip, s].astype(jnp.float32)
            acc[chip, s] = total.astype(acc.dtype)
            return 0

        lax.fori_loop(0, slots, step, 0)

    def chip_of(cx, cy, cz):
        return (cz * 2 + cy) * 2 + cx

    def out_copy(cx, cy, cz, color, target, buf, index, sem):
        lo, n = span[color]
        chip = chip_of(cx, cy, cz)
        return pltpu.make_async_remote_copy(src_ref=acc.at[chip, pl.ds(lo, n)], dst_ref=buf.at[index, pl.ds(0, n)],
            send_sem=send_sem.at[chip, color], recv_sem=sem.at[index], device_id=(target,), device_id_type=MESH)

    def arrived(buf, index, sem, color):
        lo, n = span[color]
        pltpu.make_async_remote_copy(src_ref=acc.at[0, pl.ds(lo, n)], dst_ref=buf.at[index, pl.ds(0, n)],
            send_sem=send_sem.at[0, color], recv_sem=sem.at[index], device_id=(sibling,), device_id_type=MESH).wait_recv()

    def add(cx, cy, cz, color, pieces):
        lo, n = span[color]
        chip = chip_of(cx, cy, cz)
        for buf, index, sem in pieces:
            arrived(buf, index, sem, color)
        def step(s, _):
            total = acc[chip, lo + s].astype(jnp.float32)
            for buf, index, _sem in pieces:
                total = total + buf[index, s].astype(jnp.float32)
            acc[chip, lo + s] = total.astype(acc.dtype)
            return 0
        lax.fori_loop(0, n, step, 0)

    def X(i): return (xin, i, xsem)
    def Y(i): return (yin, i, ysem)
    def Z(i): return (zin, i, zsem)

    def term_x(q, color, i):
        cy = (y, y2)[i]
        out_copy(x2, cy, q, color, x_peer, xin, (8 if color == 2 else 0) + 2 * q + i, xsem).start()

    def term_y(q, color, i):
        cx = (x, x2)[i]
        out_copy(cx, y2, q, color, y_peer, yin, (8 if color == 2 else 0) + 2 * q + i, ysem).start()

    def term_a(q):
        ready(x2, y2, q)
        term_x(q, 1, 1)
        term_y(q, 0, 1)

    def term_c(q):

        @pl.when(is0)
        def _():
            term_y(q, 2, 1)
            term_y(q, 2, 0)

        @pl.when(is1)
        def _():
            term_x(q, 2, 1)
            term_x(q, 2, 0)

        ready(x, y, q)

    def term_b(q):
        ready(x2, y, q)
        term_x(q, 1, 0)
        ready(x, y2, q)
        term_y(q, 0, 0)

    def plane_two(q):
        @pl.when(is0)
        def _():
            add(x2, y, q, 2, [Y(8 + 2 * q + 1)])
            out_copy(x2, y, q, 2, x_peer, xin, 8 + 2 * q, xsem).start()
        @pl.when(is1)
        def _():
            add(x, y2, q, 2, [X(8 + 2 * q + 1)])
            out_copy(x, y2, q, 2, y_peer, yin, 8 + 2 * q, ysem).start()

    def column(part, q, sign, dist):
        target = up if sign == 1 else down
        more = zdown if sign == 1 else zup
        at_target = dist == 1
        base_out = (20 if (at_target and sign == 1) else 5 * q)
        kinds = (
            (0, x, y, 2, [X(8 + 2 * q), Y(8 + 2 * q)]),
            (1, x, y, 0, [Y(2 * q)]),
            (2, x, y, 1, [X(2 * q)]),
            (3, x2, y, 0, [Y(2 * q + 1)]),
            (4, x, y2, 1, [X(2 * q + 1)]),
        )
        for k, cx, cy, color, pieces in ((kinds[4], kinds[3], kinds[2], kinds[1]), (kinds[0],))[part]:
            @pl.when(more)
            def _():
                add(cx, cy, q, color, pieces + [Z(5 * q + k)])
            @pl.when(jnp.logical_not(more))
            def _():
                add(cx, cy, q, color, pieces)
            out_copy(cx, cy, q, color, target, zin, base_out + k, zsem).start()

    planes = functools.partial(column, 0)
    last = functools.partial(column, 1)
    run(3, term_a)
    run(3, term_b)
    run(3, term_c)
    row_step(0)
    run_signed(3, planes)
    run(2, term_a)
    run(2, term_b)
    run(2, term_c)
    run(3, plane_two)
    run(1, begin_gives)
    run_signed(3, last)
    run(1, term_a)
    run(1, term_b)
    run(1, term_c)
    row_step(1)
    run_signed(2, planes)
    begin_gives(z)
    run(2, plane_two)
    term_a(z)
    term_b(z)
    term_c(z)
    run_signed(2, last)
    row_step(2)
    run_signed(1, planes)
    run(1, plane_two)
    run_signed(1, last)
    row_step(3)
    plane_two(z)
    row_step(4)
    total_ref[...] = sums[10]

    def own(k, cx, cy, color, pieces):
        @pl.when(zup & zdown)
        def _():
            add(cx, cy, z, color, pieces + [Z(5 * z + k), Z(20 + k)])
        @pl.when(zup & jnp.logical_not(zdown))
        def _():
            add(cx, cy, z, color, pieces + [Z(5 * z + k)])
        @pl.when(zdown & jnp.logical_not(zup))
        def _():
            add(cx, cy, z, color, pieces + [Z(20 + k)])
    own(3, x2, y, 0, [Y(2 * z + 1)])
    out_copy(x2, y, z, 0, x_peer, xin, 16, xsem).start()
    own(4, x, y2, 1, [X(2 * z + 1)])
    out_copy(x, y2, z, 1, y_peer, yin, 16, ysem).start()
    own(0, x, y, 2, [X(8 + 2 * z), Y(8 + 2 * z)])
    own(1, x, y, 0, [Y(2 * z), X(16)])
    own(2, x, y, 1, [X(2 * z), Y(16)])
    pltpu.sync_copy(acc.at[chip_of(x, y, z)], out_ref)
    for chip in range(16):
        give(chip).wait_send()
        for color in range(3):
            @pl.when(chip != chip_of(x, y, z))
            def _():
                lo, n = span[color]
                pltpu.make_async_remote_copy(src_ref=acc.at[chip, pl.ds(lo, n)], dst_ref=xin.at[0, pl.ds(0, n)],
                    send_sem=send_sem.at[chip, color], recv_sem=xsem.at[0], device_id=(sibling,), device_id_type=MESH).wait_send()

def scatter_blocks(part, rows, cid=2):
    _, slots, height, feats = part.shape
    most = max(n for _, n in spans(slots))
    chunk = (most, height, feats)
    dt = part.dtype
    return pl.pallas_call(
        functools.partial(scatter_kernel, slots),
        out_shape=(
            jax.ShapeDtypeStruct(part.shape[1:], dt),
            jax.ShapeDtypeStruct(rows.shape, rows.dtype),
        ),
        in_specs=[pl.BlockSpec(memory_space=pl.ANY), pl.BlockSpec(memory_space=pltpu.VMEM)],
        out_specs=(pl.BlockSpec(memory_space=pl.ANY), pl.BlockSpec(memory_space=pltpu.VMEM)),
        scratch_shapes=[
            pltpu.VMEM((16, slots, height, feats), dt),
            pltpu.VMEM((16, slots, height, feats), dt),
            pltpu.VMEM((17,) + chunk, dt),
            pltpu.VMEM((17,) + chunk, dt),
            pltpu.VMEM((25,) + chunk, dt),
            pltpu.VMEM((11,) + rows.shape, rows.dtype),
            pltpu.SemaphoreType.DMA((16,)),
            pltpu.SemaphoreType.DMA((16,)),
            pltpu.SemaphoreType.DMA((16,)),
            pltpu.SemaphoreType.DMA((16, 3)),
            pltpu.SemaphoreType.DMA((17,)),
            pltpu.SemaphoreType.DMA((17,)),
            pltpu.SemaphoreType.DMA((25,)),
            pltpu.SemaphoreType.DMA((5,)),
            pltpu.SemaphoreType.DMA((5,)),
        ],
        compiler_params=pltpu.CompilerParams(collective_id=cid, has_side_effects=True, vmem_limit_bytes=58 * 2**20),
        name="scatter_blocks",
    )(part, rows)


ROW_TILE = 16
BIG_TILE = 64
CHUNKS = 8
LANES = 128
VMEM_BYTES = 60 * 2**20


def rows_at(index, size=ROW_TILE):
    return pl.ds(pl.multiple_of(index * size, size), size)


def fetch_blocks(slot_ref, pool_ref, store_ref, sem, first_block, place, count):
    def step(b, carry):
        for k in range(4):
            pltpu.make_async_copy(
                pool_ref.at[slot_ref[first_block + 4 * b + k]], store_ref.at[place + 4 * b + k], sem
            ).start()
        return carry

    lax.fori_loop(0, count // 4, step, 0)


def await_blocks(pool_ref, store_ref, sem, place, count):
    pltpu.make_async_copy(
        pool_ref.at[pl.ds(0, count)], store_ref.at[pl.ds(place, count)], sem
    ).wait()


def times_weight(left_ref, store_ref, place, count, write, width=512):
    features = store_ref.shape[2]

    def step(n, carry):
        cols = pl.ds(pl.multiple_of(n * width, width), width)
        right = store_ref[place : place + count, :, cols].reshape(count * BLOCK_ROWS, width)
        write(cols, jnp.dot(left_ref[...], right, preferred_element_type=jnp.float32))
        return carry

    lax.fori_loop(0, features // width, step, 0)


def times_weight_back(left_ref, store_ref, place, count, write, width=1024):
    blocks = width // BLOCK_ROWS

    def step(n, carry):
        cols = pl.ds(pl.multiple_of(n * width, width), width)
        right = store_ref[pl.ds(place + n * blocks, blocks)].reshape(width, store_ref.shape[2])
        write(cols, product_back(left_ref[...], right))
        return carry

    lax.fori_loop(0, count // blocks, step, 0)


def weight_gradient(left_ref, right_ref, own, slot_ref, grad_ref, store_ref, sem, first_block, place, width=1024):
    blocks = width // BLOCK_ROWS
    steps = left_ref.shape[1] // width

    def step(n, carry):
        cols = pl.ds(pl.multiple_of(n * width, width), width)
        piece = product_left(left_ref[0:own, cols], right_ref[0:own])
        at = place + n * blocks
        store_ref[pl.ds(at, blocks)] = piece.astype(store_ref.dtype).reshape(blocks, *store_ref.shape[1:])

        def put(b, inner):
            for k in range(4):
                pltpu.make_async_copy(
                    store_ref.at[at + 4 * b + k],
                    grad_ref.at[slot_ref[first_block + n * blocks + 4 * b + k]],
                    sem,
                ).start()
            return inner

        return lax.fori_loop(0, blocks // 4, put, carry)

    lax.fori_loop(0, steps, step, 0)


def await_gradient(store_ref, grad_ref, sem, place, count):
    pltpu.make_async_copy(
        store_ref.at[pl.ds(place, count)], grad_ref.at[pl.ds(0, count)], sem
    ).wait()


def for_rows(rows, work, sums=()):
    own = rows - ROW_TILE

    def step(j, carry):
        out = work(pl.multiple_of(j * BIG_TILE, BIG_TILE), BIG_TILE, *carry)
        return carry if out is None else out

    sums = lax.fori_loop(0, own // BIG_TILE, step, sums)
    return sums


def fold(piece):
    return jnp.sum(piece.reshape(-1, CHUNKS, piece.shape[1]), axis=0)


def unit_norm(values):
    centered = values - jnp.mean(values, axis=1, keepdims=True)
    inverse = lax.rsqrt(jnp.mean(centered * centered, axis=1, keepdims=True) + NORM_EPS)
    return centered * inverse, inverse


def merge(first, second):
    top = jnp.maximum(first[2], second[2])
    one, two = jnp.exp(first[2] - top), jnp.exp(second[2] - top)
    return (one * first[0] + two * second[0], one * first[1] + two * second[1], top)


def aged(state, distance, alive, rate):
    return (state[0], state[1], jnp.where(alive > 0.5, state[2] - distance * rate, NEGATIVE))


def reset(state, start):
    cut = start > 0.5
    return (
        jnp.where(cut, 0.0, state[0]),
        jnp.where(cut, 0.0, state[1]),
        jnp.where(cut, NEGATIVE, state[2]),
    )


def advance(state, key, value, rate):
    older = state[2] - rate
    top = jnp.maximum(older, key)
    old, new = jnp.exp(older - top), jnp.exp(key - top)
    return (old * state[0] + new * value, old * state[1] + new, top)


def shift_in(ext, own):
    ext[0:8] = jnp.concatenate([ext[own + 10 : own + 11], ext[own : own + 7]], axis=0)


def halo_previous(ext, own, features):
    return jnp.concatenate(
        [
            ext[own + 7 : own + 8],
            ext[own + 8 : own + 9],
            ext[own + 11 : own + 12],
            jnp.zeros((ROW_TILE - 3, features), jnp.float32),
        ],
        axis=0,
    )


def normed_pair(ext, marks_ref, first, size):
    here = ext[pl.ds(pl.multiple_of(first + 8, 8), size)]
    before = ext[pl.ds(first, size)] * marks_ref[pl.ds(first, size), 1:2]
    return here, before


def take_step(wide, first, length):
    at = pl.ds(first, CHUNKS, stride=length)
    return jnp.concatenate([wide[k, at] for k in range(wide.shape[0])], axis=1)


def put_step(wide, first, length, tile):
    at = pl.ds(first, CHUNKS, stride=length)
    lanes = wide.shape[2]
    for k in range(wide.shape[0]):
        wide[k, at] = tile[:, k * lanes : (k + 1) * lanes]


def take_rows(wide, at):
    return jnp.concatenate([wide[k, at] for k in range(wide.shape[0])], axis=1)


def put_rows(wide, at, tile):
    lanes = wide.shape[2]
    for k in range(wide.shape[0]):
        wide[k, at] = tile[:, k * lanes : (k + 1) * lanes]


def none_between(offsets, low, high):
    hit = None
    for offset in offsets:
        inside = (low <= offset) & (offset <= high)
        hit = inside if hit is None else hit | inside
    return jnp.where(hit, 0.0, 1.0)


def write_marks(doc_ref, marks_ref, chunk_ref, link_ref, flag_ref, own, devices):
    rows = marks_ref.shape[0]
    length = own // CHUNKS
    total = own * devices
    me = lax.axis_index("seq")
    first = me * own
    offsets = [jnp.int32(0)]
    for k in range(doc_ref.shape[0] - 1):
        offsets.append(offsets[-1] + doc_ref[k])
    row = lax.broadcasted_iota(jnp.int32, (rows, 1), 0)
    chunk, step = lax.rem(row, CHUNKS), row // CHUNKS
    extra = jnp.where(row < own + 2, row, own - 1 - (row - (own + 2)) - own)
    place = first + jnp.where(row < own, chunk * length + step, extra)
    inside = (place >= 0) & (place < total)
    keep = jnp.where(inside, none_between(offsets, place, place), 0.0)
    begin = first + chunk * length
    marks_ref[:, 0:1] = 1.0 - keep
    marks_ref[:, 1:2] = keep
    marks_ref[:, 2:3] = jnp.where(row < own, none_between(offsets, begin, place), 1.0)
    marks_ref[:, 3:4] = jnp.where(row < own, none_between(offsets, place + 1, begin + length - 1), 1.0)
    chunk = lax.broadcasted_iota(jnp.int32, (CHUNKS, 1), 0)
    begin = first + chunk * length
    end = begin + length - 1
    chunk_ref[:, 0:1] = none_between(offsets, begin, end)
    chunk_ref[:, 1:2] = jnp.where(first > 0, none_between(offsets, first - 1, begin - 1), 0.0)
    chunk_ref[:, 2:3] = none_between(offsets, begin, end - 1)
    chunk_ref[:, 3:4] = (1 + chunk * length).astype(jnp.float32)
    chunk_ref[:, 4:5] = jnp.where(first + own < total, none_between(offsets, end + 1, first + own), 0.0)
    chunk_ref[:, 5:6] = (1 + (CHUNKS - 1 - chunk) * length).astype(jnp.float32)
    count = link_ref.shape[0]
    group = devices // count
    span = own * group
    here = me // group
    other = lax.broadcasted_iota(jnp.int32, (count, 1), 0)
    link_ref[:, 0:1] = jnp.where(other < here, none_between(offsets, span * (other + 1) - 1, span * here - 2), 0.0)
    link_ref[:, 1:2] = (span * (here - 1 - other)).astype(jnp.float32)
    link_ref[:, 2:3] = jnp.where(other > here, none_between(offsets, span * (here + 1) + 1, span * other), 0.0)
    link_ref[:, 3:4] = (span * (other - here - 1)).astype(jnp.float32)
    pair = span * here + jnp.zeros((1, 1), jnp.int32)
    flag_ref[:, 0:1] = none_between(offsets, pair + own - 1, pair + 2 * own - 2)
    flag_ref[:, 1:2] = none_between(offsets, pair - 1, pair + own - 2)
    flag_ref[:, 2:3] = none_between(offsets, pair + 1, pair + own)
    flag_ref[:, 3:4] = none_between(offsets, pair + own + 1, pair + 2 * own)


def mask_column(pad_ref, column):
    for k in range(pad_ref.shape[0]):
        row = pad_ref[k : k + 1].astype(jnp.float32)
        column[k * LANES : (k + 1) * LANES] = jnp.broadcast_to(row, (LANES, LANES)).T[:, 0:1]


def normed_rows(x_ref, vec_ref, ext, first, size, tile):
    x_ref[pl.ds(first, size)] = tile.astype(jnp.bfloat16)
    unit, _ = unit_norm(tile)
    ext[pl.ds(pl.multiple_of(first + 8, 8), size)] = unit * vec_ref[0:1] + vec_ref[1:2]


def prepare_own(devices, doc_ref, tokens_ref, grads_ref, column, vec_ref, x_ref, grad_ref, marks, ext, wide, wide_grad):
    rows = x_ref.shape[0]
    own = rows - ROW_TILE
    length = own // CHUNKS
    write_marks(doc_ref, *marks, own, devices)

    def widen(first, size):
        at = pl.ds(first, size)
        put_rows(wide, at, tokens_ref[at].astype(jnp.float32))
        put_rows(wide_grad, at, grads_ref[at].astype(jnp.float32) * column[at])

    for_rows(rows, widen)

    def arrange(first, size):
        steps = [first // CHUNKS + k for k in range(size // CHUNKS)]
        tile = jnp.concatenate([take_step(wide, i, length) for i in steps], axis=0)
        normed_rows(x_ref, vec_ref, ext, first, size, tile)
        tile = jnp.concatenate([take_step(wide_grad, i, length) for i in steps], axis=0)
        grad_ref[pl.ds(first, size)] = tile.astype(jnp.bfloat16)

    for_rows(rows, arrange)


def prepare_halo(devices, after_ref, after_grad_ref, before_ref, vec_ref, x_ref, grad_ref, marks_ref, lows, ext):
    rows, features = x_ref.shape
    own = rows - ROW_TILE
    me = lax.axis_index("seq")
    more, less = me < devices - 1, me > 0
    later = jnp.where(more, after_ref[...].astype(jnp.float32), 0.0)[0:2]
    earlier = jnp.where(less, before_ref[...].astype(jnp.float32), 0.0)
    blank_rows = jnp.zeros((ROW_TILE - 4, features), jnp.float32)
    tile = jnp.concatenate(
        [later, earlier[ROW_TILE - 1 :], earlier[ROW_TILE - 2 : ROW_TILE - 1], blank_rows], axis=0
    )
    normed_rows(x_ref, vec_ref, ext, own, ROW_TILE, tile)
    later_grad = jnp.where(more, after_grad_ref[...].astype(jnp.float32), 0.0)[0:2]
    grad_ref[own:rows] = jnp.concatenate([later_grad, blank_rows, blank_rows[:2]], axis=0).astype(jnp.bfloat16)
    shift_in(ext, own)

    def mix(first, size, here, before):
        for row, ref in zip((2, 3, 4), lows):
            weight = vec_ref[row : row + 1]
            ref[pl.ds(first, size)] = (weight * here + (1.0 - weight) * before).astype(jnp.bfloat16)

    for_rows(rows, lambda first, size: mix(first, size, *normed_pair(ext, marks_ref, first, size)))
    mix(own, ROW_TILE, ext[own + 8 : own + 8 + ROW_TILE], halo_previous(ext, own, features) * marks_ref[own:rows, 1:2])


def prepared_shapes(devices, own, features):
    rows = own + ROW_TILE
    count = devices // 2 if devices == GRID_DEVICES else devices
    low = jax.ShapeDtypeStruct((rows, features), jnp.bfloat16)
    small = lambda *shape: jax.ShapeDtypeStruct(shape, jnp.float32)
    shapes = (low, low, small(rows, 4), small(CHUNKS, 6), small(count, 4), small(1, 4), low, low, low)
    scratch = [
        pltpu.VMEM((own, 1), jnp.float32),
        pltpu.VMEM((rows + 8, features), jnp.float32),
        pltpu.VMEM((features // LANES, own, LANES), jnp.float32),
        pltpu.VMEM((features // LANES, own, LANES), jnp.float32),
    ]
    return shapes, scratch


def prepare_kernel(
    devices, doc_ref, tokens_ref, grads_ref, pad_ref, after_ref, after_grad_ref, before_ref, vec_ref,
    x_ref, grad_ref, marks_ref, chunk_ref, link_ref, flag_ref, in_key, in_value, in_recept,
    column, ext, wide, wide_grad,
):
    mask_column(pad_ref, column)
    marks = (marks_ref, chunk_ref, link_ref, flag_ref)
    prepare_own(devices, doc_ref, tokens_ref, grads_ref, column, vec_ref, x_ref, grad_ref, marks, ext, wide, wide_grad)
    lows = (in_key, in_value, in_recept)
    prepare_halo(devices, after_ref, after_grad_ref, before_ref, vec_ref, x_ref, grad_ref, marks_ref, lows, ext)


def prepare_pass(devices, doc_lengths, tokens_in, cotangent, pad_rows, halo, vectors):
    shapes, scratch = prepared_shapes(devices, *tokens_in.shape)
    vmem = pl.BlockSpec(memory_space=pltpu.VMEM)
    return pl.pallas_call(
        functools.partial(prepare_kernel, devices),
        out_shape=shapes,
        in_specs=[pl.BlockSpec(memory_space=pltpu.SMEM)] + [vmem] * 7,
        out_specs=(vmem,) * len(shapes),
        scratch_shapes=scratch,
        compiler_params=pltpu.CompilerParams(vmem_limit_bytes=VMEM_BYTES),
        name="prepare_pass",
    )(doc_lengths, tokens_in, cotangent, pad_rows, *halo, vectors)


def open_kernel(
    slot_ref, vec_ref, marks_ref, chunk_ref, in_key, in_value, in_recept, pool_ref,
    key_ref, value_ref, recept_ref, num_ref, den_ref, max_ref, prefix_ref, summary_ref,
    store, sem,
):
    rows, features = in_key.shape
    own = rows - ROW_TILE
    length = own // CHUNKS
    per = EMBED_SIZE // BLOCK_ROWS
    for m in range(3):
        fetch_blocks(slot_ref, pool_ref, store, sem.at[m], m * per, m * per, per)
    for m, (left, out) in enumerate(((in_key, key_ref), (in_value, value_ref), (in_recept, recept_ref))):
        await_blocks(pool_ref, store, sem.at[m], m * per, per)

        def write(cols, piece, out=out):
            out[:, cols] = piece

        times_weight(left, store, m * per, per, write)
    rate = jnp.exp(vec_ref[5:6])

    def token(i, state, key, value):
        state = reset(state, marks_ref[rows_at(i, CHUNKS), 0:1])
        num_ref[rows_at(i, CHUNKS)], den_ref[rows_at(i, CHUNKS)], max_ref[rows_at(i, CHUNKS)] = state
        return advance(state, key, value, rate)

    def step(i, state):
        return token(i, state, key_ref[rows_at(i, CHUNKS)], value_ref[rows_at(i, CHUNKS)])

    blank = jnp.zeros((CHUNKS, features), jnp.float32)
    state = lax.fori_loop(0, length - 1, step, (blank, blank, blank + NEGATIVE))
    late = tuple(item[CHUNKS - 1 :] for item in state)
    ends = step(length - 1, state)
    prior = (value_ref[own + 2 : own + 3], jnp.ones((1, features), jnp.float32), key_ref[own + 2 : own + 3])
    for c in range(CHUNKS):
        for k in range(3):
            prefix_ref[k, c : c + 1] = prior[k]
        if c < CHUNKS - 1:
            old = aged(prior, float(length), chunk_ref[c : c + 1, 0:1], rate)
            prior = merge(tuple(item[c : c + 1] for item in ends), old)
    last = merge(late, aged(prior, float(length - 1), chunk_ref[CHUNKS - 1 :, 2:3], rate))
    summary_ref[...] = jnp.concatenate(last, axis=0)


def open_pass(slots, vectors, marks, chunk_marks, lows, pool):
    rows, features = lows[0].shape
    own = rows - ROW_TILE
    full = jax.ShapeDtypeStruct((rows, features), jnp.float32)
    part = jax.ShapeDtypeStruct((own, features), jnp.float32)
    small = lambda *shape: jax.ShapeDtypeStruct(shape, jnp.float32)
    vmem = pl.BlockSpec(memory_space=pltpu.VMEM)
    return pl.pallas_call(
        open_kernel,
        out_shape=(full, full, full, part, part, part, small(3, CHUNKS, features), small(3, features)),
        in_specs=[pl.BlockSpec(memory_space=pltpu.SMEM)] + [vmem] * 6 + [pl.BlockSpec(memory_space=pl.ANY)],
        out_specs=(vmem,) * 8,
        scratch_shapes=[
            pltpu.VMEM((3 * EMBED_SIZE // BLOCK_ROWS, BLOCK_ROWS, features), jnp.bfloat16),
            pltpu.SemaphoreType.DMA((3,)),
        ],
        compiler_params=pltpu.CompilerParams(vmem_limit_bytes=VMEM_BYTES),
        name="open_pass",
    )(slots, vectors, marks, chunk_marks, *lows, pool)


def middle_kernel(
    slot_ref, x_ref, grad_ref, vec_ref, marks_ref, chunk_ref, incoming_ref, prefix_ref,
    key_ref, value_ref, recept_ref, num_ref, den_ref, max_ref, pool_ref,
    layer_ref, resid_grad, wkv, gw, own_share, recept_grad, suffix_ref, summary_ref, sums_ref,
    full_out, back_out, slot_grad,
    full_num, full_den, full_max, mixed, ext, unit, inverse, low_key, low_recept, hidden, squared, value_acc, gate, gcv, gcg, hidden_grad,
    attn_grad, top_log, wide, store, sem, out_sem, state_sem,
):
    rows, features = x_ref.shape
    own = rows - ROW_TILE
    tiles = rows // ROW_TILE
    length = own // CHUNKS
    per = EMBED_SIZE // BLOCK_ROWS
    ff = FF // BLOCK_ROWS
    at_out, at_recept, at_key, at_value = 0, per, 2 * per, 2 * per + ff
    fetch_blocks(slot_ref, pool_ref, store, sem.at[0], 3 * per, at_out, per)
    fetch_blocks(slot_ref, pool_ref, store, sem.at[1], 5 * per, at_key, ff)
    fetch_blocks(slot_ref, pool_ref, store, sem.at[2], 5 * per + ff, at_value, ff)
    fetch_blocks(slot_ref, pool_ref, store, sem.at[3], 4 * per, at_recept, per)
    rate = jnp.exp(vec_ref[5:6])
    bonus = vec_ref[6:7]
    incoming = tuple(incoming_ref[k : k + 1] for k in range(3))
    carry = merge(
        tuple(prefix_ref[k] for k in range(3)),
        aged(tuple(jnp.broadcast_to(v, (CHUNKS, features)) for v in incoming), chunk_ref[:, 3:4], chunk_ref[:, 1:2], rate),
    )

    def attend(j, size, state, key, value, recept):
        own_log = bonus + key
        top = jnp.maximum(state[2], own_log)
        old, new = jnp.exp(state[2] - top), jnp.exp(own_log - top)
        scale = 1.0 / (old * state[1] + new)
        out = (old * state[0] + new * value) * scale
        wkv[rows_at(j, size)] = out
        own_share[rows_at(j, size)] = new * scale
        top_log[rows_at(j, size)] = top
        value_acc[rows_at(j, size)] = scale
        ext[rows_at(j, size)] = jax.nn.sigmoid(recept) * out

    def attend_step(i, state_carry):
        at = rows_at(i, CHUNKS)
        alive = marks_ref[at, 2:3]
        distance = jnp.float32(i) if isinstance(i, int) else i.astype(jnp.float32)
        state = merge((num_ref[at], den_ref[at], max_ref[at]), aged(carry, distance, alive, rate))
        full_num[at], full_den[at], full_max[at] = state
        attend(i, CHUNKS, state, key_ref[at], value_ref[at], recept_ref[at])
        return state_carry

    lax.fori_loop(0, length, attend_step, 0)

    def row(ref, r):
        return ref[r : r + 1]

    def state_copy(k, target):
        return pltpu.make_async_copy((full_num, full_den, full_max)[k], target.at[k], state_sem.at[k])

    for k in range(3):
        state_copy(k, full_out).start()
    end = advance(
        (row(full_num, own - 1), row(full_den, own - 1), row(full_max, own - 1)),
        row(key_ref, own - 1), row(value_ref, own - 1), rate,
    )
    halo_one = reset(end, marks_ref[own : own + 1, 0:1])
    halo_two = reset(
        advance(halo_one, row(key_ref, own), row(value_ref, own), rate), marks_ref[own + 1 : own + 2, 0:1]
    )
    halo_zero = reset(incoming, marks_ref[own + 2 : own + 3, 0:1])
    rest = jnp.zeros((ROW_TILE - 3, features), jnp.float32)
    halo_state = tuple(
        jnp.concatenate([halo_one[k], halo_two[k], halo_zero[k], rest + (NEGATIVE if k == 2 else 0.0)], axis=0)
        for k in range(3)
    )
    attend(tiles - 1, ROW_TILE, halo_state, key_ref[own:rows], value_ref[own:rows], recept_ref[own:rows])

    def pack(first, size):
        at = pl.ds(first, size)
        mixed[at] = ext[at].astype(jnp.bfloat16)
        gw[at] = value_acc[at]

    for_rows(rows, pack)
    pack(own, ROW_TILE)
    await_blocks(pool_ref, store, sem.at[0], at_out, per)

    def write_resid(cols, piece):
        unit[:, cols] = x_ref[:, cols].astype(jnp.float32) + piece

    times_weight(mixed, store, at_out, per, write_resid)

    def norm(first, size):
        at = pl.ds(first, size)
        resid = unit[at]
        resid_grad[at] = resid
        out, inv = unit_norm(resid)
        unit[at] = out
        inverse[at] = inv
        ext[pl.ds(pl.multiple_of(first + 8, 8), size)] = out * vec_ref[7:8] + vec_ref[8:9]

    for_rows(rows, norm)
    norm(own, ROW_TILE)
    shift_in(ext, own)

    def mix(first, size, here, before):
        for r, ref in ((9, low_key), (10, low_recept)):
            weight = vec_ref[r : r + 1]
            ref[pl.ds(first, size)] = (weight * here + (1.0 - weight) * before).astype(jnp.bfloat16)

    for_rows(rows, lambda first, size: mix(first, size, *normed_pair(ext, marks_ref, first, size)))
    mix(own, ROW_TILE, ext[own + 8 : own + 8 + ROW_TILE], halo_previous(ext, own, features) * marks_ref[own:rows, 1:2])

    await_blocks(pool_ref, store, sem.at[1], at_key, ff)

    def write_hidden(cols, piece):
        up = jnp.maximum(piece, 0.0)
        hidden[:, cols] = up
        squared[:, cols] = (up * up).astype(jnp.bfloat16)

    times_weight_back(low_key, store, at_key, ff, write_hidden)
    await_blocks(pool_ref, store, sem.at[2], at_value, ff)

    def write_value(cols, piece):
        value_acc[:, cols] = piece

    times_weight(squared, store, at_value, ff, write_value)
    await_blocks(pool_ref, store, sem.at[3], at_recept, per)

    def write_gate(cols, piece):
        gate[:, cols] = piece

    times_weight(low_recept, store, at_recept, per, write_gate)

    def finish(first, size):
        at = pl.ds(first, size)
        opened = jax.nn.sigmoid(gate[at])
        value = value_acc[at]
        grad = grad_ref[at].astype(jnp.float32) * opened
        gcv[at] = grad.astype(jnp.bfloat16)
        gcg[at] = (grad * value * (1.0 - opened)).astype(jnp.bfloat16)
        return resid_grad[at] + opened * value

    def finish_own(first, size):
        out = finish(first, size)
        for k in range(size // CHUNKS):
            put_step(wide, first // CHUNKS + k, length, out[CHUNKS * k : CHUNKS * (k + 1)])

    for_rows(rows, finish_own)
    finish(own, ROW_TILE)

    def emit(first, size):
        layer_ref[pl.ds(first, size)] = take_rows(wide, pl.ds(first, size)).astype(jnp.bfloat16)

    for_rows(rows, emit)

    def write_hidden_grad(cols, piece):
        hidden_grad[:, cols] = (piece * (2.0 * hidden[:, cols])).astype(jnp.bfloat16)

    times_weight_back(gcv, store, at_value, ff, write_hidden_grad)
    weight_gradient(squared, gcv, own, slot_ref, slot_grad, store, out_sem.at[2], 5 * per + ff, at_value)
    times_weight(hidden_grad, store, at_key, ff, write_value)
    weight_gradient(hidden_grad, low_key, own, slot_ref, slot_grad, store, out_sem.at[1], 5 * per, at_key)
    times_weight_back(gcg, store, at_recept, per, write_gate)
    weight_gradient(low_recept, gcg, own, slot_ref, slot_grad, store, out_sem.at[3], 4 * per, at_recept)
    carried = hidden.at[:, 0:features]
    mix_key, mix_recept = vec_ref[9:10], vec_ref[10:11]

    def carry_over(first, size):
        at = pl.ds(first, size)
        carried[at] = marks_ref[at, 1:2] * ((1.0 - mix_key) * value_acc[at] + (1.0 - mix_recept) * gate[at])

    for_rows(rows, carry_over)
    carry_over(own, ROW_TILE)
    halo_next = jnp.concatenate(
        [carried[own + 1 : own + 2], jnp.zeros((ROW_TILE - 1, features), jnp.float32)], axis=0
    )
    carried[own : own + 8] = jnp.concatenate([carried[1:8], carried[own : own + 1]], axis=0)

    def norm_back(first, size, following):
        at = pl.ds(first, size)
        grad = mix_key * value_acc[at] + mix_recept * gate[at] + following
        scaled = grad * vec_ref[7:8]
        inner = (
            scaled
            - jnp.mean(scaled, axis=1, keepdims=True)
            - unit[at] * jnp.mean(scaled * unit[at], axis=1, keepdims=True)
        )
        total = grad_ref[at].astype(jnp.float32) + inner * inverse[at]
        resid_grad[at] = total
        attn_grad[at] = total.astype(jnp.bfloat16)
        return grad

    def back_step(first, size, *sums):
        at = pl.ds(first, size)
        grad = norm_back(first, size, carried[pl.ds(pl.multiple_of(first + 8, 8), size)])
        here, before = normed_pair(ext, marks_ref, first, size)
        spread = here - before
        return (
            sums[0] + fold(grad * unit[at]),
            sums[1] + fold(grad),
            sums[2] + fold(value_acc[at] * spread),
            sums[3] + fold(gate[at] * spread),
        )

    blank = jnp.zeros((CHUNKS, features), jnp.float32)
    sums = for_rows(rows, back_step, (blank,) * 4)
    for k in range(4):
        sums_ref[k : k + 1] = jnp.sum(sums[k], axis=0, keepdims=True)
    norm_back(own, ROW_TILE, halo_next)

    times_weight_back(attn_grad, store, at_out, per, write_gate)
    weight_gradient(mixed, attn_grad, own, slot_ref, slot_grad, store, out_sem.at[0], 3 * per, at_out)

    def gate_back(first, size):
        at = pl.ds(first, size)
        opened = jax.nn.sigmoid(recept_ref[at])
        grad = gate[at] * opened
        ext[at] = grad * gw[at]
        gw[at] = grad
        recept_grad[at] = (grad * wkv[at] * (1.0 - opened)).astype(jnp.bfloat16)

    for_rows(rows, gate_back)
    gate_back(own, ROW_TILE)

    def back_token(state, share, out, top, start):
        older = state[2] - rate
        high = jnp.maximum(older, -top)
        old, new = jnp.exp(older - high), jnp.exp(-top - high)
        return reset((old * state[0] + new * share, old * state[1] - new * share * out, high), start)

    for k in range(3):
        state_copy(k, full_out).wait()
    back_num, back_den, back_max = full_num, full_den, full_max

    def back_scan(n, state):
        i = length - 1 - n
        at = rows_at(i, CHUNKS)
        back_num[at], back_den[at], back_max[at] = state
        return back_token(state, ext[at], wkv[at], top_log[at], marks_ref[at, 0:1])

    heads = lax.fori_loop(0, length, back_scan, (blank, blank, blank + NEGATIVE))
    for k in range(3):
        state_copy(k, back_out).start()
    nothing = jnp.zeros((1, features), jnp.float32)
    after = back_token(
        (nothing, nothing, nothing + NEGATIVE),
        row(ext, own), row(wkv, own), row(top_log, own), marks_ref[own : own + 1, 0:1],
    )
    for c in range(CHUNKS - 1, -1, -1):
        for k in range(3):
            suffix_ref[k, c : c + 1] = after[k]
        if c > 0:
            old = aged(after, float(length), chunk_ref[c : c + 1, 0:1], rate)
            after = merge(tuple(item[c : c + 1] for item in heads), old)
    first = (row(back_num, 0), row(back_den, 0), row(back_max, 0))
    last = merge(first, aged(after, float(length - 1), marks_ref[0:1, 3:4], rate))
    summary_ref[...] = jnp.concatenate(last, axis=0)
    for k, (place, count) in enumerate(((at_out, per), (at_key, ff), (at_value, ff), (at_recept, per))):
        await_gradient(store, slot_grad, out_sem.at[k], place, count)
    for k in range(3):
        state_copy(k, back_out).wait()


def middle_pass(slots, x_rows, grad_rows, vectors, marks, chunk_marks, incoming, opened, pool):
    key, value, recept, num, den, top, prefix = opened
    rows, features = x_rows.shape
    own = rows - ROW_TILE
    full = jax.ShapeDtypeStruct((rows, features), jnp.float32)
    part = jax.ShapeDtypeStruct((own, features), jnp.float32)
    low = jax.ShapeDtypeStruct((rows, features), jnp.bfloat16)
    vmem = pl.BlockSpec(memory_space=pltpu.VMEM)
    anywhere = pl.BlockSpec(memory_space=pl.ANY)
    f32 = lambda *shape: pltpu.VMEM(shape, jnp.float32)
    b16 = lambda *shape: pltpu.VMEM(shape, jnp.bfloat16)
    return pl.pallas_call(
        middle_kernel,
        out_shape=(
            jax.ShapeDtypeStruct((own, features), jnp.bfloat16),
            full, full, full, full, low,
            jax.ShapeDtypeStruct((3, CHUNKS, features), jnp.float32),
            jax.ShapeDtypeStruct((3, features), jnp.float32),
            jax.ShapeDtypeStruct((4, features), jnp.float32),
            jax.ShapeDtypeStruct((3, own, features), jnp.float32),
            jax.ShapeDtypeStruct((3, own, features), jnp.float32),
            jax.ShapeDtypeStruct(pool.shape, jnp.bfloat16),
        ),
        in_specs=[pl.BlockSpec(memory_space=pltpu.SMEM)] + [vmem] * 13 + [anywhere],
        out_specs=(vmem,) * 9 + (anywhere,) * 3,
        scratch_shapes=[
            f32(own, features),
            f32(own, features),
            f32(own, features),
            b16(rows, features),
            f32(rows + 8, features),
            f32(rows, features),
            f32(rows, 1),
            b16(rows, features),
            b16(rows, features),
            f32(rows, FF),
            b16(rows, FF),
            f32(rows, features),
            f32(rows, features),
            b16(rows, features),
            b16(rows, features),
            b16(rows, FF),
            b16(rows, features),
            f32(rows, features),
            f32(features // LANES, own, LANES),
            b16((2 * EMBED_SIZE + 2 * FF) // BLOCK_ROWS, BLOCK_ROWS, features),
            pltpu.SemaphoreType.DMA((4,)),
            pltpu.SemaphoreType.DMA((4,)),
            pltpu.SemaphoreType.DMA((3,)),
        ],
        compiler_params=pltpu.CompilerParams(vmem_limit_bytes=VMEM_BYTES),
        name="middle_pass",
    )(slots, x_rows, grad_rows, vectors, marks, chunk_marks, incoming, prefix, key, value, recept, num, den, top, pool)


def close_kernel(
    slot_ref, x_ref, vec_ref, marks_ref, chunk_ref, incoming_ref, suffix_ref, key_ref, value_ref,
    in_key, in_value, in_recept, resid_grad, wkv, gw, own_share, recept_grad, sums_two_ref, full_ref, back_ref,
    pool_ref, grads_in,
    input_ref, sums_ref, slot_grad,
    ext, unit, inverse, key_wide, value_wide, key_grad, value_grad, grad_key_in, grad_value_in, grad_recept_in,
    carried, wide, store, sem, out_sem,
):
    rows, features = x_ref.shape
    own = rows - ROW_TILE
    tiles = rows // ROW_TILE
    length = own // CHUNKS
    per = EMBED_SIZE // BLOCK_ROWS
    for m in range(3):
        fetch_blocks(slot_ref, pool_ref, store, sem.at[m], m * per, m * per, per)
    rate = jnp.exp(vec_ref[5:6])
    incoming = tuple(incoming_ref[k : k + 1] for k in range(3))
    carry = merge(
        tuple(suffix_ref[k] for k in range(3)),
        aged(tuple(jnp.broadcast_to(v, (CHUNKS, features)) for v in incoming), chunk_ref[:, 5:6], chunk_ref[:, 4:5], rate),
    )

    def spread_back(state, key, value, share, grad, out):
        direct = share * grad
        bonus_grad = direct * (value - out)
        lift = jnp.exp(key + state[2])
        return bonus_grad + lift * (state[0] * value + state[1]), direct + lift * state[0], bonus_grad

    def token(i, sums):
        at = rows_at(i, CHUNKS)
        distance = (length - 1 - i).astype(jnp.float32)
        state = merge(tuple(back_ref[k, at] for k in range(3)), aged(carry, distance, marks_ref[at, 3:4], rate))
        key_g, value_g, bonus_grad = spread_back(state, key_ref[at], value_ref[at], own_share[at], gw[at], wkv[at])
        key_wide[at] = key_g
        value_wide[at] = value_g
        fade = jnp.exp(state[2] + full_ref[2, at] - rate) * (state[0] * full_ref[0, at] + state[1] * full_ref[1, at])
        return sums[0] + fade, sums[1] + bonus_grad

    blank = jnp.zeros((CHUNKS, features), jnp.float32)
    fade, bonus_sum = lax.fori_loop(0, length, token, (blank, blank))
    sums_ref[5:6] = -rate * jnp.sum(fade, axis=0, keepdims=True)
    sums_ref[6:7] = jnp.sum(bonus_sum, axis=0, keepdims=True)
    halo = tuple(
        jnp.concatenate([incoming[k], jnp.zeros((ROW_TILE - 1, features), jnp.float32) + (NEGATIVE if k == 2 else 0.0)], axis=0)
        for k in range(3)
    )
    key_g, value_g, _ = spread_back(
        halo, key_ref[own:rows], value_ref[own:rows], own_share[own:rows], gw[own:rows], wkv[own:rows]
    )
    key_wide[own:rows] = key_g
    value_wide[own:rows] = value_g

    def pack(first, size):
        at = pl.ds(first, size)
        key_grad[at] = key_wide[at].astype(jnp.bfloat16)
        value_grad[at] = value_wide[at].astype(jnp.bfloat16)

    for_rows(rows, pack)
    pack(own, ROW_TILE)
    products = (
        (key_grad, grad_key_in, in_key),
        (value_grad, grad_value_in, in_value),
        (recept_grad, grad_recept_in, in_recept),
    )
    for m, (left, out, inputs) in enumerate(products):
        await_blocks(pool_ref, store, sem.at[m], m * per, per)

        def write(cols, piece, out=out):
            out[:, cols] = piece

        times_weight_back(left, store, m * per, per, write)
        weight_gradient(inputs, left, own, slot_ref, slot_grad, store, out_sem.at[m], m * per, m * per)

    def norm(first, size):
        at = pl.ds(first, size)
        out, inv = unit_norm(x_ref[at].astype(jnp.float32))
        unit[at] = out
        inverse[at] = inv
        ext[pl.ds(pl.multiple_of(first + 8, 8), size)] = out * vec_ref[0:1] + vec_ref[1:2]

    for_rows(rows, norm)
    norm(own, ROW_TILE)
    shift_in(ext, own)
    mixes = tuple(vec_ref[k : k + 1] for k in (2, 3, 4))

    def carry_over(first, size):
        at = pl.ds(first, size)
        total = (1.0 - mixes[0]) * grad_key_in[at] + (1.0 - mixes[1]) * grad_value_in[at] + (1.0 - mixes[2]) * grad_recept_in[at]
        carried[at] = marks_ref[at, 1:2] * total

    for_rows(rows, carry_over)
    carry_over(own, ROW_TILE)
    carried[own : own + 8] = jnp.concatenate([carried[1:8], carried[own : own + 1]], axis=0)

    def back_step(first, size, *sums):
        at = pl.ds(first, size)
        grads = (grad_key_in[at], grad_value_in[at], grad_recept_in[at])
        grad = carried[pl.ds(pl.multiple_of(first + 8, 8), size)]
        for weight, piece in zip(mixes, grads):
            grad = grad + weight * piece
        scaled = grad * vec_ref[0:1]
        inner = (
            scaled
            - jnp.mean(scaled, axis=1, keepdims=True)
            - unit[at] * jnp.mean(scaled * unit[at], axis=1, keepdims=True)
        )
        out = resid_grad[at] + inner * inverse[at]
        for k in range(size // CHUNKS):
            put_step(wide, first // CHUNKS + k, length, out[CHUNKS * k : CHUNKS * (k + 1)])
        here, before = normed_pair(ext, marks_ref, first, size)
        spread = here - before
        return (sums[0] + fold(grad * unit[at]), sums[1] + fold(grad)) + tuple(
            s + fold(piece * spread) for s, piece in zip(sums[2:], grads)
        )

    sums = for_rows(rows, back_step, (blank,) * 5)
    for k in range(5):
        sums_ref[k : k + 1] = jnp.sum(sums[k], axis=0, keepdims=True)
    sums_ref[7:] = sums_two_ref[...]

    def emit(first, size):
        input_ref[pl.ds(first, size)] = take_rows(wide, pl.ds(first, size))

    for_rows(rows, emit)
    for m in range(3):
        await_gradient(store, slot_grad, out_sem.at[m], m * per, per)


def close_pass(slots, x_rows, vectors, marks, chunk_marks, incoming, suffix, key, value, lows, kept, pool, slot_grad):
    rows, features = x_rows.shape
    own = rows - ROW_TILE
    vmem = pl.BlockSpec(memory_space=pltpu.VMEM)
    anywhere = pl.BlockSpec(memory_space=pl.ANY)
    f32 = lambda *shape: pltpu.VMEM(shape, jnp.float32)
    b16 = lambda *shape: pltpu.VMEM(shape, jnp.bfloat16)
    operands = (slots, x_rows, vectors, marks, chunk_marks, incoming, suffix, key, value) + lows + kept + (pool, slot_grad)
    return pl.pallas_call(
        close_kernel,
        out_shape=(
            jax.ShapeDtypeStruct((own, features), jnp.float32),
            jax.ShapeDtypeStruct(vectors.shape, jnp.float32),
            jax.ShapeDtypeStruct(pool.shape, jnp.bfloat16),
        ),
        in_specs=[pl.BlockSpec(memory_space=pltpu.SMEM)] + [vmem] * (len(operands) - 3) + [anywhere] * 2,
        out_specs=(vmem, vmem, anywhere),
        input_output_aliases={len(operands) - 1: 2},
        scratch_shapes=[
            f32(rows + 8, features),
            f32(rows, features),
            f32(rows, 1),
            f32(rows, features),
            f32(rows, features),
            b16(rows, features),
            b16(rows, features),
            f32(rows, features),
            f32(rows, features),
            f32(rows, features),
            f32(rows, features),
            f32(features // LANES, own, LANES),
            b16(3 * EMBED_SIZE // BLOCK_ROWS, BLOCK_ROWS, features),
            pltpu.SemaphoreType.DMA((3,)),
            pltpu.SemaphoreType.DMA((3,)),
        ],
        compiler_params=pltpu.CompilerParams(vmem_limit_bytes=VMEM_BYTES),
        name="close_pass",
    )(*operands)


def chain_kernel(forward, tokens, own_ref, vec_ref, link_ref, flag_ref, out_ref, near, chips, joint, send_sem, recv_sem):
    me, core, _, _, _ = grid_place()
    chip = me // 2
    count = GRID_DEVICES // 2
    sign = 1 if forward else -1
    before = chip if forward else count - 1 - chip
    sibling = me + 1 - 2 * core
    chips[...] = jnp.zeros_like(chips)
    bar = pltpu.get_barrier_semaphore()
    pl.semaphore_signal(bar, inc=1, device_id=(sibling,), device_id_type=MESH)
    for o in range(1, count):
        @pl.when(o <= before)
        def _():
            pl.semaphore_signal(bar, inc=1, device_id=(me - 2 * sign * o,), device_id_type=MESH)
    pl.semaphore_wait(bar, count - before)
    swap = pltpu.make_async_remote_copy(
        src_ref=own_ref, dst_ref=near, send_sem=send_sem.at[0], recv_sem=recv_sem.at[0],
        device_id=(sibling,), device_id_type=MESH,
    )
    swap.start()
    rate = jnp.exp(vec_ref[5:6])
    at = 0 if forward else 2
    swap.wait()
    mine = tuple(own_ref[k : k + 1] for k in range(3))
    other = tuple(near[k : k + 1] for k in range(3))
    second = (core == 1) if forward else (core == 0)
    one = tuple(jnp.where(second, b, a) for a, b in zip(mine, other))
    two = tuple(jnp.where(second, a, b) for a, b in zip(mine, other))
    joint[...] = jnp.concatenate(merge(two, aged(one, float(tokens), flag_ref[0:1, at : at + 1], rate)), axis=0)

    def copy(o, place, peer):
        return pltpu.make_async_remote_copy(
            src_ref=joint, dst_ref=chips.at[place], send_sem=send_sem.at[o], recv_sem=recv_sem.at[o],
            device_id=(peer,), device_id_type=MESH,
        )

    for o in range(1, count):
        @pl.when(o < count - before)
        def _():
            copy(o, chip, me + 2 * sign * o).start()
    for o in range(1, count):
        @pl.when(o <= before)
        def _():
            copy(o, chip - sign * o, sibling).wait_recv()
    logs = jnp.where(link_ref[:, at : at + 1] > 0.5, chips[:, 2] - link_ref[:, at + 1 : at + 2] * rate, NEGATIVE)
    top = jnp.max(logs, axis=0, keepdims=True)
    weight = jnp.exp(logs - top)
    prior = (
        jnp.sum(weight * chips[:, 0], axis=0, keepdims=True),
        jnp.sum(weight * chips[:, 1], axis=0, keepdims=True),
        top,
    )
    beside = merge(one, aged(prior, float(tokens), flag_ref[0:1, at + 1 : at + 2], rate))
    out_ref[...] = jnp.concatenate([jnp.where(second, b, a) for a, b in zip(prior, beside)], axis=0)
    for o in range(1, count):
        @pl.when(o < count - before)
        def _():
            copy(o, chip, me + 2 * sign * o).wait_send()


def chain_state(rows, vectors, links, flags, forward, tokens, cid):
    devices = lax.axis_size("seq")
    if devices != GRID_DEVICES:
        every = lax.all_gather(rows[None], "seq", axis=0, tiled=True)
        at = 0 if forward else 2
        aged_logs = every[:, 2] - links[:, at + 1 : at + 2] * jnp.exp(vectors[5])
        logs = jnp.where(links[:, at : at + 1] > 0.5, aged_logs, NEGATIVE)
        top = jnp.max(logs, axis=0)
        weight = jnp.exp(logs - top)
        return jnp.stack([jnp.sum(weight * every[:, 0], axis=0), jnp.sum(weight * every[:, 1], axis=0), top])
    count = devices // 2
    vmem = pl.BlockSpec(memory_space=pltpu.VMEM)
    return pl.pallas_call(
        functools.partial(chain_kernel, forward, tokens),
        out_shape=jax.ShapeDtypeStruct(rows.shape, jnp.float32),
        in_specs=[vmem] * 4,
        out_specs=vmem,
        scratch_shapes=[
            pltpu.VMEM(rows.shape, jnp.float32),
            pltpu.VMEM((count,) + rows.shape, jnp.float32),
            pltpu.VMEM(rows.shape, jnp.float32),
            pltpu.SemaphoreType.DMA((count,)),
            pltpu.SemaphoreType.DMA((count,)),
        ],
        compiler_params=pltpu.CompilerParams(collective_id=cid, has_side_effects=True),
        name="chain_forward" if forward else "chain_backward",
    )(rows, vectors, links, flags)


def body(
    tokens_in,
    cotangent,
    pad_mask,
    doc_lengths,
    masters,
    moment_one,
    moment_two,
    block_slot,
    vectors,
    vector_one,
    vector_two,
):
    tokens, features = tokens_in.shape
    devices = lax.axis_size("seq")
    device_place = lax.axis_index("seq")
    pad_rows = pad_mask.reshape(-1, LANES)
    if devices == GRID_DEVICES:
        gathered, *prepared = gather_blocks(masters, doc_lengths, tokens_in, cotangent, pad_rows, vectors)
        gathered = gathered.reshape(-1, BLOCK_ROWS, features)
    else:
        gathered = lax.all_gather(masters.astype(jnp.bfloat16), "seq", axis=0, tiled=True)
        head_grad = cotangent[:ROW_TILE] * pad_mask[:ROW_TILE].astype(cotangent.dtype)[:, None]
        halo = [
            shifted(tokens_in[:ROW_TILE], "seq", -1),
            shifted(head_grad, "seq", -1),
            shifted(tokens_in[tokens - ROW_TILE :], "seq", 1),
        ]
        prepared = prepare_pass(devices, doc_lengths, tokens_in, cotangent, pad_rows, halo, vectors)
    x_rows, grad_rows, marks, chunk_marks, links, flags, *lows = prepared
    lows = tuple(lows)
    key, value, recept, num, den, top, prefix, summary = open_pass(
        block_slot, vectors, marks, chunk_marks, lows, gathered
    )
    incoming = chain_state(summary, vectors, links, flags, True, tokens, 3)
    (
        layer_out, resid_grad, wkv, gw, own_share, recept_grad, suffix, back_summary, sums_two,
        full_state, back_state, slot_grad,
    ) = middle_pass(
        block_slot, x_rows, grad_rows, vectors, marks, chunk_marks, incoming,
        (key, value, recept, num, den, top, prefix), gathered,
    )
    back_incoming = chain_state(back_summary, vectors, links, flags, False, tokens, 4)
    input_grad, stacked, slot_grad = close_pass(
        block_slot, x_rows, vectors, marks, chunk_marks, back_incoming, suffix, key, value,
        lows,
        (resid_grad, wkv, gw, own_share, recept_grad, sums_two, full_state, back_state),
        gathered, slot_grad,
    )
    own_slots = device_place * masters.shape[0] + jnp.arange(masters.shape[0], dtype=jnp.int32)
    named = jnp.any(own_slots[:, None] == block_slot[None, :], axis=1)
    if devices == GRID_DEVICES:
        owner_grad, vector_grad = scatter_blocks(slot_grad.reshape((devices,) + masters.shape), stacked)
        owner_grad = owner_grad.astype(jnp.float32)
    else:
        owner_grad = lax.psum_scatter(
            slot_grad.astype(jnp.float32), "seq", scatter_dimension=0, tiled=True
        )
        vector_grad = lax.psum(stacked, "seq")
    owner_grad = jnp.where(named[:, None, None], owner_grad, 0.0)
    new_one, new_two, new_master = adam_update(
        masters, moment_one, moment_two, owner_grad, MATRIX_RATE, WEIGHT_DECAY
    )
    vector_rates = jnp.array(VECTOR_RATE, jnp.float32)[:, None]
    vector_first, vector_second, vector_next = adam_update(
        vectors, vector_one, vector_two, vector_grad, vector_rates, 0.0
    )
    return (
        layer_out,
        input_grad,
        new_one,
        new_two,
        new_master,
        vector_first,
        vector_second,
        vector_next,
    )


def solution(mesh):
    placed = (
        P("seq", None),
        P("seq", None),
        P("seq"),
        P(),
        P("seq", None, None),
        P("seq", None, None),
        P("seq", None, None),
        P(),
        P(),
        P(),
        P(),
    )
    return jax.shard_map(
        body,
        mesh=mesh,
        in_specs=placed,
        out_specs=(
            P("seq", None),
            P("seq", None),
            P("seq", None, None),
            P("seq", None, None),
            P("seq", None, None),
            P(),
            P(),
            P(),
        ),
        check_vma=False,
    )
```

```python
import functools

import jax
import jax.numpy as jnp
from jax import lax
from jax.experimental import pallas as pl
from jax.experimental.pallas import tpu as pltpu
from jax.sharding import PartitionSpec as P

EMBED_SIZE = 1024
FF = 4096
BLOCK_ROWS = 32
ROWS_ALL = 13312
BLOCKS = 416
STEP = 10
GRID_DEVICES = 32
MESH = pl.DeviceIdType.MESH


NEGATIVE = -1e30
NORM_EPS = 1e-05
BETA_ONE = 0.9
BETA_TWO = 0.999
ADAM_EPS = 1e-08
MATRIX_RATE = 0.05
WEIGHT_DECAY = 0.01
VECTOR_RATE = (0.25, 0.25, 0.25, 0.25, 0.25, 2.0, 0.25, 0.25, 0.25, 0.25, 0.25)


def shifted(block, axis, distance):
    devices = range(lax.axis_size(axis))
    route = [(i - distance, i) for i in devices if i - distance in devices]
    return lax.ppermute(block, axis, route)


def product_back(left_side, right_side):
    return lax.dot_general(
        left_side, right_side, (((1,), (1,)), ((), ())), preferred_element_type=jnp.float32
    )


def product_left(left_side, right_side):
    return lax.dot_general(
        left_side, right_side, (((0,), (0,)), ((), ())), preferred_element_type=jnp.float32
    )


def adam_update(weight, first_moment, second_moment, gradient, step_rate, feature_fade_speed):
    first_moment = BETA_ONE * first_moment + (1.0 - BETA_ONE) * gradient
    second_moment = BETA_TWO * second_moment + (1.0 - BETA_TWO) * gradient * gradient
    first_fixed = first_moment / (1.0 - BETA_ONE**STEP)
    second_fixed = second_moment / (1.0 - BETA_TWO**STEP)
    weight = weight - step_rate * (
        first_fixed / (jnp.sqrt(second_fixed) + ADAM_EPS) + feature_fade_speed * weight
    )
    return (first_moment, second_moment, weight)


def grid_place():
    me = lax.axis_index("seq")
    return me, lax.rem(me, 2), lax.rem(me // 2, 2), lax.rem(me // 4, 2), me // 8

def spans(slots):
    side = 4 * slots // 15
    cuts = [0, side, 2 * side, slots]
    return [(cuts[i], cuts[i + 1] - cuts[i]) for i in range(3)]

def gather_kernel(
    slots, doc_ref, master_ref, tokens_ref, cot_ref, pad_ref, vec_ref,
    out_ref, x_ref, grad_ref, marks_ref, chunk_ref, link_ref, in_key, in_value, in_recept,
    column, ext, wide, wide_grad, own_ref, head_grad, after_ref, after_grad_ref, before_ref,
    *scratch,
):
    send_sem, recv_sem, sib_send, sib_recv, own_sem, halo_send, halo_recv = scratch
    me, core, x, y, z = grid_place()
    sib = me + 1 - 2 * core
    x_peer = me + 2 - 4 * x
    y_peer = me + 4 - 8 * y
    up = me + 8
    down = me - 8
    bar = pltpu.get_barrier_semaphore()
    pl.semaphore_signal(bar, inc=1, device_id=(sib,), device_id_type=MESH)
    pl.semaphore_signal(bar, inc=1, device_id=(x_peer,), device_id_type=MESH)
    pl.semaphore_signal(bar, inc=1, device_id=(y_peer,), device_id_type=MESH)
    @pl.when(z < 3)
    def _():
        pl.semaphore_signal(bar, inc=1, device_id=(up,), device_id_type=MESH)
    @pl.when(z > 0)
    def _():
        pl.semaphore_signal(bar, inc=1, device_id=(down,), device_id_type=MESH)
    more, less = me < GRID_DEVICES - 1, me > 0

    @pl.when(more)
    def _():
        pl.semaphore_signal(bar, inc=1, device_id=(me + 1,), device_id_type=MESH)

    @pl.when(less)
    def _():
        pl.semaphore_signal(bar, inc=1, device_id=(me - 1,), device_id_type=MESH)

    def lower(s, carry):
        own_ref[s] = master_ref[s].astype(own_ref.dtype)
        return carry

    lax.fori_loop(0, slots, lower, 0)
    mask_column(pad_ref, column)
    head_grad[...] = (cot_ref[0:ROW_TILE].astype(jnp.float32) * column[0:ROW_TILE]).astype(jnp.bfloat16)
    halos = jnp.where(more, 1, 0) + jnp.where(less, 1, 0)
    pl.semaphore_wait(bar, 4 + jnp.where((z > 0) & (z < 3), 1, 0) + halos)
    tokens = tokens_ref.shape[0]

    def halo_copy(k):
        src, dst, peer = (
            (tokens_ref.at[pl.ds(0, ROW_TILE)], after_ref, me - 1),
            (head_grad, after_grad_ref, me - 1),
            (tokens_ref.at[pl.ds(tokens - ROW_TILE, ROW_TILE)], before_ref, me + 1),
        )[k]
        return pltpu.make_async_remote_copy(src_ref=src, dst_ref=dst, send_sem=halo_send.at[k],
            recv_sem=halo_recv.at[k], device_id=(peer,), device_id_type=MESH)
    span = spans(slots)
    targets = (x_peer, y_peer, up, down)

    def chip(cx, cy, cz):
        return (cz * 2 + cy) * 2 + cx

    def view(cx, cy, cz, color, c=None):
        dev = chip(cx, cy, cz) * 2 + (core if c is None else c)
        lo, n = span[color]
        return out_ref.at[dev, pl.ds(lo, n)]

    def send(cx, cy, cz, color, way, own=False):
        lo, n = span[color]
        src = own_ref.at[pl.ds(lo, n)] if own else view(cx, cy, cz, color)
        idx = chip(cx, cy, cz)
        return pltpu.make_async_remote_copy(src_ref=src, dst_ref=view(cx, cy, cz, color),
            send_sem=send_sem.at[idx, color, way], recv_sem=recv_sem.at[idx, color],
            device_id=(targets[way],), device_id_type=MESH)

    def send_sib(cx, cy, cz, color, own=False):
        lo, n = span[color]
        src = own_ref.at[pl.ds(lo, n)] if own else view(cx, cy, cz, color)
        idx = chip(cx, cy, cz)
        return pltpu.make_async_remote_copy(src_ref=src, dst_ref=view(cx, cy, cz, color),
            send_sem=sib_send.at[idx, color], recv_sem=sib_recv.at[idx, color],
            device_id=(sib,), device_id_type=MESH)

    x2, y2 = 1 - x, 1 - y
    pending = []

    def go(copy, cond=None):
        if cond is None:
            copy.start()
        else:
            @pl.when(cond)
            def _():
                copy.start()
        pending.append((copy, cond))

    zup, zdown = z < 3, z > 0
    own_copies = []
    for color in range(3):
        lo, n = span[color]
        cp = pltpu.make_async_copy(own_ref.at[pl.ds(lo, n)], view(x, y, z, color), own_sem.at[color])
        cp.start()
        own_copies.append(cp)
    order = {0: (0, 2, 1), 1: (1, 2, 0)}
    for color in (0, 1, 2):
        go(send(x, y, z, color, 2, True), zup)
        go(send(x, y, z, color, 3, True), zdown)
    for color, way in ((0, 0), (1, 1), (2, 0), (2, 1), (0, 1), (1, 0)):
        go(send(x, y, z, color, way, True))
    for color in range(3):
        go(send_sib(x, y, z, color, True))

    @pl.when(less)
    def _():
        for k in (0, 1):
            halo_copy(k).start()

    @pl.when(more)
    def _():
        halo_copy(2).start()

    marks = (marks_ref, chunk_ref, link_ref)
    prepare_own(
        GRID_DEVICES, doc_ref, tokens_ref, cot_ref, column, vec_ref, x_ref, grad_ref, marks, ext, wide, wide_grad
    )

    def arrive(cx, cy, cz, color):
        send(cx, cy, cz, color, 0).wait_recv()

    def sibling(cx, cy, cz, color):
        go(send_sib(cx, cy, cz, color))

    is0, is1 = core == 0, core == 1
    px = jnp.where(is0, x2, x)
    py = jnp.where(is0, y, y2)
    qx = jnp.where(is0, x, x2)
    qy = jnp.where(is0, y2, y)
    first = lambda cx, cy, cz: (go(send(cx, cy, cz, 2, 0), is0), go(send(cx, cy, cz, 2, 1), is1))
    last = lambda cx, cy, cz: (go(send(cx, cy, cz, 2, 1), is0), go(send(cx, cy, cz, 2, 0), is1))

    arrive(x2, y, z, 0)
    go(send(x2, y, z, 0, 2), zup)
    go(send(x2, y, z, 0, 3), zdown)
    go(send(x2, y, z, 0, 1))
    sibling(x2, y, z, 0)
    arrive(x, y2, z, 1)
    go(send(x, y2, z, 1, 2), zup)
    go(send(x, y2, z, 1, 3), zdown)
    go(send(x, y2, z, 1, 0))
    sibling(x, y2, z, 1)
    arrive(px, py, z, 2)
    last(px, py, z)
    sibling(px, py, z, 2)

    def wait_halo():
        @pl.when(less)
        def _():
            for k in (0, 1):
                halo_copy(k).wait_send()
            halo_copy(2).wait_recv()

        @pl.when(more)
        def _():
            halo_copy(2).wait_send()
            for k in (0, 1):
                halo_copy(k).wait_recv()

    for dist in (1, 2, 3):
        sides = []
        for sign, fwd, guard_f in ((1, 3, zdown), (-1, 2, zup)):
            q = z + sign * dist
            have = (q >= 0) & (q < 4)
            sides.append((q, fwd, have, guard_f))
        for which in ("c", "a", "b", "a2", "b2"):
            for q, fwd, have, gf in sides:
                @pl.when(have)
                def _(q=q, fwd=fwd, gf=gf, which=which):
                    if which == "c":
                        arrive(x, y, q, 2)
                        cp = send(x, y, q, 2, fwd)
                        pl.when(gf)(lambda: cp.start())
                        for w in (0, 1):
                            send(x, y, q, 2, w).start()
                        send_sib(x, y, q, 2).start()
                    else:
                        color = 0 if which[0] == "a" else 1
                        cx, cy = {"a": (x, y), "b": (x, y), "a2": (x2, y), "b2": (x, y2)}[which]
                        arrive(cx, cy, q, color)
                        cp = send(cx, cy, q, color, fwd)
                        pl.when(gf)(lambda: cp.start())
                        send(cx, cy, q, color, 1 if color == 0 else 0).start()
                        send_sib(cx, cy, q, color).start()
        for q, fwd, have, gf in sides:
            @pl.when(have)
            def _(q=q):
                arrive(px, py, q, 2)
                pl.when(is0)(lambda: send(px, py, q, 2, 1).start())
                pl.when(is1)(lambda: send(px, py, q, 2, 0).start())
                send_sib(px, py, q, 2).start()
        if dist == 1:
            tail_list = [(z, None)]
        else:
            tail_list = []
        if dist == 1:
            wait_halo()
            lows = (in_key, in_value, in_recept)
            prepare_halo(
                GRID_DEVICES, after_ref, after_grad_ref, before_ref, vec_ref, x_ref, grad_ref, marks_ref, lows, ext
            )
        def terminal(q):
            for cx, cy, color in ((x, y2, 0), (x2, y2, 0), (x2, y, 1), (x2, y2, 1), (qx, qy, 2), (x2, y2, 2)):
                arrive(cx, cy, q, color)
                send_sib(cx, cy, q, color).start()
        if dist == 1:
            terminal(z)
        else:
            for sign in (1, -1):
                q = z + sign * (dist - 1)
                pl.when((q >= 0) & (q < 4))(lambda q=q: terminal(q))
        if dist == 3:
            for sign in (1, -1):
                q = z + sign * 3
                pl.when((q >= 0) & (q < 4))(lambda q=q: terminal(q))
    for cp in own_copies:
        cp.wait()
    for color in range(3):
        pl.when(zup)(lambda color=color: send(x, y, z, color, 2).wait_send())
        pl.when(zdown)(lambda color=color: send(x, y, z, color, 3).wait_send())
        for w in (0, 1):
            send(x, y, z, color, w).wait_send()
    for cx, cy, color, w in ((x2, y, 0, 1), (x, y2, 1, 0)):
        pl.when(zup)(lambda: send(cx, cy, z, color, 2).wait_send())
        pl.when(zdown)(lambda: send(cx, cy, z, color, 3).wait_send())
        send(cx, cy, z, color, w).wait_send()
    pl.when(is0)(lambda: send(px, py, z, 2, 1).wait_send())
    pl.when(is1)(lambda: send(px, py, z, 2, 0).wait_send())
    for dist in (1, 2, 3):
        for sign, fwd, gf in ((1, 3, zdown), (-1, 2, zup)):
            q = z + sign * dist
            @pl.when((q >= 0) & (q < 4))
            def _(q=q, fwd=fwd, gf=gf):
                for cx, cy, color in ((x, y, 2), (x, y, 0), (x, y, 1), (x2, y, 0), (x, y2, 1)):
                    pl.when(gf)(lambda: send(cx, cy, q, color, fwd).wait_send())
                    ways = (0, 1) if color == 2 else ((1,) if color == 0 else (0,))
                    for w in ways:
                        send(cx, cy, q, color, w).wait_send()
                pl.when(is0)(lambda: send(px, py, q, 2, 1).wait_send())
                pl.when(is1)(lambda: send(px, py, q, 2, 0).wait_send())
    for cz in range(4):
        for cy in range(2):
            for cx in range(2):
                for color in range(3):
                    cp = send_sib(cx, cy, cz, color)
                    cp.wait_send()
                    cp.wait_recv()

def gather_blocks(masters, doc_lengths, tokens_in, cotangent, pad_rows, vectors, cid=1):
    slots = masters.shape[0]
    shapes, scratch = prepared_shapes(GRID_DEVICES, *tokens_in.shape)
    anywhere = pl.BlockSpec(memory_space=pl.ANY)
    vmem = pl.BlockSpec(memory_space=pltpu.VMEM)
    halo = pltpu.VMEM((ROW_TILE,) + tokens_in.shape[1:], jnp.bfloat16)
    return pl.pallas_call(
        functools.partial(gather_kernel, slots),
        out_shape=(jax.ShapeDtypeStruct((GRID_DEVICES,) + masters.shape, jnp.bfloat16),) + shapes,
        in_specs=[pl.BlockSpec(memory_space=pltpu.SMEM)] + [vmem] * 5,
        out_specs=(anywhere,) + (vmem,) * len(shapes),
        scratch_shapes=scratch + [
            pltpu.VMEM(masters.shape, jnp.bfloat16),
            halo, halo, halo, halo,
            pltpu.SemaphoreType.DMA((16, 3, 4)),
            pltpu.SemaphoreType.DMA((16, 3)),
            pltpu.SemaphoreType.DMA((16, 3)),
            pltpu.SemaphoreType.DMA((16, 3)),
            pltpu.SemaphoreType.DMA((3,)),
            pltpu.SemaphoreType.DMA((3,)),
            pltpu.SemaphoreType.DMA((3,)),
        ],
        compiler_params=pltpu.CompilerParams(collective_id=cid, has_side_effects=True, vmem_limit_bytes=VMEM_BYTES),
        name="gather_blocks",
    )(doc_lengths, masters, tokens_in, cotangent, pad_rows, vectors)


def scatter_spans(slots):
    side = 4 * slots // 15
    cuts = [0, side, 2 * side, 2 * side + (slots - 2 * side + 1) // 2, slots]
    return [(cuts[i], cuts[i + 1] - cuts[i]) for i in range(4)]


def scatter_kernel(
    slots, part_ref, rows_ref, vec_ref, marks_ref, x_hbm, resid_hbm, key_hbm, value_hbm, recept_hbm, weights_hbm,
    out_ref, total_ref, input_hbm,
    acc, ring, ub, uc, ud, va, vc, vd, zs, zc, zd, sums,
    x_ref, resid_ref, key_grad, value_grad, recept_grad, weights, grad_key_in, grad_value_in, grad_recept_in,
    ext, unit, inverse, carried, wide, input_ref,
    load_sem, sib_send, sib_recv, send_sem, usem, vsem, zsem, row_send, row_recv, tail_sem, input_sem,
):
    me, core, x, y, z = grid_place()
    sibling = me + 1 - 2 * core
    x_peer = me + 2 - 4 * x
    y_peer = me + 4 - 8 * y
    up, down = me + 8, me - 8
    zup, zdown = z < 3, z > 0
    bar = pltpu.get_barrier_semaphore()
    for peer in (sibling, x_peer, y_peer):
        pl.semaphore_signal(bar, inc=1, device_id=(peer,), device_id_type=MESH)
    @pl.when(zup)
    def _():
        pl.semaphore_signal(bar, inc=1, device_id=(up,), device_id_type=MESH)
    @pl.when(zdown)
    def _():
        pl.semaphore_signal(bar, inc=1, device_id=(down,), device_id_type=MESH)
    far = me + 16 - 32 * (z // 2)
    pl.semaphore_signal(bar, inc=1, device_id=(far,), device_id_type=MESH)
    row_peers = (sibling, x_peer, y_peer, me + 8 - 16 * lax.rem(z, 2), far)
    tail_loads = [
        pltpu.make_async_copy(src, dst, tail_sem.at[k])
        for k, (src, dst) in enumerate(
            (
                (key_hbm, key_grad), (value_hbm, value_grad), (recept_hbm, recept_grad),
                (x_hbm, x_ref), (resid_hbm, resid_ref), (weights_hbm, weights),
            )
        )
    ]
    span = scatter_spans(slots)
    u, v = jnp.where(core == 0, x, y), jnp.where(core == 0, y, x)
    u_peer, v_peer = jnp.where(core == 0, x_peer, y_peer), jnp.where(core == 0, y_peer, x_peer)
    u2, v2 = 1 - u, 1 - v

    def row_copy(k):
        return pltpu.make_async_remote_copy(src_ref=sums.at[2 * k], dst_ref=sums.at[2 * k + 1],
            send_sem=row_send.at[k], recv_sem=row_recv.at[k], device_id=(row_peers[k],), device_id_type=MESH)

    def row_step(k):
        row_copy(k).wait()
        sums[2 * k + 2] = sums[2 * k] + sums[2 * k + 1]
        if k < 4:
            row_copy(k + 1).start()

    def load(i, q):
        chip = 4 * q + plane_order()[i]
        return pltpu.make_async_copy(part_ref.at[2 * chip + core], ring.at[i], load_sem.at[i])

    def next_level(q):
        inner = jnp.where(q == 3, jnp.where(z == 1, 2, 1), jnp.where(q == 0, jnp.where(z == 1, 1, 3), jnp.where(z == 1, 0, 2)))
        return jnp.where(z == 0, q - 1, jnp.where(z == 3, q + 1, inner))

    def give(chip):
        return pltpu.make_async_remote_copy(src_ref=part_ref.at[2 * chip + 1 - core], dst_ref=acc.at[chip],
            send_sem=sib_send.at[chip], recv_sem=sib_recv.at[chip], device_id=(sibling,), device_id_type=MESH)

    levels = []
    for dist in (3, 2, 1):
        for sign in (1, -1):
            q = z + sign * dist
            levels.append((dist, sign, q, (q >= 0) & (q < 4)))

    def run(dist, work):
        for d, sign, q, have in levels:
            if d == dist:
                pl.when(have)(functools.partial(work, q))

    def run_signed(dist, work):
        for d, sign, q, have in levels:
            if d == dist:
                pl.when(have)(functools.partial(work, q, sign, dist))

    def begin_gives(q):
        for i in plane_order():
            give(4 * q + i).start()

    def chip_of(cu, cv, cz):
        return cz * 4 + jnp.where(core == 0, cv * 2 + cu, cu * 2 + cv)

    def plane_order():
        return (chip_of(u2, v2, 0), chip_of(u2, v, 0), chip_of(u, v2, 0), chip_of(u, v, 0))

    for i in range(4):
        load(i, jnp.where(z >= 2, 0, 3)).start()
    for copy in tail_loads:
        copy.start()
    pl.semaphore_wait(bar, 5 + jnp.where(zup & zdown, 1, 0))
    run(3, begin_gives)
    run(2, begin_gives)

    def ready(i, q):
        chip = 4 * q + plane_order()[i]
        load(i, q).wait()
        give(chip).wait_recv()

        def step(s, carry):
            total = acc[chip, s].astype(jnp.float32) + ring[i, s].astype(jnp.float32)
            acc[chip, s] = total.astype(acc.dtype)
            return carry

        lax.fori_loop(0, slots, step, 0)

        @pl.when(q != z)
        def _():
            load(i, next_level(q)).start()

    def out_copy(cu, cv, cz, color, target, place):
        lo, n = span[color]
        chip = chip_of(cu, cv, cz)
        buf, index, sem, flag = place
        return pltpu.make_async_remote_copy(src_ref=acc.at[chip, pl.ds(lo, n)], dst_ref=buf.at[index],
            send_sem=send_sem.at[chip, color], recv_sem=sem.at[flag], device_id=(target,), device_id_type=MESH)

    def arrived(place, color):
        lo, n = span[color]
        buf, index, sem, flag = place
        pltpu.make_async_remote_copy(src_ref=acc.at[0, pl.ds(lo, n)], dst_ref=buf.at[index],
            send_sem=send_sem.at[0, color], recv_sem=sem.at[flag], device_id=(sibling,), device_id_type=MESH).wait_recv()

    def add(cu, cv, cz, color, pieces):
        lo, n = span[color]
        chip = chip_of(cu, cv, cz)
        for place in pieces:
            arrived(place, color)

        def step(s, carry):
            total = acc[chip, lo + s].astype(jnp.float32)
            for buf, index, _, _ in pieces:
                total = total + buf[index, s].astype(jnp.float32)
            acc[chip, lo + s] = total.astype(acc.dtype)
            return carry

        lax.fori_loop(0, n, step, 0)

    def UB(q, i): return (ub, 2 * q + i, usem, 2 * q + i)
    def UD(q, i): return (ud, 2 * q + i, usem, 9 + 2 * q + i)
    def UC(q): return (uc, q, usem, 17 + q)
    def VA(q, i): return (va, 2 * q + i, vsem, 2 * q + i)
    def VC(q, i): return (vc, 2 * q + i, vsem, 9 + 2 * q + i)
    def VD(q): return (vd, q, vsem, 17 + q)
    def Z(q, k): return ((zc, zd, zs)[min(k, 2)], q if k < 2 else 4 * q + k - 2, zsem, 6 * q + k)

    def send_u(q, color, i):
        out_copy(u2, (v, v2)[i], q, color, u_peer, UB(q, i) if color == 1 else UD(q, i)).start()

    def send_v(q, color, i):
        out_copy((u, u2)[i], v2, q, color, v_peer, VA(q, i) if color == 0 else VC(q, i)).start()

    def term_a(q):
        ready(0, q)
        send_u(q, 1, 1)
        send_v(q, 0, 1)

    def term_c(q):
        send_v(q, 2, 1)
        send_u(q, 3, 1)

    def term_b(q):
        ready(1, q)
        send_u(q, 1, 0)
        ready(2, q)
        send_v(q, 0, 0)

    def term_d(q):
        send_u(q, 3, 0)
        send_v(q, 2, 0)
        ready(3, q)

    def plane_two(q):
        add(u2, v, q, 2, [VC(q, 1)])
        out_copy(u2, v, q, 2, u_peer, UC(q)).start()
        add(u, v2, q, 3, [UD(q, 1)])
        out_copy(u, v2, q, 3, v_peer, VD(q)).start()

    def column(part, q, sign, dist):
        target = up if sign == 1 else down
        more = zdown if sign == 1 else zup
        level = 4 if (dist == 1 and sign == 1) else q
        kinds = (
            (0, u, v, 2, [UC(q), VC(q, 0)]),
            (1, u, v, 3, [VD(q), UD(q, 0)]),
            (2, u, v, 0, [VA(q, 0)]),
            (3, u, v, 1, [UB(q, 0)]),
            (4, u2, v, 0, [VA(q, 1)]),
            (5, u, v2, 1, [UB(q, 1)]),
        )
        for k, cu, cv, color, pieces in ((kinds[5], kinds[4], kinds[3], kinds[2]), (kinds[0], kinds[1]))[part]:
            @pl.when(more)
            def _():
                add(cu, cv, q, color, pieces + [Z(q, k)])

            @pl.when(jnp.logical_not(more))
            def _():
                add(cu, cv, q, color, pieces)

            out_copy(cu, cv, q, color, target, Z(level, k)).start()

    planes = functools.partial(column, 0)
    last = functools.partial(column, 1)
    def begin_tail():
        for copy in tail_loads:
            copy.wait()
        sums[0] = rows_ref[...]

    tail = tail_steps(
        x_ref, vec_ref, marks_ref, resid_ref, (key_grad, value_grad, recept_grad), weights,
        (grad_key_in, grad_value_in, grad_recept_in), ext, unit, inverse, carried, wide, input_ref, sums.at[0],
    )
    send_input = pltpu.make_async_copy(input_ref, input_hbm, input_sem)
    run(3, term_a)
    run(3, term_c)
    run(3, term_b)
    run(3, term_d)
    begin_tail()
    tail[0]()
    run_signed(3, planes)
    tail[1]()
    run(2, term_a)
    run(2, term_c)
    run(3, plane_two)
    run(2, term_b)
    run(2, term_d)
    tail[2]()
    run(1, begin_gives)
    run_signed(3, last)
    tail[3]()
    run(1, term_a)
    run(1, term_c)
    run_signed(2, planes)
    begin_gives(z)
    tail[4]()
    run(2, plane_two)
    run(1, term_b)
    run(1, term_d)
    run_signed(2, last)
    term_a(z)
    term_c(z)
    tail[5]()
    row_copy(0).start()
    run_signed(1, planes)
    row_step(0)
    run(1, plane_two)
    term_b(z)
    term_d(z)
    row_step(1)
    run_signed(1, last)
    tail[6]()
    send_input.start()
    row_step(2)
    plane_two(z)
    row_step(3)

    def own(k, cu, cv, color, pieces):
        @pl.when(zup & zdown)
        def _():
            add(cu, cv, z, color, pieces + [Z(z, k), Z(4, k)])

        @pl.when(zup & jnp.logical_not(zdown))
        def _():
            add(cu, cv, z, color, pieces + [Z(z, k)])

        @pl.when(zdown & jnp.logical_not(zup))
        def _():
            add(cu, cv, z, color, pieces + [Z(4, k)])

    own(4, u2, v, 0, [VA(z, 1)])
    out_copy(u2, v, z, 0, u_peer, UB(4, 0)).start()
    own(5, u, v2, 1, [UB(z, 1)])
    out_copy(u, v2, z, 1, v_peer, VA(4, 0)).start()
    own(0, u, v, 2, [UC(z), VC(z, 0)])
    own(1, u, v, 3, [VD(z), UD(z, 0)])
    row_step(4)
    total_ref[...] = sums[10]
    own(2, u, v, 0, [VA(z, 0), UB(4, 0)])
    own(3, u, v, 1, [UB(z, 0), VA(4, 0)])
    pltpu.sync_copy(acc.at[chip_of(u, v, z)], out_ref)
    send_input.wait()
    for chip in range(16):
        give(chip).wait_send()
        for color in range(4):
            @pl.when(chip != chip_of(u, v, z))
            def _():
                lo, n = span[color]
                pltpu.make_async_remote_copy(src_ref=acc.at[chip, pl.ds(lo, n)], dst_ref=acc.at[chip, pl.ds(lo, n)],
                    send_sem=send_sem.at[chip, color], recv_sem=usem.at[0], device_id=(sibling,), device_id_type=MESH).wait_send()

def scatter_blocks(part, rows, tail, cid=2):
    vectors, marks, x_rows, resid_grad, *grads, weights = tail
    _, slots, height, feats = part.shape
    own = x_rows.shape[0] - ROW_TILE
    size_a, size_b, size_c, size_d = (n for _, n in scatter_spans(slots))
    dt = part.dtype
    block = lambda *shape: pltpu.VMEM(shape + (height, feats), dt)
    like = lambda array: pltpu.VMEM(array.shape, array.dtype)
    anywhere = pl.BlockSpec(memory_space=pl.ANY)
    vmem = pl.BlockSpec(memory_space=pltpu.VMEM)
    wide_shapes, tail_scratch = tail_shapes(x_rows.shape)
    return pl.pallas_call(
        functools.partial(scatter_kernel, slots),
        out_shape=(
            jax.ShapeDtypeStruct(part.shape[1:], dt),
            jax.ShapeDtypeStruct(rows.shape, rows.dtype),
            jax.ShapeDtypeStruct((own, feats), jnp.float32),
        ),
        in_specs=[anywhere] + [vmem] * 3 + [anywhere] * 6,
        out_specs=(anywhere, vmem, anywhere),
        scratch_shapes=[
            block(16, slots),
            block(4, slots),
            block(9, size_b),
            block(4, size_c),
            block(8, size_d),
            block(9, size_a),
            block(8, size_c),
            block(4, size_d),
            block(20, size_a),
            block(5, size_c),
            block(5, size_d),
            pltpu.VMEM((11,) + rows.shape, rows.dtype),
            like(x_rows), like(resid_grad), *(like(g) for g in grads), like(weights),
            *wide_shapes,
            *tail_scratch,
            pltpu.VMEM((own, feats), jnp.float32),
            pltpu.SemaphoreType.DMA((4,)),
            pltpu.SemaphoreType.DMA((16,)),
            pltpu.SemaphoreType.DMA((16,)),
            pltpu.SemaphoreType.DMA((16, 4)),
            pltpu.SemaphoreType.DMA((21,)),
            pltpu.SemaphoreType.DMA((21,)),
            pltpu.SemaphoreType.DMA((30,)),
            pltpu.SemaphoreType.DMA((5,)),
            pltpu.SemaphoreType.DMA((5,)),
            pltpu.SemaphoreType.DMA((6,)),
            pltpu.SemaphoreType.DMA,
        ],
        compiler_params=pltpu.CompilerParams(collective_id=cid, has_side_effects=True, vmem_limit_bytes=VMEM_BYTES),
        name="scatter_blocks",
    )(part, rows, vectors, marks, x_rows, resid_grad, *grads, weights)


ROW_TILE = 16
BIG_TILE = 64
PIECES = 4
STEP_TILE = 32
CHUNKS = 8
LANES = 128
PLANE = 8
PLANES = GRID_DEVICES // PLANE
VMEM_BYTES = 60 * 2**20


def rows_at(index, size=ROW_TILE):
    return pl.ds(pl.multiple_of(index * size, size), size)


def fetch_blocks(slot_ref, pool_ref, store_ref, sem, first_block, place, count):
    def step(b, carry):
        for k in range(4):
            pltpu.make_async_copy(
                pool_ref.at[slot_ref[first_block + 4 * b + k]], store_ref.at[place + 4 * b + k], sem
            ).start()
        return carry

    lax.fori_loop(0, count // 4, step, 0)


def await_blocks(pool_ref, store_ref, sem, place, count):
    pltpu.make_async_copy(
        pool_ref.at[pl.ds(0, count)], store_ref.at[pl.ds(place, count)], sem
    ).wait()


def times_weight(left_ref, store_ref, place, count, write, width=512):
    features = store_ref.shape[2]

    def step(n, carry):
        cols = pl.ds(pl.multiple_of(n * width, width), width)
        right = store_ref[place : place + count, :, cols].reshape(count * BLOCK_ROWS, width)
        write(cols, jnp.dot(left_ref[...], right, preferred_element_type=jnp.float32))
        return carry

    lax.fori_loop(0, features // width, step, 0)


def times_weight_back(left_ref, store_ref, place, count, write, width=1024):
    blocks = width // BLOCK_ROWS

    def step(n, carry):
        cols = pl.ds(pl.multiple_of(n * width, width), width)
        right = store_ref[pl.ds(place + n * blocks, blocks)].reshape(width, store_ref.shape[2])
        write(cols, product_back(left_ref[...], right))
        return carry

    lax.fori_loop(0, count // blocks, step, 0)


def weight_gradient(left_ref, right_ref, own, slot_ref, grad_ref, store_ref, sem, first_block, place, width=1024):
    blocks = width // BLOCK_ROWS
    steps = left_ref.shape[1] // width

    def step(n, carry):
        cols = pl.ds(pl.multiple_of(n * width, width), width)
        piece = product_left(left_ref[0:own, cols], right_ref[0:own])
        at = place + n * blocks
        store_ref[pl.ds(at, blocks)] = piece.astype(store_ref.dtype).reshape(blocks, *store_ref.shape[1:])

        def put(b, inner):
            for k in range(4):
                pltpu.make_async_copy(
                    store_ref.at[at + 4 * b + k],
                    grad_ref.at[slot_ref[first_block + n * blocks + 4 * b + k]],
                    sem,
                ).start()
            return inner

        return lax.fori_loop(0, blocks // 4, put, carry)

    lax.fori_loop(0, steps, step, 0)


def await_gradient(store_ref, grad_ref, sem, place, count):
    pltpu.make_async_copy(
        store_ref.at[pl.ds(place, count)], grad_ref.at[pl.ds(0, count)], sem
    ).wait()


def start_pieces(pairs, sems, own):
    for p in range(PIECES + 1):
        for k, (src, dst) in enumerate(pairs):
            if p < PIECES or dst.shape[0] > own:
                piece_copy(src, dst, sems, own, k, p).start()


def piece_copy(src, dst, sems, own, k, p):
    size = own // PIECES
    at = pl.ds(p * size, size) if p < PIECES else pl.ds(own, ROW_TILE)
    return pltpu.make_async_copy(src.at[at], dst.at[at], sems.at[k, p])


def wait_piece(pairs, sems, own, p):
    for k, (src, dst) in enumerate(pairs):
        if p < PIECES or dst.shape[0] > own:
            piece_copy(src, dst, sems, own, k, p).wait()


def for_rows(rows, work, sums=()):
    own = rows - ROW_TILE

    def step(j, carry):
        out = work(pl.multiple_of(j * BIG_TILE, BIG_TILE), BIG_TILE, *carry)
        return carry if out is None else out

    sums = lax.fori_loop(0, own // BIG_TILE, step, sums)
    return sums


def fold(piece):
    return jnp.sum(piece.reshape(-1, CHUNKS, piece.shape[1]), axis=0)


def unit_norm(values):
    centered = values - jnp.mean(values, axis=1, keepdims=True)
    inverse = lax.rsqrt(jnp.mean(centered * centered, axis=1, keepdims=True) + NORM_EPS)
    return centered * inverse, inverse


def merge(first, second):
    top = jnp.maximum(first[2], second[2])
    one, two = jnp.exp(first[2] - top), jnp.exp(second[2] - top)
    return (one * first[0] + two * second[0], one * first[1] + two * second[1], top)


def aged(state, distance, alive, rate):
    return (state[0], state[1], jnp.where(alive > 0.5, state[2] - distance * rate, NEGATIVE))


def reset(state, start):
    cut = start > 0.5
    return (
        jnp.where(cut, 0.0, state[0]),
        jnp.where(cut, 0.0, state[1]),
        jnp.where(cut, NEGATIVE, state[2]),
    )


def advance(state, key, value, rate):
    older = state[2] - rate
    top = jnp.maximum(older, key)
    old, new = jnp.exp(older - top), jnp.exp(key - top)
    return (old * state[0] + new * value, old * state[1] + new, top)


def shift_in(ext, own):
    ext[0:8] = jnp.concatenate([ext[own + 10 : own + 11], ext[own : own + 7]], axis=0)


def halo_previous(ext, own, features):
    return jnp.concatenate(
        [
            ext[own + 7 : own + 8],
            ext[own + 8 : own + 9],
            ext[own + 11 : own + 12],
            jnp.zeros((ROW_TILE - 3, features), jnp.float32),
        ],
        axis=0,
    )


def normed_pair(ext, marks_ref, first, size):
    here = ext[pl.ds(pl.multiple_of(first + 8, 8), size)]
    before = ext[pl.ds(first, size)] * marks_ref[pl.ds(first, size), 1:2]
    return here, before


def take_step(wide, first, length):
    at = pl.ds(first, CHUNKS, stride=length)
    return jnp.concatenate([wide[k, at] for k in range(wide.shape[0])], axis=1)


def put_step(wide, first, length, tile):
    at = pl.ds(first, CHUNKS, stride=length)
    lanes = wide.shape[2]
    for k in range(wide.shape[0]):
        wide[k, at] = tile[:, k * lanes : (k + 1) * lanes]


def take_rows(wide, at):
    return jnp.concatenate([wide[k, at] for k in range(wide.shape[0])], axis=1)


def put_rows(wide, at, tile):
    lanes = wide.shape[2]
    for k in range(wide.shape[0]):
        wide[k, at] = tile[:, k * lanes : (k + 1) * lanes]


def none_between(offsets, low, high):
    hit = None
    for offset in offsets:
        inside = (low <= offset) & (offset <= high)
        hit = inside if hit is None else hit | inside
    return jnp.where(hit, 0.0, 1.0)


def write_marks(doc_ref, marks_ref, chunk_ref, link_ref, own, devices):
    rows = marks_ref.shape[0]
    length = own // CHUNKS
    total = own * devices
    me = lax.axis_index("seq")
    first = me * own
    offsets = [jnp.int32(0)]
    for k in range(doc_ref.shape[0] - 1):
        offsets.append(offsets[-1] + doc_ref[k])
    row = lax.broadcasted_iota(jnp.int32, (rows, 1), 0)
    chunk, step = lax.rem(row, CHUNKS), row // CHUNKS
    extra = jnp.where(row < own + 2, row, own - 1 - (row - (own + 2)) - own)
    place = first + jnp.where(row < own, chunk * length + step, extra)
    inside = (place >= 0) & (place < total)
    keep = jnp.where(inside, none_between(offsets, place, place), 0.0)
    begin = first + chunk * length
    marks_ref[:, 0:1] = 1.0 - keep
    marks_ref[:, 1:2] = keep
    marks_ref[:, 2:3] = jnp.where(row < own, none_between(offsets, begin, place), 1.0)
    marks_ref[:, 3:4] = jnp.where(row < own, none_between(offsets, place + 1, begin + length - 1), 1.0)
    chunk = lax.broadcasted_iota(jnp.int32, (CHUNKS, 1), 0)
    begin = first + chunk * length
    end = begin + length - 1
    chunk_ref[:, 0:1] = none_between(offsets, begin, end)
    chunk_ref[:, 1:2] = jnp.where(first > 0, none_between(offsets, first - 1, begin - 1), 0.0)
    chunk_ref[:, 2:3] = none_between(offsets, begin, end - 1)
    chunk_ref[:, 3:4] = (1 + chunk * length).astype(jnp.float32)
    chunk_ref[:, 4:5] = jnp.where(first + own < total, none_between(offsets, end + 1, first + own), 0.0)
    chunk_ref[:, 5:6] = (1 + (CHUNKS - 1 - chunk) * length).astype(jnp.float32)
    def put(rows, col, valid, distance):
        link_ref[rows, col : col + 1] = valid
        link_ref[rows, col + 1 : col + 2] = distance.astype(jnp.float32)

    if devices != GRID_DEVICES:
        other = lax.broadcasted_iota(jnp.int32, (devices, 1), 0)
        every = slice(0, devices)
        put(every, 0, jnp.where(other < me, none_between(offsets, own * (other + 1) - 1, own * me - 2), 0.0), own * (me - 1 - other))
        put(every, 2, jnp.where(other > me, none_between(offsets, own * (me + 1) + 1, own * other), 0.0), own * (other - me - 1))
        return
    z = me // PLANE
    base = z * PLANE
    end = base + PLANE
    other = base + lax.broadcasted_iota(jnp.int32, (PLANE, 1), 0)
    rows = slice(0, PLANE)
    put(rows, 0, jnp.where(other < me, none_between(offsets, own * (other + 1) - 1, own * me - 2), 0.0), own * (me - 1 - other))
    put(rows, 2, jnp.where(other > me, none_between(offsets, own * (me + 1) + 1, own * other), 0.0), own * (other - me - 1))
    rows = slice(PLANE, 2 * PLANE)
    put(rows, 0, none_between(offsets, own * (other + 1) - 1, own * end - 2), own * (end - 1 - other))
    put(rows, 2, none_between(offsets, own * base + 1, own * other), own * (other - base))
    rows = slice(2 * PLANE, 2 * PLANE + PLANES)
    far = lax.broadcasted_iota(jnp.int32, (PLANES, 1), 0)
    span = own * PLANE
    put(rows, 0, jnp.where(far < z, none_between(offsets, span * (far + 1) - 1, span * z - 2), 0.0), span * (z - 1 - far))
    put(rows, 2, jnp.where(far > z, none_between(offsets, span * (z + 1) + 1, span * far), 0.0), span * (far - z - 1))
    rows = slice(2 * PLANE + PLANES, 2 * PLANE + PLANES + 1)
    here = me + jnp.zeros((1, 1), jnp.int32)
    put(rows, 0, none_between(offsets, own * base - 1, own * here - 2), own * (here - base))
    put(rows, 2, none_between(offsets, own * (here + 1) + 1, own * end), own * (end - 1 - here))


def mask_column(pad_ref, column):
    for k in range(pad_ref.shape[0]):
        row = pad_ref[k : k + 1].astype(jnp.float32)
        column[k * LANES : (k + 1) * LANES] = jnp.broadcast_to(row, (LANES, LANES)).T[:, 0:1]


def normed_rows(x_ref, vec_ref, ext, first, size, tile):
    x_ref[pl.ds(first, size)] = tile.astype(jnp.bfloat16)
    unit, _ = unit_norm(tile)
    ext[pl.ds(pl.multiple_of(first + 8, 8), size)] = unit * vec_ref[0:1] + vec_ref[1:2]


def prepare_own(devices, doc_ref, tokens_ref, grads_ref, column, vec_ref, x_ref, grad_ref, marks, ext, wide, wide_grad):
    rows = x_ref.shape[0]
    own = rows - ROW_TILE
    length = own // CHUNKS
    write_marks(doc_ref, *marks, own, devices)

    def widen(first, size):
        at = pl.ds(first, size)
        put_rows(wide, at, tokens_ref[at].astype(jnp.float32))
        put_rows(wide_grad, at, grads_ref[at].astype(jnp.float32) * column[at])

    for_rows(rows, widen)

    def arrange(first, size):
        steps = [first // CHUNKS + k for k in range(size // CHUNKS)]
        tile = jnp.concatenate([take_step(wide, i, length) for i in steps], axis=0)
        normed_rows(x_ref, vec_ref, ext, first, size, tile)
        tile = jnp.concatenate([take_step(wide_grad, i, length) for i in steps], axis=0)
        grad_ref[pl.ds(first, size)] = tile.astype(jnp.bfloat16)

    for_rows(rows, arrange)


def prepare_halo(devices, after_ref, after_grad_ref, before_ref, vec_ref, x_ref, grad_ref, marks_ref, lows, ext):
    rows, features = x_ref.shape
    own = rows - ROW_TILE
    me = lax.axis_index("seq")
    more, less = me < devices - 1, me > 0
    later = jnp.where(more, after_ref[...].astype(jnp.float32), 0.0)[0:2]
    earlier = jnp.where(less, before_ref[...].astype(jnp.float32), 0.0)
    blank_rows = jnp.zeros((ROW_TILE - 4, features), jnp.float32)
    tile = jnp.concatenate(
        [later, earlier[ROW_TILE - 1 :], earlier[ROW_TILE - 2 : ROW_TILE - 1], blank_rows], axis=0
    )
    normed_rows(x_ref, vec_ref, ext, own, ROW_TILE, tile)
    later_grad = jnp.where(more, after_grad_ref[...].astype(jnp.float32), 0.0)[0:2]
    grad_ref[own:rows] = jnp.concatenate([later_grad, blank_rows, blank_rows[:2]], axis=0).astype(jnp.bfloat16)
    shift_in(ext, own)

    def mix(first, size, here, before):
        for row, ref in zip((2, 3, 4), lows):
            weight = vec_ref[row : row + 1]
            ref[pl.ds(first, size)] = (weight * here + (1.0 - weight) * before).astype(jnp.bfloat16)

    for_rows(rows, lambda first, size: mix(first, size, *normed_pair(ext, marks_ref, first, size)))
    mix(own, ROW_TILE, ext[own + 8 : own + 8 + ROW_TILE], halo_previous(ext, own, features) * marks_ref[own:rows, 1:2])


def prepared_shapes(devices, own, features):
    rows = own + ROW_TILE
    count = 2 * PLANE + PLANES + 1 if devices == GRID_DEVICES else devices
    low = jax.ShapeDtypeStruct((rows, features), jnp.bfloat16)
    small = lambda *shape: jax.ShapeDtypeStruct(shape, jnp.float32)
    shapes = (low, low, small(rows, 4), small(CHUNKS, 6), small(count, 4), low, low, low)
    scratch = [
        pltpu.VMEM((own, 1), jnp.float32),
        pltpu.VMEM((rows + 8, features), jnp.float32),
        pltpu.VMEM((features // LANES, own, LANES), jnp.float32),
        pltpu.VMEM((features // LANES, own, LANES), jnp.float32),
    ]
    return shapes, scratch


def prepare_kernel(
    devices, doc_ref, tokens_ref, grads_ref, pad_ref, after_ref, after_grad_ref, before_ref, vec_ref,
    x_ref, grad_ref, marks_ref, chunk_ref, link_ref, in_key, in_value, in_recept,
    column, ext, wide, wide_grad,
):
    mask_column(pad_ref, column)
    marks = (marks_ref, chunk_ref, link_ref)
    prepare_own(devices, doc_ref, tokens_ref, grads_ref, column, vec_ref, x_ref, grad_ref, marks, ext, wide, wide_grad)
    lows = (in_key, in_value, in_recept)
    prepare_halo(devices, after_ref, after_grad_ref, before_ref, vec_ref, x_ref, grad_ref, marks_ref, lows, ext)


def prepare_pass(devices, doc_lengths, tokens_in, cotangent, pad_rows, halo, vectors):
    shapes, scratch = prepared_shapes(devices, *tokens_in.shape)
    vmem = pl.BlockSpec(memory_space=pltpu.VMEM)
    return pl.pallas_call(
        functools.partial(prepare_kernel, devices),
        out_shape=shapes,
        in_specs=[pl.BlockSpec(memory_space=pltpu.SMEM)] + [vmem] * 7,
        out_specs=(vmem,) * len(shapes),
        scratch_shapes=scratch,
        compiler_params=pltpu.CompilerParams(vmem_limit_bytes=VMEM_BYTES),
        name="prepare_pass",
    )(doc_lengths, tokens_in, cotangent, pad_rows, *halo, vectors)


def open_kernel(
    slot_ref, vec_ref, marks_ref, chunk_ref, in_key, in_value, in_recept, pool_ref,
    prefix_ref, summary_ref, key_out, value_out, recept_out, state_out, weights_ref,
    key_ref, value_ref, recept_ref, num_ref, den_ref, max_ref, store, sem, out_sem,
):
    rows, features = in_key.shape
    own = rows - ROW_TILE
    length = own // CHUNKS
    per = EMBED_SIZE // BLOCK_ROWS
    for m in range(3):
        fetch_blocks(slot_ref, pool_ref, store, sem.at[m], m * per, m * per, per)
    for m, (left, out) in enumerate(((in_key, key_ref), (in_value, value_ref), (in_recept, recept_ref))):
        await_blocks(pool_ref, store, sem.at[m], m * per, per)

        def write(cols, piece, out=out):
            out[:, cols] = piece

        times_weight(left, store, m * per, per, write)
    sent = [
        pltpu.make_async_copy(src, dst, out_sem.at[k])
        for k, (src, dst) in enumerate(
            (
                (key_ref, key_out), (value_ref, value_out), (recept_ref, recept_out), (store, weights_ref),
                (num_ref, state_out.at[0]), (den_ref, state_out.at[1]), (max_ref, state_out.at[2]),
            )
        )
    ]
    for copy in sent[:4]:
        copy.start()
    rate = jnp.exp(vec_ref[5:6])

    def token(i, state, key, value):
        state = reset(state, marks_ref[rows_at(i, CHUNKS), 0:1])
        num_ref[rows_at(i, CHUNKS)], den_ref[rows_at(i, CHUNKS)], max_ref[rows_at(i, CHUNKS)] = state
        return advance(state, key, value, rate)

    def step(i, state):
        return token(i, state, key_ref[rows_at(i, CHUNKS)], value_ref[rows_at(i, CHUNKS)])

    blank = jnp.zeros((CHUNKS, features), jnp.float32)
    state = lax.fori_loop(0, length - 1, step, (blank, blank, blank + NEGATIVE))
    late = tuple(item[CHUNKS - 1 :] for item in state)
    ends = step(length - 1, state)
    for copy in sent[4:]:
        copy.start()
    prior = (value_ref[own + 2 : own + 3], jnp.ones((1, features), jnp.float32), key_ref[own + 2 : own + 3])
    for c in range(CHUNKS):
        for k in range(3):
            prefix_ref[k, c : c + 1] = prior[k]
        if c < CHUNKS - 1:
            old = aged(prior, float(length), chunk_ref[c : c + 1, 0:1], rate)
            prior = merge(tuple(item[c : c + 1] for item in ends), old)
    last = merge(late, aged(prior, float(length - 1), chunk_ref[CHUNKS - 1 :, 2:3], rate))
    summary_ref[...] = jnp.concatenate(last, axis=0)
    for copy in sent:
        copy.wait()


def open_pass(slots, vectors, marks, chunk_marks, lows, pool):
    rows, features = lows[0].shape
    own = rows - ROW_TILE
    full = jax.ShapeDtypeStruct((rows, features), jnp.float32)
    small = lambda *shape: jax.ShapeDtypeStruct(shape, jnp.float32)
    vmem = pl.BlockSpec(memory_space=pltpu.VMEM)
    anywhere = pl.BlockSpec(memory_space=pl.ANY)
    f32 = lambda *shape: pltpu.VMEM(shape, jnp.float32)
    blocks = (3 * EMBED_SIZE // BLOCK_ROWS, BLOCK_ROWS, features)
    return pl.pallas_call(
        open_kernel,
        out_shape=(
            small(3, CHUNKS, features), small(3, features), full, full, full, small(3, own, features),
            jax.ShapeDtypeStruct(blocks, jnp.bfloat16),
        ),
        in_specs=[pl.BlockSpec(memory_space=pltpu.SMEM)] + [vmem] * 6 + [anywhere],
        out_specs=(vmem,) * 2 + (anywhere,) * 5,
        scratch_shapes=[f32(rows, features)] * 3 + [f32(own, features)] * 3 + [
            pltpu.VMEM(blocks, jnp.bfloat16),
            pltpu.SemaphoreType.DMA((3,)),
            pltpu.SemaphoreType.DMA((7,)),
        ],
        compiler_params=pltpu.CompilerParams(vmem_limit_bytes=VMEM_BYTES),
        name="open_pass",
    )(slots, vectors, marks, chunk_marks, *lows, pool)


def middle_kernel(
    slot_ref, vec_ref, marks_ref, chunk_ref, incoming_ref, prefix_ref,
    x_in, grad_in, key_in, value_in, recept_in, state_in, pool_ref,
    suffix_ref, summary_ref, sums_ref, fade_ref,
    layer_out, resid_out, key_out, value_out, recept_out, slot_grad,
    x_ref, grad_ref, key_ref, value_ref, recept_ref, layer_ref, resid_grad, wkv, gw, own_share, recept_grad,
    full_num, full_den, full_max, mixed, ext, unit, inverse, low_key, low_recept, hidden, squared, value_acc, gate, gcv, gcg, hidden_grad,
    attn_grad, top_log, wide, store, sem, out_sem, in_sem, piece_sem, done_sem,
):
    rows, features = x_ref.shape
    own = rows - ROW_TILE
    tiles = rows // ROW_TILE
    length = own // CHUNKS
    per = EMBED_SIZE // BLOCK_ROWS
    ff = FF // BLOCK_ROWS
    at_out, at_recept, at_key, at_value = 0, per, 2 * per, 2 * per + ff
    pairs = [(key_in, key_ref), (value_in, value_ref), (recept_in, recept_ref)]
    pairs += [(state_in.at[k], ref) for k, ref in enumerate((full_num, full_den, full_max))]
    start_pieces(pairs, piece_sem, own)
    arrive_x = pltpu.make_async_copy(x_in, x_ref, in_sem.at[0])
    arrive_grad = pltpu.make_async_copy(grad_in, grad_ref, in_sem.at[1])
    sent = [
        pltpu.make_async_copy(src, dst, done_sem.at[k])
        for k, (src, dst) in enumerate(
            (
                (layer_ref, layer_out), (resid_grad, resid_out), (recept_grad, recept_out),
                (gw, key_out), (own_share, value_out),
            )
        )
    ]
    fetch_blocks(slot_ref, pool_ref, store, sem.at[0], 3 * per, at_out, per)
    arrive_x.start()
    arrive_grad.start()
    fetch_blocks(slot_ref, pool_ref, store, sem.at[1], 5 * per, at_key, ff)
    fetch_blocks(slot_ref, pool_ref, store, sem.at[2], 5 * per + ff, at_value, ff)
    fetch_blocks(slot_ref, pool_ref, store, sem.at[3], 4 * per, at_recept, per)
    rate = jnp.exp(vec_ref[5:6])
    bonus = vec_ref[6:7]
    incoming = tuple(incoming_ref[k : k + 1] for k in range(3))
    carry = merge(
        tuple(prefix_ref[k] for k in range(3)),
        aged(tuple(jnp.broadcast_to(v, (CHUNKS, features)) for v in incoming), chunk_ref[:, 3:4], chunk_ref[:, 1:2], rate),
    )

    def attend(j, size, state, key, value, recept):
        own_log = bonus + key
        top = jnp.maximum(state[2], own_log)
        old, new = jnp.exp(state[2] - top), jnp.exp(own_log - top)
        scale = 1.0 / (old * state[1] + new)
        out = (old * state[0] + new * value) * scale
        wkv[rows_at(j, size)] = out
        own_share[rows_at(j, size)] = new * scale
        top_log[rows_at(j, size)] = top
        value_acc[rows_at(j, size)] = scale
        ext[rows_at(j, size)] = jax.nn.sigmoid(recept) * out

    carry_wide = tuple(jnp.concatenate([item] * (STEP_TILE // CHUNKS), axis=0) for item in carry)
    ramp = lax.broadcasted_iota(jnp.int32, (STEP_TILE, 1), 0) // CHUNKS

    def attend_step(i, state_carry):
        at = rows_at(i, STEP_TILE)
        alive = marks_ref[at, 2:3]
        distance = (i * (STEP_TILE // CHUNKS) + ramp).astype(jnp.float32)
        state = merge((full_num[at], full_den[at], full_max[at]), aged(carry_wide, distance, alive, rate))
        full_num[at], full_den[at], full_max[at] = state
        attend(i, STEP_TILE, state, key_ref[at], value_ref[at], recept_ref[at])
        return state_carry

    for p in range(PIECES):
        wait_piece(pairs, piece_sem, own, p)
        count = own // STEP_TILE
        lax.fori_loop(p * count // PIECES, (p + 1) * count // PIECES, attend_step, 0)
    wait_piece(pairs, piece_sem, own, PIECES)

    def row(ref, r):
        return ref[r : r + 1]

    end = advance(
        (row(full_num, own - 1), row(full_den, own - 1), row(full_max, own - 1)),
        row(key_ref, own - 1), row(value_ref, own - 1), rate,
    )
    halo_one = reset(end, marks_ref[own : own + 1, 0:1])
    halo_two = reset(
        advance(halo_one, row(key_ref, own), row(value_ref, own), rate), marks_ref[own + 1 : own + 2, 0:1]
    )
    halo_zero = reset(incoming, marks_ref[own + 2 : own + 3, 0:1])
    rest = jnp.zeros((ROW_TILE - 3, features), jnp.float32)
    halo_state = tuple(
        jnp.concatenate([halo_one[k], halo_two[k], halo_zero[k], rest + (NEGATIVE if k == 2 else 0.0)], axis=0)
        for k in range(3)
    )
    attend(tiles - 1, ROW_TILE, halo_state, key_ref[own:rows], value_ref[own:rows], recept_ref[own:rows])

    def pack(first, size):
        at = pl.ds(first, size)
        mixed[at] = ext[at].astype(jnp.bfloat16)
        gw[at] = value_acc[at]

    for_rows(rows, pack)
    pack(own, ROW_TILE)
    await_blocks(pool_ref, store, sem.at[0], at_out, per)
    arrive_x.wait()

    def write_resid(cols, piece):
        unit[:, cols] = x_ref[:, cols].astype(jnp.float32) + piece

    times_weight(mixed, store, at_out, per, write_resid)

    def norm(first, size):
        at = pl.ds(first, size)
        resid = unit[at]
        resid_grad[at] = resid
        out, inv = unit_norm(resid)
        unit[at] = out
        inverse[at] = inv
        ext[pl.ds(pl.multiple_of(first + 8, 8), size)] = out * vec_ref[7:8] + vec_ref[8:9]

    for_rows(rows, norm)
    norm(own, ROW_TILE)
    shift_in(ext, own)

    def mix(first, size, here, before):
        for r, ref in ((9, low_key), (10, low_recept)):
            weight = vec_ref[r : r + 1]
            ref[pl.ds(first, size)] = (weight * here + (1.0 - weight) * before).astype(jnp.bfloat16)

    for_rows(rows, lambda first, size: mix(first, size, *normed_pair(ext, marks_ref, first, size)))
    mix(own, ROW_TILE, ext[own + 8 : own + 8 + ROW_TILE], halo_previous(ext, own, features) * marks_ref[own:rows, 1:2])

    await_blocks(pool_ref, store, sem.at[1], at_key, ff)

    def write_hidden(cols, piece):
        up = jnp.maximum(piece, 0.0)
        hidden[:, cols] = up
        squared[:, cols] = (up * up).astype(jnp.bfloat16)

    times_weight_back(low_key, store, at_key, ff, write_hidden)
    await_blocks(pool_ref, store, sem.at[2], at_value, ff)

    def write_value(cols, piece):
        value_acc[:, cols] = piece

    times_weight(squared, store, at_value, ff, write_value)
    await_blocks(pool_ref, store, sem.at[3], at_recept, per)

    def write_gate(cols, piece):
        gate[:, cols] = piece

    times_weight(low_recept, store, at_recept, per, write_gate)

    arrive_grad.wait()

    def finish(first, size):
        at = pl.ds(first, size)
        opened = jax.nn.sigmoid(gate[at])
        value = value_acc[at]
        grad = grad_ref[at].astype(jnp.float32) * opened
        gcv[at] = grad.astype(jnp.bfloat16)
        gcg[at] = (grad * value * (1.0 - opened)).astype(jnp.bfloat16)
        return resid_grad[at] + opened * value

    def finish_own(first, size):
        out = finish(first, size)
        for k in range(size // CHUNKS):
            put_step(wide, first // CHUNKS + k, length, out[CHUNKS * k : CHUNKS * (k + 1)])

    for_rows(rows, finish_own)
    finish(own, ROW_TILE)

    def emit(first, size):
        layer_ref[pl.ds(first, size)] = take_rows(wide, pl.ds(first, size)).astype(jnp.bfloat16)

    for_rows(rows, emit)
    sent[0].start()

    def write_hidden_grad(cols, piece):
        hidden_grad[:, cols] = (piece * (2.0 * hidden[:, cols])).astype(jnp.bfloat16)

    times_weight_back(gcv, store, at_value, ff, write_hidden_grad)
    weight_gradient(squared, gcv, own, slot_ref, slot_grad, store, out_sem.at[2], 5 * per + ff, at_value)
    times_weight(hidden_grad, store, at_key, ff, write_value)
    weight_gradient(hidden_grad, low_key, own, slot_ref, slot_grad, store, out_sem.at[1], 5 * per, at_key)
    times_weight_back(gcg, store, at_recept, per, write_gate)
    weight_gradient(low_recept, gcg, own, slot_ref, slot_grad, store, out_sem.at[3], 4 * per, at_recept)
    carried = hidden.at[:, 0:features]
    mix_key, mix_recept = vec_ref[9:10], vec_ref[10:11]

    def carry_over(first, size):
        at = pl.ds(first, size)
        carried[at] = marks_ref[at, 1:2] * ((1.0 - mix_key) * value_acc[at] + (1.0 - mix_recept) * gate[at])

    for_rows(rows, carry_over)
    carry_over(own, ROW_TILE)
    halo_next = jnp.concatenate(
        [carried[own + 1 : own + 2], jnp.zeros((ROW_TILE - 1, features), jnp.float32)], axis=0
    )
    carried[own : own + 8] = jnp.concatenate([carried[1:8], carried[own : own + 1]], axis=0)

    def norm_back(first, size, following):
        at = pl.ds(first, size)
        grad = mix_key * value_acc[at] + mix_recept * gate[at] + following
        scaled = grad * vec_ref[7:8]
        inner = (
            scaled
            - jnp.mean(scaled, axis=1, keepdims=True)
            - unit[at] * jnp.mean(scaled * unit[at], axis=1, keepdims=True)
        )
        total = grad_ref[at].astype(jnp.float32) + inner * inverse[at]
        resid_grad[at] = total
        attn_grad[at] = total.astype(jnp.bfloat16)
        return grad

    def back_step(first, size, *sums):
        at = pl.ds(first, size)
        grad = norm_back(first, size, carried[pl.ds(pl.multiple_of(first + 8, 8), size)])
        here, before = normed_pair(ext, marks_ref, first, size)
        spread = here - before
        return (
            sums[0] + fold(grad * unit[at]),
            sums[1] + fold(grad),
            sums[2] + fold(value_acc[at] * spread),
            sums[3] + fold(gate[at] * spread),
        )

    blank = jnp.zeros((CHUNKS, features), jnp.float32)
    sums = for_rows(rows, back_step, (blank,) * 4)
    for k in range(4):
        sums_ref[k : k + 1] = jnp.sum(sums[k], axis=0, keepdims=True)
    norm_back(own, ROW_TILE, halo_next)
    sent[1].start()

    times_weight_back(attn_grad, store, at_out, per, write_gate)
    weight_gradient(mixed, attn_grad, own, slot_ref, slot_grad, store, out_sem.at[0], 3 * per, at_out)

    def gate_back(first, size):
        at = pl.ds(first, size)
        opened = jax.nn.sigmoid(recept_ref[at])
        grad = gate[at] * opened
        ext[at] = grad * gw[at]
        gw[at] = grad
        recept_grad[at] = (grad * wkv[at] * (1.0 - opened)).astype(jnp.bfloat16)

    for_rows(rows, gate_back)
    gate_back(own, ROW_TILE)
    sent[2].start()

    def back_token(state, share, out, top, start):
        older = state[2] - rate
        high = jnp.maximum(older, -top)
        old, new = jnp.exp(older - high), jnp.exp(-top - high)
        return reset((old * state[0] + new * share, old * state[1] - new * share * out, high), start)

    def back_scan(n, items):
        state, joint, sums = items[:3], items[3:6], items[6:]
        i = length - 1 - n
        at = rows_at(i, CHUNKS)
        value, out = value_ref[at], wkv[at]
        direct = own_share[at] * gw[at]
        bonus_grad = direct * (value - out)
        lift = jnp.exp(key_ref[at] + state[2])
        gw[at] = bonus_grad + lift * (state[0] * value + state[1])
        own_share[at] = direct + lift * state[0]
        whole = (full_num[at], full_den[at], full_max[at])
        fade = jnp.exp(state[2] + whole[2] - rate) * (state[0] * whole[0] + state[1] * whole[1])
        joint = merge(joint, aged(whole, (length - i).astype(jnp.float32), marks_ref[at, 3:4], rate))
        state = back_token(state, ext[at], out, top_log[at], marks_ref[at, 0:1])
        return state + joint + (sums[0] + fade, sums[1] + bonus_grad)

    empty = (blank, blank, blank + NEGATIVE)
    items = lax.fori_loop(0, length - 1, back_scan, empty + empty + (blank, blank))
    first = tuple(item[0:1] for item in items[:3])
    items = back_scan(jnp.int32(length - 1), items)
    heads = items[:3]
    for k in range(3):
        fade_ref[k] = items[3 + k]
    for k in range(2):
        sums_ref[4 + k : 5 + k] = jnp.sum(items[6 + k], axis=0, keepdims=True)
    tile = slice(own, rows)
    direct = own_share[tile] * gw[tile]
    gw[tile] = direct * (value_ref[tile] - wkv[tile])
    own_share[tile] = direct
    sent[3].start()
    sent[4].start()
    nothing = jnp.zeros((1, features), jnp.float32)
    after = back_token(
        (nothing, nothing, nothing + NEGATIVE),
        row(ext, own), row(wkv, own), row(top_log, own), marks_ref[own : own + 1, 0:1],
    )
    for c in range(CHUNKS - 1, -1, -1):
        for k in range(3):
            suffix_ref[k, c : c + 1] = after[k]
        if c > 0:
            old = aged(after, float(length), chunk_ref[c : c + 1, 0:1], rate)
            after = merge(tuple(item[c : c + 1] for item in heads), old)
    last = merge(first, aged(after, float(length - 1), marks_ref[0:1, 3:4], rate))
    summary_ref[...] = jnp.concatenate(last, axis=0)
    for k, (place, count) in enumerate(((at_out, per), (at_key, ff), (at_value, ff), (at_recept, per))):
        await_gradient(store, slot_grad, out_sem.at[k], place, count)
    for copy in sent:
        copy.wait()


def middle_pass(slots, x_rows, grad_rows, vectors, marks, chunk_marks, incoming, opened, pool):
    key, value, recept, states, prefix = opened
    rows, features = x_rows.shape
    own = rows - ROW_TILE
    full = jax.ShapeDtypeStruct((rows, features), jnp.float32)
    low = jax.ShapeDtypeStruct((rows, features), jnp.bfloat16)
    vmem = pl.BlockSpec(memory_space=pltpu.VMEM)
    anywhere = pl.BlockSpec(memory_space=pl.ANY)
    f32 = lambda *shape: pltpu.VMEM(shape, jnp.float32)
    b16 = lambda *shape: pltpu.VMEM(shape, jnp.bfloat16)
    return pl.pallas_call(
        middle_kernel,
        out_shape=(
            jax.ShapeDtypeStruct((3, CHUNKS, features), jnp.float32),
            jax.ShapeDtypeStruct((3, features), jnp.float32),
            jax.ShapeDtypeStruct((6, features), jnp.float32),
            jax.ShapeDtypeStruct((3, CHUNKS, features), jnp.float32),
            jax.ShapeDtypeStruct((own, features), jnp.bfloat16),
            full, full, full, low,
            jax.ShapeDtypeStruct(pool.shape, jnp.bfloat16),
        ),
        in_specs=[pl.BlockSpec(memory_space=pltpu.SMEM)] + [vmem] * 5 + [anywhere] * 7,
        out_specs=(vmem,) * 4 + (anywhere,) * 6,
        scratch_shapes=[
            b16(rows, features),
            b16(rows, features),
            f32(rows, features),
            f32(rows, features),
            f32(rows, features),
            b16(own, features),
            f32(rows, features),
            f32(rows, features),
            f32(rows, features),
            f32(rows, features),
            b16(rows, features),
            f32(own, features),
            f32(own, features),
            f32(own, features),
            b16(rows, features),
            f32(rows + 8, features),
            f32(rows, features),
            f32(rows, 1),
            b16(rows, features),
            b16(rows, features),
            f32(rows, FF),
            b16(rows, FF),
            f32(rows, features),
            f32(rows, features),
            b16(rows, features),
            b16(rows, features),
            b16(rows, FF),
            b16(rows, features),
            f32(rows, features),
            f32(features // LANES, own, LANES),
            b16((2 * EMBED_SIZE + 2 * FF) // BLOCK_ROWS, BLOCK_ROWS, features),
            pltpu.SemaphoreType.DMA((4,)),
            pltpu.SemaphoreType.DMA((4,)),
            pltpu.SemaphoreType.DMA((2,)),
            pltpu.SemaphoreType.DMA((6, PIECES + 1)),
            pltpu.SemaphoreType.DMA((5,)),
        ],
        compiler_params=pltpu.CompilerParams(vmem_limit_bytes=VMEM_BYTES),
        name="middle_pass",
    )(slots, vectors, marks, chunk_marks, incoming, prefix, x_rows, grad_rows, key, value, recept, states, pool)


def tail_shapes(shape):
    rows, features = shape
    own = rows - ROW_TILE
    f32 = lambda *dims: pltpu.VMEM(dims, jnp.float32)
    grads = [f32(rows, features)] * 3
    rest = [
        f32(rows + 8, features),
        f32(rows, features),
        f32(rows, 1),
        f32(rows, features),
        f32(features // LANES, own, LANES),
    ]
    return grads, rest


def tail_steps(x_ref, vec_ref, marks_ref, resid_ref, lows, weights, outs, ext, unit, inverse, carried, wide, input_ref, sums_ref):
    rows, features = x_ref.shape
    own = rows - ROW_TILE
    length = own // CHUNKS
    per = EMBED_SIZE // BLOCK_ROWS

    def back(m):
        def write(cols, piece):
            outs[m][:, cols] = piece

        times_weight_back(lows[m], weights, m * per, per, write)

    def norm(first, size):
        at = pl.ds(first, size)
        out, inv = unit_norm(x_ref[at].astype(jnp.float32))
        unit[at] = out
        inverse[at] = inv
        ext[pl.ds(pl.multiple_of(first + 8, 8), size)] = out * vec_ref[0:1] + vec_ref[1:2]

    def norms():
        for_rows(rows, norm)
        norm(own, ROW_TILE)
        shift_in(ext, own)

    mixes = tuple(vec_ref[k : k + 1] for k in (2, 3, 4))

    def carry_over(first, size):
        at = pl.ds(first, size)
        total = (1.0 - mixes[0]) * outs[0][at] + (1.0 - mixes[1]) * outs[1][at] + (1.0 - mixes[2]) * outs[2][at]
        carried[at] = marks_ref[at, 1:2] * total

    def carry_all():
        for_rows(rows, carry_over)
        carry_over(own, ROW_TILE)
        carried[own : own + 8] = jnp.concatenate([carried[1:8], carried[own : own + 1]], axis=0)

    def back_step(first, size, *sums):
        at = pl.ds(first, size)
        grads = (outs[0][at], outs[1][at], outs[2][at])
        grad = carried[pl.ds(pl.multiple_of(first + 8, 8), size)]
        for weight, piece in zip(mixes, grads):
            grad = grad + weight * piece
        scaled = grad * vec_ref[0:1]
        inner = (
            scaled
            - jnp.mean(scaled, axis=1, keepdims=True)
            - unit[at] * jnp.mean(scaled * unit[at], axis=1, keepdims=True)
        )
        out = resid_ref[at] + inner * inverse[at]
        for k in range(size // CHUNKS):
            put_step(wide, first // CHUNKS + k, length, out[CHUNKS * k : CHUNKS * (k + 1)])
        here, before = normed_pair(ext, marks_ref, first, size)
        spread = here - before
        return (sums[0] + fold(grad * unit[at]), sums[1] + fold(grad)) + tuple(
            s + fold(piece * spread) for s, piece in zip(sums[2:], grads)
        )

    def back_all():
        blank = jnp.zeros((CHUNKS, features), jnp.float32)
        sums = for_rows(rows, back_step, (blank,) * 5)
        for k in range(5):
            sums_ref[k : k + 1] = jnp.sum(sums[k], axis=0, keepdims=True)

    def emit(first, size):
        input_ref[pl.ds(first, size)] = take_rows(wide, pl.ds(first, size))

    return [
        functools.partial(back, 0), functools.partial(back, 1), functools.partial(back, 2),
        norms, carry_all, back_all, lambda: for_rows(rows, emit),
    ]


def tail_kernel(
    vec_ref, marks_ref, x_ref, resid_ref, key_grad, value_grad, recept_grad, weights, rows_ref,
    input_ref, sums_ref, grad_key_in, grad_value_in, grad_recept_in, ext, unit, inverse, carried, wide,
):
    sums_ref[...] = rows_ref[...]
    steps = tail_steps(
        x_ref, vec_ref, marks_ref, resid_ref, (key_grad, value_grad, recept_grad), weights,
        (grad_key_in, grad_value_in, grad_recept_in), ext, unit, inverse, carried, wide, input_ref, sums_ref,
    )
    for step in steps:
        step()


def tail_pass(rows, tail):
    x_rows = tail[2]
    own, features = x_rows.shape[0] - ROW_TILE, x_rows.shape[1]
    grads, rest = tail_shapes(x_rows.shape)
    vmem = pl.BlockSpec(memory_space=pltpu.VMEM)
    return pl.pallas_call(
        tail_kernel,
        out_shape=(jax.ShapeDtypeStruct((own, features), jnp.float32), jax.ShapeDtypeStruct(rows.shape, rows.dtype)),
        in_specs=[vmem] * 9,
        out_specs=(vmem, vmem),
        scratch_shapes=grads + rest,
        compiler_params=pltpu.CompilerParams(vmem_limit_bytes=VMEM_BYTES),
        name="tail_pass",
    )(*tail, rows)


def close_kernel(
    slot_ref, vec_ref, marks_ref, chunk_ref, incoming_ref, suffix_ref, sums_two_ref, fade_ref,
    key_hbm, value_hbm, in_key_hbm, in_value_hbm, in_recept_hbm, key_part_hbm, value_part_hbm, recept_hbm, grads_in,
    key_grad, value_grad, sums_ref, slot_grad,
    key_ref, value_ref, in_key, in_value, in_recept, key_wide, value_wide, recept_grad,
    store, out_sem, in_sem, piece_sem,
):
    rows, features = key_ref.shape
    own = rows - ROW_TILE
    length = own // CHUNKS
    per = EMBED_SIZE // BLOCK_ROWS
    early = [
        pltpu.make_async_copy(src, dst, in_sem.at[k])
        for k, (src, dst) in enumerate(
            ((in_recept_hbm, in_recept), (recept_hbm, recept_grad), (in_key_hbm, in_key), (in_value_hbm, in_value))
        )
    ]
    early[0].start()
    early[1].start()
    pairs = [(key_hbm, key_ref), (value_hbm, value_ref), (key_part_hbm, key_wide), (value_part_hbm, value_wide)]
    start_pieces(pairs, piece_sem, own)
    early[2].start()
    early[3].start()
    early[0].wait()
    early[1].wait()
    weight_gradient(in_recept, recept_grad, own, slot_ref, slot_grad, store, out_sem.at[2], 2 * per, 2 * per)
    rate = jnp.exp(vec_ref[5:6])
    incoming = tuple(incoming_ref[k : k + 1] for k in range(3))
    carry = merge(
        tuple(suffix_ref[k] for k in range(3)),
        aged(tuple(jnp.broadcast_to(v, (CHUNKS, features)) for v in incoming), chunk_ref[:, 5:6], chunk_ref[:, 4:5], rate),
    )
    fade = jnp.exp(carry[2] + fade_ref[2]) * (carry[0] * fade_ref[0] + carry[1] * fade_ref[1])
    sums_ref[0:5] = jnp.zeros((5, features), jnp.float32)
    sums_ref[5:6] = -rate * (sums_two_ref[4:5] + jnp.sum(fade, axis=0, keepdims=True))
    sums_ref[6:7] = sums_two_ref[5:6]
    sums_ref[7:] = sums_two_ref[0:4]

    def spread_back(at, state):
        value = value_ref[at]
        lift = jnp.exp(key_ref[at] + state[2])
        key_grad[at] = (key_wide[at] + lift * (state[0] * value + state[1])).astype(jnp.bfloat16)
        value_grad[at] = (value_wide[at] + lift * state[0]).astype(jnp.bfloat16)

    carry_wide = tuple(jnp.concatenate([item] * (STEP_TILE // CHUNKS), axis=0) for item in carry)
    ramp = lax.broadcasted_iota(jnp.int32, (STEP_TILE, 1), 0) // CHUNKS

    def token(i, c):
        at = rows_at(i, STEP_TILE)
        distance = (length - 1 - i * (STEP_TILE // CHUNKS) - ramp).astype(jnp.float32)
        spread_back(at, aged(carry_wide, distance, marks_ref[at, 3:4], rate))
        return c

    for p in range(PIECES):
        wait_piece(pairs, piece_sem, own, p)
        count = own // STEP_TILE
        lax.fori_loop(p * count // PIECES, (p + 1) * count // PIECES, token, 0)
    wait_piece(pairs, piece_sem, own, PIECES)
    halo = tuple(
        jnp.concatenate([incoming[k], jnp.zeros((ROW_TILE - 1, features), jnp.float32) + (NEGATIVE if k == 2 else 0.0)], axis=0)
        for k in range(3)
    )
    spread_back(slice(own, rows), halo)
    early[2].wait()
    early[3].wait()
    weight_gradient(in_key, key_grad, own, slot_ref, slot_grad, store, out_sem.at[0], 0, 0)
    weight_gradient(in_value, value_grad, own, slot_ref, slot_grad, store, out_sem.at[1], per, per)
    for m in range(3):
        await_gradient(store, slot_grad, out_sem.at[m], m * per, per)


def close_pass(slots, vectors, marks, chunk_marks, incoming, suffix, sums_two, fade, kept, slot_grad):
    rows, features = kept[0].shape
    vmem = pl.BlockSpec(memory_space=pltpu.VMEM)
    anywhere = pl.BlockSpec(memory_space=pl.ANY)
    low = jax.ShapeDtypeStruct((rows, features), jnp.bfloat16)
    operands = (slots, vectors, marks, chunk_marks, incoming, suffix, sums_two, fade) + kept + (slot_grad,)
    return pl.pallas_call(
        close_kernel,
        out_shape=(
            low,
            low,
            jax.ShapeDtypeStruct(vectors.shape, jnp.float32),
            jax.ShapeDtypeStruct(slot_grad.shape, jnp.bfloat16),
        ),
        in_specs=[pl.BlockSpec(memory_space=pltpu.SMEM)] + [vmem] * 7 + [anywhere] * (len(kept) + 1),
        out_specs=(vmem, vmem, vmem, anywhere),
        input_output_aliases={len(operands) - 1: 3},
        scratch_shapes=[pltpu.VMEM(k.shape, k.dtype) for k in kept] + [
            pltpu.VMEM((3 * EMBED_SIZE // BLOCK_ROWS, BLOCK_ROWS, features), jnp.bfloat16),
            pltpu.SemaphoreType.DMA((3,)),
            pltpu.SemaphoreType.DMA((4,)),
            pltpu.SemaphoreType.DMA((4, PIECES + 1)),
        ],
        compiler_params=pltpu.CompilerParams(vmem_limit_bytes=VMEM_BYTES),
        name="close_pass",
    )(*operands)


def chain_kernel(forward, own_ref, vec_ref, link_ref, out_ref, plane, planes, joint, send_sem, recv_sem, far_send, far_recv):
    me, _, _, _, z = grid_place()
    place = lax.rem(me, PLANE)
    base = me - place
    at = 0 if forward else 2
    before = z if forward else PLANES - 1 - z
    step = PLANE if forward else -PLANE
    planes[...] = jnp.zeros_like(planes)
    bar = pltpu.get_barrier_semaphore()
    for o in range(1, PLANE):
        peer = base + lax.rem(place + o, PLANE)
        pl.semaphore_signal(bar, inc=1, device_id=(peer,), device_id_type=MESH)
    for o in range(1, PLANES):
        @pl.when(o <= before)
        def _():
            pl.semaphore_signal(bar, inc=1, device_id=(me - step * o,), device_id_type=MESH)
    plane[pl.ds(place, 1)] = own_ref[...][None]
    rate = jnp.exp(vec_ref[5:6])
    pl.semaphore_wait(bar, PLANE - 1 + PLANES - 1 - before)

    def near_copy(o, source, peer):
        return pltpu.make_async_remote_copy(
            src_ref=own_ref, dst_ref=plane.at[source], send_sem=send_sem.at[o], recv_sem=recv_sem.at[o],
            device_id=(peer,), device_id_type=MESH,
        )

    def far_copy(o, source, peer):
        return pltpu.make_async_remote_copy(
            src_ref=joint, dst_ref=planes.at[source], send_sem=far_send.at[o], recv_sem=far_recv.at[o],
            device_id=(peer,), device_id_type=MESH,
        )

    for o in range(PLANE - 1, 0, -1):
        near_copy(o, place, base + lax.rem(place + o, PLANE)).start()
    for o in range(1, PLANE):
        source = lax.rem(place - o + PLANE, PLANE)
        near_copy(o, source, base + source).wait_recv()

    def gather_states(ref, first, count):
        valid = link_ref[first : first + count, at : at + 1]
        logs = jnp.where(valid > 0.5, ref[:, 2] - link_ref[first : first + count, at + 1 : at + 2] * rate, NEGATIVE)
        top = jnp.max(logs, axis=0, keepdims=True)
        weight = jnp.exp(logs - top)
        return (
            jnp.sum(weight * ref[:, 0], axis=0, keepdims=True),
            jnp.sum(weight * ref[:, 1], axis=0, keepdims=True),
            top,
        )

    joint[...] = jnp.concatenate(gather_states(plane, PLANE, PLANE), axis=0)
    for o in range(PLANES - 1, 0, -1):
        @pl.when(o < PLANES - before)
        def _():
            far_copy(o, z, me + step * o).start()
    near = gather_states(plane, 0, PLANE)
    for o in range(1, PLANES):
        @pl.when(o <= before)
        def _():
            source = z - o if forward else z + o
            far_copy(o, source, me - step * o).wait_recv()
    last = 2 * PLANE + PLANES
    old = gather_states(planes, 2 * PLANE, PLANES)
    old = aged(old, link_ref[last : last + 1, at + 1 : at + 2], link_ref[last : last + 1, at : at + 1], rate)
    out_ref[...] = jnp.concatenate(merge(near, old), axis=0)
    for o in range(1, PLANE):
        near_copy(o, place, base + lax.rem(place + o, PLANE)).wait_send()
    for o in range(1, PLANES):
        @pl.when(o < PLANES - before)
        def _():
            far_copy(o, z, me + step * o).wait_send()


def chain_state(rows, vectors, links, forward, cid):
    devices = lax.axis_size("seq")
    if devices != GRID_DEVICES:
        every = lax.all_gather(rows[None], "seq", axis=0, tiled=True)
        at = 0 if forward else 2
        aged_logs = every[:, 2] - links[:, at + 1 : at + 2] * jnp.exp(vectors[5])
        logs = jnp.where(links[:, at : at + 1] > 0.5, aged_logs, NEGATIVE)
        top = jnp.max(logs, axis=0)
        weight = jnp.exp(logs - top)
        return jnp.stack([jnp.sum(weight * every[:, 0], axis=0), jnp.sum(weight * every[:, 1], axis=0), top])
    vmem = pl.BlockSpec(memory_space=pltpu.VMEM)
    return pl.pallas_call(
        functools.partial(chain_kernel, forward),
        out_shape=jax.ShapeDtypeStruct(rows.shape, jnp.float32),
        in_specs=[vmem] * 3,
        out_specs=vmem,
        scratch_shapes=[
            pltpu.VMEM((PLANE,) + rows.shape, jnp.float32),
            pltpu.VMEM((PLANES,) + rows.shape, jnp.float32),
            pltpu.VMEM(rows.shape, jnp.float32),
            pltpu.SemaphoreType.DMA((PLANE,)),
            pltpu.SemaphoreType.DMA((PLANE,)),
            pltpu.SemaphoreType.DMA((PLANES,)),
            pltpu.SemaphoreType.DMA((PLANES,)),
        ],
        compiler_params=pltpu.CompilerParams(collective_id=cid, has_side_effects=True),
        name="chain_forward" if forward else "chain_backward",
    )(rows, vectors, links)


def body(
    tokens_in,
    cotangent,
    pad_mask,
    doc_lengths,
    masters,
    moment_one,
    moment_two,
    block_slot,
    vectors,
    vector_one,
    vector_two,
):
    tokens, features = tokens_in.shape
    devices = lax.axis_size("seq")
    device_place = lax.axis_index("seq")
    pad_rows = pad_mask.reshape(-1, LANES)
    if devices == GRID_DEVICES:
        gathered, *prepared = gather_blocks(masters, doc_lengths, tokens_in, cotangent, pad_rows, vectors)
        gathered = gathered.reshape(-1, BLOCK_ROWS, features)
    else:
        gathered = lax.all_gather(masters.astype(jnp.bfloat16), "seq", axis=0, tiled=True)
        head_grad = cotangent[:ROW_TILE] * pad_mask[:ROW_TILE].astype(cotangent.dtype)[:, None]
        halo = [
            shifted(tokens_in[:ROW_TILE], "seq", -1),
            shifted(head_grad, "seq", -1),
            shifted(tokens_in[tokens - ROW_TILE :], "seq", 1),
        ]
        prepared = prepare_pass(devices, doc_lengths, tokens_in, cotangent, pad_rows, halo, vectors)
    x_rows, grad_rows, marks, chunk_marks, links, *lows = prepared
    lows = tuple(lows)
    prefix, summary, key, value, recept, states, weights = open_pass(
        block_slot, vectors, marks, chunk_marks, lows, gathered
    )
    incoming = chain_state(summary, vectors, links, True, 3)
    (
        suffix, back_summary, sums_two, fade,
        layer_out, resid_grad, key_part, value_part, recept_grad, slot_grad,
    ) = middle_pass(
        block_slot, x_rows, grad_rows, vectors, marks, chunk_marks, incoming,
        (key, value, recept, states, prefix), gathered,
    )
    back_incoming = chain_state(back_summary, vectors, links, False, 4)
    key_grad, value_grad, stacked, slot_grad = close_pass(
        block_slot, vectors, marks, chunk_marks, back_incoming, suffix, sums_two, fade,
        (key, value) + lows + (key_part, value_part, recept_grad), slot_grad,
    )
    tail = (vectors, marks, x_rows, resid_grad, key_grad, value_grad, recept_grad, weights)
    own_slots = device_place * masters.shape[0] + jnp.arange(masters.shape[0], dtype=jnp.int32)
    named = jnp.any(own_slots[:, None] == block_slot[None, :], axis=1)
    if devices == GRID_DEVICES:
        owner_grad, vector_grad, input_grad = scatter_blocks(
            slot_grad.reshape((devices,) + masters.shape), stacked, tail
        )
        owner_grad = owner_grad.astype(jnp.float32)
    else:
        input_grad, stacked = tail_pass(stacked, tail)
        owner_grad = lax.psum_scatter(
            slot_grad.astype(jnp.float32), "seq", scatter_dimension=0, tiled=True
        )
        vector_grad = lax.psum(stacked, "seq")
    owner_grad = jnp.where(named[:, None, None], owner_grad, 0.0)
    new_one, new_two, new_master = adam_update(
        masters, moment_one, moment_two, owner_grad, MATRIX_RATE, WEIGHT_DECAY
    )
    vector_rates = jnp.array(VECTOR_RATE, jnp.float32)[:, None]
    vector_first, vector_second, vector_next = adam_update(
        vectors, vector_one, vector_two, vector_grad, vector_rates, 0.0
    )
    return (
        layer_out,
        input_grad,
        new_one,
        new_two,
        new_master,
        vector_first,
        vector_second,
        vector_next,
    )


def solution(mesh):
    placed = (
        P("seq", None),
        P("seq", None),
        P("seq"),
        P(),
        P("seq", None, None),
        P("seq", None, None),
        P("seq", None, None),
        P(),
        P(),
        P(),
        P(),
    )
    return jax.shard_map(
        body,
        mesh=mesh,
        in_specs=placed,
        out_specs=(
            P("seq", None),
            P("seq", None),
            P("seq", None, None),
            P("seq", None, None),
            P("seq", None, None),
            P(),
            P(),
            P(),
        ),
        check_vma=False,
    )
```

```python
import functools

import jax
import jax.numpy as jnp
from jax import lax
from jax.experimental import pallas as pl
from jax.experimental.pallas import tpu as pltpu
from jax.sharding import PartitionSpec as P

EMBED_SIZE = 1024
FF = 4096
BLOCK_ROWS = 32
ROWS_ALL = 13312
BLOCKS = 416
STEP = 10
GRID_DEVICES = 32
MESH = pl.DeviceIdType.MESH


NEGATIVE = -1e30
NORM_EPS = 1e-05
BETA_ONE = 0.9
BETA_TWO = 0.999
ADAM_EPS = 1e-08
MATRIX_RATE = 0.05
WEIGHT_DECAY = 0.01
VECTOR_RATE = (0.25, 0.25, 0.25, 0.25, 0.25, 2.0, 0.25, 0.25, 0.25, 0.25, 0.25)


def shifted(block, axis, distance):
    devices = range(lax.axis_size(axis))
    route = [(i - distance, i) for i in devices if i - distance in devices]
    return lax.ppermute(block, axis, route)


def product_back(left_side, right_side):
    return lax.dot_general(
        left_side, right_side, (((1,), (1,)), ((), ())), preferred_element_type=jnp.float32
    )


def product_left(left_side, right_side):
    return lax.dot_general(
        left_side, right_side, (((0,), (0,)), ((), ())), preferred_element_type=jnp.float32
    )


def adam_update(weight, first_moment, second_moment, gradient, step_rate, feature_fade_speed):
    first_moment = BETA_ONE * first_moment + (1.0 - BETA_ONE) * gradient
    second_moment = BETA_TWO * second_moment + (1.0 - BETA_TWO) * gradient * gradient
    first_fixed = first_moment / (1.0 - BETA_ONE**STEP)
    second_fixed = second_moment / (1.0 - BETA_TWO**STEP)
    weight = weight - step_rate * (
        first_fixed / (jnp.sqrt(second_fixed) + ADAM_EPS) + feature_fade_speed * weight
    )
    return (first_moment, second_moment, weight)


def grid_place():
    me = lax.axis_index("seq")
    return me, lax.rem(me, 2), lax.rem(me // 2, 2), lax.rem(me // 4, 2), me // 8

def spans(slots):
    side = 4 * slots // 15
    cuts = [0, side, 2 * side, slots]
    return [(cuts[i], cuts[i + 1] - cuts[i]) for i in range(3)]

def gather_kernel(
    slots, doc_ref, master_ref, tokens_ref, cot_ref, pad_ref, vec_ref,
    out_ref, x_ref, grad_ref, marks_ref, chunk_ref, link_ref, in_key, in_value, in_recept,
    column, ext, wide, wide_grad, own_ref, head_grad, after_ref, after_grad_ref, before_ref,
    *scratch,
):
    send_sem, recv_sem, sib_send, sib_recv, own_sem, halo_send, halo_recv = scratch
    me, core, x, y, z = grid_place()
    sib = me + 1 - 2 * core
    x_peer = me + 2 - 4 * x
    y_peer = me + 4 - 8 * y
    up = me + 8
    down = me - 8
    bar = pltpu.get_barrier_semaphore()
    pl.semaphore_signal(bar, inc=1, device_id=(sib,), device_id_type=MESH)
    pl.semaphore_signal(bar, inc=1, device_id=(x_peer,), device_id_type=MESH)
    pl.semaphore_signal(bar, inc=1, device_id=(y_peer,), device_id_type=MESH)
    @pl.when(z < 3)
    def _():
        pl.semaphore_signal(bar, inc=1, device_id=(up,), device_id_type=MESH)
    @pl.when(z > 0)
    def _():
        pl.semaphore_signal(bar, inc=1, device_id=(down,), device_id_type=MESH)
    more, less = me < GRID_DEVICES - 1, me > 0

    @pl.when(more)
    def _():
        pl.semaphore_signal(bar, inc=1, device_id=(me + 1,), device_id_type=MESH)

    @pl.when(less)
    def _():
        pl.semaphore_signal(bar, inc=1, device_id=(me - 1,), device_id_type=MESH)

    def lower(s, carry):
        own_ref[s] = master_ref[s].astype(own_ref.dtype)
        return carry

    lax.fori_loop(0, slots, lower, 0)
    mask_column(pad_ref, column)
    head_grad[...] = (cot_ref[0:ROW_TILE].astype(jnp.float32) * column[0:ROW_TILE]).astype(jnp.bfloat16)
    halos = jnp.where(more, 1, 0) + jnp.where(less, 1, 0)
    pl.semaphore_wait(bar, 4 + jnp.where((z > 0) & (z < 3), 1, 0) + halos)
    tokens = tokens_ref.shape[0]

    def halo_copy(k):
        src, dst, peer = (
            (tokens_ref.at[pl.ds(0, ROW_TILE)], after_ref, me - 1),
            (head_grad, after_grad_ref, me - 1),
            (tokens_ref.at[pl.ds(tokens - ROW_TILE, ROW_TILE)], before_ref, me + 1),
        )[k]
        return pltpu.make_async_remote_copy(src_ref=src, dst_ref=dst, send_sem=halo_send.at[k],
            recv_sem=halo_recv.at[k], device_id=(peer,), device_id_type=MESH)
    span = spans(slots)
    targets = (x_peer, y_peer, up, down)

    def chip(cx, cy, cz):
        return (cz * 2 + cy) * 2 + cx

    def view(cx, cy, cz, color, c=None):
        dev = chip(cx, cy, cz) * 2 + (core if c is None else c)
        lo, n = span[color]
        return out_ref.at[dev, pl.ds(lo, n)]

    def send(cx, cy, cz, color, way, own=False):
        lo, n = span[color]
        src = own_ref.at[pl.ds(lo, n)] if own else view(cx, cy, cz, color)
        idx = chip(cx, cy, cz)
        return pltpu.make_async_remote_copy(src_ref=src, dst_ref=view(cx, cy, cz, color),
            send_sem=send_sem.at[idx, color, way], recv_sem=recv_sem.at[idx, color],
            device_id=(targets[way],), device_id_type=MESH)

    def send_sib(cx, cy, cz, color, own=False):
        lo, n = span[color]
        src = own_ref.at[pl.ds(lo, n)] if own else view(cx, cy, cz, color)
        idx = chip(cx, cy, cz)
        return pltpu.make_async_remote_copy(src_ref=src, dst_ref=view(cx, cy, cz, color),
            send_sem=sib_send.at[idx, color], recv_sem=sib_recv.at[idx, color],
            device_id=(sib,), device_id_type=MESH)

    x2, y2 = 1 - x, 1 - y
    pending = []

    def go(copy, cond=None):
        if cond is None:
            copy.start()
        else:
            @pl.when(cond)
            def _():
                copy.start()
        pending.append((copy, cond))

    zup, zdown = z < 3, z > 0
    own_copies = []
    for color in range(3):
        lo, n = span[color]
        cp = pltpu.make_async_copy(own_ref.at[pl.ds(lo, n)], view(x, y, z, color), own_sem.at[color])
        cp.start()
        own_copies.append(cp)
    order = {0: (0, 2, 1), 1: (1, 2, 0)}
    for color in (0, 1, 2):
        go(send(x, y, z, color, 2, True), zup)
        go(send(x, y, z, color, 3, True), zdown)
    for color, way in ((0, 0), (1, 1), (2, 0), (2, 1), (0, 1), (1, 0)):
        go(send(x, y, z, color, way, True))
    for color in range(3):
        go(send_sib(x, y, z, color, True))

    @pl.when(less)
    def _():
        for k in (0, 1):
            halo_copy(k).start()

    @pl.when(more)
    def _():
        halo_copy(2).start()

    marks = (marks_ref, chunk_ref, link_ref)
    prepare_own(
        GRID_DEVICES, doc_ref, tokens_ref, cot_ref, column, vec_ref, x_ref, grad_ref, marks, ext, wide, wide_grad
    )

    def arrive(cx, cy, cz, color):
        send(cx, cy, cz, color, 0).wait_recv()

    def sibling(cx, cy, cz, color):
        go(send_sib(cx, cy, cz, color))

    is0, is1 = core == 0, core == 1
    px = jnp.where(is0, x2, x)
    py = jnp.where(is0, y, y2)
    qx = jnp.where(is0, x, x2)
    qy = jnp.where(is0, y2, y)
    first = lambda cx, cy, cz: (go(send(cx, cy, cz, 2, 0), is0), go(send(cx, cy, cz, 2, 1), is1))
    last = lambda cx, cy, cz: (go(send(cx, cy, cz, 2, 1), is0), go(send(cx, cy, cz, 2, 0), is1))

    arrive(x2, y, z, 0)
    go(send(x2, y, z, 0, 2), zup)
    go(send(x2, y, z, 0, 3), zdown)
    go(send(x2, y, z, 0, 1))
    sibling(x2, y, z, 0)
    arrive(x, y2, z, 1)
    go(send(x, y2, z, 1, 2), zup)
    go(send(x, y2, z, 1, 3), zdown)
    go(send(x, y2, z, 1, 0))
    sibling(x, y2, z, 1)
    arrive(px, py, z, 2)
    last(px, py, z)
    sibling(px, py, z, 2)

    def wait_halo():
        @pl.when(less)
        def _():
            for k in (0, 1):
                halo_copy(k).wait_send()
            halo_copy(2).wait_recv()

        @pl.when(more)
        def _():
            halo_copy(2).wait_send()
            for k in (0, 1):
                halo_copy(k).wait_recv()

    for dist in (1, 2, 3):
        sides = []
        for sign, fwd, guard_f in ((1, 3, zdown), (-1, 2, zup)):
            q = z + sign * dist
            have = (q >= 0) & (q < 4)
            sides.append((q, fwd, have, guard_f))
        for which in ("c", "a", "b", "a2", "b2"):
            for q, fwd, have, gf in sides:
                @pl.when(have)
                def _(q=q, fwd=fwd, gf=gf, which=which):
                    if which == "c":
                        arrive(x, y, q, 2)
                        cp = send(x, y, q, 2, fwd)
                        pl.when(gf)(lambda: cp.start())
                        for w in (0, 1):
                            send(x, y, q, 2, w).start()
                        send_sib(x, y, q, 2).start()
                    else:
                        color = 0 if which[0] == "a" else 1
                        cx, cy = {"a": (x, y), "b": (x, y), "a2": (x2, y), "b2": (x, y2)}[which]
                        arrive(cx, cy, q, color)
                        cp = send(cx, cy, q, color, fwd)
                        pl.when(gf)(lambda: cp.start())
                        send(cx, cy, q, color, 1 if color == 0 else 0).start()
                        send_sib(cx, cy, q, color).start()
        for q, fwd, have, gf in sides:
            @pl.when(have)
            def _(q=q):
                arrive(px, py, q, 2)
                pl.when(is0)(lambda: send(px, py, q, 2, 1).start())
                pl.when(is1)(lambda: send(px, py, q, 2, 0).start())
                send_sib(px, py, q, 2).start()
        if dist == 1:
            tail_list = [(z, None)]
        else:
            tail_list = []
        if dist == 1:
            wait_halo()
            lows = (in_key, in_value, in_recept)
            prepare_halo(
                GRID_DEVICES, after_ref, after_grad_ref, before_ref, vec_ref, x_ref, grad_ref, marks_ref, lows, ext
            )
        def terminal(q):
            for cx, cy, color in ((x, y2, 0), (x2, y2, 0), (x2, y, 1), (x2, y2, 1), (qx, qy, 2), (x2, y2, 2)):
                arrive(cx, cy, q, color)
                send_sib(cx, cy, q, color).start()
        if dist == 1:
            terminal(z)
        else:
            for sign in (1, -1):
                q = z + sign * (dist - 1)
                pl.when((q >= 0) & (q < 4))(lambda q=q: terminal(q))
        if dist == 3:
            for sign in (1, -1):
                q = z + sign * 3
                pl.when((q >= 0) & (q < 4))(lambda q=q: terminal(q))
    for cp in own_copies:
        cp.wait()
    for color in range(3):
        pl.when(zup)(lambda color=color: send(x, y, z, color, 2).wait_send())
        pl.when(zdown)(lambda color=color: send(x, y, z, color, 3).wait_send())
        for w in (0, 1):
            send(x, y, z, color, w).wait_send()
    for cx, cy, color, w in ((x2, y, 0, 1), (x, y2, 1, 0)):
        pl.when(zup)(lambda: send(cx, cy, z, color, 2).wait_send())
        pl.when(zdown)(lambda: send(cx, cy, z, color, 3).wait_send())
        send(cx, cy, z, color, w).wait_send()
    pl.when(is0)(lambda: send(px, py, z, 2, 1).wait_send())
    pl.when(is1)(lambda: send(px, py, z, 2, 0).wait_send())
    for dist in (1, 2, 3):
        for sign, fwd, gf in ((1, 3, zdown), (-1, 2, zup)):
            q = z + sign * dist
            @pl.when((q >= 0) & (q < 4))
            def _(q=q, fwd=fwd, gf=gf):
                for cx, cy, color in ((x, y, 2), (x, y, 0), (x, y, 1), (x2, y, 0), (x, y2, 1)):
                    pl.when(gf)(lambda: send(cx, cy, q, color, fwd).wait_send())
                    ways = (0, 1) if color == 2 else ((1,) if color == 0 else (0,))
                    for w in ways:
                        send(cx, cy, q, color, w).wait_send()
                pl.when(is0)(lambda: send(px, py, q, 2, 1).wait_send())
                pl.when(is1)(lambda: send(px, py, q, 2, 0).wait_send())
    for cz in range(4):
        for cy in range(2):
            for cx in range(2):
                for color in range(3):
                    cp = send_sib(cx, cy, cz, color)
                    cp.wait_send()
                    cp.wait_recv()

def gather_blocks(masters, doc_lengths, tokens_in, cotangent, pad_rows, vectors, cid=1):
    slots = masters.shape[0]
    shapes, scratch = prepared_shapes(GRID_DEVICES, *tokens_in.shape)
    anywhere = pl.BlockSpec(memory_space=pl.ANY)
    vmem = pl.BlockSpec(memory_space=pltpu.VMEM)
    halo = pltpu.VMEM((ROW_TILE,) + tokens_in.shape[1:], jnp.bfloat16)
    return pl.pallas_call(
        functools.partial(gather_kernel, slots),
        out_shape=(jax.ShapeDtypeStruct((GRID_DEVICES,) + masters.shape, jnp.bfloat16),) + shapes,
        in_specs=[pl.BlockSpec(memory_space=pltpu.SMEM)] + [vmem] * 5,
        out_specs=(anywhere,) + (vmem,) * len(shapes),
        scratch_shapes=scratch + [
            pltpu.VMEM(masters.shape, jnp.bfloat16),
            halo, halo, halo, halo,
            pltpu.SemaphoreType.DMA((16, 3, 4)),
            pltpu.SemaphoreType.DMA((16, 3)),
            pltpu.SemaphoreType.DMA((16, 3)),
            pltpu.SemaphoreType.DMA((16, 3)),
            pltpu.SemaphoreType.DMA((3,)),
            pltpu.SemaphoreType.DMA((3,)),
            pltpu.SemaphoreType.DMA((3,)),
        ],
        compiler_params=pltpu.CompilerParams(collective_id=cid, has_side_effects=True, vmem_limit_bytes=VMEM_BYTES),
        name="gather_blocks",
    )(doc_lengths, masters, tokens_in, cotangent, pad_rows, vectors)


def scatter_spans(slots):
    side = 4 * slots // 15
    cuts = [0, side, 2 * side, 2 * side + (slots - 2 * side + 1) // 2, slots]
    return [(cuts[i], cuts[i + 1] - cuts[i]) for i in range(4)]


def scatter_kernel(
    slots, part_ref, rows_ref, vec_ref, marks_ref, x_hbm, resid_hbm, key_hbm, value_hbm, recept_hbm, weights_hbm,
    out_ref, total_ref, input_hbm,
    acc, ring, ub, uc, ud, va, vc, vd, zs, zc, zd, sums,
    x_ref, resid_ref, key_grad, value_grad, recept_grad, weights, grad_key_in, grad_value_in, grad_recept_in,
    ext, unit, inverse, carried, wide, input_ref,
    load_sem, sib_send, sib_recv, send_sem, usem, vsem, zsem, row_send, row_recv, tail_sem, input_sem,
):
    me, core, x, y, z = grid_place()
    sibling = me + 1 - 2 * core
    x_peer = me + 2 - 4 * x
    y_peer = me + 4 - 8 * y
    up, down = me + 8, me - 8
    zup, zdown = z < 3, z > 0
    bar = pltpu.get_barrier_semaphore()
    for peer in (sibling, x_peer, y_peer):
        pl.semaphore_signal(bar, inc=1, device_id=(peer,), device_id_type=MESH)
    @pl.when(zup)
    def _():
        pl.semaphore_signal(bar, inc=1, device_id=(up,), device_id_type=MESH)
    @pl.when(zdown)
    def _():
        pl.semaphore_signal(bar, inc=1, device_id=(down,), device_id_type=MESH)
    far = me + 16 - 32 * (z // 2)
    pl.semaphore_signal(bar, inc=1, device_id=(far,), device_id_type=MESH)
    row_peers = (sibling, x_peer, y_peer, me + 8 - 16 * lax.rem(z, 2), far)
    tail_loads = [
        pltpu.make_async_copy(src, dst, tail_sem.at[k])
        for k, (src, dst) in enumerate(
            (
                (key_hbm, key_grad), (value_hbm, value_grad), (recept_hbm, recept_grad),
                (x_hbm, x_ref), (resid_hbm, resid_ref), (weights_hbm, weights),
            )
        )
    ]
    span = scatter_spans(slots)
    u, v = jnp.where(core == 0, x, y), jnp.where(core == 0, y, x)
    u_peer, v_peer = jnp.where(core == 0, x_peer, y_peer), jnp.where(core == 0, y_peer, x_peer)
    u2, v2 = 1 - u, 1 - v

    def row_copy(k):
        return pltpu.make_async_remote_copy(src_ref=sums.at[2 * k], dst_ref=sums.at[2 * k + 1],
            send_sem=row_send.at[k], recv_sem=row_recv.at[k], device_id=(row_peers[k],), device_id_type=MESH)

    def row_step(k):
        row_copy(k).wait()
        sums[2 * k + 2] = sums[2 * k] + sums[2 * k + 1]
        if k < 4:
            row_copy(k + 1).start()

    def load(i, q):
        chip = 4 * q + plane_order()[i]
        return pltpu.make_async_copy(part_ref.at[2 * chip + core], ring.at[i], load_sem.at[i])

    first_level = jnp.where(z >= 2, 0, 3)

    def next_level(q):
        inner = jnp.where(q == 3, jnp.where(z == 1, 2, 1), jnp.where(q == 0, jnp.where(z == 1, 1, 3), jnp.where(z == 1, 0, 2)))
        return jnp.where(z == 0, q - 1, jnp.where(z == 3, q + 1, inner))

    def give(chip):
        return pltpu.make_async_remote_copy(src_ref=part_ref.at[2 * chip + 1 - core], dst_ref=acc.at[chip],
            send_sem=sib_send.at[chip], recv_sem=sib_recv.at[chip], device_id=(sibling,), device_id_type=MESH)

    levels = []
    for dist in (3, 2, 1):
        for sign in (1, -1):
            q = z + sign * dist
            levels.append((dist, sign, q, (q >= 0) & (q < 4)))

    def run(dist, work):
        for d, sign, q, have in levels:
            if d == dist:
                pl.when(have)(functools.partial(work, q))

    def run_signed(dist, work):
        for d, sign, q, have in levels:
            if d == dist:
                pl.when(have)(functools.partial(work, q, sign, dist))

    def chip_of(cu, cv, cz):
        return cz * 4 + jnp.where(core == 0, cv * 2 + cu, cu * 2 + cv)

    def plane_order():
        return (chip_of(u2, v2, 0), chip_of(u2, v, 0), chip_of(u, v2, 0), chip_of(u, v, 0))

    def sibling_order():
        return tuple(plane_order()[i] for i in (0, 2, 1, 3))

    for i in range(4):
        load(i, first_level).start()
    for copy in tail_loads:
        copy.start()
    pl.semaphore_wait(bar, 5 + jnp.where(zup & zdown, 1, 0))
    for i in range(2):
        give(4 * first_level + sibling_order()[i]).start()

    def ready(i, q):
        chip = 4 * q + plane_order()[i]
        load(i, q).wait()
        give(chip).wait_recv()

        def step(s, carry):
            total = acc[chip, s].astype(jnp.float32) + ring[i, s].astype(jnp.float32)
            acc[chip, s] = total.astype(acc.dtype)
            return carry

        lax.fori_loop(0, slots, step, 0)

        if i < 2:
            @pl.when(q == first_level)
            def _():
                give(4 * q + sibling_order()[i + 2]).start()

        @pl.when(q != z)
        def _():
            load(i, next_level(q)).start()
            give(4 * next_level(q) + sibling_order()[i]).start()

    def out_copy(cu, cv, cz, color, target, place):
        lo, n = span[color]
        chip = chip_of(cu, cv, cz)
        buf, index, sem, flag = place
        return pltpu.make_async_remote_copy(src_ref=acc.at[chip, pl.ds(lo, n)], dst_ref=buf.at[index],
            send_sem=send_sem.at[chip, color], recv_sem=sem.at[flag], device_id=(target,), device_id_type=MESH)

    def arrived(place, color):
        lo, n = span[color]
        buf, index, sem, flag = place
        pltpu.make_async_remote_copy(src_ref=acc.at[0, pl.ds(lo, n)], dst_ref=buf.at[index],
            send_sem=send_sem.at[0, color], recv_sem=sem.at[flag], device_id=(sibling,), device_id_type=MESH).wait_recv()

    def add(cu, cv, cz, color, pieces):
        lo, n = span[color]
        chip = chip_of(cu, cv, cz)
        for place in pieces:
            arrived(place, color)

        def step(s, carry):
            total = acc[chip, lo + s].astype(jnp.float32)
            for buf, index, _, _ in pieces:
                total = total + buf[index, s].astype(jnp.float32)
            acc[chip, lo + s] = total.astype(acc.dtype)
            return carry

        lax.fori_loop(0, n, step, 0)

    def UB(q, i): return (ub, 2 * q + i, usem, 2 * q + i)
    def UD(q, i): return (ud, 2 * q + i, usem, 9 + 2 * q + i)
    def UC(q): return (uc, q, usem, 17 + q)
    def VA(q, i): return (va, 2 * q + i, vsem, 2 * q + i)
    def VC(q, i): return (vc, 2 * q + i, vsem, 9 + 2 * q + i)
    def VD(q): return (vd, q, vsem, 17 + q)
    def Z(q, k): return ((zc, zd, zs)[min(k, 2)], q if k < 2 else 4 * q + k - 2, zsem, 6 * q + k)

    def send_u(q, color, i):
        out_copy(u2, (v, v2)[i], q, color, u_peer, UB(q, i) if color == 1 else UD(q, i)).start()

    def send_v(q, color, i):
        out_copy((u, u2)[i], v2, q, color, v_peer, VA(q, i) if color == 0 else VC(q, i)).start()

    def term_a(q):
        ready(0, q)
        send_u(q, 1, 1)
        send_v(q, 0, 1)

    def term_c(q):
        send_v(q, 2, 1)
        send_u(q, 3, 1)

    def term_b(q):
        ready(1, q)
        send_u(q, 1, 0)
        ready(2, q)
        send_v(q, 0, 0)

    def term_d(q):
        send_u(q, 3, 0)
        send_v(q, 2, 0)
        ready(3, q)

    def plane_two(q):
        add(u2, v, q, 2, [VC(q, 1)])
        out_copy(u2, v, q, 2, u_peer, UC(q)).start()
        add(u, v2, q, 3, [UD(q, 1)])
        out_copy(u, v2, q, 3, v_peer, VD(q)).start()

    def column(part, q, sign, dist):
        target = up if sign == 1 else down
        more = zdown if sign == 1 else zup
        level = 4 if (dist == 1 and sign == 1) else q
        kinds = (
            (0, u, v, 2, [UC(q), VC(q, 0)]),
            (1, u, v, 3, [VD(q), UD(q, 0)]),
            (2, u, v, 0, [VA(q, 0)]),
            (3, u, v, 1, [UB(q, 0)]),
            (4, u2, v, 0, [VA(q, 1)]),
            (5, u, v2, 1, [UB(q, 1)]),
        )
        for k, cu, cv, color, pieces in ((kinds[5], kinds[4], kinds[3], kinds[2]), (kinds[0], kinds[1]), (kinds[5], kinds[4]), (kinds[3], kinds[2]))[part]:
            @pl.when(more)
            def _():
                add(cu, cv, q, color, pieces + [Z(q, k)])

            @pl.when(jnp.logical_not(more))
            def _():
                add(cu, cv, q, color, pieces)

            out_copy(cu, cv, q, color, target, Z(level, k)).start()

    planes = functools.partial(column, 0)
    last = functools.partial(column, 1)
    def begin_tail():
        for copy in tail_loads:
            copy.wait()
        sums[0] = rows_ref[...]

    tail = tail_steps(
        x_ref, vec_ref, marks_ref, resid_ref, (key_grad, value_grad, recept_grad), weights,
        (grad_key_in, grad_value_in, grad_recept_in), ext, unit, inverse, carried, wide, input_ref, sums.at[0],
    )
    send_input = pltpu.make_async_copy(input_ref, input_hbm, input_sem)
    run(3, term_a)
    run(3, term_c)
    run(3, term_b)
    run(3, term_d)
    begin_tail()
    tail[0]()
    run_signed(3, functools.partial(column, 2))
    run(2, term_a)
    run_signed(3, functools.partial(column, 3))
    tail[1]()
    run(3, plane_two)
    run(2, term_c)
    run_signed(3, last)
    tail[2]()
    run(2, term_b)
    run(2, term_d)
    tail[3]()
    run_signed(2, functools.partial(column, 2))
    run(1, term_a)
    run_signed(2, functools.partial(column, 3))
    tail[4]()
    run(2, plane_two)
    run(1, term_c)
    run_signed(2, last)
    tail[5]()
    run(1, term_b)
    run(1, term_d)
    row_copy(0).start()
    run_signed(1, functools.partial(column, 2))
    term_a(z)
    row_step(0)
    run_signed(1, functools.partial(column, 3))
    run(1, plane_two)
    term_c(z)
    row_step(1)
    run_signed(1, last)
    term_b(z)
    term_d(z)
    row_step(2)
    tail[6]()
    send_input.start()
    plane_two(z)
    row_step(3)

    def own(k, cu, cv, color, pieces):
        @pl.when(zup & zdown)
        def _():
            add(cu, cv, z, color, pieces + [Z(z, k), Z(4, k)])

        @pl.when(zup & jnp.logical_not(zdown))
        def _():
            add(cu, cv, z, color, pieces + [Z(z, k)])

        @pl.when(zdown & jnp.logical_not(zup))
        def _():
            add(cu, cv, z, color, pieces + [Z(4, k)])

    own(4, u2, v, 0, [VA(z, 1)])
    out_copy(u2, v, z, 0, u_peer, UB(4, 0)).start()
    own(5, u, v2, 1, [UB(z, 1)])
    out_copy(u, v2, z, 1, v_peer, VA(4, 0)).start()
    own(0, u, v, 2, [UC(z), VC(z, 0)])
    own(1, u, v, 3, [VD(z), UD(z, 0)])
    row_step(4)
    total_ref[...] = sums[10]
    own(2, u, v, 0, [VA(z, 0), UB(4, 0)])
    own(3, u, v, 1, [UB(z, 0), VA(4, 0)])
    pltpu.sync_copy(acc.at[chip_of(u, v, z)], out_ref)
    send_input.wait()
    for chip in range(16):
        give(chip).wait_send()
        for color in range(4):
            @pl.when(chip != chip_of(u, v, z))
            def _():
                lo, n = span[color]
                pltpu.make_async_remote_copy(src_ref=acc.at[chip, pl.ds(lo, n)], dst_ref=acc.at[chip, pl.ds(lo, n)],
                    send_sem=send_sem.at[chip, color], recv_sem=usem.at[0], device_id=(sibling,), device_id_type=MESH).wait_send()

def scatter_blocks(part, rows, tail, cid=2):
    vectors, marks, x_rows, resid_grad, *grads, weights = tail
    _, slots, height, feats = part.shape
    own = x_rows.shape[0] - ROW_TILE
    size_a, size_b, size_c, size_d = (n for _, n in scatter_spans(slots))
    dt = part.dtype
    block = lambda *shape: pltpu.VMEM(shape + (height, feats), dt)
    like = lambda array: pltpu.VMEM(array.shape, array.dtype)
    anywhere = pl.BlockSpec(memory_space=pl.ANY)
    vmem = pl.BlockSpec(memory_space=pltpu.VMEM)
    wide_shapes, tail_scratch = tail_shapes(x_rows.shape)
    return pl.pallas_call(
        functools.partial(scatter_kernel, slots),
        out_shape=(
            jax.ShapeDtypeStruct(part.shape[1:], dt),
            jax.ShapeDtypeStruct(rows.shape, rows.dtype),
            jax.ShapeDtypeStruct((own, feats), jnp.float32),
        ),
        in_specs=[anywhere] + [vmem] * 3 + [anywhere] * 6,
        out_specs=(anywhere, vmem, anywhere),
        scratch_shapes=[
            block(16, slots),
            block(4, slots),
            block(9, size_b),
            block(4, size_c),
            block(8, size_d),
            block(9, size_a),
            block(8, size_c),
            block(4, size_d),
            block(20, size_a),
            block(5, size_c),
            block(5, size_d),
            pltpu.VMEM((11,) + rows.shape, rows.dtype),
            like(x_rows), like(resid_grad), *(like(g) for g in grads), like(weights),
            *wide_shapes,
            *tail_scratch,
            pltpu.VMEM((own, feats), jnp.float32),
            pltpu.SemaphoreType.DMA((4,)),
            pltpu.SemaphoreType.DMA((16,)),
            pltpu.SemaphoreType.DMA((16,)),
            pltpu.SemaphoreType.DMA((16, 4)),
            pltpu.SemaphoreType.DMA((21,)),
            pltpu.SemaphoreType.DMA((21,)),
            pltpu.SemaphoreType.DMA((30,)),
            pltpu.SemaphoreType.DMA((5,)),
            pltpu.SemaphoreType.DMA((5,)),
            pltpu.SemaphoreType.DMA((6,)),
            pltpu.SemaphoreType.DMA,
        ],
        compiler_params=pltpu.CompilerParams(collective_id=cid, has_side_effects=True, vmem_limit_bytes=VMEM_BYTES),
        name="scatter_blocks",
    )(part, rows, vectors, marks, x_rows, resid_grad, *grads, weights)


ROW_TILE = 16
BIG_TILE = 64
PIECES = 4
STEP_TILE = 32
CHUNKS = 8
LANES = 128
PLANE = 8
PLANES = GRID_DEVICES // PLANE
VMEM_BYTES = 60 * 2**20


def rows_at(index, size=ROW_TILE):
    return pl.ds(pl.multiple_of(index * size, size), size)


def fetch_blocks(slot_ref, pool_ref, store_ref, sem, first_block, place, count):
    def step(b, carry):
        for k in range(4):
            pltpu.make_async_copy(
                pool_ref.at[slot_ref[first_block + 4 * b + k]], store_ref.at[place + 4 * b + k], sem
            ).start()
        return carry

    lax.fori_loop(0, count // 4, step, 0)


def await_blocks(pool_ref, store_ref, sem, place, count):
    pltpu.make_async_copy(
        pool_ref.at[pl.ds(0, count)], store_ref.at[pl.ds(place, count)], sem
    ).wait()


def times_weight(left_ref, store_ref, place, count, write, width=512):
    features = store_ref.shape[2]

    def step(n, carry):
        cols = pl.ds(pl.multiple_of(n * width, width), width)
        right = store_ref[place : place + count, :, cols].reshape(count * BLOCK_ROWS, width)
        write(cols, jnp.dot(left_ref[...], right, preferred_element_type=jnp.float32))
        return carry

    lax.fori_loop(0, features // width, step, 0)


def times_weight_back(left_ref, store_ref, place, count, write, width=1024):
    blocks = width // BLOCK_ROWS

    def step(n, carry):
        cols = pl.ds(pl.multiple_of(n * width, width), width)
        right = store_ref[pl.ds(place + n * blocks, blocks)].reshape(width, store_ref.shape[2])
        write(cols, product_back(left_ref[...], right))
        return carry

    lax.fori_loop(0, count // blocks, step, 0)


def weight_gradient(left_ref, right_ref, own, slot_ref, grad_ref, store_ref, sem, first_block, place, width=1024):
    blocks = width // BLOCK_ROWS
    steps = left_ref.shape[1] // width

    def step(n, carry):
        cols = pl.ds(pl.multiple_of(n * width, width), width)
        piece = product_left(left_ref[0:own, cols], right_ref[0:own])
        at = place + n * blocks
        store_ref[pl.ds(at, blocks)] = piece.astype(store_ref.dtype).reshape(blocks, *store_ref.shape[1:])

        def put(b, inner):
            for k in range(4):
                pltpu.make_async_copy(
                    store_ref.at[at + 4 * b + k],
                    grad_ref.at[slot_ref[first_block + n * blocks + 4 * b + k]],
                    sem,
                ).start()
            return inner

        return lax.fori_loop(0, blocks // 4, put, carry)

    lax.fori_loop(0, steps, step, 0)


def await_gradient(store_ref, grad_ref, sem, place, count):
    pltpu.make_async_copy(
        store_ref.at[pl.ds(place, count)], grad_ref.at[pl.ds(0, count)], sem
    ).wait()


def start_pieces(pairs, sems, own):
    for p in range(PIECES + 1):
        for k, (src, dst) in enumerate(pairs):
            if p < PIECES or dst.shape[0] > own:
                piece_copy(src, dst, sems, own, k, p).start()


def piece_copy(src, dst, sems, own, k, p):
    size = own // PIECES
    at = pl.ds(p * size, size) if p < PIECES else pl.ds(own, ROW_TILE)
    return pltpu.make_async_copy(src.at[at], dst.at[at], sems.at[k, p])


def wait_piece(pairs, sems, own, p):
    for k, (src, dst) in enumerate(pairs):
        if p < PIECES or dst.shape[0] > own:
            piece_copy(src, dst, sems, own, k, p).wait()


def for_rows(rows, work, sums=()):
    own = rows - ROW_TILE

    def step(j, carry):
        out = work(pl.multiple_of(j * BIG_TILE, BIG_TILE), BIG_TILE, *carry)
        return carry if out is None else out

    sums = lax.fori_loop(0, own // BIG_TILE, step, sums)
    return sums


def fold(piece):
    return jnp.sum(piece.reshape(-1, CHUNKS, piece.shape[1]), axis=0)


def unit_norm(values):
    centered = values - jnp.mean(values, axis=1, keepdims=True)
    inverse = lax.rsqrt(jnp.mean(centered * centered, axis=1, keepdims=True) + NORM_EPS)
    return centered * inverse, inverse


def merge(first, second):
    top = jnp.maximum(first[2], second[2])
    one, two = jnp.exp(first[2] - top), jnp.exp(second[2] - top)
    return (one * first[0] + two * second[0], one * first[1] + two * second[1], top)


def aged(state, distance, alive, rate):
    return (state[0], state[1], jnp.where(alive > 0.5, state[2] - distance * rate, NEGATIVE))


def reset(state, start):
    cut = start > 0.5
    return (
        jnp.where(cut, 0.0, state[0]),
        jnp.where(cut, 0.0, state[1]),
        jnp.where(cut, NEGATIVE, state[2]),
    )


def advance(state, key, value, rate):
    older = state[2] - rate
    top = jnp.maximum(older, key)
    old, new = jnp.exp(older - top), jnp.exp(key - top)
    return (old * state[0] + new * value, old * state[1] + new, top)


def shift_in(ext, own):
    ext[0:8] = jnp.concatenate([ext[own + 10 : own + 11], ext[own : own + 7]], axis=0)


def halo_previous(ext, own, features):
    return jnp.concatenate(
        [
            ext[own + 7 : own + 8],
            ext[own + 8 : own + 9],
            ext[own + 11 : own + 12],
            jnp.zeros((ROW_TILE - 3, features), jnp.float32),
        ],
        axis=0,
    )


def normed_pair(ext, marks_ref, first, size):
    here = ext[pl.ds(pl.multiple_of(first + 8, 8), size)]
    before = ext[pl.ds(first, size)] * marks_ref[pl.ds(first, size), 1:2]
    return here, before


def take_step(wide, first, length):
    at = pl.ds(first, CHUNKS, stride=length)
    return jnp.concatenate([wide[k, at] for k in range(wide.shape[0])], axis=1)


def put_step(wide, first, length, tile):
    at = pl.ds(first, CHUNKS, stride=length)
    lanes = wide.shape[2]
    for k in range(wide.shape[0]):
        wide[k, at] = tile[:, k * lanes : (k + 1) * lanes]


def take_rows(wide, at):
    return jnp.concatenate([wide[k, at] for k in range(wide.shape[0])], axis=1)


def put_rows(wide, at, tile):
    lanes = wide.shape[2]
    for k in range(wide.shape[0]):
        wide[k, at] = tile[:, k * lanes : (k + 1) * lanes]


def none_between(offsets, low, high):
    hit = None
    for offset in offsets:
        inside = (low <= offset) & (offset <= high)
        hit = inside if hit is None else hit | inside
    return jnp.where(hit, 0.0, 1.0)


def write_marks(doc_ref, marks_ref, chunk_ref, link_ref, own, devices):
    rows = marks_ref.shape[0]
    length = own // CHUNKS
    total = own * devices
    me = lax.axis_index("seq")
    first = me * own
    offsets = [jnp.int32(0)]
    for k in range(doc_ref.shape[0] - 1):
        offsets.append(offsets[-1] + doc_ref[k])
    row = lax.broadcasted_iota(jnp.int32, (rows, 1), 0)
    chunk, step = lax.rem(row, CHUNKS), row // CHUNKS
    extra = jnp.where(row < own + 2, row, own - 1 - (row - (own + 2)) - own)
    place = first + jnp.where(row < own, chunk * length + step, extra)
    inside = (place >= 0) & (place < total)
    keep = jnp.where(inside, none_between(offsets, place, place), 0.0)
    begin = first + chunk * length
    marks_ref[:, 0:1] = 1.0 - keep
    marks_ref[:, 1:2] = keep
    marks_ref[:, 2:3] = jnp.where(row < own, none_between(offsets, begin, place), 1.0)
    marks_ref[:, 3:4] = jnp.where(row < own, none_between(offsets, place + 1, begin + length - 1), 1.0)
    chunk = lax.broadcasted_iota(jnp.int32, (CHUNKS, 1), 0)
    begin = first + chunk * length
    end = begin + length - 1
    chunk_ref[:, 0:1] = none_between(offsets, begin, end)
    chunk_ref[:, 1:2] = jnp.where(first > 0, none_between(offsets, first - 1, begin - 1), 0.0)
    chunk_ref[:, 2:3] = none_between(offsets, begin, end - 1)
    chunk_ref[:, 3:4] = (1 + chunk * length).astype(jnp.float32)
    chunk_ref[:, 4:5] = jnp.where(first + own < total, none_between(offsets, end + 1, first + own), 0.0)
    chunk_ref[:, 5:6] = (1 + (CHUNKS - 1 - chunk) * length).astype(jnp.float32)
    def put(rows, col, valid, distance):
        link_ref[rows, col : col + 1] = valid
        link_ref[rows, col + 1 : col + 2] = distance.astype(jnp.float32)

    if devices != GRID_DEVICES:
        other = lax.broadcasted_iota(jnp.int32, (devices, 1), 0)
        every = slice(0, devices)
        put(every, 0, jnp.where(other < me, none_between(offsets, own * (other + 1) - 1, own * me - 2), 0.0), own * (me - 1 - other))
        put(every, 2, jnp.where(other > me, none_between(offsets, own * (me + 1) + 1, own * other), 0.0), own * (other - me - 1))
        return
    z = me // PLANE
    base = z * PLANE
    end = base + PLANE
    other = base + lax.broadcasted_iota(jnp.int32, (PLANE, 1), 0)
    rows = slice(0, PLANE)
    put(rows, 0, jnp.where(other < me, none_between(offsets, own * (other + 1) - 1, own * me - 2), 0.0), own * (me - 1 - other))
    put(rows, 2, jnp.where(other > me, none_between(offsets, own * (me + 1) + 1, own * other), 0.0), own * (other - me - 1))
    rows = slice(PLANE, 2 * PLANE)
    put(rows, 0, none_between(offsets, own * (other + 1) - 1, own * end - 2), own * (end - 1 - other))
    put(rows, 2, none_between(offsets, own * base + 1, own * other), own * (other - base))
    rows = slice(2 * PLANE, 2 * PLANE + PLANES)
    far = lax.broadcasted_iota(jnp.int32, (PLANES, 1), 0)
    span = own * PLANE
    put(rows, 0, jnp.where(far < z, none_between(offsets, span * (far + 1) - 1, span * z - 2), 0.0), span * (z - 1 - far))
    put(rows, 2, jnp.where(far > z, none_between(offsets, span * (z + 1) + 1, span * far), 0.0), span * (far - z - 1))
    rows = slice(2 * PLANE + PLANES, 2 * PLANE + PLANES + 1)
    here = me + jnp.zeros((1, 1), jnp.int32)
    put(rows, 0, none_between(offsets, own * base - 1, own * here - 2), own * (here - base))
    put(rows, 2, none_between(offsets, own * (here + 1) + 1, own * end), own * (end - 1 - here))


def mask_column(pad_ref, column):
    for k in range(pad_ref.shape[0]):
        row = pad_ref[k : k + 1].astype(jnp.float32)
        column[k * LANES : (k + 1) * LANES] = jnp.broadcast_to(row, (LANES, LANES)).T[:, 0:1]


def normed_rows(x_ref, vec_ref, ext, first, size, tile):
    x_ref[pl.ds(first, size)] = tile.astype(jnp.bfloat16)
    unit, _ = unit_norm(tile)
    ext[pl.ds(pl.multiple_of(first + 8, 8), size)] = unit * vec_ref[0:1] + vec_ref[1:2]


def prepare_own(devices, doc_ref, tokens_ref, grads_ref, column, vec_ref, x_ref, grad_ref, marks, ext, wide, wide_grad):
    rows = x_ref.shape[0]
    own = rows - ROW_TILE
    length = own // CHUNKS
    write_marks(doc_ref, *marks, own, devices)

    def widen(first, size):
        at = pl.ds(first, size)
        put_rows(wide, at, tokens_ref[at].astype(jnp.float32))
        put_rows(wide_grad, at, grads_ref[at].astype(jnp.float32) * column[at])

    for_rows(rows, widen)

    def arrange(first, size):
        steps = [first // CHUNKS + k for k in range(size // CHUNKS)]
        tile = jnp.concatenate([take_step(wide, i, length) for i in steps], axis=0)
        normed_rows(x_ref, vec_ref, ext, first, size, tile)
        tile = jnp.concatenate([take_step(wide_grad, i, length) for i in steps], axis=0)
        grad_ref[pl.ds(first, size)] = tile.astype(jnp.bfloat16)

    for_rows(rows, arrange)


def prepare_halo(devices, after_ref, after_grad_ref, before_ref, vec_ref, x_ref, grad_ref, marks_ref, lows, ext):
    rows, features = x_ref.shape
    own = rows - ROW_TILE
    me = lax.axis_index("seq")
    more, less = me < devices - 1, me > 0
    later = jnp.where(more, after_ref[...].astype(jnp.float32), 0.0)[0:2]
    earlier = jnp.where(less, before_ref[...].astype(jnp.float32), 0.0)
    blank_rows = jnp.zeros((ROW_TILE - 4, features), jnp.float32)
    tile = jnp.concatenate(
        [later, earlier[ROW_TILE - 1 :], earlier[ROW_TILE - 2 : ROW_TILE - 1], blank_rows], axis=0
    )
    normed_rows(x_ref, vec_ref, ext, own, ROW_TILE, tile)
    later_grad = jnp.where(more, after_grad_ref[...].astype(jnp.float32), 0.0)[0:2]
    grad_ref[own:rows] = jnp.concatenate([later_grad, blank_rows, blank_rows[:2]], axis=0).astype(jnp.bfloat16)
    shift_in(ext, own)

    def mix(first, size, here, before):
        for row, ref in zip((2, 3, 4), lows):
            weight = vec_ref[row : row + 1]
            ref[pl.ds(first, size)] = (weight * here + (1.0 - weight) * before).astype(jnp.bfloat16)

    for_rows(rows, lambda first, size: mix(first, size, *normed_pair(ext, marks_ref, first, size)))
    mix(own, ROW_TILE, ext[own + 8 : own + 8 + ROW_TILE], halo_previous(ext, own, features) * marks_ref[own:rows, 1:2])


def prepared_shapes(devices, own, features):
    rows = own + ROW_TILE
    count = 2 * PLANE + PLANES + 1 if devices == GRID_DEVICES else devices
    low = jax.ShapeDtypeStruct((rows, features), jnp.bfloat16)
    small = lambda *shape: jax.ShapeDtypeStruct(shape, jnp.float32)
    shapes = (low, low, small(rows, 4), small(CHUNKS, 6), small(count, 4), low, low, low)
    scratch = [
        pltpu.VMEM((own, 1), jnp.float32),
        pltpu.VMEM((rows + 8, features), jnp.float32),
        pltpu.VMEM((features // LANES, own, LANES), jnp.float32),
        pltpu.VMEM((features // LANES, own, LANES), jnp.float32),
    ]
    return shapes, scratch


def prepare_kernel(
    devices, doc_ref, tokens_ref, grads_ref, pad_ref, after_ref, after_grad_ref, before_ref, vec_ref,
    x_ref, grad_ref, marks_ref, chunk_ref, link_ref, in_key, in_value, in_recept,
    column, ext, wide, wide_grad,
):
    mask_column(pad_ref, column)
    marks = (marks_ref, chunk_ref, link_ref)
    prepare_own(devices, doc_ref, tokens_ref, grads_ref, column, vec_ref, x_ref, grad_ref, marks, ext, wide, wide_grad)
    lows = (in_key, in_value, in_recept)
    prepare_halo(devices, after_ref, after_grad_ref, before_ref, vec_ref, x_ref, grad_ref, marks_ref, lows, ext)


def prepare_pass(devices, doc_lengths, tokens_in, cotangent, pad_rows, halo, vectors):
    shapes, scratch = prepared_shapes(devices, *tokens_in.shape)
    vmem = pl.BlockSpec(memory_space=pltpu.VMEM)
    return pl.pallas_call(
        functools.partial(prepare_kernel, devices),
        out_shape=shapes,
        in_specs=[pl.BlockSpec(memory_space=pltpu.SMEM)] + [vmem] * 7,
        out_specs=(vmem,) * len(shapes),
        scratch_shapes=scratch,
        compiler_params=pltpu.CompilerParams(vmem_limit_bytes=VMEM_BYTES),
        name="prepare_pass",
    )(doc_lengths, tokens_in, cotangent, pad_rows, *halo, vectors)


def open_kernel(
    slot_ref, vec_ref, marks_ref, chunk_ref, in_key, in_value, in_recept, pool_ref,
    prefix_ref, summary_ref, key_out, value_out, recept_out, state_out, weights_ref,
    key_ref, value_ref, recept_ref, num_ref, den_ref, max_ref, store, sem, out_sem,
):
    rows, features = in_key.shape
    own = rows - ROW_TILE
    length = own // CHUNKS
    per = EMBED_SIZE // BLOCK_ROWS
    for m in range(3):
        fetch_blocks(slot_ref, pool_ref, store, sem.at[m], m * per, m * per, per)
    for m, (left, out) in enumerate(((in_key, key_ref), (in_value, value_ref), (in_recept, recept_ref))):
        await_blocks(pool_ref, store, sem.at[m], m * per, per)

        def write(cols, piece, out=out):
            out[:, cols] = piece

        times_weight(left, store, m * per, per, write)
    sent = [
        pltpu.make_async_copy(src, dst, out_sem.at[k])
        for k, (src, dst) in enumerate(
            (
                (key_ref, key_out), (value_ref, value_out), (recept_ref, recept_out), (store, weights_ref),
                (num_ref, state_out.at[0]), (den_ref, state_out.at[1]), (max_ref, state_out.at[2]),
            )
        )
    ]
    for copy in sent[:4]:
        copy.start()
    rate = jnp.exp(vec_ref[5:6])

    def token(i, state, key, value):
        state = reset(state, marks_ref[rows_at(i, CHUNKS), 0:1])
        num_ref[rows_at(i, CHUNKS)], den_ref[rows_at(i, CHUNKS)], max_ref[rows_at(i, CHUNKS)] = state
        return advance(state, key, value, rate)

    def step(i, state):
        return token(i, state, key_ref[rows_at(i, CHUNKS)], value_ref[rows_at(i, CHUNKS)])

    blank = jnp.zeros((CHUNKS, features), jnp.float32)
    state = lax.fori_loop(0, length - 1, step, (blank, blank, blank + NEGATIVE))
    late = tuple(item[CHUNKS - 1 :] for item in state)
    ends = step(length - 1, state)
    for copy in sent[4:]:
        copy.start()
    prior = (value_ref[own + 2 : own + 3], jnp.ones((1, features), jnp.float32), key_ref[own + 2 : own + 3])
    for c in range(CHUNKS):
        for k in range(3):
            prefix_ref[k, c : c + 1] = prior[k]
        if c < CHUNKS - 1:
            old = aged(prior, float(length), chunk_ref[c : c + 1, 0:1], rate)
            prior = merge(tuple(item[c : c + 1] for item in ends), old)
    last = merge(late, aged(prior, float(length - 1), chunk_ref[CHUNKS - 1 :, 2:3], rate))
    summary_ref[...] = jnp.concatenate(last, axis=0)
    for copy in sent:
        copy.wait()


def open_pass(slots, vectors, marks, chunk_marks, lows, pool):
    rows, features = lows[0].shape
    own = rows - ROW_TILE
    full = jax.ShapeDtypeStruct((rows, features), jnp.float32)
    small = lambda *shape: jax.ShapeDtypeStruct(shape, jnp.float32)
    vmem = pl.BlockSpec(memory_space=pltpu.VMEM)
    anywhere = pl.BlockSpec(memory_space=pl.ANY)
    f32 = lambda *shape: pltpu.VMEM(shape, jnp.float32)
    blocks = (3 * EMBED_SIZE // BLOCK_ROWS, BLOCK_ROWS, features)
    return pl.pallas_call(
        open_kernel,
        out_shape=(
            small(3, CHUNKS, features), small(3, features), full, full, full, small(3, own, features),
            jax.ShapeDtypeStruct(blocks, jnp.bfloat16),
        ),
        in_specs=[pl.BlockSpec(memory_space=pltpu.SMEM)] + [vmem] * 6 + [anywhere],
        out_specs=(vmem,) * 2 + (anywhere,) * 5,
        scratch_shapes=[f32(rows, features)] * 3 + [f32(own, features)] * 3 + [
            pltpu.VMEM(blocks, jnp.bfloat16),
            pltpu.SemaphoreType.DMA((3,)),
            pltpu.SemaphoreType.DMA((7,)),
        ],
        compiler_params=pltpu.CompilerParams(vmem_limit_bytes=VMEM_BYTES),
        name="open_pass",
    )(slots, vectors, marks, chunk_marks, *lows, pool)


def middle_kernel(
    slot_ref, vec_ref, marks_ref, chunk_ref, incoming_ref, prefix_ref,
    x_in, grad_in, key_in, value_in, recept_in, state_in, pool_ref,
    suffix_ref, summary_ref, sums_ref, fade_ref,
    layer_out, resid_out, key_out, value_out, recept_out, slot_grad,
    x_ref, grad_ref, key_ref, value_ref, recept_ref, layer_ref, resid_grad, wkv, gw, own_share, recept_grad,
    full_num, full_den, full_max, mixed, ext, unit, inverse, low_key, low_recept, hidden, squared, value_acc, gate, gcv, gcg, hidden_grad,
    attn_grad, top_log, wide, store, sem, out_sem, in_sem, piece_sem, done_sem,
):
    rows, features = x_ref.shape
    own = rows - ROW_TILE
    tiles = rows // ROW_TILE
    length = own // CHUNKS
    per = EMBED_SIZE // BLOCK_ROWS
    ff = FF // BLOCK_ROWS
    at_out, at_recept, at_key, at_value = 0, per, 2 * per, 2 * per + ff
    pairs = [(key_in, key_ref), (value_in, value_ref), (recept_in, recept_ref)]
    pairs += [(state_in.at[k], ref) for k, ref in enumerate((full_num, full_den, full_max))]
    start_pieces(pairs, piece_sem, own)
    arrive_x = pltpu.make_async_copy(x_in, x_ref, in_sem.at[0])
    arrive_grad = pltpu.make_async_copy(grad_in, grad_ref, in_sem.at[1])
    sent = [
        pltpu.make_async_copy(src, dst, done_sem.at[k])
        for k, (src, dst) in enumerate(
            (
                (layer_ref, layer_out), (resid_grad, resid_out), (recept_grad, recept_out),
                (gw, key_out), (own_share, value_out),
            )
        )
    ]
    fetch_blocks(slot_ref, pool_ref, store, sem.at[0], 3 * per, at_out, per)
    arrive_x.start()
    arrive_grad.start()
    fetch_blocks(slot_ref, pool_ref, store, sem.at[1], 5 * per, at_key, ff)
    fetch_blocks(slot_ref, pool_ref, store, sem.at[2], 5 * per + ff, at_value, ff)
    fetch_blocks(slot_ref, pool_ref, store, sem.at[3], 4 * per, at_recept, per)
    rate = jnp.exp(vec_ref[5:6])
    bonus = vec_ref[6:7]
    incoming = tuple(incoming_ref[k : k + 1] for k in range(3))
    carry = merge(
        tuple(prefix_ref[k] for k in range(3)),
        aged(tuple(jnp.broadcast_to(v, (CHUNKS, features)) for v in incoming), chunk_ref[:, 3:4], chunk_ref[:, 1:2], rate),
    )

    def attend(j, size, state, key, value, recept):
        own_log = bonus + key
        top = jnp.maximum(state[2], own_log)
        old, new = jnp.exp(state[2] - top), jnp.exp(own_log - top)
        scale = 1.0 / (old * state[1] + new)
        out = (old * state[0] + new * value) * scale
        wkv[rows_at(j, size)] = out
        own_share[rows_at(j, size)] = new * scale
        top_log[rows_at(j, size)] = top
        value_acc[rows_at(j, size)] = scale
        ext[rows_at(j, size)] = jax.nn.sigmoid(recept) * out

    carry_wide = tuple(jnp.concatenate([item] * (STEP_TILE // CHUNKS), axis=0) for item in carry)
    ramp = lax.broadcasted_iota(jnp.int32, (STEP_TILE, 1), 0) // CHUNKS

    def attend_step(i, state_carry):
        at = rows_at(i, STEP_TILE)
        alive = marks_ref[at, 2:3]
        distance = (i * (STEP_TILE // CHUNKS) + ramp).astype(jnp.float32)
        state = merge((full_num[at], full_den[at], full_max[at]), aged(carry_wide, distance, alive, rate))
        full_num[at], full_den[at], full_max[at] = state
        attend(i, STEP_TILE, state, key_ref[at], value_ref[at], recept_ref[at])
        return state_carry

    for p in range(PIECES):
        wait_piece(pairs, piece_sem, own, p)
        count = own // STEP_TILE
        lax.fori_loop(p * count // PIECES, (p + 1) * count // PIECES, attend_step, 0)
    wait_piece(pairs, piece_sem, own, PIECES)

    def row(ref, r):
        return ref[r : r + 1]

    end = advance(
        (row(full_num, own - 1), row(full_den, own - 1), row(full_max, own - 1)),
        row(key_ref, own - 1), row(value_ref, own - 1), rate,
    )
    halo_one = reset(end, marks_ref[own : own + 1, 0:1])
    halo_two = reset(
        advance(halo_one, row(key_ref, own), row(value_ref, own), rate), marks_ref[own + 1 : own + 2, 0:1]
    )
    halo_zero = reset(incoming, marks_ref[own + 2 : own + 3, 0:1])
    rest = jnp.zeros((ROW_TILE - 3, features), jnp.float32)
    halo_state = tuple(
        jnp.concatenate([halo_one[k], halo_two[k], halo_zero[k], rest + (NEGATIVE if k == 2 else 0.0)], axis=0)
        for k in range(3)
    )
    attend(tiles - 1, ROW_TILE, halo_state, key_ref[own:rows], value_ref[own:rows], recept_ref[own:rows])

    def pack(first, size):
        at = pl.ds(first, size)
        mixed[at] = ext[at].astype(jnp.bfloat16)
        gw[at] = value_acc[at]

    for_rows(rows, pack)
    pack(own, ROW_TILE)
    await_blocks(pool_ref, store, sem.at[0], at_out, per)
    arrive_x.wait()

    def write_resid(cols, piece):
        unit[:, cols] = x_ref[:, cols].astype(jnp.float32) + piece

    times_weight(mixed, store, at_out, per, write_resid)

    def norm(first, size):
        at = pl.ds(first, size)
        resid = unit[at]
        resid_grad[at] = resid
        out, inv = unit_norm(resid)
        unit[at] = out
        inverse[at] = inv
        ext[pl.ds(pl.multiple_of(first + 8, 8), size)] = out * vec_ref[7:8] + vec_ref[8:9]

    for_rows(rows, norm)
    norm(own, ROW_TILE)
    shift_in(ext, own)

    def mix(first, size, here, before):
        for r, ref in ((9, low_key), (10, low_recept)):
            weight = vec_ref[r : r + 1]
            ref[pl.ds(first, size)] = (weight * here + (1.0 - weight) * before).astype(jnp.bfloat16)

    for_rows(rows, lambda first, size: mix(first, size, *normed_pair(ext, marks_ref, first, size)))
    mix(own, ROW_TILE, ext[own + 8 : own + 8 + ROW_TILE], halo_previous(ext, own, features) * marks_ref[own:rows, 1:2])

    await_blocks(pool_ref, store, sem.at[1], at_key, ff)

    def write_hidden(cols, piece):
        up = jnp.maximum(piece, 0.0)
        hidden[:, cols] = up
        squared[:, cols] = (up * up).astype(jnp.bfloat16)

    times_weight_back(low_key, store, at_key, ff, write_hidden)
    await_blocks(pool_ref, store, sem.at[2], at_value, ff)

    def write_value(cols, piece):
        value_acc[:, cols] = piece

    times_weight(squared, store, at_value, ff, write_value)
    await_blocks(pool_ref, store, sem.at[3], at_recept, per)

    def write_gate(cols, piece):
        gate[:, cols] = piece

    times_weight(low_recept, store, at_recept, per, write_gate)

    arrive_grad.wait()

    def finish(first, size):
        at = pl.ds(first, size)
        opened = jax.nn.sigmoid(gate[at])
        value = value_acc[at]
        grad = grad_ref[at].astype(jnp.float32) * opened
        gcv[at] = grad.astype(jnp.bfloat16)
        gcg[at] = (grad * value * (1.0 - opened)).astype(jnp.bfloat16)
        return resid_grad[at] + opened * value

    def finish_own(first, size):
        out = finish(first, size)
        for k in range(size // CHUNKS):
            put_step(wide, first // CHUNKS + k, length, out[CHUNKS * k : CHUNKS * (k + 1)])

    for_rows(rows, finish_own)
    finish(own, ROW_TILE)

    def emit(first, size):
        layer_ref[pl.ds(first, size)] = take_rows(wide, pl.ds(first, size)).astype(jnp.bfloat16)

    for_rows(rows, emit)
    sent[0].start()

    def write_hidden_grad(cols, piece):
        hidden_grad[:, cols] = (piece * (2.0 * hidden[:, cols])).astype(jnp.bfloat16)

    times_weight_back(gcv, store, at_value, ff, write_hidden_grad)
    weight_gradient(squared, gcv, own, slot_ref, slot_grad, store, out_sem.at[2], 5 * per + ff, at_value)
    times_weight(hidden_grad, store, at_key, ff, write_value)
    weight_gradient(hidden_grad, low_key, own, slot_ref, slot_grad, store, out_sem.at[1], 5 * per, at_key)
    times_weight_back(gcg, store, at_recept, per, write_gate)
    weight_gradient(low_recept, gcg, own, slot_ref, slot_grad, store, out_sem.at[3], 4 * per, at_recept)
    carried = hidden.at[:, 0:features]
    mix_key, mix_recept = vec_ref[9:10], vec_ref[10:11]

    def carry_over(first, size):
        at = pl.ds(first, size)
        carried[at] = marks_ref[at, 1:2] * ((1.0 - mix_key) * value_acc[at] + (1.0 - mix_recept) * gate[at])

    for_rows(rows, carry_over)
    carry_over(own, ROW_TILE)
    halo_next = jnp.concatenate(
        [carried[own + 1 : own + 2], jnp.zeros((ROW_TILE - 1, features), jnp.float32)], axis=0
    )
    carried[own : own + 8] = jnp.concatenate([carried[1:8], carried[own : own + 1]], axis=0)

    def norm_back(first, size, following):
        at = pl.ds(first, size)
        grad = mix_key * value_acc[at] + mix_recept * gate[at] + following
        scaled = grad * vec_ref[7:8]
        inner = (
            scaled
            - jnp.mean(scaled, axis=1, keepdims=True)
            - unit[at] * jnp.mean(scaled * unit[at], axis=1, keepdims=True)
        )
        total = grad_ref[at].astype(jnp.float32) + inner * inverse[at]
        resid_grad[at] = total
        attn_grad[at] = total.astype(jnp.bfloat16)
        return grad

    def back_step(first, size, *sums):
        at = pl.ds(first, size)
        grad = norm_back(first, size, carried[pl.ds(pl.multiple_of(first + 8, 8), size)])
        here, before = normed_pair(ext, marks_ref, first, size)
        spread = here - before
        return (
            sums[0] + fold(grad * unit[at]),
            sums[1] + fold(grad),
            sums[2] + fold(value_acc[at] * spread),
            sums[3] + fold(gate[at] * spread),
        )

    blank = jnp.zeros((CHUNKS, features), jnp.float32)
    sums = for_rows(rows, back_step, (blank,) * 4)
    for k in range(4):
        sums_ref[k : k + 1] = jnp.sum(sums[k], axis=0, keepdims=True)
    norm_back(own, ROW_TILE, halo_next)
    sent[1].start()

    times_weight_back(attn_grad, store, at_out, per, write_gate)
    weight_gradient(mixed, attn_grad, own, slot_ref, slot_grad, store, out_sem.at[0], 3 * per, at_out)

    def gate_back(first, size):
        at = pl.ds(first, size)
        opened = jax.nn.sigmoid(recept_ref[at])
        grad = gate[at] * opened
        ext[at] = grad * gw[at]
        gw[at] = grad
        recept_grad[at] = (grad * wkv[at] * (1.0 - opened)).astype(jnp.bfloat16)

    for_rows(rows, gate_back)
    gate_back(own, ROW_TILE)
    sent[2].start()

    def back_token(state, share, out, top, start):
        older = state[2] - rate
        high = jnp.maximum(older, -top)
        old, new = jnp.exp(older - high), jnp.exp(-top - high)
        return reset((old * state[0] + new * share, old * state[1] - new * share * out, high), start)

    def back_scan(n, items):
        state, joint, sums = items[:3], items[3:6], items[6:]
        i = length - 1 - n
        at = rows_at(i, CHUNKS)
        value, out = value_ref[at], wkv[at]
        direct = own_share[at] * gw[at]
        bonus_grad = direct * (value - out)
        lift = jnp.exp(key_ref[at] + state[2])
        gw[at] = bonus_grad + lift * (state[0] * value + state[1])
        own_share[at] = direct + lift * state[0]
        whole = (full_num[at], full_den[at], full_max[at])
        fade = jnp.exp(state[2] + whole[2] - rate) * (state[0] * whole[0] + state[1] * whole[1])
        joint = merge(joint, aged(whole, (length - i).astype(jnp.float32), marks_ref[at, 3:4], rate))
        state = back_token(state, ext[at], out, top_log[at], marks_ref[at, 0:1])
        return state + joint + (sums[0] + fade, sums[1] + bonus_grad)

    empty = (blank, blank, blank + NEGATIVE)
    items = lax.fori_loop(0, length - 1, back_scan, empty + empty + (blank, blank))
    first = tuple(item[0:1] for item in items[:3])
    items = back_scan(jnp.int32(length - 1), items)
    heads = items[:3]
    for k in range(3):
        fade_ref[k] = items[3 + k]
    for k in range(2):
        sums_ref[4 + k : 5 + k] = jnp.sum(items[6 + k], axis=0, keepdims=True)
    tile = slice(own, rows)
    direct = own_share[tile] * gw[tile]
    gw[tile] = direct * (value_ref[tile] - wkv[tile])
    own_share[tile] = direct
    sent[3].start()
    sent[4].start()
    nothing = jnp.zeros((1, features), jnp.float32)
    after = back_token(
        (nothing, nothing, nothing + NEGATIVE),
        row(ext, own), row(wkv, own), row(top_log, own), marks_ref[own : own + 1, 0:1],
    )
    for c in range(CHUNKS - 1, -1, -1):
        for k in range(3):
            suffix_ref[k, c : c + 1] = after[k]
        if c > 0:
            old = aged(after, float(length), chunk_ref[c : c + 1, 0:1], rate)
            after = merge(tuple(item[c : c + 1] for item in heads), old)
    last = merge(first, aged(after, float(length - 1), marks_ref[0:1, 3:4], rate))
    summary_ref[...] = jnp.concatenate(last, axis=0)
    for k, (place, count) in enumerate(((at_out, per), (at_key, ff), (at_value, ff), (at_recept, per))):
        await_gradient(store, slot_grad, out_sem.at[k], place, count)
    for copy in sent:
        copy.wait()


def middle_pass(slots, x_rows, grad_rows, vectors, marks, chunk_marks, incoming, opened, pool):
    key, value, recept, states, prefix = opened
    rows, features = x_rows.shape
    own = rows - ROW_TILE
    full = jax.ShapeDtypeStruct((rows, features), jnp.float32)
    low = jax.ShapeDtypeStruct((rows, features), jnp.bfloat16)
    vmem = pl.BlockSpec(memory_space=pltpu.VMEM)
    anywhere = pl.BlockSpec(memory_space=pl.ANY)
    f32 = lambda *shape: pltpu.VMEM(shape, jnp.float32)
    b16 = lambda *shape: pltpu.VMEM(shape, jnp.bfloat16)
    return pl.pallas_call(
        middle_kernel,
        out_shape=(
            jax.ShapeDtypeStruct((3, CHUNKS, features), jnp.float32),
            jax.ShapeDtypeStruct((3, features), jnp.float32),
            jax.ShapeDtypeStruct((6, features), jnp.float32),
            jax.ShapeDtypeStruct((3, CHUNKS, features), jnp.float32),
            jax.ShapeDtypeStruct((own, features), jnp.bfloat16),
            full, full, full, low,
            jax.ShapeDtypeStruct(pool.shape, jnp.bfloat16),
        ),
        in_specs=[pl.BlockSpec(memory_space=pltpu.SMEM)] + [vmem] * 5 + [anywhere] * 7,
        out_specs=(vmem,) * 4 + (anywhere,) * 6,
        scratch_shapes=[
            b16(rows, features),
            b16(rows, features),
            f32(rows, features),
            f32(rows, features),
            f32(rows, features),
            b16(own, features),
            f32(rows, features),
            f32(rows, features),
            f32(rows, features),
            f32(rows, features),
            b16(rows, features),
            f32(own, features),
            f32(own, features),
            f32(own, features),
            b16(rows, features),
            f32(rows + 8, features),
            f32(rows, features),
            f32(rows, 1),
            b16(rows, features),
            b16(rows, features),
            f32(rows, FF),
            b16(rows, FF),
            f32(rows, features),
            f32(rows, features),
            b16(rows, features),
            b16(rows, features),
            b16(rows, FF),
            b16(rows, features),
            f32(rows, features),
            f32(features // LANES, own, LANES),
            b16((2 * EMBED_SIZE + 2 * FF) // BLOCK_ROWS, BLOCK_ROWS, features),
            pltpu.SemaphoreType.DMA((4,)),
            pltpu.SemaphoreType.DMA((4,)),
            pltpu.SemaphoreType.DMA((2,)),
            pltpu.SemaphoreType.DMA((6, PIECES + 1)),
            pltpu.SemaphoreType.DMA((5,)),
        ],
        compiler_params=pltpu.CompilerParams(vmem_limit_bytes=VMEM_BYTES),
        name="middle_pass",
    )(slots, vectors, marks, chunk_marks, incoming, prefix, x_rows, grad_rows, key, value, recept, states, pool)


def tail_shapes(shape):
    rows, features = shape
    own = rows - ROW_TILE
    f32 = lambda *dims: pltpu.VMEM(dims, jnp.float32)
    grads = [f32(rows, features)] * 3
    rest = [
        f32(rows + 8, features),
        f32(rows, features),
        f32(rows, 1),
        f32(rows, features),
        f32(features // LANES, own, LANES),
    ]
    return grads, rest


def tail_steps(x_ref, vec_ref, marks_ref, resid_ref, lows, weights, outs, ext, unit, inverse, carried, wide, input_ref, sums_ref):
    rows, features = x_ref.shape
    own = rows - ROW_TILE
    length = own // CHUNKS
    per = EMBED_SIZE // BLOCK_ROWS

    def back(m):
        def write(cols, piece):
            outs[m][:, cols] = piece

        times_weight_back(lows[m], weights, m * per, per, write)

    def norm(first, size):
        at = pl.ds(first, size)
        out, inv = unit_norm(x_ref[at].astype(jnp.float32))
        unit[at] = out
        inverse[at] = inv
        ext[pl.ds(pl.multiple_of(first + 8, 8), size)] = out * vec_ref[0:1] + vec_ref[1:2]

    def norms():
        for_rows(rows, norm)
        norm(own, ROW_TILE)
        shift_in(ext, own)

    mixes = tuple(vec_ref[k : k + 1] for k in (2, 3, 4))

    def carry_over(first, size):
        at = pl.ds(first, size)
        total = (1.0 - mixes[0]) * outs[0][at] + (1.0 - mixes[1]) * outs[1][at] + (1.0 - mixes[2]) * outs[2][at]
        carried[at] = marks_ref[at, 1:2] * total

    def carry_all():
        for_rows(rows, carry_over)
        carry_over(own, ROW_TILE)
        carried[own : own + 8] = jnp.concatenate([carried[1:8], carried[own : own + 1]], axis=0)

    def back_step(first, size, *sums):
        at = pl.ds(first, size)
        grads = (outs[0][at], outs[1][at], outs[2][at])
        grad = carried[pl.ds(pl.multiple_of(first + 8, 8), size)]
        for weight, piece in zip(mixes, grads):
            grad = grad + weight * piece
        scaled = grad * vec_ref[0:1]
        inner = (
            scaled
            - jnp.mean(scaled, axis=1, keepdims=True)
            - unit[at] * jnp.mean(scaled * unit[at], axis=1, keepdims=True)
        )
        out = resid_ref[at] + inner * inverse[at]
        for k in range(size // CHUNKS):
            put_step(wide, first // CHUNKS + k, length, out[CHUNKS * k : CHUNKS * (k + 1)])
        here, before = normed_pair(ext, marks_ref, first, size)
        spread = here - before
        return (sums[0] + fold(grad * unit[at]), sums[1] + fold(grad)) + tuple(
            s + fold(piece * spread) for s, piece in zip(sums[2:], grads)
        )

    def back_all():
        blank = jnp.zeros((CHUNKS, features), jnp.float32)
        sums = for_rows(rows, back_step, (blank,) * 5)
        for k in range(5):
            sums_ref[k : k + 1] = jnp.sum(sums[k], axis=0, keepdims=True)

    def emit(first, size):
        input_ref[pl.ds(first, size)] = take_rows(wide, pl.ds(first, size))

    return [
        functools.partial(back, 0), functools.partial(back, 1), functools.partial(back, 2),
        norms, carry_all, back_all, lambda: for_rows(rows, emit),
    ]


def tail_kernel(
    vec_ref, marks_ref, x_ref, resid_ref, key_grad, value_grad, recept_grad, weights, rows_ref,
    input_ref, sums_ref, grad_key_in, grad_value_in, grad_recept_in, ext, unit, inverse, carried, wide,
):
    sums_ref[...] = rows_ref[...]
    steps = tail_steps(
        x_ref, vec_ref, marks_ref, resid_ref, (key_grad, value_grad, recept_grad), weights,
        (grad_key_in, grad_value_in, grad_recept_in), ext, unit, inverse, carried, wide, input_ref, sums_ref,
    )
    for step in steps:
        step()


def tail_pass(rows, tail):
    x_rows = tail[2]
    own, features = x_rows.shape[0] - ROW_TILE, x_rows.shape[1]
    grads, rest = tail_shapes(x_rows.shape)
    vmem = pl.BlockSpec(memory_space=pltpu.VMEM)
    return pl.pallas_call(
        tail_kernel,
        out_shape=(jax.ShapeDtypeStruct((own, features), jnp.float32), jax.ShapeDtypeStruct(rows.shape, rows.dtype)),
        in_specs=[vmem] * 9,
        out_specs=(vmem, vmem),
        scratch_shapes=grads + rest,
        compiler_params=pltpu.CompilerParams(vmem_limit_bytes=VMEM_BYTES),
        name="tail_pass",
    )(*tail, rows)


def close_kernel(
    slot_ref, vec_ref, marks_ref, chunk_ref, incoming_ref, suffix_ref, sums_two_ref, fade_ref,
    key_hbm, value_hbm, in_key_hbm, in_value_hbm, in_recept_hbm, key_part_hbm, value_part_hbm, recept_hbm, grads_in,
    key_grad, value_grad, sums_ref, slot_grad,
    key_ref, value_ref, in_key, in_value, in_recept, key_wide, value_wide, recept_grad,
    store, out_sem, in_sem, piece_sem,
):
    rows, features = key_ref.shape
    own = rows - ROW_TILE
    length = own // CHUNKS
    per = EMBED_SIZE // BLOCK_ROWS
    early = [
        pltpu.make_async_copy(src, dst, in_sem.at[k])
        for k, (src, dst) in enumerate(
            ((in_recept_hbm, in_recept), (recept_hbm, recept_grad), (in_key_hbm, in_key), (in_value_hbm, in_value))
        )
    ]
    early[0].start()
    early[1].start()
    pairs = [(key_hbm, key_ref), (value_hbm, value_ref), (key_part_hbm, key_wide), (value_part_hbm, value_wide)]
    start_pieces(pairs, piece_sem, own)
    early[2].start()
    early[3].start()
    early[0].wait()
    early[1].wait()
    weight_gradient(in_recept, recept_grad, own, slot_ref, slot_grad, store, out_sem.at[2], 2 * per, 2 * per)
    rate = jnp.exp(vec_ref[5:6])
    incoming = tuple(incoming_ref[k : k + 1] for k in range(3))
    carry = merge(
        tuple(suffix_ref[k] for k in range(3)),
        aged(tuple(jnp.broadcast_to(v, (CHUNKS, features)) for v in incoming), chunk_ref[:, 5:6], chunk_ref[:, 4:5], rate),
    )
    fade = jnp.exp(carry[2] + fade_ref[2]) * (carry[0] * fade_ref[0] + carry[1] * fade_ref[1])
    sums_ref[0:5] = jnp.zeros((5, features), jnp.float32)
    sums_ref[5:6] = -rate * (sums_two_ref[4:5] + jnp.sum(fade, axis=0, keepdims=True))
    sums_ref[6:7] = sums_two_ref[5:6]
    sums_ref[7:] = sums_two_ref[0:4]

    def spread_back(at, state):
        value = value_ref[at]
        lift = jnp.exp(key_ref[at] + state[2])
        key_grad[at] = (key_wide[at] + lift * (state[0] * value + state[1])).astype(jnp.bfloat16)
        value_grad[at] = (value_wide[at] + lift * state[0]).astype(jnp.bfloat16)

    carry_wide = tuple(jnp.concatenate([item] * (STEP_TILE // CHUNKS), axis=0) for item in carry)
    ramp = lax.broadcasted_iota(jnp.int32, (STEP_TILE, 1), 0) // CHUNKS

    def token(i, c):
        at = rows_at(i, STEP_TILE)
        distance = (length - 1 - i * (STEP_TILE // CHUNKS) - ramp).astype(jnp.float32)
        spread_back(at, aged(carry_wide, distance, marks_ref[at, 3:4], rate))
        return c

    for p in range(PIECES):
        wait_piece(pairs, piece_sem, own, p)
        count = own // STEP_TILE
        lax.fori_loop(p * count // PIECES, (p + 1) * count // PIECES, token, 0)
    wait_piece(pairs, piece_sem, own, PIECES)
    halo = tuple(
        jnp.concatenate([incoming[k], jnp.zeros((ROW_TILE - 1, features), jnp.float32) + (NEGATIVE if k == 2 else 0.0)], axis=0)
        for k in range(3)
    )
    spread_back(slice(own, rows), halo)
    early[2].wait()
    early[3].wait()
    weight_gradient(in_key, key_grad, own, slot_ref, slot_grad, store, out_sem.at[0], 0, 0)
    weight_gradient(in_value, value_grad, own, slot_ref, slot_grad, store, out_sem.at[1], per, per)
    for m in range(3):
        await_gradient(store, slot_grad, out_sem.at[m], m * per, per)


def close_pass(slots, vectors, marks, chunk_marks, incoming, suffix, sums_two, fade, kept, slot_grad):
    rows, features = kept[0].shape
    vmem = pl.BlockSpec(memory_space=pltpu.VMEM)
    anywhere = pl.BlockSpec(memory_space=pl.ANY)
    low = jax.ShapeDtypeStruct((rows, features), jnp.bfloat16)
    operands = (slots, vectors, marks, chunk_marks, incoming, suffix, sums_two, fade) + kept + (slot_grad,)
    return pl.pallas_call(
        close_kernel,
        out_shape=(
            low,
            low,
            jax.ShapeDtypeStruct(vectors.shape, jnp.float32),
            jax.ShapeDtypeStruct(slot_grad.shape, jnp.bfloat16),
        ),
        in_specs=[pl.BlockSpec(memory_space=pltpu.SMEM)] + [vmem] * 7 + [anywhere] * (len(kept) + 1),
        out_specs=(vmem, vmem, vmem, anywhere),
        input_output_aliases={len(operands) - 1: 3},
        scratch_shapes=[pltpu.VMEM(k.shape, k.dtype) for k in kept] + [
            pltpu.VMEM((3 * EMBED_SIZE // BLOCK_ROWS, BLOCK_ROWS, features), jnp.bfloat16),
            pltpu.SemaphoreType.DMA((3,)),
            pltpu.SemaphoreType.DMA((4,)),
            pltpu.SemaphoreType.DMA((4, PIECES + 1)),
        ],
        compiler_params=pltpu.CompilerParams(vmem_limit_bytes=VMEM_BYTES),
        name="close_pass",
    )(*operands)


def chain_kernel(forward, own_ref, vec_ref, link_ref, out_ref, plane, planes, joint, send_sem, recv_sem, far_send, far_recv):
    me, _, _, _, z = grid_place()
    place = lax.rem(me, PLANE)
    base = me - place
    at = 0 if forward else 2
    before = z if forward else PLANES - 1 - z
    step = PLANE if forward else -PLANE
    planes[...] = jnp.zeros_like(planes)
    bar = pltpu.get_barrier_semaphore()
    for o in range(1, PLANE):
        peer = base + lax.rem(place + o, PLANE)
        pl.semaphore_signal(bar, inc=1, device_id=(peer,), device_id_type=MESH)
    for o in range(1, PLANES):
        @pl.when(o <= before)
        def _():
            pl.semaphore_signal(bar, inc=1, device_id=(me - step * o,), device_id_type=MESH)
    plane[pl.ds(place, 1)] = own_ref[...][None]
    rate = jnp.exp(vec_ref[5:6])
    pl.semaphore_wait(bar, PLANE - 1 + PLANES - 1 - before)

    def near_copy(o, source, peer):
        return pltpu.make_async_remote_copy(
            src_ref=own_ref, dst_ref=plane.at[source], send_sem=send_sem.at[o], recv_sem=recv_sem.at[o],
            device_id=(peer,), device_id_type=MESH,
        )

    def far_copy(o, source, peer):
        return pltpu.make_async_remote_copy(
            src_ref=joint, dst_ref=planes.at[source], send_sem=far_send.at[o], recv_sem=far_recv.at[o],
            device_id=(peer,), device_id_type=MESH,
        )

    for o in range(PLANE - 1, 0, -1):
        near_copy(o, place, base + lax.rem(place + o, PLANE)).start()
    for o in range(1, PLANE):
        source = lax.rem(place - o + PLANE, PLANE)
        near_copy(o, source, base + source).wait_recv()

    def gather_states(ref, first, count):
        valid = link_ref[first : first + count, at : at + 1]
        logs = jnp.where(valid > 0.5, ref[:, 2] - link_ref[first : first + count, at + 1 : at + 2] * rate, NEGATIVE)
        top = jnp.max(logs, axis=0, keepdims=True)
        weight = jnp.exp(logs - top)
        return (
            jnp.sum(weight * ref[:, 0], axis=0, keepdims=True),
            jnp.sum(weight * ref[:, 1], axis=0, keepdims=True),
            top,
        )

    joint[...] = jnp.concatenate(gather_states(plane, PLANE, PLANE), axis=0)
    for o in range(PLANES - 1, 0, -1):
        @pl.when(o < PLANES - before)
        def _():
            far_copy(o, z, me + step * o).start()
    near = gather_states(plane, 0, PLANE)
    for o in range(1, PLANES):
        @pl.when(o <= before)
        def _():
            source = z - o if forward else z + o
            far_copy(o, source, me - step * o).wait_recv()
    last = 2 * PLANE + PLANES
    old = gather_states(planes, 2 * PLANE, PLANES)
    old = aged(old, link_ref[last : last + 1, at + 1 : at + 2], link_ref[last : last + 1, at : at + 1], rate)
    out_ref[...] = jnp.concatenate(merge(near, old), axis=0)
    for o in range(1, PLANE):
        near_copy(o, place, base + lax.rem(place + o, PLANE)).wait_send()
    for o in range(1, PLANES):
        @pl.when(o < PLANES - before)
        def _():
            far_copy(o, z, me + step * o).wait_send()


def chain_state(rows, vectors, links, forward, cid):
    devices = lax.axis_size("seq")
    if devices != GRID_DEVICES:
        every = lax.all_gather(rows[None], "seq", axis=0, tiled=True)
        at = 0 if forward else 2
        aged_logs = every[:, 2] - links[:, at + 1 : at + 2] * jnp.exp(vectors[5])
        logs = jnp.where(links[:, at : at + 1] > 0.5, aged_logs, NEGATIVE)
        top = jnp.max(logs, axis=0)
        weight = jnp.exp(logs - top)
        return jnp.stack([jnp.sum(weight * every[:, 0], axis=0), jnp.sum(weight * every[:, 1], axis=0), top])
    vmem = pl.BlockSpec(memory_space=pltpu.VMEM)
    return pl.pallas_call(
        functools.partial(chain_kernel, forward),
        out_shape=jax.ShapeDtypeStruct(rows.shape, jnp.float32),
        in_specs=[vmem] * 3,
        out_specs=vmem,
        scratch_shapes=[
            pltpu.VMEM((PLANE,) + rows.shape, jnp.float32),
            pltpu.VMEM((PLANES,) + rows.shape, jnp.float32),
            pltpu.VMEM(rows.shape, jnp.float32),
            pltpu.SemaphoreType.DMA((PLANE,)),
            pltpu.SemaphoreType.DMA((PLANE,)),
            pltpu.SemaphoreType.DMA((PLANES,)),
            pltpu.SemaphoreType.DMA((PLANES,)),
        ],
        compiler_params=pltpu.CompilerParams(collective_id=cid, has_side_effects=True),
        name="chain_forward" if forward else "chain_backward",
    )(rows, vectors, links)


def body(
    tokens_in,
    cotangent,
    pad_mask,
    doc_lengths,
    masters,
    moment_one,
    moment_two,
    block_slot,
    vectors,
    vector_one,
    vector_two,
):
    tokens, features = tokens_in.shape
    devices = lax.axis_size("seq")
    device_place = lax.axis_index("seq")
    pad_rows = pad_mask.reshape(-1, LANES)
    if devices == GRID_DEVICES:
        gathered, *prepared = gather_blocks(masters, doc_lengths, tokens_in, cotangent, pad_rows, vectors)
        gathered = gathered.reshape(-1, BLOCK_ROWS, features)
    else:
        gathered = lax.all_gather(masters.astype(jnp.bfloat16), "seq", axis=0, tiled=True)
        head_grad = cotangent[:ROW_TILE] * pad_mask[:ROW_TILE].astype(cotangent.dtype)[:, None]
        halo = [
            shifted(tokens_in[:ROW_TILE], "seq", -1),
            shifted(head_grad, "seq", -1),
            shifted(tokens_in[tokens - ROW_TILE :], "seq", 1),
        ]
        prepared = prepare_pass(devices, doc_lengths, tokens_in, cotangent, pad_rows, halo, vectors)
    x_rows, grad_rows, marks, chunk_marks, links, *lows = prepared
    lows = tuple(lows)
    prefix, summary, key, value, recept, states, weights = open_pass(
        block_slot, vectors, marks, chunk_marks, lows, gathered
    )
    incoming = chain_state(summary, vectors, links, True, 3)
    (
        suffix, back_summary, sums_two, fade,
        layer_out, resid_grad, key_part, value_part, recept_grad, slot_grad,
    ) = middle_pass(
        block_slot, x_rows, grad_rows, vectors, marks, chunk_marks, incoming,
        (key, value, recept, states, prefix), gathered,
    )
    back_incoming = chain_state(back_summary, vectors, links, False, 4)
    key_grad, value_grad, stacked, slot_grad = close_pass(
        block_slot, vectors, marks, chunk_marks, back_incoming, suffix, sums_two, fade,
        (key, value) + lows + (key_part, value_part, recept_grad), slot_grad,
    )
    tail = (vectors, marks, x_rows, resid_grad, key_grad, value_grad, recept_grad, weights)
    own_slots = device_place * masters.shape[0] + jnp.arange(masters.shape[0], dtype=jnp.int32)
    named = jnp.any(own_slots[:, None] == block_slot[None, :], axis=1)
    if devices == GRID_DEVICES:
        owner_grad, vector_grad, input_grad = scatter_blocks(
            slot_grad.reshape((devices,) + masters.shape), stacked, tail
        )
        owner_grad = owner_grad.astype(jnp.float32)
    else:
        input_grad, stacked = tail_pass(stacked, tail)
        owner_grad = lax.psum_scatter(
            slot_grad.astype(jnp.float32), "seq", scatter_dimension=0, tiled=True
        )
        vector_grad = lax.psum(stacked, "seq")
    owner_grad = jnp.where(named[:, None, None], owner_grad, 0.0)
    new_one, new_two, new_master = adam_update(
        masters, moment_one, moment_two, owner_grad, MATRIX_RATE, WEIGHT_DECAY
    )
    vector_rates = jnp.array(VECTOR_RATE, jnp.float32)[:, None]
    vector_first, vector_second, vector_next = adam_update(
        vectors, vector_one, vector_two, vector_grad, vector_rates, 0.0
    )
    return (
        layer_out,
        input_grad,
        new_one,
        new_two,
        new_master,
        vector_first,
        vector_second,
        vector_next,
    )


def solution(mesh):
    placed = (
        P("seq", None),
        P("seq", None),
        P("seq"),
        P(),
        P("seq", None, None),
        P("seq", None, None),
        P("seq", None, None),
        P(),
        P(),
        P(),
        P(),
    )
    return jax.shard_map(
        body,
        mesh=mesh,
        in_specs=placed,
        out_specs=(
            P("seq", None),
            P("seq", None),
            P("seq", None, None),
            P("seq", None, None),
            P("seq", None, None),
            P(),
            P(),
            P(),
        ),
        check_vma=False,
    )
```

```python
import functools

import jax
import jax.numpy as jnp
from jax import lax
from jax.experimental import pallas as pl
from jax.experimental.pallas import tpu as pltpu
from jax.sharding import PartitionSpec as P

EMBED_SIZE = 1024
FF = 4096
BLOCK_ROWS = 32
ROWS_ALL = 13312
BLOCKS = 416
STEP = 10
GRID_DEVICES = 32
MESH = pl.DeviceIdType.MESH


NEGATIVE = -1e30
NORM_EPS = 1e-05
BETA_ONE = 0.9
BETA_TWO = 0.999
ADAM_EPS = 1e-08
MATRIX_RATE = 0.05
WEIGHT_DECAY = 0.01
VECTOR_RATE = (0.25, 0.25, 0.25, 0.25, 0.25, 2.0, 0.25, 0.25, 0.25, 0.25, 0.25)


def shifted(block, axis, distance):
    devices = range(lax.axis_size(axis))
    route = [(i - distance, i) for i in devices if i - distance in devices]
    return lax.ppermute(block, axis, route)


def product_back(left_side, right_side):
    return lax.dot_general(
        left_side, right_side, (((1,), (1,)), ((), ())), preferred_element_type=jnp.float32
    )


def product_left(left_side, right_side):
    return lax.dot_general(
        left_side, right_side, (((0,), (0,)), ((), ())), preferred_element_type=jnp.float32
    )


def adam_update(weight, first_moment, second_moment, gradient, step_rate, feature_fade_speed):
    first_moment = BETA_ONE * first_moment + (1.0 - BETA_ONE) * gradient
    second_moment = BETA_TWO * second_moment + (1.0 - BETA_TWO) * gradient * gradient
    first_fixed = first_moment / (1.0 - BETA_ONE**STEP)
    second_fixed = second_moment / (1.0 - BETA_TWO**STEP)
    weight = weight - step_rate * (
        first_fixed / (jnp.sqrt(second_fixed) + ADAM_EPS) + feature_fade_speed * weight
    )
    return (first_moment, second_moment, weight)


def grid_place():
    me = lax.axis_index("seq")
    return me, lax.rem(me, 2), lax.rem(me // 2, 2), lax.rem(me // 4, 2), me // 8

def spans(slots):
    side = 4 * slots // 15
    cuts = [0, side, 2 * side, slots]
    return [(cuts[i], cuts[i + 1] - cuts[i]) for i in range(3)]

def gather_kernel(
    slots, doc_ref, master_ref, tokens_ref, cot_ref, pad_ref, vec_ref,
    out_ref, x_ref, grad_ref, marks_ref, chunk_ref, link_ref, in_key, in_value, in_recept,
    column, ext, wide, wide_grad, own_ref, head_grad, after_ref, after_grad_ref, before_ref,
    *scratch,
):
    send_sem, recv_sem, sib_send, sib_recv, own_sem, halo_send, halo_recv = scratch
    me, core, x, y, z = grid_place()
    sib = me + 1 - 2 * core
    x_peer = me + 2 - 4 * x
    y_peer = me + 4 - 8 * y
    up = me + 8
    down = me - 8
    bar = pltpu.get_barrier_semaphore()
    pl.semaphore_signal(bar, inc=1, device_id=(sib,), device_id_type=MESH)
    pl.semaphore_signal(bar, inc=1, device_id=(x_peer,), device_id_type=MESH)
    pl.semaphore_signal(bar, inc=1, device_id=(y_peer,), device_id_type=MESH)
    @pl.when(z < 3)
    def _():
        pl.semaphore_signal(bar, inc=1, device_id=(up,), device_id_type=MESH)
    @pl.when(z > 0)
    def _():
        pl.semaphore_signal(bar, inc=1, device_id=(down,), device_id_type=MESH)
    more, less = me < GRID_DEVICES - 1, me > 0

    @pl.when(more)
    def _():
        pl.semaphore_signal(bar, inc=1, device_id=(me + 1,), device_id_type=MESH)

    @pl.when(less)
    def _():
        pl.semaphore_signal(bar, inc=1, device_id=(me - 1,), device_id_type=MESH)

    def lower(s, carry):
        own_ref[s] = master_ref[s].astype(own_ref.dtype)
        return carry

    lax.fori_loop(0, slots, lower, 0)
    mask_column(pad_ref, column)
    head_grad[...] = (cot_ref[0:ROW_TILE].astype(jnp.float32) * column[0:ROW_TILE]).astype(jnp.bfloat16)
    halos = jnp.where(more, 1, 0) + jnp.where(less, 1, 0)
    pl.semaphore_wait(bar, 4 + jnp.where((z > 0) & (z < 3), 1, 0) + halos)
    tokens = tokens_ref.shape[0]

    def halo_copy(k):
        src, dst, peer = (
            (tokens_ref.at[pl.ds(0, ROW_TILE)], after_ref, me - 1),
            (head_grad, after_grad_ref, me - 1),
            (tokens_ref.at[pl.ds(tokens - ROW_TILE, ROW_TILE)], before_ref, me + 1),
        )[k]
        return pltpu.make_async_remote_copy(src_ref=src, dst_ref=dst, send_sem=halo_send.at[k],
            recv_sem=halo_recv.at[k], device_id=(peer,), device_id_type=MESH)
    span = spans(slots)
    targets = (x_peer, y_peer, up, down)

    def chip(cx, cy, cz):
        return (cz * 2 + cy) * 2 + cx

    def view(cx, cy, cz, color, c=None):
        dev = chip(cx, cy, cz) * 2 + (core if c is None else c)
        lo, n = span[color]
        return out_ref.at[dev, pl.ds(lo, n)]

    def send(cx, cy, cz, color, way, own=False):
        lo, n = span[color]
        src = own_ref.at[pl.ds(lo, n)] if own else view(cx, cy, cz, color)
        idx = chip(cx, cy, cz)
        return pltpu.make_async_remote_copy(src_ref=src, dst_ref=view(cx, cy, cz, color),
            send_sem=send_sem.at[idx, color, way], recv_sem=recv_sem.at[idx, color],
            device_id=(targets[way],), device_id_type=MESH)

    def send_sib(cx, cy, cz, color, own=False):
        lo, n = span[color]
        src = own_ref.at[pl.ds(lo, n)] if own else view(cx, cy, cz, color)
        idx = chip(cx, cy, cz)
        return pltpu.make_async_remote_copy(src_ref=src, dst_ref=view(cx, cy, cz, color),
            send_sem=sib_send.at[idx, color], recv_sem=sib_recv.at[idx, color],
            device_id=(sib,), device_id_type=MESH)

    x2, y2 = 1 - x, 1 - y
    pending = []

    def go(copy, cond=None):
        if cond is None:
            copy.start()
        else:
            @pl.when(cond)
            def _():
                copy.start()
        pending.append((copy, cond))

    zup, zdown = z < 3, z > 0
    own_copies = []
    for color in range(3):
        lo, n = span[color]
        cp = pltpu.make_async_copy(own_ref.at[pl.ds(lo, n)], view(x, y, z, color), own_sem.at[color])
        cp.start()
        own_copies.append(cp)
    order = {0: (0, 2, 1), 1: (1, 2, 0)}
    for color in (0, 1, 2):
        go(send(x, y, z, color, 2, True), zup)
        go(send(x, y, z, color, 3, True), zdown)
    for color, way in ((0, 0), (1, 1), (2, 0), (2, 1), (0, 1), (1, 0)):
        go(send(x, y, z, color, way, True))
    for color in range(3):
        go(send_sib(x, y, z, color, True))

    @pl.when(less)
    def _():
        for k in (0, 1):
            halo_copy(k).start()

    @pl.when(more)
    def _():
        halo_copy(2).start()

    marks = (marks_ref, chunk_ref, link_ref)
    prepare_own(
        GRID_DEVICES, doc_ref, tokens_ref, cot_ref, column, vec_ref, x_ref, grad_ref, marks, ext, wide, wide_grad
    )

    def arrive(cx, cy, cz, color):
        send(cx, cy, cz, color, 0).wait_recv()

    def sibling(cx, cy, cz, color):
        go(send_sib(cx, cy, cz, color))

    is0, is1 = core == 0, core == 1
    px = jnp.where(is0, x2, x)
    py = jnp.where(is0, y, y2)
    qx = jnp.where(is0, x, x2)
    qy = jnp.where(is0, y2, y)
    first = lambda cx, cy, cz: (go(send(cx, cy, cz, 2, 0), is0), go(send(cx, cy, cz, 2, 1), is1))
    last = lambda cx, cy, cz: (go(send(cx, cy, cz, 2, 1), is0), go(send(cx, cy, cz, 2, 0), is1))

    arrive(x2, y, z, 0)
    go(send(x2, y, z, 0, 2), zup)
    go(send(x2, y, z, 0, 3), zdown)
    go(send(x2, y, z, 0, 1))
    sibling(x2, y, z, 0)
    arrive(x, y2, z, 1)
    go(send(x, y2, z, 1, 2), zup)
    go(send(x, y2, z, 1, 3), zdown)
    go(send(x, y2, z, 1, 0))
    sibling(x, y2, z, 1)
    arrive(px, py, z, 2)
    last(px, py, z)
    sibling(px, py, z, 2)

    def wait_halo():
        @pl.when(less)
        def _():
            for k in (0, 1):
                halo_copy(k).wait_send()
            halo_copy(2).wait_recv()

        @pl.when(more)
        def _():
            halo_copy(2).wait_send()
            for k in (0, 1):
                halo_copy(k).wait_recv()

    for dist in (1, 2, 3):
        sides = []
        for sign, fwd, guard_f in ((1, 3, zdown), (-1, 2, zup)):
            q = z + sign * dist
            have = (q >= 0) & (q < 4)
            sides.append((q, fwd, have, guard_f))
        for which in ("c", "a", "b", "a2", "b2"):
            for q, fwd, have, gf in sides:
                @pl.when(have)
                def _(q=q, fwd=fwd, gf=gf, which=which):
                    if which == "c":
                        arrive(x, y, q, 2)
                        cp = send(x, y, q, 2, fwd)
                        pl.when(gf)(lambda: cp.start())
                        for w in (0, 1):
                            send(x, y, q, 2, w).start()
                        send_sib(x, y, q, 2).start()
                    else:
                        color = 0 if which[0] == "a" else 1
                        cx, cy = {"a": (x, y), "b": (x, y), "a2": (x2, y), "b2": (x, y2)}[which]
                        arrive(cx, cy, q, color)
                        cp = send(cx, cy, q, color, fwd)
                        pl.when(gf)(lambda: cp.start())
                        send(cx, cy, q, color, 1 if color == 0 else 0).start()
                        send_sib(cx, cy, q, color).start()
        for q, fwd, have, gf in sides:
            @pl.when(have)
            def _(q=q):
                arrive(px, py, q, 2)
                pl.when(is0)(lambda: send(px, py, q, 2, 1).start())
                pl.when(is1)(lambda: send(px, py, q, 2, 0).start())
                send_sib(px, py, q, 2).start()
        if dist == 1:
            tail_list = [(z, None)]
        else:
            tail_list = []
        if dist == 1:
            wait_halo()
            lows = (in_key, in_value, in_recept)
            prepare_halo(
                GRID_DEVICES, after_ref, after_grad_ref, before_ref, vec_ref, x_ref, grad_ref, marks_ref, lows, ext
            )
        def terminal(q):
            for cx, cy, color in ((x, y2, 0), (x2, y2, 0), (x2, y, 1), (x2, y2, 1), (qx, qy, 2), (x2, y2, 2)):
                arrive(cx, cy, q, color)
                send_sib(cx, cy, q, color).start()
        if dist == 1:
            terminal(z)
        else:
            for sign in (1, -1):
                q = z + sign * (dist - 1)
                pl.when((q >= 0) & (q < 4))(lambda q=q: terminal(q))
        if dist == 3:
            for sign in (1, -1):
                q = z + sign * 3
                pl.when((q >= 0) & (q < 4))(lambda q=q: terminal(q))
    for cp in own_copies:
        cp.wait()
    for color in range(3):
        pl.when(zup)(lambda color=color: send(x, y, z, color, 2).wait_send())
        pl.when(zdown)(lambda color=color: send(x, y, z, color, 3).wait_send())
        for w in (0, 1):
            send(x, y, z, color, w).wait_send()
    for cx, cy, color, w in ((x2, y, 0, 1), (x, y2, 1, 0)):
        pl.when(zup)(lambda: send(cx, cy, z, color, 2).wait_send())
        pl.when(zdown)(lambda: send(cx, cy, z, color, 3).wait_send())
        send(cx, cy, z, color, w).wait_send()
    pl.when(is0)(lambda: send(px, py, z, 2, 1).wait_send())
    pl.when(is1)(lambda: send(px, py, z, 2, 0).wait_send())
    for dist in (1, 2, 3):
        for sign, fwd, gf in ((1, 3, zdown), (-1, 2, zup)):
            q = z + sign * dist
            @pl.when((q >= 0) & (q < 4))
            def _(q=q, fwd=fwd, gf=gf):
                for cx, cy, color in ((x, y, 2), (x, y, 0), (x, y, 1), (x2, y, 0), (x, y2, 1)):
                    pl.when(gf)(lambda: send(cx, cy, q, color, fwd).wait_send())
                    ways = (0, 1) if color == 2 else ((1,) if color == 0 else (0,))
                    for w in ways:
                        send(cx, cy, q, color, w).wait_send()
                pl.when(is0)(lambda: send(px, py, q, 2, 1).wait_send())
                pl.when(is1)(lambda: send(px, py, q, 2, 0).wait_send())
    for cz in range(4):
        for cy in range(2):
            for cx in range(2):
                for color in range(3):
                    cp = send_sib(cx, cy, cz, color)
                    cp.wait_send()
                    cp.wait_recv()

def gather_blocks(masters, doc_lengths, tokens_in, cotangent, pad_rows, vectors, cid=1):
    slots = masters.shape[0]
    shapes, scratch = prepared_shapes(GRID_DEVICES, *tokens_in.shape)
    anywhere = pl.BlockSpec(memory_space=pl.ANY)
    vmem = pl.BlockSpec(memory_space=pltpu.VMEM)
    halo = pltpu.VMEM((ROW_TILE,) + tokens_in.shape[1:], jnp.bfloat16)
    return pl.pallas_call(
        functools.partial(gather_kernel, slots),
        out_shape=(jax.ShapeDtypeStruct((GRID_DEVICES,) + masters.shape, jnp.bfloat16),) + shapes,
        in_specs=[pl.BlockSpec(memory_space=pltpu.SMEM)] + [vmem] * 5,
        out_specs=(anywhere,) + (vmem,) * len(shapes),
        scratch_shapes=scratch + [
            pltpu.VMEM(masters.shape, jnp.bfloat16),
            halo, halo, halo, halo,
            pltpu.SemaphoreType.DMA((16, 3, 4)),
            pltpu.SemaphoreType.DMA((16, 3)),
            pltpu.SemaphoreType.DMA((16, 3)),
            pltpu.SemaphoreType.DMA((16, 3)),
            pltpu.SemaphoreType.DMA((3,)),
            pltpu.SemaphoreType.DMA((3,)),
            pltpu.SemaphoreType.DMA((3,)),
        ],
        compiler_params=pltpu.CompilerParams(collective_id=cid, has_side_effects=True, vmem_limit_bytes=VMEM_BYTES),
        name="gather_blocks",
    )(doc_lengths, masters, tokens_in, cotangent, pad_rows, vectors)


def scatter_spans(slots):
    side = 4 * slots // 15
    cuts = [0, side, 2 * side, 2 * side + (slots - 2 * side + 1) // 2, slots]
    return [(cuts[i], cuts[i + 1] - cuts[i]) for i in range(4)]


def scatter_kernel(
    slots, part_ref, rows_ref, vec_ref, marks_ref, x_hbm, resid_hbm, key_hbm, value_hbm, recept_hbm, weights_hbm,
    out_ref, total_ref, input_hbm,
    acc, ring, ub, uc, ud, va, vc, vd, zs, zc, zd, sums,
    x_ref, resid_ref, key_grad, value_grad, recept_grad, weights, grad_key_in, grad_value_in, grad_recept_in,
    ext, unit, inverse, carried, wide, input_ref,
    load_sem, sib_send, sib_recv, send_sem, usem, vsem, zsem, row_send, row_recv, tail_sem, input_sem,
):
    me, core, x, y, z = grid_place()
    sibling = me + 1 - 2 * core
    x_peer = me + 2 - 4 * x
    y_peer = me + 4 - 8 * y
    up, down = me + 8, me - 8
    zup, zdown = z < 3, z > 0
    bar = pltpu.get_barrier_semaphore()
    for peer in (sibling, x_peer, y_peer):
        pl.semaphore_signal(bar, inc=1, device_id=(peer,), device_id_type=MESH)
    @pl.when(zup)
    def _():
        pl.semaphore_signal(bar, inc=1, device_id=(up,), device_id_type=MESH)
    @pl.when(zdown)
    def _():
        pl.semaphore_signal(bar, inc=1, device_id=(down,), device_id_type=MESH)
    far = me + 16 - 32 * (z // 2)
    pl.semaphore_signal(bar, inc=1, device_id=(far,), device_id_type=MESH)
    row_peers = (sibling, x_peer, y_peer, me + 8 - 16 * lax.rem(z, 2), far)
    tail_loads = [
        pltpu.make_async_copy(src, dst, tail_sem.at[k])
        for k, (src, dst) in enumerate(
            (
                (key_hbm, key_grad), (value_hbm, value_grad), (recept_hbm, recept_grad),
                (x_hbm, x_ref), (resid_hbm, resid_ref), (weights_hbm, weights),
            )
        )
    ]
    span = scatter_spans(slots)
    u, v = jnp.where(core == 0, x, y), jnp.where(core == 0, y, x)
    u_peer, v_peer = jnp.where(core == 0, x_peer, y_peer), jnp.where(core == 0, y_peer, x_peer)
    u2, v2 = 1 - u, 1 - v

    def row_copy(k):
        return pltpu.make_async_remote_copy(src_ref=sums.at[2 * k], dst_ref=sums.at[2 * k + 1],
            send_sem=row_send.at[k], recv_sem=row_recv.at[k], device_id=(row_peers[k],), device_id_type=MESH)

    def row_step(k):
        row_copy(k).wait()
        sums[2 * k + 2] = sums[2 * k] + sums[2 * k + 1]
        if k < 4:
            row_copy(k + 1).start()

    def load(i, q):
        chip = 4 * q + plane_order()[i]
        return pltpu.make_async_copy(part_ref.at[2 * chip + core], ring.at[i], load_sem.at[i])

    first_level = jnp.where(z >= 2, 0, 3)

    def next_level(q):
        inner = jnp.where(q == 3, jnp.where(z == 1, 2, 1), jnp.where(q == 0, jnp.where(z == 1, 1, 3), jnp.where(z == 1, 0, 2)))
        return jnp.where(z == 0, q - 1, jnp.where(z == 3, q + 1, inner))

    def give(chip):
        return pltpu.make_async_remote_copy(src_ref=part_ref.at[2 * chip + 1 - core], dst_ref=acc.at[chip],
            send_sem=sib_send.at[chip], recv_sem=sib_recv.at[chip], device_id=(sibling,), device_id_type=MESH)

    levels = []
    for dist in (3, 2, 1):
        for sign in (1, -1):
            q = z + sign * dist
            levels.append((dist, sign, q, (q >= 0) & (q < 4)))

    def run(dist, work):
        for d, sign, q, have in levels:
            if d == dist:
                pl.when(have)(functools.partial(work, q))

    def run_signed(dist, work):
        for d, sign, q, have in levels:
            if d == dist:
                pl.when(have)(functools.partial(work, q, sign, dist))

    def chip_of(cu, cv, cz):
        return cz * 4 + jnp.where(core == 0, cv * 2 + cu, cu * 2 + cv)

    def plane_order():
        return (chip_of(u2, v2, 0), chip_of(u2, v, 0), chip_of(u, v2, 0), chip_of(u, v, 0))

    def sibling_order():
        return tuple(plane_order()[i] for i in (0, 2, 1, 3))

    for i in range(4):
        load(i, first_level).start()
    for copy in tail_loads:
        copy.start()
    pl.semaphore_wait(bar, 5 + jnp.where(zup & zdown, 1, 0))
    for i in range(2):
        give(4 * first_level + sibling_order()[i]).start()

    def ready(i, q):
        chip = 4 * q + plane_order()[i]
        load(i, q).wait()
        give(chip).wait_recv()

        def step(s, carry):
            total = acc[chip, s].astype(jnp.float32) + ring[i, s].astype(jnp.float32)
            acc[chip, s] = total.astype(acc.dtype)
            return carry

        lax.fori_loop(0, slots, step, 0)

        if i < 2:
            @pl.when(q == first_level)
            def _():
                give(4 * q + sibling_order()[i + 2]).start()

        @pl.when(q != z)
        def _():
            load(i, next_level(q)).start()
            give(4 * next_level(q) + sibling_order()[i]).start()

    def out_copy(cu, cv, cz, color, target, place):
        lo, n = span[color]
        chip = chip_of(cu, cv, cz)
        buf, index, sem, flag = place
        return pltpu.make_async_remote_copy(src_ref=acc.at[chip, pl.ds(lo, n)], dst_ref=buf.at[index],
            send_sem=send_sem.at[chip, color], recv_sem=sem.at[flag], device_id=(target,), device_id_type=MESH)

    def arrived(place, color):
        lo, n = span[color]
        buf, index, sem, flag = place
        pltpu.make_async_remote_copy(src_ref=acc.at[0, pl.ds(lo, n)], dst_ref=buf.at[index],
            send_sem=send_sem.at[0, color], recv_sem=sem.at[flag], device_id=(sibling,), device_id_type=MESH).wait_recv()

    def add(cu, cv, cz, color, pieces):
        lo, n = span[color]
        chip = chip_of(cu, cv, cz)
        for place in pieces:
            arrived(place, color)

        def step(s, carry):
            total = acc[chip, lo + s].astype(jnp.float32)
            for buf, index, _, _ in pieces:
                total = total + buf[index, s].astype(jnp.float32)
            acc[chip, lo + s] = total.astype(acc.dtype)
            return carry

        lax.fori_loop(0, n, step, 0)

    def UB(q, i): return (ub, 2 * q + i, usem, 2 * q + i)
    def UD(q, i): return (ud, 2 * q + i, usem, 9 + 2 * q + i)
    def UC(q): return (uc, q, usem, 17 + q)
    def VA(q, i): return (va, 2 * q + i, vsem, 2 * q + i)
    def VC(q, i): return (vc, 2 * q + i, vsem, 9 + 2 * q + i)
    def VD(q): return (vd, q, vsem, 17 + q)
    def Z(q, k): return ((zc, zd, zs)[min(k, 2)], q if k < 2 else 4 * q + k - 2, zsem, 6 * q + k)

    def send_u(q, color, i):
        out_copy(u2, (v, v2)[i], q, color, u_peer, UB(q, i) if color == 1 else UD(q, i)).start()

    def send_v(q, color, i):
        out_copy((u, u2)[i], v2, q, color, v_peer, VA(q, i) if color == 0 else VC(q, i)).start()

    def term_a(q):
        ready(0, q)
        send_u(q, 1, 1)
        send_v(q, 0, 1)

    def term_c(q):
        send_v(q, 2, 1)
        send_u(q, 3, 1)

    def term_b(q):
        ready(1, q)
        send_u(q, 1, 0)
        ready(2, q)
        send_v(q, 0, 0)

    def term_d(q):
        send_u(q, 3, 0)
        send_v(q, 2, 0)
        ready(3, q)

    def plane_two(q):
        add(u2, v, q, 2, [VC(q, 1)])
        out_copy(u2, v, q, 2, u_peer, UC(q)).start()
        add(u, v2, q, 3, [UD(q, 1)])
        out_copy(u, v2, q, 3, v_peer, VD(q)).start()

    def column(part, q, sign, dist):
        target = up if sign == 1 else down
        more = zdown if sign == 1 else zup
        level = 4 if (dist == 1 and sign == 1) else q
        kinds = (
            (0, u, v, 2, [UC(q), VC(q, 0)]),
            (1, u, v, 3, [VD(q), UD(q, 0)]),
            (2, u, v, 0, [VA(q, 0)]),
            (3, u, v, 1, [UB(q, 0)]),
            (4, u2, v, 0, [VA(q, 1)]),
            (5, u, v2, 1, [UB(q, 1)]),
        )
        for k, cu, cv, color, pieces in ((kinds[5], kinds[4], kinds[3], kinds[2]), (kinds[0], kinds[1]), (kinds[5], kinds[4]), (kinds[3], kinds[2]))[part]:
            @pl.when(more)
            def _():
                add(cu, cv, q, color, pieces + [Z(q, k)])

            @pl.when(jnp.logical_not(more))
            def _():
                add(cu, cv, q, color, pieces)

            out_copy(cu, cv, q, color, target, Z(level, k)).start()

    planes = functools.partial(column, 0)
    last = functools.partial(column, 1)
    def begin_tail():
        for copy in tail_loads:
            copy.wait()
        sums[0] = rows_ref[...]

    tail = tail_steps(
        x_ref, vec_ref, marks_ref, resid_ref, (key_grad, value_grad, recept_grad), weights,
        (grad_key_in, grad_value_in, grad_recept_in), ext, unit, inverse, carried, wide, input_ref, sums.at[0],
    )
    send_input = pltpu.make_async_copy(input_ref, input_hbm, input_sem)
    run(3, term_a)
    run(3, term_c)
    run(3, term_b)
    run(3, term_d)
    begin_tail()
    tail[0]()
    run_signed(3, functools.partial(column, 2))
    run(2, term_a)
    run_signed(3, functools.partial(column, 3))
    tail[1]()
    run(3, plane_two)
    run(2, term_c)
    run_signed(3, last)
    tail[2]()
    run(2, term_b)
    run(2, term_d)
    tail[3]()
    run_signed(2, functools.partial(column, 2))
    run(1, term_a)
    run_signed(2, functools.partial(column, 3))
    tail[4]()
    run(2, plane_two)
    run(1, term_c)
    run_signed(2, last)
    tail[5]()
    run(1, term_b)
    run(1, term_d)
    row_copy(0).start()
    run_signed(1, functools.partial(column, 2))
    term_a(z)
    row_step(0)
    run_signed(1, functools.partial(column, 3))
    run(1, plane_two)
    term_c(z)
    row_step(1)
    run_signed(1, last)
    term_b(z)
    term_d(z)
    row_step(2)
    tail[6]()
    send_input.start()
    plane_two(z)
    row_step(3)

    def own(k, cu, cv, color, pieces):
        @pl.when(zup & zdown)
        def _():
            add(cu, cv, z, color, pieces + [Z(z, k), Z(4, k)])

        @pl.when(zup & jnp.logical_not(zdown))
        def _():
            add(cu, cv, z, color, pieces + [Z(z, k)])

        @pl.when(zdown & jnp.logical_not(zup))
        def _():
            add(cu, cv, z, color, pieces + [Z(4, k)])

    own(4, u2, v, 0, [VA(z, 1)])
    out_copy(u2, v, z, 0, u_peer, UB(4, 0)).start()
    own(5, u, v2, 1, [UB(z, 1)])
    out_copy(u, v2, z, 1, v_peer, VA(4, 0)).start()
    own(0, u, v, 2, [UC(z), VC(z, 0)])
    own(1, u, v, 3, [VD(z), UD(z, 0)])
    row_step(4)
    total_ref[...] = sums[10]
    own(2, u, v, 0, [VA(z, 0), UB(4, 0)])
    own(3, u, v, 1, [UB(z, 0), VA(4, 0)])
    pltpu.sync_copy(acc.at[chip_of(u, v, z)], out_ref)
    send_input.wait()
    for chip in range(16):
        give(chip).wait_send()
        for color in range(4):
            @pl.when(chip != chip_of(u, v, z))
            def _():
                lo, n = span[color]
                pltpu.make_async_remote_copy(src_ref=acc.at[chip, pl.ds(lo, n)], dst_ref=acc.at[chip, pl.ds(lo, n)],
                    send_sem=send_sem.at[chip, color], recv_sem=usem.at[0], device_id=(sibling,), device_id_type=MESH).wait_send()

def scatter_blocks(part, rows, tail, cid=2):
    vectors, marks, x_rows, resid_grad, *grads, weights = tail
    _, slots, height, feats = part.shape
    own = x_rows.shape[0] - ROW_TILE
    size_a, size_b, size_c, size_d = (n for _, n in scatter_spans(slots))
    dt = part.dtype
    block = lambda *shape: pltpu.VMEM(shape + (height, feats), dt)
    like = lambda array: pltpu.VMEM(array.shape, array.dtype)
    anywhere = pl.BlockSpec(memory_space=pl.ANY)
    vmem = pl.BlockSpec(memory_space=pltpu.VMEM)
    wide_shapes, tail_scratch = tail_shapes(x_rows.shape)
    return pl.pallas_call(
        functools.partial(scatter_kernel, slots),
        out_shape=(
            jax.ShapeDtypeStruct(part.shape[1:], dt),
            jax.ShapeDtypeStruct(rows.shape, rows.dtype),
            jax.ShapeDtypeStruct((own, feats), jnp.float32),
        ),
        in_specs=[anywhere] + [vmem] * 3 + [anywhere] * 6,
        out_specs=(anywhere, vmem, anywhere),
        scratch_shapes=[
            block(16, slots),
            block(4, slots),
            block(9, size_b),
            block(4, size_c),
            block(8, size_d),
            block(9, size_a),
            block(8, size_c),
            block(4, size_d),
            block(20, size_a),
            block(5, size_c),
            block(5, size_d),
            pltpu.VMEM((11,) + rows.shape, rows.dtype),
            like(x_rows), like(resid_grad), *(like(g) for g in grads), like(weights),
            *wide_shapes,
            *tail_scratch,
            pltpu.VMEM((own, feats), jnp.float32),
            pltpu.SemaphoreType.DMA((4,)),
            pltpu.SemaphoreType.DMA((16,)),
            pltpu.SemaphoreType.DMA((16,)),
            pltpu.SemaphoreType.DMA((16, 4)),
            pltpu.SemaphoreType.DMA((21,)),
            pltpu.SemaphoreType.DMA((21,)),
            pltpu.SemaphoreType.DMA((30,)),
            pltpu.SemaphoreType.DMA((5,)),
            pltpu.SemaphoreType.DMA((5,)),
            pltpu.SemaphoreType.DMA((6,)),
            pltpu.SemaphoreType.DMA,
        ],
        compiler_params=pltpu.CompilerParams(collective_id=cid, has_side_effects=True, vmem_limit_bytes=VMEM_BYTES),
        name="scatter_blocks",
    )(part, rows, vectors, marks, x_rows, resid_grad, *grads, weights)


ROW_TILE = 16
BIG_TILE = 64
PIECES = 4
STEP_TILE = 32
CHUNKS = 8
LANES = 128
PLANE = 8
PLANES = GRID_DEVICES // PLANE
VMEM_BYTES = 60 * 2**20


def rows_at(index, size=ROW_TILE):
    return pl.ds(pl.multiple_of(index * size, size), size)


def fetch_blocks(slot_ref, pool_ref, store_ref, sem, first_block, place, count):
    def step(b, carry):
        for k in range(4):
            pltpu.make_async_copy(
                pool_ref.at[slot_ref[first_block + 4 * b + k]], store_ref.at[place + 4 * b + k], sem
            ).start()
        return carry

    lax.fori_loop(0, count // 4, step, 0)


def await_blocks(pool_ref, store_ref, sem, place, count):
    pltpu.make_async_copy(
        pool_ref.at[pl.ds(0, count)], store_ref.at[pl.ds(place, count)], sem
    ).wait()


def times_weight(left_ref, store_ref, place, count, write, width=1024):
    features = store_ref.shape[2]

    def step(n, carry):
        cols = pl.ds(pl.multiple_of(n * width, width), width)
        right = store_ref[place : place + count, :, cols].reshape(count * BLOCK_ROWS, width)
        write(cols, jnp.dot(left_ref[...], right, preferred_element_type=jnp.float32))
        return carry

    lax.fori_loop(0, features // width, step, 0)


def times_weight_back(left_ref, store_ref, place, count, write, width=1024):
    blocks = width // BLOCK_ROWS

    def step(n, carry):
        cols = pl.ds(pl.multiple_of(n * width, width), width)
        right = store_ref[pl.ds(place + n * blocks, blocks)].reshape(width, store_ref.shape[2])
        write(cols, product_back(left_ref[...], right))
        return carry

    lax.fori_loop(0, count // blocks, step, 0)


def weight_gradient(left_ref, right_ref, own, slot_ref, grad_ref, store_ref, sem, first_block, place, width=1024):
    blocks = width // BLOCK_ROWS
    steps = left_ref.shape[1] // width

    def step(n, carry):
        cols = pl.ds(pl.multiple_of(n * width, width), width)
        piece = product_left(left_ref[0:own, cols], right_ref[0:own])
        at = place + n * blocks
        store_ref[pl.ds(at, blocks)] = piece.astype(store_ref.dtype).reshape(blocks, *store_ref.shape[1:])

        def put(b, inner):
            for k in range(4):
                pltpu.make_async_copy(
                    store_ref.at[at + 4 * b + k],
                    grad_ref.at[slot_ref[first_block + n * blocks + 4 * b + k]],
                    sem,
                ).start()
            return inner

        return lax.fori_loop(0, blocks // 4, put, carry)

    lax.fori_loop(0, steps, step, 0)


def await_gradient(store_ref, grad_ref, sem, place, count):
    pltpu.make_async_copy(
        store_ref.at[pl.ds(place, count)], grad_ref.at[pl.ds(0, count)], sem
    ).wait()


def start_pieces(pairs, sems, own):
    for p in range(PIECES + 1):
        for k, (src, dst) in enumerate(pairs):
            if p < PIECES or dst.shape[0] > own:
                piece_copy(src, dst, sems, own, k, p).start()


def piece_copy(src, dst, sems, own, k, p):
    size = own // PIECES
    at = pl.ds(p * size, size) if p < PIECES else pl.ds(own, ROW_TILE)
    return pltpu.make_async_copy(src.at[at], dst.at[at], sems.at[k, p])


def wait_piece(pairs, sems, own, p):
    for k, (src, dst) in enumerate(pairs):
        if p < PIECES or dst.shape[0] > own:
            piece_copy(src, dst, sems, own, k, p).wait()


def for_rows(rows, work, sums=()):
    own = rows - ROW_TILE

    def step(j, carry):
        out = work(pl.multiple_of(j * BIG_TILE, BIG_TILE), BIG_TILE, *carry)
        return carry if out is None else out

    sums = lax.fori_loop(0, own // BIG_TILE, step, sums)
    return sums


def fold(piece):
    return jnp.sum(piece.reshape(-1, CHUNKS, piece.shape[1]), axis=0)


def unit_norm(values):
    centered = values - jnp.mean(values, axis=1, keepdims=True)
    inverse = lax.rsqrt(jnp.mean(centered * centered, axis=1, keepdims=True) + NORM_EPS)
    return centered * inverse, inverse


def merge(first, second):
    top = jnp.maximum(first[2], second[2])
    one, two = jnp.exp(first[2] - top), jnp.exp(second[2] - top)
    return (one * first[0] + two * second[0], one * first[1] + two * second[1], top)


def aged(state, distance, alive, rate):
    return (state[0], state[1], jnp.where(alive > 0.5, state[2] - distance * rate, NEGATIVE))


def reset(state, start):
    cut = start > 0.5
    return (
        jnp.where(cut, 0.0, state[0]),
        jnp.where(cut, 0.0, state[1]),
        jnp.where(cut, NEGATIVE, state[2]),
    )


def advance(state, key, value, rate):
    older = state[2] - rate
    top = jnp.maximum(older, key)
    old, new = jnp.exp(older - top), jnp.exp(key - top)
    return (old * state[0] + new * value, old * state[1] + new, top)


def shift_in(ext, own):
    ext[0:8] = jnp.concatenate([ext[own + 10 : own + 11], ext[own : own + 7]], axis=0)


def halo_previous(ext, own, features):
    return jnp.concatenate(
        [
            ext[own + 7 : own + 8],
            ext[own + 8 : own + 9],
            ext[own + 11 : own + 12],
            jnp.zeros((ROW_TILE - 3, features), jnp.float32),
        ],
        axis=0,
    )


def normed_pair(ext, marks_ref, first, size):
    here = ext[pl.ds(pl.multiple_of(first + 8, 8), size)]
    before = ext[pl.ds(first, size)] * marks_ref[pl.ds(first, size), 1:2]
    return here, before


def take_step(wide, first, length):
    at = pl.ds(first, CHUNKS, stride=length)
    return jnp.concatenate([wide[k, at] for k in range(wide.shape[0])], axis=1)


def put_step(wide, first, length, tile):
    at = pl.ds(first, CHUNKS, stride=length)
    lanes = wide.shape[2]
    for k in range(wide.shape[0]):
        wide[k, at] = tile[:, k * lanes : (k + 1) * lanes]


def take_rows(wide, at):
    return jnp.concatenate([wide[k, at] for k in range(wide.shape[0])], axis=1)


def put_rows(wide, at, tile):
    lanes = wide.shape[2]
    for k in range(wide.shape[0]):
        wide[k, at] = tile[:, k * lanes : (k + 1) * lanes]


def none_between(offsets, low, high):
    hit = None
    for offset in offsets:
        inside = (low <= offset) & (offset <= high)
        hit = inside if hit is None else hit | inside
    return jnp.where(hit, 0.0, 1.0)


def write_marks(doc_ref, marks_ref, chunk_ref, link_ref, own, devices):
    rows = marks_ref.shape[0]
    length = own // CHUNKS
    total = own * devices
    me = lax.axis_index("seq")
    first = me * own
    offsets = [jnp.int32(0)]
    for k in range(doc_ref.shape[0] - 1):
        offsets.append(offsets[-1] + doc_ref[k])
    row = lax.broadcasted_iota(jnp.int32, (rows, 1), 0)
    chunk, step = lax.rem(row, CHUNKS), row // CHUNKS
    extra = jnp.where(row < own + 2, row, own - 1 - (row - (own + 2)) - own)
    place = first + jnp.where(row < own, chunk * length + step, extra)
    inside = (place >= 0) & (place < total)
    keep = jnp.where(inside, none_between(offsets, place, place), 0.0)
    begin = first + chunk * length
    marks_ref[:, 0:1] = 1.0 - keep
    marks_ref[:, 1:2] = keep
    marks_ref[:, 2:3] = jnp.where(row < own, none_between(offsets, begin, place), 1.0)
    marks_ref[:, 3:4] = jnp.where(row < own, none_between(offsets, place + 1, begin + length - 1), 1.0)
    chunk = lax.broadcasted_iota(jnp.int32, (CHUNKS, 1), 0)
    begin = first + chunk * length
    end = begin + length - 1
    chunk_ref[:, 0:1] = none_between(offsets, begin, end)
    chunk_ref[:, 1:2] = jnp.where(first > 0, none_between(offsets, first - 1, begin - 1), 0.0)
    chunk_ref[:, 2:3] = none_between(offsets, begin, end - 1)
    chunk_ref[:, 3:4] = (1 + chunk * length).astype(jnp.float32)
    chunk_ref[:, 4:5] = jnp.where(first + own < total, none_between(offsets, end + 1, first + own), 0.0)
    chunk_ref[:, 5:6] = (1 + (CHUNKS - 1 - chunk) * length).astype(jnp.float32)
    def put(rows, col, valid, distance):
        link_ref[rows, col : col + 1] = valid
        link_ref[rows, col + 1 : col + 2] = distance.astype(jnp.float32)

    if devices != GRID_DEVICES:
        other = lax.broadcasted_iota(jnp.int32, (devices, 1), 0)
        every = slice(0, devices)
        put(every, 0, jnp.where(other < me, none_between(offsets, own * (other + 1) - 1, own * me - 2), 0.0), own * (me - 1 - other))
        put(every, 2, jnp.where(other > me, none_between(offsets, own * (me + 1) + 1, own * other), 0.0), own * (other - me - 1))
        return
    z = me // PLANE
    base = z * PLANE
    end = base + PLANE
    other = base + lax.broadcasted_iota(jnp.int32, (PLANE, 1), 0)
    rows = slice(0, PLANE)
    put(rows, 0, jnp.where(other < me, none_between(offsets, own * (other + 1) - 1, own * me - 2), 0.0), own * (me - 1 - other))
    put(rows, 2, jnp.where(other > me, none_between(offsets, own * (me + 1) + 1, own * other), 0.0), own * (other - me - 1))
    rows = slice(PLANE, 2 * PLANE)
    put(rows, 0, none_between(offsets, own * (other + 1) - 1, own * end - 2), own * (end - 1 - other))
    put(rows, 2, none_between(offsets, own * base + 1, own * other), own * (other - base))
    rows = slice(2 * PLANE, 2 * PLANE + PLANES)
    far = lax.broadcasted_iota(jnp.int32, (PLANES, 1), 0)
    span = own * PLANE
    put(rows, 0, jnp.where(far < z, none_between(offsets, span * (far + 1) - 1, span * z - 2), 0.0), span * (z - 1 - far))
    put(rows, 2, jnp.where(far > z, none_between(offsets, span * (z + 1) + 1, span * far), 0.0), span * (far - z - 1))
    rows = slice(2 * PLANE + PLANES, 2 * PLANE + PLANES + 1)
    here = me + jnp.zeros((1, 1), jnp.int32)
    put(rows, 0, none_between(offsets, own * base - 1, own * here - 2), own * (here - base))
    put(rows, 2, none_between(offsets, own * (here + 1) + 1, own * end), own * (end - 1 - here))


def mask_column(pad_ref, column):
    for k in range(pad_ref.shape[0]):
        row = pad_ref[k : k + 1].astype(jnp.float32)
        column[k * LANES : (k + 1) * LANES] = jnp.broadcast_to(row, (LANES, LANES)).T[:, 0:1]


def normed_rows(x_ref, vec_ref, ext, first, size, tile):
    x_ref[pl.ds(first, size)] = tile.astype(jnp.bfloat16)
    unit, _ = unit_norm(tile)
    ext[pl.ds(pl.multiple_of(first + 8, 8), size)] = unit * vec_ref[0:1] + vec_ref[1:2]


def prepare_own(devices, doc_ref, tokens_ref, grads_ref, column, vec_ref, x_ref, grad_ref, marks, ext, wide, wide_grad):
    rows = x_ref.shape[0]
    own = rows - ROW_TILE
    length = own // CHUNKS
    write_marks(doc_ref, *marks, own, devices)

    def widen(first, size):
        at = pl.ds(first, size)
        put_rows(wide, at, tokens_ref[at].astype(jnp.float32))
        put_rows(wide_grad, at, grads_ref[at].astype(jnp.float32) * column[at])

    for_rows(rows, widen)

    def arrange(first, size):
        steps = [first // CHUNKS + k for k in range(size // CHUNKS)]
        tile = jnp.concatenate([take_step(wide, i, length) for i in steps], axis=0)
        normed_rows(x_ref, vec_ref, ext, first, size, tile)
        tile = jnp.concatenate([take_step(wide_grad, i, length) for i in steps], axis=0)
        grad_ref[pl.ds(first, size)] = tile.astype(jnp.bfloat16)

    for_rows(rows, arrange)


def prepare_halo(devices, after_ref, after_grad_ref, before_ref, vec_ref, x_ref, grad_ref, marks_ref, lows, ext):
    rows, features = x_ref.shape
    own = rows - ROW_TILE
    me = lax.axis_index("seq")
    more, less = me < devices - 1, me > 0
    later = jnp.where(more, after_ref[...].astype(jnp.float32), 0.0)[0:2]
    earlier = jnp.where(less, before_ref[...].astype(jnp.float32), 0.0)
    blank_rows = jnp.zeros((ROW_TILE - 4, features), jnp.float32)
    tile = jnp.concatenate(
        [later, earlier[ROW_TILE - 1 :], earlier[ROW_TILE - 2 : ROW_TILE - 1], blank_rows], axis=0
    )
    normed_rows(x_ref, vec_ref, ext, own, ROW_TILE, tile)
    later_grad = jnp.where(more, after_grad_ref[...].astype(jnp.float32), 0.0)[0:2]
    grad_ref[own:rows] = jnp.concatenate([later_grad, blank_rows, blank_rows[:2]], axis=0).astype(jnp.bfloat16)
    shift_in(ext, own)

    def mix(first, size, here, before):
        for row, ref in zip((2, 3, 4), lows):
            weight = vec_ref[row : row + 1]
            ref[pl.ds(first, size)] = (weight * here + (1.0 - weight) * before).astype(jnp.bfloat16)

    for_rows(rows, lambda first, size: mix(first, size, *normed_pair(ext, marks_ref, first, size)))
    mix(own, ROW_TILE, ext[own + 8 : own + 8 + ROW_TILE], halo_previous(ext, own, features) * marks_ref[own:rows, 1:2])


def prepared_shapes(devices, own, features):
    rows = own + ROW_TILE
    count = 2 * PLANE + PLANES + 1 if devices == GRID_DEVICES else devices
    low = jax.ShapeDtypeStruct((rows, features), jnp.bfloat16)
    small = lambda *shape: jax.ShapeDtypeStruct(shape, jnp.float32)
    shapes = (low, low, small(rows, 4), small(CHUNKS, 6), small(count, 4), low, low, low)
    scratch = [
        pltpu.VMEM((own, 1), jnp.float32),
        pltpu.VMEM((rows + 8, features), jnp.float32),
        pltpu.VMEM((features // LANES, own, LANES), jnp.float32),
        pltpu.VMEM((features // LANES, own, LANES), jnp.float32),
    ]
    return shapes, scratch


def prepare_kernel(
    devices, doc_ref, tokens_ref, grads_ref, pad_ref, after_ref, after_grad_ref, before_ref, vec_ref,
    x_ref, grad_ref, marks_ref, chunk_ref, link_ref, in_key, in_value, in_recept,
    column, ext, wide, wide_grad,
):
    mask_column(pad_ref, column)
    marks = (marks_ref, chunk_ref, link_ref)
    prepare_own(devices, doc_ref, tokens_ref, grads_ref, column, vec_ref, x_ref, grad_ref, marks, ext, wide, wide_grad)
    lows = (in_key, in_value, in_recept)
    prepare_halo(devices, after_ref, after_grad_ref, before_ref, vec_ref, x_ref, grad_ref, marks_ref, lows, ext)


def prepare_pass(devices, doc_lengths, tokens_in, cotangent, pad_rows, halo, vectors):
    shapes, scratch = prepared_shapes(devices, *tokens_in.shape)
    vmem = pl.BlockSpec(memory_space=pltpu.VMEM)
    return pl.pallas_call(
        functools.partial(prepare_kernel, devices),
        out_shape=shapes,
        in_specs=[pl.BlockSpec(memory_space=pltpu.SMEM)] + [vmem] * 7,
        out_specs=(vmem,) * len(shapes),
        scratch_shapes=scratch,
        compiler_params=pltpu.CompilerParams(vmem_limit_bytes=VMEM_BYTES),
        name="prepare_pass",
    )(doc_lengths, tokens_in, cotangent, pad_rows, *halo, vectors)


def open_kernel(
    slot_ref, vec_ref, marks_ref, chunk_ref, in_key, in_value, pool_ref,
    prefix_ref, summary_ref, key_out, value_out, state_out, weights_ref,
    key_ref, value_ref, num_ref, den_ref, max_ref, store, sem, out_sem,
):
    rows, features = in_key.shape
    own = rows - ROW_TILE
    length = own // CHUNKS
    per = EMBED_SIZE // BLOCK_ROWS
    for m in range(3):
        fetch_blocks(slot_ref, pool_ref, store, sem.at[m], m * per, m * per, per)
    for m, (left, out) in enumerate(((in_key, key_ref), (in_value, value_ref))):
        await_blocks(pool_ref, store, sem.at[m], m * per, per)

        def write(cols, piece, out=out):
            out[:, cols] = piece

        times_weight(left, store, m * per, per, write)
    await_blocks(pool_ref, store, sem.at[2], 2 * per, per)
    sent = [
        pltpu.make_async_copy(src, dst, out_sem.at[k])
        for k, (src, dst) in enumerate(
            (
                (key_ref, key_out), (value_ref, value_out), (store, weights_ref),
                (num_ref, state_out.at[0]), (den_ref, state_out.at[1]), (max_ref, state_out.at[2]),
            )
        )
    ]
    for copy in sent[:3]:
        copy.start()
    rate = jnp.exp(vec_ref[5:6])

    def token(i, state, key, value):
        state = reset(state, marks_ref[rows_at(i, CHUNKS), 0:1])
        num_ref[rows_at(i, CHUNKS)], den_ref[rows_at(i, CHUNKS)], max_ref[rows_at(i, CHUNKS)] = state
        return advance(state, key, value, rate)

    def step(i, state):
        return token(i, state, key_ref[rows_at(i, CHUNKS)], value_ref[rows_at(i, CHUNKS)])

    blank = jnp.zeros((CHUNKS, features), jnp.float32)
    state = lax.fori_loop(0, length - 1, step, (blank, blank, blank + NEGATIVE))
    late = tuple(item[CHUNKS - 1 :] for item in state)
    ends = step(length - 1, state)
    for copy in sent[3:]:
        copy.start()
    prior = (value_ref[own + 2 : own + 3], jnp.ones((1, features), jnp.float32), key_ref[own + 2 : own + 3])
    for c in range(CHUNKS):
        for k in range(3):
            prefix_ref[k, c : c + 1] = prior[k]
        if c < CHUNKS - 1:
            old = aged(prior, float(length), chunk_ref[c : c + 1, 0:1], rate)
            prior = merge(tuple(item[c : c + 1] for item in ends), old)
    last = merge(late, aged(prior, float(length - 1), chunk_ref[CHUNKS - 1 :, 2:3], rate))
    summary_ref[...] = jnp.concatenate(last, axis=0)
    for copy in sent:
        copy.wait()


def open_pass(slots, vectors, marks, chunk_marks, lows, pool):
    rows, features = lows[0].shape
    own = rows - ROW_TILE
    full = jax.ShapeDtypeStruct((rows, features), jnp.float32)
    small = lambda *shape: jax.ShapeDtypeStruct(shape, jnp.float32)
    vmem = pl.BlockSpec(memory_space=pltpu.VMEM)
    anywhere = pl.BlockSpec(memory_space=pl.ANY)
    f32 = lambda *shape: pltpu.VMEM(shape, jnp.float32)
    blocks = (3 * EMBED_SIZE // BLOCK_ROWS, BLOCK_ROWS, features)
    return pl.pallas_call(
        open_kernel,
        out_shape=(
            small(3, CHUNKS, features), small(3, features), full, full, small(3, own, features),
            jax.ShapeDtypeStruct(blocks, jnp.bfloat16),
        ),
        in_specs=[pl.BlockSpec(memory_space=pltpu.SMEM)] + [vmem] * 5 + [anywhere],
        out_specs=(vmem,) * 2 + (anywhere,) * 4,
        scratch_shapes=[f32(rows, features)] * 2 + [f32(own, features)] * 3 + [
            pltpu.VMEM(blocks, jnp.bfloat16),
            pltpu.SemaphoreType.DMA((3,)),
            pltpu.SemaphoreType.DMA((6,)),
        ],
        compiler_params=pltpu.CompilerParams(vmem_limit_bytes=VMEM_BYTES),
        name="open_pass",
    )(slots, vectors, marks, chunk_marks, *lows[:2], pool)


def middle_kernel(
    slot_ref, vec_ref, marks_ref, chunk_ref, incoming_ref, prefix_ref,
    x_in, grad_in, key_in, value_in, recept_in, state_in, pool_ref,
    suffix_ref, summary_ref, sums_ref, fade_ref,
    layer_out, resid_out, key_out, value_out, recept_out, slot_grad,
    x_ref, grad_ref, key_ref, value_ref, recept_ref, layer_ref, resid_grad, wkv, gw, own_share, recept_grad,
    full_num, full_den, full_max, mixed, ext, unit, inverse, low_key, low_recept, hidden, squared, value_acc, gate, gcv, gcg, hidden_grad,
    attn_grad, top_log, wide, store, sem, out_sem, in_sem, piece_sem, done_sem,
):
    rows, features = x_ref.shape
    own = rows - ROW_TILE
    tiles = rows // ROW_TILE
    length = own // CHUNKS
    per = EMBED_SIZE // BLOCK_ROWS
    ff = FF // BLOCK_ROWS
    at_out, at_recept, at_key, at_value = 0, per, 2 * per, 2 * per + ff
    pairs = [(key_in, key_ref), (value_in, value_ref), (recept_in, recept_ref)]
    pairs += [(state_in.at[k], ref) for k, ref in enumerate((full_num, full_den, full_max))]
    start_pieces(pairs, piece_sem, own)
    arrive_x = pltpu.make_async_copy(x_in, x_ref, in_sem.at[0])
    arrive_grad = pltpu.make_async_copy(grad_in, grad_ref, in_sem.at[1])
    sent = [
        pltpu.make_async_copy(src, dst, done_sem.at[k])
        for k, (src, dst) in enumerate(
            (
                (layer_ref, layer_out), (resid_grad, resid_out), (recept_grad, recept_out),
                (gw, key_out), (own_share, value_out),
            )
        )
    ]
    fetch_blocks(slot_ref, pool_ref, store, sem.at[0], 3 * per, at_out, per)
    arrive_x.start()
    arrive_grad.start()
    fetch_blocks(slot_ref, pool_ref, store, sem.at[1], 5 * per, at_key, ff)
    fetch_blocks(slot_ref, pool_ref, store, sem.at[2], 5 * per + ff, at_value, ff)
    fetch_blocks(slot_ref, pool_ref, store, sem.at[3], 4 * per, at_recept, per)
    rate = jnp.exp(vec_ref[5:6])
    bonus = vec_ref[6:7]
    incoming = tuple(incoming_ref[k : k + 1] for k in range(3))
    carry = merge(
        tuple(prefix_ref[k] for k in range(3)),
        aged(tuple(jnp.broadcast_to(v, (CHUNKS, features)) for v in incoming), chunk_ref[:, 3:4], chunk_ref[:, 1:2], rate),
    )

    def attend(j, size, state, key, value, recept):
        own_log = bonus + key
        top = jnp.maximum(state[2], own_log)
        old, new = jnp.exp(state[2] - top), jnp.exp(own_log - top)
        scale = 1.0 / (old * state[1] + new)
        out = (old * state[0] + new * value) * scale
        wkv[rows_at(j, size)] = out
        own_share[rows_at(j, size)] = new * scale
        top_log[rows_at(j, size)] = top
        value_acc[rows_at(j, size)] = scale
        ext[rows_at(j, size)] = jax.nn.sigmoid(recept) * out

    carry_wide = tuple(jnp.concatenate([item] * (STEP_TILE // CHUNKS), axis=0) for item in carry)
    ramp = lax.broadcasted_iota(jnp.int32, (STEP_TILE, 1), 0) // CHUNKS

    def attend_step(i, state_carry):
        at = rows_at(i, STEP_TILE)
        alive = marks_ref[at, 2:3]
        distance = (i * (STEP_TILE // CHUNKS) + ramp).astype(jnp.float32)
        state = merge((full_num[at], full_den[at], full_max[at]), aged(carry_wide, distance, alive, rate))
        full_num[at], full_den[at], full_max[at] = state
        attend(i, STEP_TILE, state, key_ref[at], value_ref[at], recept_ref[at])
        return state_carry

    for p in range(PIECES):
        wait_piece(pairs, piece_sem, own, p)
        count = own // STEP_TILE
        lax.fori_loop(p * count // PIECES, (p + 1) * count // PIECES, attend_step, 0)
    wait_piece(pairs, piece_sem, own, PIECES)

    def row(ref, r):
        return ref[r : r + 1]

    end = advance(
        (row(full_num, own - 1), row(full_den, own - 1), row(full_max, own - 1)),
        row(key_ref, own - 1), row(value_ref, own - 1), rate,
    )
    halo_one = reset(end, marks_ref[own : own + 1, 0:1])
    halo_two = reset(
        advance(halo_one, row(key_ref, own), row(value_ref, own), rate), marks_ref[own + 1 : own + 2, 0:1]
    )
    halo_zero = reset(incoming, marks_ref[own + 2 : own + 3, 0:1])
    rest = jnp.zeros((ROW_TILE - 3, features), jnp.float32)
    halo_state = tuple(
        jnp.concatenate([halo_one[k], halo_two[k], halo_zero[k], rest + (NEGATIVE if k == 2 else 0.0)], axis=0)
        for k in range(3)
    )
    attend(tiles - 1, ROW_TILE, halo_state, key_ref[own:rows], value_ref[own:rows], recept_ref[own:rows])

    def pack(first, size):
        at = pl.ds(first, size)
        mixed[at] = ext[at].astype(jnp.bfloat16)
        gw[at] = value_acc[at]

    for_rows(rows, pack)
    pack(own, ROW_TILE)
    await_blocks(pool_ref, store, sem.at[0], at_out, per)
    arrive_x.wait()

    def write_resid(cols, piece):
        unit[:, cols] = x_ref[:, cols].astype(jnp.float32) + piece

    times_weight(mixed, store, at_out, per, write_resid)

    def norm(first, size):
        at = pl.ds(first, size)
        resid = unit[at]
        resid_grad[at] = resid
        out, inv = unit_norm(resid)
        unit[at] = out
        inverse[at] = inv
        ext[pl.ds(pl.multiple_of(first + 8, 8), size)] = out * vec_ref[7:8] + vec_ref[8:9]

    for_rows(rows, norm)
    norm(own, ROW_TILE)
    shift_in(ext, own)

    def mix(first, size, here, before):
        for r, ref in ((9, low_key), (10, low_recept)):
            weight = vec_ref[r : r + 1]
            ref[pl.ds(first, size)] = (weight * here + (1.0 - weight) * before).astype(jnp.bfloat16)

    for_rows(rows, lambda first, size: mix(first, size, *normed_pair(ext, marks_ref, first, size)))
    mix(own, ROW_TILE, ext[own + 8 : own + 8 + ROW_TILE], halo_previous(ext, own, features) * marks_ref[own:rows, 1:2])

    await_blocks(pool_ref, store, sem.at[1], at_key, ff)

    def write_hidden(cols, piece):
        up = jnp.maximum(piece, 0.0)
        hidden[:, cols] = up
        squared[:, cols] = (up * up).astype(jnp.bfloat16)

    times_weight_back(low_key, store, at_key, ff, write_hidden)
    await_blocks(pool_ref, store, sem.at[2], at_value, ff)

    def write_value(cols, piece):
        value_acc[:, cols] = piece

    times_weight(squared, store, at_value, ff, write_value)
    await_blocks(pool_ref, store, sem.at[3], at_recept, per)

    def write_gate(cols, piece):
        gate[:, cols] = piece

    times_weight(low_recept, store, at_recept, per, write_gate)

    arrive_grad.wait()

    def finish(first, size):
        at = pl.ds(first, size)
        opened = jax.nn.sigmoid(gate[at])
        value = value_acc[at]
        grad = grad_ref[at].astype(jnp.float32) * opened
        gcv[at] = grad.astype(jnp.bfloat16)
        gcg[at] = (grad * value * (1.0 - opened)).astype(jnp.bfloat16)
        return resid_grad[at] + opened * value

    def finish_own(first, size):
        out = finish(first, size)
        for k in range(size // CHUNKS):
            put_step(wide, first // CHUNKS + k, length, out[CHUNKS * k : CHUNKS * (k + 1)])

    for_rows(rows, finish_own)
    finish(own, ROW_TILE)

    def emit(first, size):
        layer_ref[pl.ds(first, size)] = take_rows(wide, pl.ds(first, size)).astype(jnp.bfloat16)

    for_rows(rows, emit)
    sent[0].start()

    def write_hidden_grad(cols, piece):
        hidden_grad[:, cols] = (piece * (2.0 * hidden[:, cols])).astype(jnp.bfloat16)

    times_weight_back(gcv, store, at_value, ff, write_hidden_grad)
    weight_gradient(squared, gcv, own, slot_ref, slot_grad, store, out_sem.at[2], 5 * per + ff, at_value)
    times_weight(hidden_grad, store, at_key, ff, write_value)
    weight_gradient(hidden_grad, low_key, own, slot_ref, slot_grad, store, out_sem.at[1], 5 * per, at_key)
    times_weight_back(gcg, store, at_recept, per, write_gate)
    weight_gradient(low_recept, gcg, own, slot_ref, slot_grad, store, out_sem.at[3], 4 * per, at_recept)
    carried = hidden.at[:, 0:features]
    mix_key, mix_recept = vec_ref[9:10], vec_ref[10:11]

    def carry_over(first, size):
        at = pl.ds(first, size)
        carried[at] = marks_ref[at, 1:2] * ((1.0 - mix_key) * value_acc[at] + (1.0 - mix_recept) * gate[at])

    for_rows(rows, carry_over)
    carry_over(own, ROW_TILE)
    halo_next = jnp.concatenate(
        [carried[own + 1 : own + 2], jnp.zeros((ROW_TILE - 1, features), jnp.float32)], axis=0
    )
    carried[own : own + 8] = jnp.concatenate([carried[1:8], carried[own : own + 1]], axis=0)

    def norm_back(first, size, following):
        at = pl.ds(first, size)
        grad = mix_key * value_acc[at] + mix_recept * gate[at] + following
        scaled = grad * vec_ref[7:8]
        inner = (
            scaled
            - jnp.mean(scaled, axis=1, keepdims=True)
            - unit[at] * jnp.mean(scaled * unit[at], axis=1, keepdims=True)
        )
        total = grad_ref[at].astype(jnp.float32) + inner * inverse[at]
        resid_grad[at] = total
        attn_grad[at] = total.astype(jnp.bfloat16)
        return grad

    def back_step(first, size, *sums):
        at = pl.ds(first, size)
        grad = norm_back(first, size, carried[pl.ds(pl.multiple_of(first + 8, 8), size)])
        here, before = normed_pair(ext, marks_ref, first, size)
        spread = here - before
        return (
            sums[0] + fold(grad * unit[at]),
            sums[1] + fold(grad),
            sums[2] + fold(value_acc[at] * spread),
            sums[3] + fold(gate[at] * spread),
        )

    blank = jnp.zeros((CHUNKS, features), jnp.float32)
    sums = for_rows(rows, back_step, (blank,) * 4)
    for k in range(4):
        sums_ref[k : k + 1] = jnp.sum(sums[k], axis=0, keepdims=True)
    norm_back(own, ROW_TILE, halo_next)
    sent[1].start()

    times_weight_back(attn_grad, store, at_out, per, write_gate)
    weight_gradient(mixed, attn_grad, own, slot_ref, slot_grad, store, out_sem.at[0], 3 * per, at_out)

    def gate_back(first, size):
        at = pl.ds(first, size)
        opened = jax.nn.sigmoid(recept_ref[at])
        grad = gate[at] * opened
        ext[at] = grad * gw[at]
        gw[at] = grad
        recept_grad[at] = (grad * wkv[at] * (1.0 - opened)).astype(jnp.bfloat16)

    for_rows(rows, gate_back)
    gate_back(own, ROW_TILE)
    sent[2].start()

    def back_token(state, share, out, top, start):
        older = state[2] - rate
        high = jnp.maximum(older, -top)
        old, new = jnp.exp(older - high), jnp.exp(-top - high)
        return reset((old * state[0] + new * share, old * state[1] - new * share * out, high), start)

    def back_scan(n, items):
        state, joint, sums = items[:3], items[3:6], items[6:]
        i = length - 1 - n
        at = rows_at(i, CHUNKS)
        value, out = value_ref[at], wkv[at]
        direct = own_share[at] * gw[at]
        bonus_grad = direct * (value - out)
        lift = jnp.exp(key_ref[at] + state[2])
        gw[at] = bonus_grad + lift * (state[0] * value + state[1])
        own_share[at] = direct + lift * state[0]
        whole = (full_num[at], full_den[at], full_max[at])
        fade = jnp.exp(state[2] + whole[2] - rate) * (state[0] * whole[0] + state[1] * whole[1])
        joint = merge(joint, aged(whole, (length - i).astype(jnp.float32), marks_ref[at, 3:4], rate))
        state = back_token(state, ext[at], out, top_log[at], marks_ref[at, 0:1])
        return state + joint + (sums[0] + fade, sums[1] + bonus_grad)

    empty = (blank, blank, blank + NEGATIVE)
    items = lax.fori_loop(0, length - 1, back_scan, empty + empty + (blank, blank))
    first = tuple(item[0:1] for item in items[:3])
    items = back_scan(jnp.int32(length - 1), items)
    heads = items[:3]
    for k in range(3):
        fade_ref[k] = items[3 + k]
    for k in range(2):
        sums_ref[4 + k : 5 + k] = jnp.sum(items[6 + k], axis=0, keepdims=True)
    tile = slice(own, rows)
    direct = own_share[tile] * gw[tile]
    gw[tile] = direct * (value_ref[tile] - wkv[tile])
    own_share[tile] = direct
    sent[3].start()
    sent[4].start()
    nothing = jnp.zeros((1, features), jnp.float32)
    after = back_token(
        (nothing, nothing, nothing + NEGATIVE),
        row(ext, own), row(wkv, own), row(top_log, own), marks_ref[own : own + 1, 0:1],
    )
    for c in range(CHUNKS - 1, -1, -1):
        for k in range(3):
            suffix_ref[k, c : c + 1] = after[k]
        if c > 0:
            old = aged(after, float(length), chunk_ref[c : c + 1, 0:1], rate)
            after = merge(tuple(item[c : c + 1] for item in heads), old)
    last = merge(first, aged(after, float(length - 1), marks_ref[0:1, 3:4], rate))
    summary_ref[...] = jnp.concatenate(last, axis=0)
    for k, (place, count) in enumerate(((at_out, per), (at_key, ff), (at_value, ff), (at_recept, per))):
        await_gradient(store, slot_grad, out_sem.at[k], place, count)
    for copy in sent:
        copy.wait()


def middle_pass(slots, x_rows, grad_rows, vectors, marks, chunk_marks, incoming, opened, pool):
    key, value, recept, states, prefix = opened
    rows, features = x_rows.shape
    own = rows - ROW_TILE
    full = jax.ShapeDtypeStruct((rows, features), jnp.float32)
    low = jax.ShapeDtypeStruct((rows, features), jnp.bfloat16)
    vmem = pl.BlockSpec(memory_space=pltpu.VMEM)
    anywhere = pl.BlockSpec(memory_space=pl.ANY)
    f32 = lambda *shape: pltpu.VMEM(shape, jnp.float32)
    b16 = lambda *shape: pltpu.VMEM(shape, jnp.bfloat16)
    return pl.pallas_call(
        middle_kernel,
        out_shape=(
            jax.ShapeDtypeStruct((3, CHUNKS, features), jnp.float32),
            jax.ShapeDtypeStruct((3, features), jnp.float32),
            jax.ShapeDtypeStruct((6, features), jnp.float32),
            jax.ShapeDtypeStruct((3, CHUNKS, features), jnp.float32),
            jax.ShapeDtypeStruct((own, features), jnp.bfloat16),
            full, full, full, low,
            jax.ShapeDtypeStruct(pool.shape, jnp.bfloat16),
        ),
        in_specs=[pl.BlockSpec(memory_space=pltpu.SMEM)] + [vmem] * 5 + [anywhere] * 7,
        out_specs=(vmem,) * 4 + (anywhere,) * 6,
        scratch_shapes=[
            b16(rows, features),
            b16(rows, features),
            f32(rows, features),
            f32(rows, features),
            f32(rows, features),
            b16(own, features),
            f32(rows, features),
            f32(rows, features),
            f32(rows, features),
            f32(rows, features),
            b16(rows, features),
            f32(own, features),
            f32(own, features),
            f32(own, features),
            b16(rows, features),
            f32(rows + 8, features),
            f32(rows, features),
            f32(rows, 1),
            b16(rows, features),
            b16(rows, features),
            f32(rows, FF),
            b16(rows, FF),
            f32(rows, features),
            f32(rows, features),
            b16(rows, features),
            b16(rows, features),
            b16(rows, FF),
            b16(rows, features),
            f32(rows, features),
            f32(features // LANES, own, LANES),
            b16((2 * EMBED_SIZE + 2 * FF) // BLOCK_ROWS, BLOCK_ROWS, features),
            pltpu.SemaphoreType.DMA((4,)),
            pltpu.SemaphoreType.DMA((4,)),
            pltpu.SemaphoreType.DMA((2,)),
            pltpu.SemaphoreType.DMA((6, PIECES + 1)),
            pltpu.SemaphoreType.DMA((5,)),
        ],
        compiler_params=pltpu.CompilerParams(vmem_limit_bytes=VMEM_BYTES),
        name="middle_pass",
    )(slots, vectors, marks, chunk_marks, incoming, prefix, x_rows, grad_rows, key, value, recept, states, pool)


def tail_shapes(shape):
    rows, features = shape
    own = rows - ROW_TILE
    f32 = lambda *dims: pltpu.VMEM(dims, jnp.float32)
    grads = [f32(rows, features)] * 3
    rest = [
        f32(rows + 8, features),
        f32(rows, features),
        f32(rows, 1),
        f32(rows, features),
        f32(features // LANES, own, LANES),
    ]
    return grads, rest


def tail_steps(x_ref, vec_ref, marks_ref, resid_ref, lows, weights, outs, ext, unit, inverse, carried, wide, input_ref, sums_ref):
    rows, features = x_ref.shape
    own = rows - ROW_TILE
    length = own // CHUNKS
    per = EMBED_SIZE // BLOCK_ROWS

    def back(m):
        def write(cols, piece):
            outs[m][:, cols] = piece

        times_weight_back(lows[m], weights, m * per, per, write)

    def norm(first, size):
        at = pl.ds(first, size)
        out, inv = unit_norm(x_ref[at].astype(jnp.float32))
        unit[at] = out
        inverse[at] = inv
        ext[pl.ds(pl.multiple_of(first + 8, 8), size)] = out * vec_ref[0:1] + vec_ref[1:2]

    def norms():
        for_rows(rows, norm)
        norm(own, ROW_TILE)
        shift_in(ext, own)

    mixes = tuple(vec_ref[k : k + 1] for k in (2, 3, 4))

    def carry_over(first, size):
        at = pl.ds(first, size)
        total = (1.0 - mixes[0]) * outs[0][at] + (1.0 - mixes[1]) * outs[1][at] + (1.0 - mixes[2]) * outs[2][at]
        carried[at] = marks_ref[at, 1:2] * total

    def carry_all():
        for_rows(rows, carry_over)
        carry_over(own, ROW_TILE)
        carried[own : own + 8] = jnp.concatenate([carried[1:8], carried[own : own + 1]], axis=0)

    def back_step(first, size, *sums):
        at = pl.ds(first, size)
        grads = (outs[0][at], outs[1][at], outs[2][at])
        grad = carried[pl.ds(pl.multiple_of(first + 8, 8), size)]
        for weight, piece in zip(mixes, grads):
            grad = grad + weight * piece
        scaled = grad * vec_ref[0:1]
        inner = (
            scaled
            - jnp.mean(scaled, axis=1, keepdims=True)
            - unit[at] * jnp.mean(scaled * unit[at], axis=1, keepdims=True)
        )
        out = resid_ref[at] + inner * inverse[at]
        for k in range(size // CHUNKS):
            put_step(wide, first // CHUNKS + k, length, out[CHUNKS * k : CHUNKS * (k + 1)])
        here, before = normed_pair(ext, marks_ref, first, size)
        spread = here - before
        return (sums[0] + fold(grad * unit[at]), sums[1] + fold(grad)) + tuple(
            s + fold(piece * spread) for s, piece in zip(sums[2:], grads)
        )

    def back_all():
        blank = jnp.zeros((CHUNKS, features), jnp.float32)
        sums = for_rows(rows, back_step, (blank,) * 5)
        for k in range(5):
            sums_ref[k : k + 1] = jnp.sum(sums[k], axis=0, keepdims=True)

    def emit(first, size):
        input_ref[pl.ds(first, size)] = take_rows(wide, pl.ds(first, size))

    return [
        functools.partial(back, 0), functools.partial(back, 1), functools.partial(back, 2),
        norms, carry_all, back_all, lambda: for_rows(rows, emit),
    ]


def tail_kernel(
    vec_ref, marks_ref, x_ref, resid_ref, key_grad, value_grad, recept_grad, weights, rows_ref,
    input_ref, sums_ref, grad_key_in, grad_value_in, grad_recept_in, ext, unit, inverse, carried, wide,
):
    sums_ref[...] = rows_ref[...]
    steps = tail_steps(
        x_ref, vec_ref, marks_ref, resid_ref, (key_grad, value_grad, recept_grad), weights,
        (grad_key_in, grad_value_in, grad_recept_in), ext, unit, inverse, carried, wide, input_ref, sums_ref,
    )
    for step in steps:
        step()


def tail_pass(rows, tail):
    x_rows = tail[2]
    own, features = x_rows.shape[0] - ROW_TILE, x_rows.shape[1]
    grads, rest = tail_shapes(x_rows.shape)
    vmem = pl.BlockSpec(memory_space=pltpu.VMEM)
    return pl.pallas_call(
        tail_kernel,
        out_shape=(jax.ShapeDtypeStruct((own, features), jnp.float32), jax.ShapeDtypeStruct(rows.shape, rows.dtype)),
        in_specs=[vmem] * 9,
        out_specs=(vmem, vmem),
        scratch_shapes=grads + rest,
        compiler_params=pltpu.CompilerParams(vmem_limit_bytes=VMEM_BYTES),
        name="tail_pass",
    )(*tail, rows)


def close_kernel(
    slot_ref, vec_ref, marks_ref, chunk_ref, incoming_ref, suffix_ref, sums_two_ref, fade_ref,
    key_hbm, value_hbm, in_key_hbm, in_value_hbm, in_recept_hbm, key_part_hbm, value_part_hbm, recept_hbm, grads_in,
    key_grad, value_grad, sums_ref, slot_grad,
    key_ref, value_ref, in_key, in_value, in_recept, key_wide, value_wide, recept_grad,
    store, out_sem, in_sem, piece_sem,
):
    rows, features = key_ref.shape
    own = rows - ROW_TILE
    length = own // CHUNKS
    per = EMBED_SIZE // BLOCK_ROWS
    early = [
        pltpu.make_async_copy(src, dst, in_sem.at[k])
        for k, (src, dst) in enumerate(
            ((in_recept_hbm, in_recept), (recept_hbm, recept_grad), (in_key_hbm, in_key), (in_value_hbm, in_value))
        )
    ]
    early[0].start()
    early[1].start()
    pairs = [(key_hbm, key_ref), (value_hbm, value_ref), (key_part_hbm, key_wide), (value_part_hbm, value_wide)]
    start_pieces(pairs, piece_sem, own)
    early[2].start()
    early[3].start()
    early[0].wait()
    early[1].wait()
    weight_gradient(in_recept, recept_grad, own, slot_ref, slot_grad, store, out_sem.at[2], 2 * per, 2 * per)
    rate = jnp.exp(vec_ref[5:6])
    incoming = tuple(incoming_ref[k : k + 1] for k in range(3))
    carry = merge(
        tuple(suffix_ref[k] for k in range(3)),
        aged(tuple(jnp.broadcast_to(v, (CHUNKS, features)) for v in incoming), chunk_ref[:, 5:6], chunk_ref[:, 4:5], rate),
    )
    fade = jnp.exp(carry[2] + fade_ref[2]) * (carry[0] * fade_ref[0] + carry[1] * fade_ref[1])
    sums_ref[0:5] = jnp.zeros((5, features), jnp.float32)
    sums_ref[5:6] = -rate * (sums_two_ref[4:5] + jnp.sum(fade, axis=0, keepdims=True))
    sums_ref[6:7] = sums_two_ref[5:6]
    sums_ref[7:] = sums_two_ref[0:4]

    def spread_back(at, state):
        value = value_ref[at]
        lift = jnp.exp(key_ref[at] + state[2])
        key_grad[at] = (key_wide[at] + lift * (state[0] * value + state[1])).astype(jnp.bfloat16)
        value_grad[at] = (value_wide[at] + lift * state[0]).astype(jnp.bfloat16)

    carry_wide = tuple(jnp.concatenate([item] * (STEP_TILE // CHUNKS), axis=0) for item in carry)
    ramp = lax.broadcasted_iota(jnp.int32, (STEP_TILE, 1), 0) // CHUNKS

    def token(i, c):
        at = rows_at(i, STEP_TILE)
        distance = (length - 1 - i * (STEP_TILE // CHUNKS) - ramp).astype(jnp.float32)
        spread_back(at, aged(carry_wide, distance, marks_ref[at, 3:4], rate))
        return c

    for p in range(PIECES):
        wait_piece(pairs, piece_sem, own, p)
        count = own // STEP_TILE
        lax.fori_loop(p * count // PIECES, (p + 1) * count // PIECES, token, 0)
    wait_piece(pairs, piece_sem, own, PIECES)
    halo = tuple(
        jnp.concatenate([incoming[k], jnp.zeros((ROW_TILE - 1, features), jnp.float32) + (NEGATIVE if k == 2 else 0.0)], axis=0)
        for k in range(3)
    )
    spread_back(slice(own, rows), halo)
    early[2].wait()
    early[3].wait()
    weight_gradient(in_key, key_grad, own, slot_ref, slot_grad, store, out_sem.at[0], 0, 0)
    weight_gradient(in_value, value_grad, own, slot_ref, slot_grad, store, out_sem.at[1], per, per)
    for m in range(3):
        await_gradient(store, slot_grad, out_sem.at[m], m * per, per)


def close_pass(slots, vectors, marks, chunk_marks, incoming, suffix, sums_two, fade, kept, slot_grad):
    rows, features = kept[0].shape
    vmem = pl.BlockSpec(memory_space=pltpu.VMEM)
    anywhere = pl.BlockSpec(memory_space=pl.ANY)
    low = jax.ShapeDtypeStruct((rows, features), jnp.bfloat16)
    operands = (slots, vectors, marks, chunk_marks, incoming, suffix, sums_two, fade) + kept + (slot_grad,)
    return pl.pallas_call(
        close_kernel,
        out_shape=(
            low,
            low,
            jax.ShapeDtypeStruct(vectors.shape, jnp.float32),
            jax.ShapeDtypeStruct(slot_grad.shape, jnp.bfloat16),
        ),
        in_specs=[pl.BlockSpec(memory_space=pltpu.SMEM)] + [vmem] * 7 + [anywhere] * (len(kept) + 1),
        out_specs=(vmem, vmem, vmem, anywhere),
        input_output_aliases={len(operands) - 1: 3},
        scratch_shapes=[pltpu.VMEM(k.shape, k.dtype) for k in kept] + [
            pltpu.VMEM((3 * EMBED_SIZE // BLOCK_ROWS, BLOCK_ROWS, features), jnp.bfloat16),
            pltpu.SemaphoreType.DMA((3,)),
            pltpu.SemaphoreType.DMA((4,)),
            pltpu.SemaphoreType.DMA((4, PIECES + 1)),
        ],
        compiler_params=pltpu.CompilerParams(vmem_limit_bytes=VMEM_BYTES),
        name="close_pass",
    )(*operands)


def chain_kernel(forward, own_ref, vec_ref, link_ref, *refs):
    if forward:
        left_hbm, weights_hbm, out_ref, product_hbm, *refs = refs
        *refs, left, weights, product_ref, work_sem = refs
    else:
        out_ref, *refs = refs
    plane, planes, joint, send_sem, recv_sem, far_send, far_recv = refs
    me, _, _, _, z = grid_place()
    place = lax.rem(me, PLANE)
    base = me - place
    at = 0 if forward else 2
    before = z if forward else PLANES - 1 - z
    step = PLANE if forward else -PLANE
    if forward:
        per = EMBED_SIZE // BLOCK_ROWS
        loads = (
            pltpu.make_async_copy(left_hbm, left, work_sem.at[0]),
            pltpu.make_async_copy(weights_hbm.at[pl.ds(2 * per, per)], weights, work_sem.at[1]),
        )
        for copy in loads:
            copy.start()
    planes[...] = jnp.zeros_like(planes)
    bar = pltpu.get_barrier_semaphore()
    for o in range(1, PLANE):
        peer = base + lax.rem(place + o, PLANE)
        pl.semaphore_signal(bar, inc=1, device_id=(peer,), device_id_type=MESH)
    for o in range(1, PLANES):
        @pl.when(o <= before)
        def _():
            pl.semaphore_signal(bar, inc=1, device_id=(me - step * o,), device_id_type=MESH)
    plane[pl.ds(place, 1)] = own_ref[...][None]
    rate = jnp.exp(vec_ref[5:6])
    pl.semaphore_wait(bar, PLANE - 1 + PLANES - 1 - before)

    def near_copy(o, source, peer):
        return pltpu.make_async_remote_copy(
            src_ref=own_ref, dst_ref=plane.at[source], send_sem=send_sem.at[o], recv_sem=recv_sem.at[o],
            device_id=(peer,), device_id_type=MESH,
        )

    def far_copy(o, source, peer):
        return pltpu.make_async_remote_copy(
            src_ref=joint, dst_ref=planes.at[source], send_sem=far_send.at[o], recv_sem=far_recv.at[o],
            device_id=(peer,), device_id_type=MESH,
        )

    for o in range(PLANE - 1, 0, -1):
        near_copy(o, place, base + lax.rem(place + o, PLANE)).start()
    if forward:
        for copy in loads:
            copy.wait()

        def write(cols, piece):
            product_ref[:, cols] = piece

        times_weight(left, weights, 0, per, write)
        leave = pltpu.make_async_copy(product_ref, product_hbm, work_sem.at[2])
        leave.start()
    for o in range(1, PLANE):
        source = lax.rem(place - o + PLANE, PLANE)
        near_copy(o, source, base + source).wait_recv()

    def gather_states(ref, first, count):
        valid = link_ref[first : first + count, at : at + 1]
        logs = jnp.where(valid > 0.5, ref[:, 2] - link_ref[first : first + count, at + 1 : at + 2] * rate, NEGATIVE)
        top = jnp.max(logs, axis=0, keepdims=True)
        weight = jnp.exp(logs - top)
        return (
            jnp.sum(weight * ref[:, 0], axis=0, keepdims=True),
            jnp.sum(weight * ref[:, 1], axis=0, keepdims=True),
            top,
        )

    joint[...] = jnp.concatenate(gather_states(plane, PLANE, PLANE), axis=0)
    for o in range(PLANES - 1, 0, -1):
        @pl.when(o < PLANES - before)
        def _():
            far_copy(o, z, me + step * o).start()
    near = gather_states(plane, 0, PLANE)
    for o in range(1, PLANES):
        @pl.when(o <= before)
        def _():
            source = z - o if forward else z + o
            far_copy(o, source, me - step * o).wait_recv()
    last = 2 * PLANE + PLANES
    old = gather_states(planes, 2 * PLANE, PLANES)
    old = aged(old, link_ref[last : last + 1, at + 1 : at + 2], link_ref[last : last + 1, at : at + 1], rate)
    out_ref[...] = jnp.concatenate(merge(near, old), axis=0)
    if forward:
        leave.wait()
    for o in range(1, PLANE):
        near_copy(o, place, base + lax.rem(place + o, PLANE)).wait_send()
    for o in range(1, PLANES):
        @pl.when(o < PLANES - before)
        def _():
            far_copy(o, z, me + step * o).wait_send()


def chain_state(rows, vectors, links, forward, cid, work=()):
    devices = lax.axis_size("seq")
    if devices != GRID_DEVICES:
        every = lax.all_gather(rows[None], "seq", axis=0, tiled=True)
        at = 0 if forward else 2
        aged_logs = every[:, 2] - links[:, at + 1 : at + 2] * jnp.exp(vectors[5])
        logs = jnp.where(links[:, at : at + 1] > 0.5, aged_logs, NEGATIVE)
        top = jnp.max(logs, axis=0)
        weight = jnp.exp(logs - top)
        state = jnp.stack([jnp.sum(weight * every[:, 0], axis=0), jnp.sum(weight * every[:, 1], axis=0), top])
        if not forward:
            return state
        left, weights = work
        right = weights[2 * EMBED_SIZE // BLOCK_ROWS :].reshape(EMBED_SIZE, -1)
        return state, jnp.dot(left, right, preferred_element_type=jnp.float32)
    vmem = pl.BlockSpec(memory_space=pltpu.VMEM)
    anywhere = pl.BlockSpec(memory_space=pl.ANY)
    out_shape, out_specs, extra = jax.ShapeDtypeStruct(rows.shape, jnp.float32), vmem, []
    if forward:
        left, weights = work
        wide = jax.ShapeDtypeStruct(left.shape, jnp.float32)
        out_shape, out_specs = (out_shape, wide), (vmem, anywhere)
        extra = [
            pltpu.VMEM(left.shape, left.dtype),
            pltpu.VMEM((EMBED_SIZE // BLOCK_ROWS,) + weights.shape[1:], weights.dtype),
            pltpu.VMEM(left.shape, jnp.float32),
            pltpu.SemaphoreType.DMA((3,)),
        ]
    return pl.pallas_call(
        functools.partial(chain_kernel, forward),
        out_shape=out_shape,
        in_specs=[vmem] * 3 + [anywhere] * len(work),
        out_specs=out_specs,
        scratch_shapes=[
            pltpu.VMEM((PLANE,) + rows.shape, jnp.float32),
            pltpu.VMEM((PLANES,) + rows.shape, jnp.float32),
            pltpu.VMEM(rows.shape, jnp.float32),
            pltpu.SemaphoreType.DMA((PLANE,)),
            pltpu.SemaphoreType.DMA((PLANE,)),
            pltpu.SemaphoreType.DMA((PLANES,)),
            pltpu.SemaphoreType.DMA((PLANES,)),
        ] + extra,
        compiler_params=pltpu.CompilerParams(collective_id=cid, has_side_effects=True, vmem_limit_bytes=VMEM_BYTES),
        name="chain_forward" if forward else "chain_backward",
    )(rows, vectors, links, *work)


def body(
    tokens_in,
    cotangent,
    pad_mask,
    doc_lengths,
    masters,
    moment_one,
    moment_two,
    block_slot,
    vectors,
    vector_one,
    vector_two,
):
    tokens, features = tokens_in.shape
    devices = lax.axis_size("seq")
    device_place = lax.axis_index("seq")
    pad_rows = pad_mask.reshape(-1, LANES)
    if devices == GRID_DEVICES:
        gathered, *prepared = gather_blocks(masters, doc_lengths, tokens_in, cotangent, pad_rows, vectors)
        gathered = gathered.reshape(-1, BLOCK_ROWS, features)
    else:
        gathered = lax.all_gather(masters.astype(jnp.bfloat16), "seq", axis=0, tiled=True)
        head_grad = cotangent[:ROW_TILE] * pad_mask[:ROW_TILE].astype(cotangent.dtype)[:, None]
        halo = [
            shifted(tokens_in[:ROW_TILE], "seq", -1),
            shifted(head_grad, "seq", -1),
            shifted(tokens_in[tokens - ROW_TILE :], "seq", 1),
        ]
        prepared = prepare_pass(devices, doc_lengths, tokens_in, cotangent, pad_rows, halo, vectors)
    x_rows, grad_rows, marks, chunk_marks, links, *lows = prepared
    lows = tuple(lows)
    prefix, summary, key, value, states, weights = open_pass(
        block_slot, vectors, marks, chunk_marks, lows, gathered
    )
    incoming, recept = chain_state(summary, vectors, links, True, 3, (lows[2], weights))
    (
        suffix, back_summary, sums_two, fade,
        layer_out, resid_grad, key_part, value_part, recept_grad, slot_grad,
    ) = middle_pass(
        block_slot, x_rows, grad_rows, vectors, marks, chunk_marks, incoming,
        (key, value, recept, states, prefix), gathered,
    )
    back_incoming = chain_state(back_summary, vectors, links, False, 4)
    key_grad, value_grad, stacked, slot_grad = close_pass(
        block_slot, vectors, marks, chunk_marks, back_incoming, suffix, sums_two, fade,
        (key, value) + lows + (key_part, value_part, recept_grad), slot_grad,
    )
    tail = (vectors, marks, x_rows, resid_grad, key_grad, value_grad, recept_grad, weights)
    own_slots = device_place * masters.shape[0] + jnp.arange(masters.shape[0], dtype=jnp.int32)
    named = jnp.any(own_slots[:, None] == block_slot[None, :], axis=1)
    if devices == GRID_DEVICES:
        owner_grad, vector_grad, input_grad = scatter_blocks(
            slot_grad.reshape((devices,) + masters.shape), stacked, tail
        )
        owner_grad = owner_grad.astype(jnp.float32)
    else:
        input_grad, stacked = tail_pass(stacked, tail)
        owner_grad = lax.psum_scatter(
            slot_grad.astype(jnp.float32), "seq", scatter_dimension=0, tiled=True
        )
        vector_grad = lax.psum(stacked, "seq")
    owner_grad = jnp.where(named[:, None, None], owner_grad, 0.0)
    new_one, new_two, new_master = adam_update(
        masters, moment_one, moment_two, owner_grad, MATRIX_RATE, WEIGHT_DECAY
    )
    vector_rates = jnp.array(VECTOR_RATE, jnp.float32)[:, None]
    vector_first, vector_second, vector_next = adam_update(
        vectors, vector_one, vector_two, vector_grad, vector_rates, 0.0
    )
    return (
        layer_out,
        input_grad,
        new_one,
        new_two,
        new_master,
        vector_first,
        vector_second,
        vector_next,
    )


def solution(mesh):
    placed = (
        P("seq", None),
        P("seq", None),
        P("seq"),
        P(),
        P("seq", None, None),
        P("seq", None, None),
        P("seq", None, None),
        P(),
        P(),
        P(),
        P(),
    )
    return jax.shard_map(
        body,
        mesh=mesh,
        in_specs=placed,
        out_specs=(
            P("seq", None),
            P("seq", None),
            P("seq", None, None),
            P("seq", None, None),
            P("seq", None, None),
            P(),
            P(),
            P(),
        ),
        check_vma=False,
    )
```

```python
import functools

import jax
import jax.numpy as jnp
from jax import lax
from jax.experimental import pallas as pl
from jax.experimental.pallas import tpu as pltpu
from jax.sharding import PartitionSpec as P

EMBED_SIZE = 1024
FF = 4096
BLOCK_ROWS = 32
ROWS_ALL = 13312
BLOCKS = 416
STEP = 10
GRID_DEVICES = 32
MESH = pl.DeviceIdType.MESH


NEGATIVE = -1e30
NORM_EPS = 1e-05
BETA_ONE = 0.9
BETA_TWO = 0.999
ADAM_EPS = 1e-08
MATRIX_RATE = 0.05
WEIGHT_DECAY = 0.01
VECTOR_RATE = (0.25, 0.25, 0.25, 0.25, 0.25, 2.0, 0.25, 0.25, 0.25, 0.25, 0.25)


def shifted(block, axis, distance):
    devices = range(lax.axis_size(axis))
    route = [(i - distance, i) for i in devices if i - distance in devices]
    return lax.ppermute(block, axis, route)


def product_back(left_side, right_side):
    return lax.dot_general(
        left_side, right_side, (((1,), (1,)), ((), ())), preferred_element_type=jnp.float32
    )


def product_left(left_side, right_side):
    return lax.dot_general(
        left_side, right_side, (((0,), (0,)), ((), ())), preferred_element_type=jnp.float32
    )


def adam_update(weight, first_moment, second_moment, gradient, step_rate, feature_fade_speed):
    first_moment = BETA_ONE * first_moment + (1.0 - BETA_ONE) * gradient
    second_moment = BETA_TWO * second_moment + (1.0 - BETA_TWO) * gradient * gradient
    first_fixed = first_moment / (1.0 - BETA_ONE**STEP)
    second_fixed = second_moment / (1.0 - BETA_TWO**STEP)
    weight = weight - step_rate * (
        first_fixed / (jnp.sqrt(second_fixed) + ADAM_EPS) + feature_fade_speed * weight
    )
    return (first_moment, second_moment, weight)


def grid_place():
    me = lax.axis_index("seq")
    return me, lax.rem(me, 2), lax.rem(me // 2, 2), lax.rem(me // 4, 2), me // 8

def spans(slots):
    side = 4 * slots // 15
    cuts = [0, side, 2 * side, slots]
    return [(cuts[i], cuts[i + 1] - cuts[i]) for i in range(3)]

def gather_kernel(
    slots, doc_ref, tokens_ref, cot_ref, pad_ref, vec_ref, master_hbm,
    out_ref, x_ref, grad_ref, marks_ref, chunk_ref, link_ref, in_key, in_value, in_recept,
    column, ext, wide, wide_grad, master_ref, own_ref, head_grad, after_ref, after_grad_ref, before_ref,
    *scratch,
):
    send_sem, recv_sem, sib_send, sib_recv, own_sem, halo_send, halo_recv, master_sem = scratch
    master_loads = [
        pltpu.make_async_copy(master_hbm.at[pl.ds(lo, n)], master_ref.at[pl.ds(lo, n)], master_sem.at[k])
        for k, (lo, n) in enumerate(spans(slots))
    ]
    for copy in master_loads:
        copy.start()
    me, core, x, y, z = grid_place()
    sib = me + 1 - 2 * core
    x_peer = me + 2 - 4 * x
    y_peer = me + 4 - 8 * y
    up = me + 8
    down = me - 8
    bar = pltpu.get_barrier_semaphore()
    pl.semaphore_signal(bar, inc=1, device_id=(sib,), device_id_type=MESH)
    pl.semaphore_signal(bar, inc=1, device_id=(x_peer,), device_id_type=MESH)
    pl.semaphore_signal(bar, inc=1, device_id=(y_peer,), device_id_type=MESH)
    @pl.when(z < 3)
    def _():
        pl.semaphore_signal(bar, inc=1, device_id=(up,), device_id_type=MESH)
    @pl.when(z > 0)
    def _():
        pl.semaphore_signal(bar, inc=1, device_id=(down,), device_id_type=MESH)
    more, less = me < GRID_DEVICES - 1, me > 0

    @pl.when(more)
    def _():
        pl.semaphore_signal(bar, inc=1, device_id=(me + 1,), device_id_type=MESH)

    @pl.when(less)
    def _():
        pl.semaphore_signal(bar, inc=1, device_id=(me - 1,), device_id_type=MESH)

    def lower(s, carry):
        own_ref[s] = master_ref[s].astype(own_ref.dtype)
        return carry

    for copy, (lo, n) in zip(master_loads, spans(slots)):
        copy.wait()
        lax.fori_loop(lo, lo + n, lower, 0)
    halos = jnp.where(more, 1, 0) + jnp.where(less, 1, 0)
    pl.semaphore_wait(bar, 4 + jnp.where((z > 0) & (z < 3), 1, 0) + halos)
    tokens = tokens_ref.shape[0]

    def halo_copy(k):
        src, dst, peer = (
            (tokens_ref.at[pl.ds(0, ROW_TILE)], after_ref, me - 1),
            (head_grad, after_grad_ref, me - 1),
            (tokens_ref.at[pl.ds(tokens - ROW_TILE, ROW_TILE)], before_ref, me + 1),
        )[k]
        return pltpu.make_async_remote_copy(src_ref=src, dst_ref=dst, send_sem=halo_send.at[k],
            recv_sem=halo_recv.at[k], device_id=(peer,), device_id_type=MESH)
    span = spans(slots)
    targets = (x_peer, y_peer, up, down)

    def chip(cx, cy, cz):
        return (cz * 2 + cy) * 2 + cx

    def view(cx, cy, cz, color, c=None):
        dev = chip(cx, cy, cz) * 2 + (core if c is None else c)
        lo, n = span[color]
        return out_ref.at[dev, pl.ds(lo, n)]

    def send(cx, cy, cz, color, way, own=False):
        lo, n = span[color]
        src = own_ref.at[pl.ds(lo, n)] if own else view(cx, cy, cz, color)
        idx = chip(cx, cy, cz)
        return pltpu.make_async_remote_copy(src_ref=src, dst_ref=view(cx, cy, cz, color),
            send_sem=send_sem.at[idx, color, way], recv_sem=recv_sem.at[idx, color],
            device_id=(targets[way],), device_id_type=MESH)

    def send_sib(cx, cy, cz, color, own=False):
        lo, n = span[color]
        src = own_ref.at[pl.ds(lo, n)] if own else view(cx, cy, cz, color)
        idx = chip(cx, cy, cz)
        return pltpu.make_async_remote_copy(src_ref=src, dst_ref=view(cx, cy, cz, color),
            send_sem=sib_send.at[idx, color], recv_sem=sib_recv.at[idx, color],
            device_id=(sib,), device_id_type=MESH)

    x2, y2 = 1 - x, 1 - y
    pending = []

    def go(copy, cond=None):
        if cond is None:
            copy.start()
        else:
            @pl.when(cond)
            def _():
                copy.start()
        pending.append((copy, cond))

    zup, zdown = z < 3, z > 0
    own_copies = []
    for color in range(3):
        lo, n = span[color]
        cp = pltpu.make_async_copy(own_ref.at[pl.ds(lo, n)], view(x, y, z, color), own_sem.at[color])
        cp.start()
        own_copies.append(cp)
    order = {0: (0, 2, 1), 1: (1, 2, 0)}
    for color in (0, 1, 2):
        go(send(x, y, z, color, 2, True), zup)
        go(send(x, y, z, color, 3, True), zdown)
    for color, way in ((0, 0), (1, 1), (2, 0), (2, 1), (0, 1), (1, 0)):
        go(send(x, y, z, color, way, True))
    for color in range(3):
        go(send_sib(x, y, z, color, True))

    mask_column(pad_ref, column)
    head_grad[...] = (cot_ref[0:ROW_TILE].astype(jnp.float32) * column[0:ROW_TILE]).astype(jnp.bfloat16)

    @pl.when(less)
    def _():
        for k in (0, 1):
            halo_copy(k).start()

    @pl.when(more)
    def _():
        halo_copy(2).start()

    marks = (marks_ref, chunk_ref, link_ref)
    prepare_own(
        GRID_DEVICES, doc_ref, tokens_ref, cot_ref, column, vec_ref, x_ref, grad_ref, marks, ext, wide, wide_grad
    )

    def arrive(cx, cy, cz, color):
        send(cx, cy, cz, color, 0).wait_recv()

    def sibling(cx, cy, cz, color):
        go(send_sib(cx, cy, cz, color))

    is0, is1 = core == 0, core == 1
    px = jnp.where(is0, x2, x)
    py = jnp.where(is0, y, y2)
    qx = jnp.where(is0, x, x2)
    qy = jnp.where(is0, y2, y)
    first = lambda cx, cy, cz: (go(send(cx, cy, cz, 2, 0), is0), go(send(cx, cy, cz, 2, 1), is1))
    last = lambda cx, cy, cz: (go(send(cx, cy, cz, 2, 1), is0), go(send(cx, cy, cz, 2, 0), is1))

    arrive(x2, y, z, 0)
    go(send(x2, y, z, 0, 2), zup)
    go(send(x2, y, z, 0, 3), zdown)
    go(send(x2, y, z, 0, 1))
    sibling(x2, y, z, 0)
    arrive(x, y2, z, 1)
    go(send(x, y2, z, 1, 2), zup)
    go(send(x, y2, z, 1, 3), zdown)
    go(send(x, y2, z, 1, 0))
    sibling(x, y2, z, 1)
    arrive(px, py, z, 2)
    last(px, py, z)
    sibling(px, py, z, 2)

    def wait_halo():
        @pl.when(less)
        def _():
            for k in (0, 1):
                halo_copy(k).wait_send()
            halo_copy(2).wait_recv()

        @pl.when(more)
        def _():
            halo_copy(2).wait_send()
            for k in (0, 1):
                halo_copy(k).wait_recv()

    for dist in (1, 2, 3):
        sides = []
        for sign, fwd, guard_f in ((1, 3, zdown), (-1, 2, zup)):
            q = z + sign * dist
            have = (q >= 0) & (q < 4)
            sides.append((q, fwd, have, guard_f))
        for which in ("c", "a", "b", "a2", "b2"):
            for q, fwd, have, gf in sides:
                @pl.when(have)
                def _(q=q, fwd=fwd, gf=gf, which=which):
                    if which == "c":
                        arrive(x, y, q, 2)
                        cp = send(x, y, q, 2, fwd)
                        pl.when(gf)(lambda: cp.start())
                        for w in (0, 1):
                            send(x, y, q, 2, w).start()
                        send_sib(x, y, q, 2).start()
                    else:
                        color = 0 if which[0] == "a" else 1
                        cx, cy = {"a": (x, y), "b": (x, y), "a2": (x2, y), "b2": (x, y2)}[which]
                        arrive(cx, cy, q, color)
                        cp = send(cx, cy, q, color, fwd)
                        pl.when(gf)(lambda: cp.start())
                        send(cx, cy, q, color, 1 if color == 0 else 0).start()
                        send_sib(cx, cy, q, color).start()
        for q, fwd, have, gf in sides:
            @pl.when(have)
            def _(q=q):
                arrive(px, py, q, 2)
                pl.when(is0)(lambda: send(px, py, q, 2, 1).start())
                pl.when(is1)(lambda: send(px, py, q, 2, 0).start())
                send_sib(px, py, q, 2).start()
        if dist == 1:
            tail_list = [(z, None)]
        else:
            tail_list = []
        if dist == 1:
            wait_halo()
            lows = (in_key, in_value, in_recept)
            prepare_halo(
                GRID_DEVICES, after_ref, after_grad_ref, before_ref, vec_ref, x_ref, grad_ref, marks_ref, lows, ext
            )
        def terminal(q):
            for cx, cy, color in ((x, y2, 0), (x2, y2, 0), (x2, y, 1), (x2, y2, 1), (qx, qy, 2), (x2, y2, 2)):
                arrive(cx, cy, q, color)
                send_sib(cx, cy, q, color).start()
        if dist == 1:
            terminal(z)
        else:
            for sign in (1, -1):
                q = z + sign * (dist - 1)
                pl.when((q >= 0) & (q < 4))(lambda q=q: terminal(q))
        if dist == 3:
            for sign in (1, -1):
                q = z + sign * 3
                pl.when((q >= 0) & (q < 4))(lambda q=q: terminal(q))
    for cp in own_copies:
        cp.wait()
    for color in range(3):
        pl.when(zup)(lambda color=color: send(x, y, z, color, 2).wait_send())
        pl.when(zdown)(lambda color=color: send(x, y, z, color, 3).wait_send())
        for w in (0, 1):
            send(x, y, z, color, w).wait_send()
    for cx, cy, color, w in ((x2, y, 0, 1), (x, y2, 1, 0)):
        pl.when(zup)(lambda: send(cx, cy, z, color, 2).wait_send())
        pl.when(zdown)(lambda: send(cx, cy, z, color, 3).wait_send())
        send(cx, cy, z, color, w).wait_send()
    pl.when(is0)(lambda: send(px, py, z, 2, 1).wait_send())
    pl.when(is1)(lambda: send(px, py, z, 2, 0).wait_send())
    for dist in (1, 2, 3):
        for sign, fwd, gf in ((1, 3, zdown), (-1, 2, zup)):
            q = z + sign * dist
            @pl.when((q >= 0) & (q < 4))
            def _(q=q, fwd=fwd, gf=gf):
                for cx, cy, color in ((x, y, 2), (x, y, 0), (x, y, 1), (x2, y, 0), (x, y2, 1)):
                    pl.when(gf)(lambda: send(cx, cy, q, color, fwd).wait_send())
                    ways = (0, 1) if color == 2 else ((1,) if color == 0 else (0,))
                    for w in ways:
                        send(cx, cy, q, color, w).wait_send()
                pl.when(is0)(lambda: send(px, py, q, 2, 1).wait_send())
                pl.when(is1)(lambda: send(px, py, q, 2, 0).wait_send())
    for cz in range(4):
        for cy in range(2):
            for cx in range(2):
                for color in range(3):
                    cp = send_sib(cx, cy, cz, color)
                    cp.wait_send()
                    cp.wait_recv()

def gather_blocks(masters, doc_lengths, tokens_in, cotangent, pad_rows, vectors, cid=1):
    slots = masters.shape[0]
    shapes, scratch = prepared_shapes(GRID_DEVICES, *tokens_in.shape)
    anywhere = pl.BlockSpec(memory_space=pl.ANY)
    vmem = pl.BlockSpec(memory_space=pltpu.VMEM)
    halo = pltpu.VMEM((ROW_TILE,) + tokens_in.shape[1:], jnp.bfloat16)
    return pl.pallas_call(
        functools.partial(gather_kernel, slots),
        out_shape=(jax.ShapeDtypeStruct((GRID_DEVICES,) + masters.shape, jnp.bfloat16),) + shapes,
        in_specs=[pl.BlockSpec(memory_space=pltpu.SMEM)] + [vmem] * 4 + [anywhere],
        out_specs=(anywhere,) + (vmem,) * len(shapes),
        scratch_shapes=scratch + [
            pltpu.VMEM(masters.shape, jnp.float32),
            pltpu.VMEM(masters.shape, jnp.bfloat16),
            halo, halo, halo, halo,
            pltpu.SemaphoreType.DMA((16, 3, 4)),
            pltpu.SemaphoreType.DMA((16, 3)),
            pltpu.SemaphoreType.DMA((16, 3)),
            pltpu.SemaphoreType.DMA((16, 3)),
            pltpu.SemaphoreType.DMA((3,)),
            pltpu.SemaphoreType.DMA((3,)),
            pltpu.SemaphoreType.DMA((3,)),
            pltpu.SemaphoreType.DMA((3,)),
        ],
        compiler_params=pltpu.CompilerParams(collective_id=cid, has_side_effects=True, vmem_limit_bytes=VMEM_BYTES),
        name="gather_blocks",
    )(doc_lengths, tokens_in, cotangent, pad_rows, vectors, masters)


def scatter_spans(slots):
    side = 4 * slots // 15
    cuts = [0, side, 2 * side, 2 * side + (slots - 2 * side + 1) // 2, slots]
    return [(cuts[i], cuts[i + 1] - cuts[i]) for i in range(4)]


def scatter_kernel(
    slots, part_ref, rows_ref, vec_ref, marks_ref, x_hbm, resid_hbm, key_hbm, value_hbm, recept_hbm, weights_hbm,
    out_ref, total_ref, input_hbm,
    acc, ring, ub, uc, ud, va, vc, vd, zs, zc, zd, sums,
    x_ref, resid_ref, key_grad, value_grad, recept_grad, weights, grad_key_in, grad_value_in, grad_recept_in,
    ext, unit, inverse, carried, wide, input_ref,
    load_sem, sib_send, sib_recv, send_sem, usem, vsem, zsem, row_send, row_recv, tail_sem, input_sem,
):
    me, core, x, y, z = grid_place()
    sibling = me + 1 - 2 * core
    x_peer = me + 2 - 4 * x
    y_peer = me + 4 - 8 * y
    up, down = me + 8, me - 8
    zup, zdown = z < 3, z > 0
    bar = pltpu.get_barrier_semaphore()
    for peer in (sibling, x_peer, y_peer):
        pl.semaphore_signal(bar, inc=1, device_id=(peer,), device_id_type=MESH)
    @pl.when(zup)
    def _():
        pl.semaphore_signal(bar, inc=1, device_id=(up,), device_id_type=MESH)
    @pl.when(zdown)
    def _():
        pl.semaphore_signal(bar, inc=1, device_id=(down,), device_id_type=MESH)
    far = me + 16 - 32 * (z // 2)
    pl.semaphore_signal(bar, inc=1, device_id=(far,), device_id_type=MESH)
    row_peers = (sibling, x_peer, y_peer, me + 8 - 16 * lax.rem(z, 2), far)
    tail_loads = [
        pltpu.make_async_copy(src, dst, tail_sem.at[k])
        for k, (src, dst) in enumerate(
            (
                (key_hbm, key_grad), (value_hbm, value_grad), (recept_hbm, recept_grad),
                (x_hbm, x_ref), (resid_hbm, resid_ref), (weights_hbm, weights),
            )
        )
    ]
    span = scatter_spans(slots)
    u, v = jnp.where(core == 0, x, y), jnp.where(core == 0, y, x)
    u_peer, v_peer = jnp.where(core == 0, x_peer, y_peer), jnp.where(core == 0, y_peer, x_peer)
    u2, v2 = 1 - u, 1 - v

    def row_copy(k):
        return pltpu.make_async_remote_copy(src_ref=sums.at[2 * k], dst_ref=sums.at[2 * k + 1],
            send_sem=row_send.at[k], recv_sem=row_recv.at[k], device_id=(row_peers[k],), device_id_type=MESH)

    def row_step(k):
        row_copy(k).wait()
        sums[2 * k + 2] = sums[2 * k] + sums[2 * k + 1]
        if k < 4:
            row_copy(k + 1).start()

    def load(i, q):
        chip = 4 * q + plane_order()[i]
        return pltpu.make_async_copy(part_ref.at[2 * chip + core], ring.at[i], load_sem.at[i])

    first_level = jnp.where(z >= 2, 0, 3)

    def next_level(q):
        inner = jnp.where(q == 3, jnp.where(z == 1, 2, 1), jnp.where(q == 0, jnp.where(z == 1, 1, 3), jnp.where(z == 1, 0, 2)))
        return jnp.where(z == 0, q - 1, jnp.where(z == 3, q + 1, inner))

    def give(chip):
        return pltpu.make_async_remote_copy(src_ref=part_ref.at[2 * chip + 1 - core], dst_ref=acc.at[chip],
            send_sem=sib_send.at[chip], recv_sem=sib_recv.at[chip], device_id=(sibling,), device_id_type=MESH)

    levels = []
    for dist in (3, 2, 1):
        for sign in (1, -1):
            q = z + sign * dist
            levels.append((dist, sign, q, (q >= 0) & (q < 4)))

    def run(dist, work):
        for d, sign, q, have in levels:
            if d == dist:
                pl.when(have)(functools.partial(work, q))

    def run_signed(dist, work):
        for d, sign, q, have in levels:
            if d == dist:
                pl.when(have)(functools.partial(work, q, sign, dist))

    def chip_of(cu, cv, cz):
        return cz * 4 + jnp.where(core == 0, cv * 2 + cu, cu * 2 + cv)

    def plane_order():
        return (chip_of(u2, v2, 0), chip_of(u2, v, 0), chip_of(u, v2, 0), chip_of(u, v, 0))

    def sibling_order():
        return tuple(plane_order()[i] for i in (0, 2, 1, 3))

    for i in range(4):
        load(i, first_level).start()
    for copy in tail_loads:
        copy.start()
    pl.semaphore_wait(bar, 5 + jnp.where(zup & zdown, 1, 0))
    for i in range(2):
        give(4 * first_level + sibling_order()[i]).start()

    def ready(i, q):
        chip = 4 * q + plane_order()[i]
        load(i, q).wait()
        give(chip).wait_recv()

        def step(s, carry):
            total = acc[chip, s].astype(jnp.float32) + ring[i, s].astype(jnp.float32)
            acc[chip, s] = total.astype(acc.dtype)
            return carry

        lax.fori_loop(0, slots, step, 0)

        if i < 2:
            @pl.when(q == first_level)
            def _():
                give(4 * q + sibling_order()[i + 2]).start()

        @pl.when(q != z)
        def _():
            load(i, next_level(q)).start()
            give(4 * next_level(q) + sibling_order()[i]).start()

    def out_copy(cu, cv, cz, color, target, place):
        lo, n = span[color]
        chip = chip_of(cu, cv, cz)
        buf, index, sem, flag = place
        return pltpu.make_async_remote_copy(src_ref=acc.at[chip, pl.ds(lo, n)], dst_ref=buf.at[index],
            send_sem=send_sem.at[chip, color], recv_sem=sem.at[flag], device_id=(target,), device_id_type=MESH)

    def arrived(place, color):
        lo, n = span[color]
        buf, index, sem, flag = place
        pltpu.make_async_remote_copy(src_ref=acc.at[0, pl.ds(lo, n)], dst_ref=buf.at[index],
            send_sem=send_sem.at[0, color], recv_sem=sem.at[flag], device_id=(sibling,), device_id_type=MESH).wait_recv()

    def add(cu, cv, cz, color, pieces):
        lo, n = span[color]
        chip = chip_of(cu, cv, cz)
        for place in pieces:
            arrived(place, color)

        def step(s, carry):
            total = acc[chip, lo + s].astype(jnp.float32)
            for buf, index, _, _ in pieces:
                total = total + buf[index, s].astype(jnp.float32)
            acc[chip, lo + s] = total.astype(acc.dtype)
            return carry

        lax.fori_loop(0, n, step, 0)

    def UB(q, i): return (ub, 2 * q + i, usem, 2 * q + i)
    def UD(q, i): return (ud, 2 * q + i, usem, 9 + 2 * q + i)
    def UC(q): return (uc, q, usem, 17 + q)
    def VA(q, i): return (va, 2 * q + i, vsem, 2 * q + i)
    def VC(q, i): return (vc, 2 * q + i, vsem, 9 + 2 * q + i)
    def VD(q): return (vd, q, vsem, 17 + q)
    def Z(q, k): return ((zc, zd, zs)[min(k, 2)], q if k < 2 else 4 * q + k - 2, zsem, 6 * q + k)

    def send_u(q, color, i):
        out_copy(u2, (v, v2)[i], q, color, u_peer, UB(q, i) if color == 1 else UD(q, i)).start()

    def send_v(q, color, i):
        out_copy((u, u2)[i], v2, q, color, v_peer, VA(q, i) if color == 0 else VC(q, i)).start()

    def term_a(q):
        ready(0, q)
        send_u(q, 1, 1)
        send_v(q, 0, 1)

    def term_c(q):
        send_v(q, 2, 1)
        send_u(q, 3, 1)

    def term_b(q):
        ready(1, q)
        send_u(q, 1, 0)
        ready(2, q)
        send_v(q, 0, 0)

    def term_d(q):
        send_u(q, 3, 0)
        send_v(q, 2, 0)
        ready(3, q)

    def plane_two(q):
        add(u2, v, q, 2, [VC(q, 1)])
        out_copy(u2, v, q, 2, u_peer, UC(q)).start()
        add(u, v2, q, 3, [UD(q, 1)])
        out_copy(u, v2, q, 3, v_peer, VD(q)).start()

    def column(part, q, sign, dist):
        target = up if sign == 1 else down
        more = zdown if sign == 1 else zup
        level = 4 if (dist == 1 and sign == 1) else q
        kinds = (
            (0, u, v, 2, [UC(q), VC(q, 0)]),
            (1, u, v, 3, [VD(q), UD(q, 0)]),
            (2, u, v, 0, [VA(q, 0)]),
            (3, u, v, 1, [UB(q, 0)]),
            (4, u2, v, 0, [VA(q, 1)]),
            (5, u, v2, 1, [UB(q, 1)]),
        )
        for k, cu, cv, color, pieces in ((kinds[5], kinds[4], kinds[3], kinds[2]), (kinds[0], kinds[1]), (kinds[5], kinds[4]), (kinds[3], kinds[2]))[part]:
            @pl.when(more)
            def _():
                add(cu, cv, q, color, pieces + [Z(q, k)])

            @pl.when(jnp.logical_not(more))
            def _():
                add(cu, cv, q, color, pieces)

            out_copy(cu, cv, q, color, target, Z(level, k)).start()

    planes = functools.partial(column, 0)
    last = functools.partial(column, 1)
    def begin_tail():
        for copy in tail_loads:
            copy.wait()
        sums[0] = rows_ref[...]

    tail = tail_steps(
        x_ref, vec_ref, marks_ref, resid_ref, (key_grad, value_grad, recept_grad), weights,
        (grad_key_in, grad_value_in, grad_recept_in), ext, unit, inverse, carried, wide, input_ref, sums.at[0],
    )
    send_input = pltpu.make_async_copy(input_ref, input_hbm, input_sem)
    run(3, term_a)
    run(3, term_c)
    run(3, term_b)
    run(3, term_d)
    begin_tail()
    tail[0]()
    run_signed(3, functools.partial(column, 2))
    run(2, term_a)
    run_signed(3, functools.partial(column, 3))
    tail[1]()
    run(3, plane_two)
    run(2, term_c)
    run_signed(3, last)
    tail[2]()
    run(2, term_b)
    run(2, term_d)
    tail[3]()
    run_signed(2, functools.partial(column, 2))
    run(1, term_a)
    run_signed(2, functools.partial(column, 3))
    tail[4]()
    run(2, plane_two)
    run(1, term_c)
    run_signed(2, last)
    tail[5]()
    run(1, term_b)
    run(1, term_d)
    row_copy(0).start()
    run_signed(1, functools.partial(column, 2))
    term_a(z)
    row_step(0)
    run_signed(1, functools.partial(column, 3))
    run(1, plane_two)
    term_c(z)
    row_step(1)
    run_signed(1, last)
    term_b(z)
    term_d(z)
    row_step(2)
    tail[6]()
    send_input.start()
    plane_two(z)
    row_step(3)

    def own(k, cu, cv, color, pieces):
        @pl.when(zup & zdown)
        def _():
            add(cu, cv, z, color, pieces + [Z(z, k), Z(4, k)])

        @pl.when(zup & jnp.logical_not(zdown))
        def _():
            add(cu, cv, z, color, pieces + [Z(z, k)])

        @pl.when(zdown & jnp.logical_not(zup))
        def _():
            add(cu, cv, z, color, pieces + [Z(4, k)])

    own(4, u2, v, 0, [VA(z, 1)])
    out_copy(u2, v, z, 0, u_peer, UB(4, 0)).start()
    own(5, u, v2, 1, [UB(z, 1)])
    out_copy(u, v2, z, 1, v_peer, VA(4, 0)).start()
    own(0, u, v, 2, [UC(z), VC(z, 0)])
    own(1, u, v, 3, [VD(z), UD(z, 0)])
    row_step(4)
    total_ref[...] = sums[10]
    own(2, u, v, 0, [VA(z, 0), UB(4, 0)])
    own(3, u, v, 1, [UB(z, 0), VA(4, 0)])
    pltpu.sync_copy(acc.at[chip_of(u, v, z)], out_ref)
    send_input.wait()
    for chip in range(16):
        give(chip).wait_send()
        for color in range(4):
            @pl.when(chip != chip_of(u, v, z))
            def _():
                lo, n = span[color]
                pltpu.make_async_remote_copy(src_ref=acc.at[chip, pl.ds(lo, n)], dst_ref=acc.at[chip, pl.ds(lo, n)],
                    send_sem=send_sem.at[chip, color], recv_sem=usem.at[0], device_id=(sibling,), device_id_type=MESH).wait_send()

def scatter_blocks(part, rows, tail, cid=2):
    vectors, marks, x_rows, resid_grad, *grads, weights = tail
    _, slots, height, feats = part.shape
    own = x_rows.shape[0] - ROW_TILE
    size_a, size_b, size_c, size_d = (n for _, n in scatter_spans(slots))
    dt = part.dtype
    block = lambda *shape: pltpu.VMEM(shape + (height, feats), dt)
    like = lambda array: pltpu.VMEM(array.shape, array.dtype)
    anywhere = pl.BlockSpec(memory_space=pl.ANY)
    vmem = pl.BlockSpec(memory_space=pltpu.VMEM)
    wide_shapes, tail_scratch = tail_shapes(x_rows.shape)
    return pl.pallas_call(
        functools.partial(scatter_kernel, slots),
        out_shape=(
            jax.ShapeDtypeStruct(part.shape[1:], dt),
            jax.ShapeDtypeStruct(rows.shape, rows.dtype),
            jax.ShapeDtypeStruct((own, feats), jnp.float32),
        ),
        in_specs=[anywhere] + [vmem] * 3 + [anywhere] * 6,
        out_specs=(anywhere, vmem, anywhere),
        scratch_shapes=[
            block(16, slots),
            block(4, slots),
            block(9, size_b),
            block(4, size_c),
            block(8, size_d),
            block(9, size_a),
            block(8, size_c),
            block(4, size_d),
            block(20, size_a),
            block(5, size_c),
            block(5, size_d),
            pltpu.VMEM((11,) + rows.shape, rows.dtype),
            like(x_rows), like(resid_grad), *(like(g) for g in grads), like(weights),
            *wide_shapes,
            *tail_scratch,
            pltpu.VMEM((own, feats), jnp.float32),
            pltpu.SemaphoreType.DMA((4,)),
            pltpu.SemaphoreType.DMA((16,)),
            pltpu.SemaphoreType.DMA((16,)),
            pltpu.SemaphoreType.DMA((16, 4)),
            pltpu.SemaphoreType.DMA((21,)),
            pltpu.SemaphoreType.DMA((21,)),
            pltpu.SemaphoreType.DMA((30,)),
            pltpu.SemaphoreType.DMA((5,)),
            pltpu.SemaphoreType.DMA((5,)),
            pltpu.SemaphoreType.DMA((6,)),
            pltpu.SemaphoreType.DMA,
        ],
        compiler_params=pltpu.CompilerParams(collective_id=cid, has_side_effects=True, vmem_limit_bytes=VMEM_BYTES),
        name="scatter_blocks",
    )(part, rows, vectors, marks, x_rows, resid_grad, *grads, weights)


ROW_TILE = 16
BIG_TILE = 64
PIECES = 4
STEP_TILE = 32
CHUNKS = 8
LANES = 128
PLANE = 8
PLANES = GRID_DEVICES // PLANE
VMEM_BYTES = 60 * 2**20


def rows_at(index, size=ROW_TILE):
    return pl.ds(pl.multiple_of(index * size, size), size)


def fetch_blocks(slot_ref, pool_ref, store_ref, sem, first_block, place, count):
    def step(b, carry):
        for k in range(4):
            pltpu.make_async_copy(
                pool_ref.at[slot_ref[first_block + 4 * b + k]], store_ref.at[place + 4 * b + k], sem
            ).start()
        return carry

    lax.fori_loop(0, count // 4, step, 0)


def await_blocks(pool_ref, store_ref, sem, place, count):
    pltpu.make_async_copy(
        pool_ref.at[pl.ds(0, count)], store_ref.at[pl.ds(place, count)], sem
    ).wait()


def times_weight(left_ref, store_ref, place, count, write, width=1024):
    features = store_ref.shape[2]

    def step(n, carry):
        cols = pl.ds(pl.multiple_of(n * width, width), width)
        right = store_ref[place : place + count, :, cols].reshape(count * BLOCK_ROWS, width)
        write(cols, jnp.dot(left_ref[...], right, preferred_element_type=jnp.float32))
        return carry

    lax.fori_loop(0, features // width, step, 0)


def times_weight_back(left_ref, store_ref, place, count, write, width=1024):
    blocks = width // BLOCK_ROWS

    def step(n, carry):
        cols = pl.ds(pl.multiple_of(n * width, width), width)
        right = store_ref[pl.ds(place + n * blocks, blocks)].reshape(width, store_ref.shape[2])
        write(cols, product_back(left_ref[...], right))
        return carry

    lax.fori_loop(0, count // blocks, step, 0)


def weight_gradient(left_ref, right_ref, own, slot_ref, grad_ref, store_ref, sem, first_block, place, width=1024):
    blocks = width // BLOCK_ROWS
    steps = left_ref.shape[1] // width

    def step(n, carry):
        cols = pl.ds(pl.multiple_of(n * width, width), width)
        piece = product_left(left_ref[0:own, cols], right_ref[0:own])
        at = place + n * blocks
        store_ref[pl.ds(at, blocks)] = piece.astype(store_ref.dtype).reshape(blocks, *store_ref.shape[1:])

        def put(b, inner):
            for k in range(4):
                pltpu.make_async_copy(
                    store_ref.at[at + 4 * b + k],
                    grad_ref.at[slot_ref[first_block + n * blocks + 4 * b + k]],
                    sem,
                ).start()
            return inner

        return lax.fori_loop(0, blocks // 4, put, carry)

    lax.fori_loop(0, steps, step, 0)


def await_gradient(store_ref, grad_ref, sem, place, count):
    pltpu.make_async_copy(
        store_ref.at[pl.ds(place, count)], grad_ref.at[pl.ds(0, count)], sem
    ).wait()


def start_pieces(pairs, sems, own):
    for p in range(PIECES + 1):
        for k, (src, dst) in enumerate(pairs):
            if p < PIECES or dst.shape[0] > own:
                piece_copy(src, dst, sems, own, k, p).start()


def piece_copy(src, dst, sems, own, k, p):
    size = own // PIECES
    at = pl.ds(p * size, size) if p < PIECES else pl.ds(own, ROW_TILE)
    return pltpu.make_async_copy(src.at[at], dst.at[at], sems.at[k, p])


def wait_piece(pairs, sems, own, p):
    for k, (src, dst) in enumerate(pairs):
        if p < PIECES or dst.shape[0] > own:
            piece_copy(src, dst, sems, own, k, p).wait()


def for_rows(rows, work, sums=()):
    own = rows - ROW_TILE

    def step(j, carry):
        out = work(pl.multiple_of(j * BIG_TILE, BIG_TILE), BIG_TILE, *carry)
        return carry if out is None else out

    sums = lax.fori_loop(0, own // BIG_TILE, step, sums)
    return sums


def fold(piece):
    return jnp.sum(piece.reshape(-1, CHUNKS, piece.shape[1]), axis=0)


def unit_norm(values):
    centered = values - jnp.mean(values, axis=1, keepdims=True)
    inverse = lax.rsqrt(jnp.mean(centered * centered, axis=1, keepdims=True) + NORM_EPS)
    return centered * inverse, inverse


def merge(first, second):
    top = jnp.maximum(first[2], second[2])
    one, two = jnp.exp(first[2] - top), jnp.exp(second[2] - top)
    return (one * first[0] + two * second[0], one * first[1] + two * second[1], top)


def aged(state, distance, alive, rate):
    return (state[0], state[1], jnp.where(alive > 0.5, state[2] - distance * rate, NEGATIVE))


def reset(state, start):
    cut = start > 0.5
    return (
        jnp.where(cut, 0.0, state[0]),
        jnp.where(cut, 0.0, state[1]),
        jnp.where(cut, NEGATIVE, state[2]),
    )


def advance(state, key, value, rate):
    older = state[2] - rate
    top = jnp.maximum(older, key)
    old, new = jnp.exp(older - top), jnp.exp(key - top)
    return (old * state[0] + new * value, old * state[1] + new, top)


def shift_in(ext, own):
    ext[0:8] = jnp.concatenate([ext[own + 10 : own + 11], ext[own : own + 7]], axis=0)


def halo_previous(ext, own, features):
    return jnp.concatenate(
        [
            ext[own + 7 : own + 8],
            ext[own + 8 : own + 9],
            ext[own + 11 : own + 12],
            jnp.zeros((ROW_TILE - 3, features), jnp.float32),
        ],
        axis=0,
    )


def normed_pair(ext, marks_ref, first, size):
    here = ext[pl.ds(pl.multiple_of(first + 8, 8), size)]
    before = ext[pl.ds(first, size)] * marks_ref[pl.ds(first, size), 1:2]
    return here, before


def take_step(wide, first, length):
    at = pl.ds(first, CHUNKS, stride=length)
    return jnp.concatenate([wide[k, at] for k in range(wide.shape[0])], axis=1)


def put_step(wide, first, length, tile):
    at = pl.ds(first, CHUNKS, stride=length)
    lanes = wide.shape[2]
    for k in range(wide.shape[0]):
        wide[k, at] = tile[:, k * lanes : (k + 1) * lanes]


def take_rows(wide, at):
    return jnp.concatenate([wide[k, at] for k in range(wide.shape[0])], axis=1)


def put_rows(wide, at, tile):
    lanes = wide.shape[2]
    for k in range(wide.shape[0]):
        wide[k, at] = tile[:, k * lanes : (k + 1) * lanes]


def none_between(offsets, low, high):
    hit = None
    for offset in offsets:
        inside = (low <= offset) & (offset <= high)
        hit = inside if hit is None else hit | inside
    return jnp.where(hit, 0.0, 1.0)


def write_marks(doc_ref, marks_ref, chunk_ref, link_ref, own, devices):
    rows = marks_ref.shape[0]
    length = own // CHUNKS
    total = own * devices
    me = lax.axis_index("seq")
    first = me * own
    offsets = [jnp.int32(0)]
    for k in range(doc_ref.shape[0] - 1):
        offsets.append(offsets[-1] + doc_ref[k])
    row = lax.broadcasted_iota(jnp.int32, (rows, 1), 0)
    chunk, step = lax.rem(row, CHUNKS), row // CHUNKS
    extra = jnp.where(row < own + 2, row, own - 1 - (row - (own + 2)) - own)
    place = first + jnp.where(row < own, chunk * length + step, extra)
    inside = (place >= 0) & (place < total)
    keep = jnp.where(inside, none_between(offsets, place, place), 0.0)
    begin = first + chunk * length
    marks_ref[:, 0:1] = 1.0 - keep
    marks_ref[:, 1:2] = keep
    marks_ref[:, 2:3] = jnp.where(row < own, none_between(offsets, begin, place), 1.0)
    marks_ref[:, 3:4] = jnp.where(row < own, none_between(offsets, place + 1, begin + length - 1), 1.0)
    chunk = lax.broadcasted_iota(jnp.int32, (CHUNKS, 1), 0)
    begin = first + chunk * length
    end = begin + length - 1
    chunk_ref[:, 0:1] = none_between(offsets, begin, end)
    chunk_ref[:, 1:2] = jnp.where(first > 0, none_between(offsets, first - 1, begin - 1), 0.0)
    chunk_ref[:, 2:3] = none_between(offsets, begin, end - 1)
    chunk_ref[:, 3:4] = (1 + chunk * length).astype(jnp.float32)
    chunk_ref[:, 4:5] = jnp.where(first + own < total, none_between(offsets, end + 1, first + own), 0.0)
    chunk_ref[:, 5:6] = (1 + (CHUNKS - 1 - chunk) * length).astype(jnp.float32)
    def put(rows, col, valid, distance):
        link_ref[rows, col : col + 1] = valid
        link_ref[rows, col + 1 : col + 2] = distance.astype(jnp.float32)

    if devices != GRID_DEVICES:
        other = lax.broadcasted_iota(jnp.int32, (devices, 1), 0)
        every = slice(0, devices)
        put(every, 0, jnp.where(other < me, none_between(offsets, own * (other + 1) - 1, own * me - 2), 0.0), own * (me - 1 - other))
        put(every, 2, jnp.where(other > me, none_between(offsets, own * (me + 1) + 1, own * other), 0.0), own * (other - me - 1))
        return
    z = me // PLANE
    base = z * PLANE
    end = base + PLANE
    other = base + lax.broadcasted_iota(jnp.int32, (PLANE, 1), 0)
    rows = slice(0, PLANE)
    put(rows, 0, jnp.where(other < me, none_between(offsets, own * (other + 1) - 1, own * me - 2), 0.0), own * (me - 1 - other))
    put(rows, 2, jnp.where(other > me, none_between(offsets, own * (me + 1) + 1, own * other), 0.0), own * (other - me - 1))
    rows = slice(PLANE, 2 * PLANE)
    put(rows, 0, none_between(offsets, own * (other + 1) - 1, own * end - 2), own * (end - 1 - other))
    put(rows, 2, none_between(offsets, own * base + 1, own * other), own * (other - base))
    rows = slice(2 * PLANE, 2 * PLANE + PLANES)
    far = lax.broadcasted_iota(jnp.int32, (PLANES, 1), 0)
    span = own * PLANE
    put(rows, 0, jnp.where(far < z, none_between(offsets, span * (far + 1) - 1, span * z - 2), 0.0), span * (z - 1 - far))
    put(rows, 2, jnp.where(far > z, none_between(offsets, span * (z + 1) + 1, span * far), 0.0), span * (far - z - 1))
    rows = slice(2 * PLANE + PLANES, 2 * PLANE + PLANES + 1)
    here = me + jnp.zeros((1, 1), jnp.int32)
    put(rows, 0, none_between(offsets, own * base - 1, own * here - 2), own * (here - base))
    put(rows, 2, none_between(offsets, own * (here + 1) + 1, own * end), own * (end - 1 - here))


def mask_column(pad_ref, column):
    for k in range(pad_ref.shape[0]):
        row = pad_ref[k : k + 1].astype(jnp.float32)
        column[k * LANES : (k + 1) * LANES] = jnp.broadcast_to(row, (LANES, LANES)).T[:, 0:1]


def normed_rows(x_ref, vec_ref, ext, first, size, tile):
    x_ref[pl.ds(first, size)] = tile.astype(jnp.bfloat16)
    unit, _ = unit_norm(tile)
    ext[pl.ds(pl.multiple_of(first + 8, 8), size)] = unit * vec_ref[0:1] + vec_ref[1:2]


def prepare_own(devices, doc_ref, tokens_ref, grads_ref, column, vec_ref, x_ref, grad_ref, marks, ext, wide, wide_grad):
    rows = x_ref.shape[0]
    own = rows - ROW_TILE
    length = own // CHUNKS
    write_marks(doc_ref, *marks, own, devices)

    def widen(first, size):
        at = pl.ds(first, size)
        put_rows(wide, at, tokens_ref[at].astype(jnp.float32))
        put_rows(wide_grad, at, grads_ref[at].astype(jnp.float32) * column[at])

    for_rows(rows, widen)

    def arrange(first, size):
        steps = [first // CHUNKS + k for k in range(size // CHUNKS)]
        tile = jnp.concatenate([take_step(wide, i, length) for i in steps], axis=0)
        normed_rows(x_ref, vec_ref, ext, first, size, tile)
        tile = jnp.concatenate([take_step(wide_grad, i, length) for i in steps], axis=0)
        grad_ref[pl.ds(first, size)] = tile.astype(jnp.bfloat16)

    for_rows(rows, arrange)


def prepare_halo(devices, after_ref, after_grad_ref, before_ref, vec_ref, x_ref, grad_ref, marks_ref, lows, ext):
    rows, features = x_ref.shape
    own = rows - ROW_TILE
    me = lax.axis_index("seq")
    more, less = me < devices - 1, me > 0
    later = jnp.where(more, after_ref[...].astype(jnp.float32), 0.0)[0:2]
    earlier = jnp.where(less, before_ref[...].astype(jnp.float32), 0.0)
    blank_rows = jnp.zeros((ROW_TILE - 4, features), jnp.float32)
    tile = jnp.concatenate(
        [later, earlier[ROW_TILE - 1 :], earlier[ROW_TILE - 2 : ROW_TILE - 1], blank_rows], axis=0
    )
    normed_rows(x_ref, vec_ref, ext, own, ROW_TILE, tile)
    later_grad = jnp.where(more, after_grad_ref[...].astype(jnp.float32), 0.0)[0:2]
    grad_ref[own:rows] = jnp.concatenate([later_grad, blank_rows, blank_rows[:2]], axis=0).astype(jnp.bfloat16)
    shift_in(ext, own)

    def mix(first, size, here, before):
        for row, ref in zip((2, 3, 4), lows):
            weight = vec_ref[row : row + 1]
            ref[pl.ds(first, size)] = (weight * here + (1.0 - weight) * before).astype(jnp.bfloat16)

    for_rows(rows, lambda first, size: mix(first, size, *normed_pair(ext, marks_ref, first, size)))
    mix(own, ROW_TILE, ext[own + 8 : own + 8 + ROW_TILE], halo_previous(ext, own, features) * marks_ref[own:rows, 1:2])


def prepared_shapes(devices, own, features):
    rows = own + ROW_TILE
    count = 2 * PLANE + PLANES + 1 if devices == GRID_DEVICES else devices
    low = jax.ShapeDtypeStruct((rows, features), jnp.bfloat16)
    small = lambda *shape: jax.ShapeDtypeStruct(shape, jnp.float32)
    shapes = (low, low, small(rows, 4), small(CHUNKS, 6), small(count, 4), low, low, low)
    scratch = [
        pltpu.VMEM((own, 1), jnp.float32),
        pltpu.VMEM((rows + 8, features), jnp.float32),
        pltpu.VMEM((features // LANES, own, LANES), jnp.float32),
        pltpu.VMEM((features // LANES, own, LANES), jnp.float32),
    ]
    return shapes, scratch


def prepare_kernel(
    devices, doc_ref, tokens_ref, grads_ref, pad_ref, after_ref, after_grad_ref, before_ref, vec_ref,
    x_ref, grad_ref, marks_ref, chunk_ref, link_ref, in_key, in_value, in_recept,
    column, ext, wide, wide_grad,
):
    mask_column(pad_ref, column)
    marks = (marks_ref, chunk_ref, link_ref)
    prepare_own(devices, doc_ref, tokens_ref, grads_ref, column, vec_ref, x_ref, grad_ref, marks, ext, wide, wide_grad)
    lows = (in_key, in_value, in_recept)
    prepare_halo(devices, after_ref, after_grad_ref, before_ref, vec_ref, x_ref, grad_ref, marks_ref, lows, ext)


def prepare_pass(devices, doc_lengths, tokens_in, cotangent, pad_rows, halo, vectors):
    shapes, scratch = prepared_shapes(devices, *tokens_in.shape)
    vmem = pl.BlockSpec(memory_space=pltpu.VMEM)
    return pl.pallas_call(
        functools.partial(prepare_kernel, devices),
        out_shape=shapes,
        in_specs=[pl.BlockSpec(memory_space=pltpu.SMEM)] + [vmem] * 7,
        out_specs=(vmem,) * len(shapes),
        scratch_shapes=scratch,
        compiler_params=pltpu.CompilerParams(vmem_limit_bytes=VMEM_BYTES),
        name="prepare_pass",
    )(doc_lengths, tokens_in, cotangent, pad_rows, *halo, vectors)


def open_kernel(
    slot_ref, vec_ref, marks_ref, chunk_ref, in_key, in_value, pool_ref,
    prefix_ref, summary_ref, key_out, value_out, state_out, weights_ref,
    key_ref, value_ref, num_ref, den_ref, max_ref, store, sem, out_sem,
):
    rows, features = in_key.shape
    own = rows - ROW_TILE
    length = own // CHUNKS
    per = EMBED_SIZE // BLOCK_ROWS
    for m in range(3):
        fetch_blocks(slot_ref, pool_ref, store, sem.at[m], m * per, m * per, per)
    for m, (left, out) in enumerate(((in_key, key_ref), (in_value, value_ref))):
        await_blocks(pool_ref, store, sem.at[m], m * per, per)

        def write(cols, piece, out=out):
            out[:, cols] = piece

        times_weight(left, store, m * per, per, write)
    await_blocks(pool_ref, store, sem.at[2], 2 * per, per)
    sent = [
        pltpu.make_async_copy(src, dst, out_sem.at[k])
        for k, (src, dst) in enumerate(
            (
                (key_ref, key_out), (value_ref, value_out), (store, weights_ref),
                (num_ref, state_out.at[0]), (den_ref, state_out.at[1]), (max_ref, state_out.at[2]),
            )
        )
    ]
    for copy in sent[:3]:
        copy.start()
    rate = jnp.exp(vec_ref[5:6])

    def token(i, state, key, value):
        state = reset(state, marks_ref[rows_at(i, CHUNKS), 0:1])
        num_ref[rows_at(i, CHUNKS)], den_ref[rows_at(i, CHUNKS)], max_ref[rows_at(i, CHUNKS)] = state
        return advance(state, key, value, rate)

    def step(i, state):
        return token(i, state, key_ref[rows_at(i, CHUNKS)], value_ref[rows_at(i, CHUNKS)])

    blank = jnp.zeros((CHUNKS, features), jnp.float32)
    state = lax.fori_loop(0, length - 1, step, (blank, blank, blank + NEGATIVE))
    late = tuple(item[CHUNKS - 1 :] for item in state)
    ends = step(length - 1, state)
    for copy in sent[3:]:
        copy.start()
    prior = (value_ref[own + 2 : own + 3], jnp.ones((1, features), jnp.float32), key_ref[own + 2 : own + 3])
    for c in range(CHUNKS):
        for k in range(3):
            prefix_ref[k, c : c + 1] = prior[k]
        if c < CHUNKS - 1:
            old = aged(prior, float(length), chunk_ref[c : c + 1, 0:1], rate)
            prior = merge(tuple(item[c : c + 1] for item in ends), old)
    last = merge(late, aged(prior, float(length - 1), chunk_ref[CHUNKS - 1 :, 2:3], rate))
    summary_ref[...] = jnp.concatenate(last, axis=0)
    for copy in sent:
        copy.wait()


def open_pass(slots, vectors, marks, chunk_marks, lows, pool):
    rows, features = lows[0].shape
    own = rows - ROW_TILE
    full = jax.ShapeDtypeStruct((rows, features), jnp.float32)
    small = lambda *shape: jax.ShapeDtypeStruct(shape, jnp.float32)
    vmem = pl.BlockSpec(memory_space=pltpu.VMEM)
    anywhere = pl.BlockSpec(memory_space=pl.ANY)
    f32 = lambda *shape: pltpu.VMEM(shape, jnp.float32)
    blocks = (3 * EMBED_SIZE // BLOCK_ROWS, BLOCK_ROWS, features)
    return pl.pallas_call(
        open_kernel,
        out_shape=(
            small(3, CHUNKS, features), small(3, features), full, full, small(3, own, features),
            jax.ShapeDtypeStruct(blocks, jnp.bfloat16),
        ),
        in_specs=[pl.BlockSpec(memory_space=pltpu.SMEM)] + [vmem] * 5 + [anywhere],
        out_specs=(vmem,) * 2 + (anywhere,) * 4,
        scratch_shapes=[f32(rows, features)] * 2 + [f32(own, features)] * 3 + [
            pltpu.VMEM(blocks, jnp.bfloat16),
            pltpu.SemaphoreType.DMA((3,)),
            pltpu.SemaphoreType.DMA((6,)),
        ],
        compiler_params=pltpu.CompilerParams(vmem_limit_bytes=VMEM_BYTES),
        name="open_pass",
    )(slots, vectors, marks, chunk_marks, *lows[:2], pool)


def middle_kernel(
    slot_ref, vec_ref, marks_ref, chunk_ref, incoming_ref, prefix_ref,
    x_in, grad_in, key_in, value_in, recept_in, state_in, pool_ref,
    suffix_ref, summary_ref, sums_ref, fade_ref,
    layer_out, resid_out, key_out, value_out, recept_out, slot_grad,
    x_ref, grad_ref, key_ref, value_ref, recept_ref, layer_ref, resid_grad, wkv, gw, own_share, recept_grad,
    full_num, full_den, full_max, mixed, ext, unit, inverse, low_key, low_recept, hidden, squared, value_acc, gate, gcv, gcg, hidden_grad,
    attn_grad, top_log, wide, store, sem, out_sem, in_sem, piece_sem, done_sem,
):
    rows, features = x_ref.shape
    own = rows - ROW_TILE
    tiles = rows // ROW_TILE
    length = own // CHUNKS
    per = EMBED_SIZE // BLOCK_ROWS
    ff = FF // BLOCK_ROWS
    at_out, at_recept, at_key, at_value = 0, per, 2 * per, 2 * per + ff
    pairs = [(key_in, key_ref), (value_in, value_ref), (recept_in, recept_ref)]
    pairs += [(state_in.at[k], ref) for k, ref in enumerate((full_num, full_den, full_max))]
    start_pieces(pairs, piece_sem, own)
    arrive_x = pltpu.make_async_copy(x_in, x_ref, in_sem.at[0])
    arrive_grad = pltpu.make_async_copy(grad_in, grad_ref, in_sem.at[1])
    sent = [
        pltpu.make_async_copy(src, dst, done_sem.at[k])
        for k, (src, dst) in enumerate(
            (
                (layer_ref, layer_out), (resid_grad, resid_out), (recept_grad, recept_out),
                (gw, key_out), (own_share, value_out),
            )
        )
    ]
    fetch_blocks(slot_ref, pool_ref, store, sem.at[0], 3 * per, at_out, per)
    arrive_x.start()
    arrive_grad.start()
    fetch_blocks(slot_ref, pool_ref, store, sem.at[1], 5 * per, at_key, ff)
    fetch_blocks(slot_ref, pool_ref, store, sem.at[2], 5 * per + ff, at_value, ff)
    fetch_blocks(slot_ref, pool_ref, store, sem.at[3], 4 * per, at_recept, per)
    rate = jnp.exp(vec_ref[5:6])
    bonus = vec_ref[6:7]
    incoming = tuple(incoming_ref[k : k + 1] for k in range(3))
    carry = merge(
        tuple(prefix_ref[k] for k in range(3)),
        aged(tuple(jnp.broadcast_to(v, (CHUNKS, features)) for v in incoming), chunk_ref[:, 3:4], chunk_ref[:, 1:2], rate),
    )

    def attend(j, size, state, key, value, recept):
        own_log = bonus + key
        top = jnp.maximum(state[2], own_log)
        old, new = jnp.exp(state[2] - top), jnp.exp(own_log - top)
        scale = 1.0 / (old * state[1] + new)
        out = (old * state[0] + new * value) * scale
        wkv[rows_at(j, size)] = out
        own_share[rows_at(j, size)] = new * scale
        top_log[rows_at(j, size)] = top
        value_acc[rows_at(j, size)] = scale
        ext[rows_at(j, size)] = jax.nn.sigmoid(recept) * out

    carry_wide = tuple(jnp.concatenate([item] * (STEP_TILE // CHUNKS), axis=0) for item in carry)
    ramp = lax.broadcasted_iota(jnp.int32, (STEP_TILE, 1), 0) // CHUNKS

    def attend_step(i, state_carry):
        at = rows_at(i, STEP_TILE)
        alive = marks_ref[at, 2:3]
        distance = (i * (STEP_TILE // CHUNKS) + ramp).astype(jnp.float32)
        state = merge((full_num[at], full_den[at], full_max[at]), aged(carry_wide, distance, alive, rate))
        full_num[at], full_den[at], full_max[at] = state
        attend(i, STEP_TILE, state, key_ref[at], value_ref[at], recept_ref[at])
        return state_carry

    for p in range(PIECES):
        wait_piece(pairs, piece_sem, own, p)
        count = own // STEP_TILE
        lax.fori_loop(p * count // PIECES, (p + 1) * count // PIECES, attend_step, 0)
    wait_piece(pairs, piece_sem, own, PIECES)

    def row(ref, r):
        return ref[r : r + 1]

    end = advance(
        (row(full_num, own - 1), row(full_den, own - 1), row(full_max, own - 1)),
        row(key_ref, own - 1), row(value_ref, own - 1), rate,
    )
    halo_one = reset(end, marks_ref[own : own + 1, 0:1])
    halo_two = reset(
        advance(halo_one, row(key_ref, own), row(value_ref, own), rate), marks_ref[own + 1 : own + 2, 0:1]
    )
    halo_zero = reset(incoming, marks_ref[own + 2 : own + 3, 0:1])
    rest = jnp.zeros((ROW_TILE - 3, features), jnp.float32)
    halo_state = tuple(
        jnp.concatenate([halo_one[k], halo_two[k], halo_zero[k], rest + (NEGATIVE if k == 2 else 0.0)], axis=0)
        for k in range(3)
    )
    attend(tiles - 1, ROW_TILE, halo_state, key_ref[own:rows], value_ref[own:rows], recept_ref[own:rows])

    def pack(first, size):
        at = pl.ds(first, size)
        mixed[at] = ext[at].astype(jnp.bfloat16)
        gw[at] = value_acc[at]

    for_rows(rows, pack)
    pack(own, ROW_TILE)
    await_blocks(pool_ref, store, sem.at[0], at_out, per)
    arrive_x.wait()

    def write_resid(cols, piece):
        unit[:, cols] = x_ref[:, cols].astype(jnp.float32) + piece

    times_weight(mixed, store, at_out, per, write_resid)

    def norm(first, size):
        at = pl.ds(first, size)
        resid = unit[at]
        resid_grad[at] = resid
        out, inv = unit_norm(resid)
        unit[at] = out
        inverse[at] = inv
        ext[pl.ds(pl.multiple_of(first + 8, 8), size)] = out * vec_ref[7:8] + vec_ref[8:9]

    for_rows(rows, norm)
    norm(own, ROW_TILE)
    shift_in(ext, own)

    def mix(first, size, here, before):
        for r, ref in ((9, low_key), (10, low_recept)):
            weight = vec_ref[r : r + 1]
            ref[pl.ds(first, size)] = (weight * here + (1.0 - weight) * before).astype(jnp.bfloat16)

    for_rows(rows, lambda first, size: mix(first, size, *normed_pair(ext, marks_ref, first, size)))
    mix(own, ROW_TILE, ext[own + 8 : own + 8 + ROW_TILE], halo_previous(ext, own, features) * marks_ref[own:rows, 1:2])

    await_blocks(pool_ref, store, sem.at[1], at_key, ff)

    def write_hidden(cols, piece):
        up = jnp.maximum(piece, 0.0)
        hidden[:, cols] = up
        squared[:, cols] = (up * up).astype(jnp.bfloat16)

    times_weight_back(low_key, store, at_key, ff, write_hidden)
    await_blocks(pool_ref, store, sem.at[2], at_value, ff)

    def write_value(cols, piece):
        value_acc[:, cols] = piece

    times_weight(squared, store, at_value, ff, write_value)
    await_blocks(pool_ref, store, sem.at[3], at_recept, per)

    def write_gate(cols, piece):
        gate[:, cols] = piece

    times_weight(low_recept, store, at_recept, per, write_gate)

    arrive_grad.wait()

    def finish(first, size):
        at = pl.ds(first, size)
        opened = jax.nn.sigmoid(gate[at])
        value = value_acc[at]
        grad = grad_ref[at].astype(jnp.float32) * opened
        gcv[at] = grad.astype(jnp.bfloat16)
        gcg[at] = (grad * value * (1.0 - opened)).astype(jnp.bfloat16)
        return resid_grad[at] + opened * value

    def finish_own(first, size):
        out = finish(first, size)
        for k in range(size // CHUNKS):
            put_step(wide, first // CHUNKS + k, length, out[CHUNKS * k : CHUNKS * (k + 1)])

    for_rows(rows, finish_own)
    finish(own, ROW_TILE)

    def emit(first, size):
        layer_ref[pl.ds(first, size)] = take_rows(wide, pl.ds(first, size)).astype(jnp.bfloat16)

    for_rows(rows, emit)
    sent[0].start()

    def write_hidden_grad(cols, piece):
        hidden_grad[:, cols] = (piece * (2.0 * hidden[:, cols])).astype(jnp.bfloat16)

    times_weight_back(gcv, store, at_value, ff, write_hidden_grad)
    weight_gradient(squared, gcv, own, slot_ref, slot_grad, store, out_sem.at[2], 5 * per + ff, at_value)
    times_weight(hidden_grad, store, at_key, ff, write_value)
    weight_gradient(hidden_grad, low_key, own, slot_ref, slot_grad, store, out_sem.at[1], 5 * per, at_key)
    times_weight_back(gcg, store, at_recept, per, write_gate)
    weight_gradient(low_recept, gcg, own, slot_ref, slot_grad, store, out_sem.at[3], 4 * per, at_recept)
    carried = hidden.at[:, 0:features]
    mix_key, mix_recept = vec_ref[9:10], vec_ref[10:11]

    def carry_over(first, size):
        at = pl.ds(first, size)
        carried[at] = marks_ref[at, 1:2] * ((1.0 - mix_key) * value_acc[at] + (1.0 - mix_recept) * gate[at])

    for_rows(rows, carry_over)
    carry_over(own, ROW_TILE)
    halo_next = jnp.concatenate(
        [carried[own + 1 : own + 2], jnp.zeros((ROW_TILE - 1, features), jnp.float32)], axis=0
    )
    carried[own : own + 8] = jnp.concatenate([carried[1:8], carried[own : own + 1]], axis=0)

    def norm_back(first, size, following):
        at = pl.ds(first, size)
        grad = mix_key * value_acc[at] + mix_recept * gate[at] + following
        scaled = grad * vec_ref[7:8]
        inner = (
            scaled
            - jnp.mean(scaled, axis=1, keepdims=True)
            - unit[at] * jnp.mean(scaled * unit[at], axis=1, keepdims=True)
        )
        total = grad_ref[at].astype(jnp.float32) + inner * inverse[at]
        resid_grad[at] = total
        attn_grad[at] = total.astype(jnp.bfloat16)
        return grad

    def back_step(first, size, *sums):
        at = pl.ds(first, size)
        grad = norm_back(first, size, carried[pl.ds(pl.multiple_of(first + 8, 8), size)])
        here, before = normed_pair(ext, marks_ref, first, size)
        spread = here - before
        return (
            sums[0] + fold(grad * unit[at]),
            sums[1] + fold(grad),
            sums[2] + fold(value_acc[at] * spread),
            sums[3] + fold(gate[at] * spread),
        )

    blank = jnp.zeros((CHUNKS, features), jnp.float32)
    sums = for_rows(rows, back_step, (blank,) * 4)
    for k in range(4):
        sums_ref[k : k + 1] = jnp.sum(sums[k], axis=0, keepdims=True)
    norm_back(own, ROW_TILE, halo_next)
    sent[1].start()

    times_weight_back(attn_grad, store, at_out, per, write_gate)
    weight_gradient(mixed, attn_grad, own, slot_ref, slot_grad, store, out_sem.at[0], 3 * per, at_out)

    def gate_back(first, size):
        at = pl.ds(first, size)
        opened = jax.nn.sigmoid(recept_ref[at])
        grad = gate[at] * opened
        ext[at] = grad * gw[at]
        gw[at] = grad
        recept_grad[at] = (grad * wkv[at] * (1.0 - opened)).astype(jnp.bfloat16)

    for_rows(rows, gate_back)
    gate_back(own, ROW_TILE)
    sent[2].start()

    def back_token(state, share, out, top, start):
        older = state[2] - rate
        high = jnp.maximum(older, -top)
        old, new = jnp.exp(older - high), jnp.exp(-top - high)
        return reset((old * state[0] + new * share, old * state[1] - new * share * out, high), start)

    def back_scan(n, items):
        state, joint, sums = items[:3], items[3:6], items[6:]
        i = length - 1 - n
        at = rows_at(i, CHUNKS)
        value, out = value_ref[at], wkv[at]
        direct = own_share[at] * gw[at]
        bonus_grad = direct * (value - out)
        lift = jnp.exp(key_ref[at] + state[2])
        gw[at] = bonus_grad + lift * (state[0] * value + state[1])
        own_share[at] = direct + lift * state[0]
        whole = (full_num[at], full_den[at], full_max[at])
        fade = jnp.exp(state[2] + whole[2] - rate) * (state[0] * whole[0] + state[1] * whole[1])
        joint = merge(joint, aged(whole, (length - i).astype(jnp.float32), marks_ref[at, 3:4], rate))
        state = back_token(state, ext[at], out, top_log[at], marks_ref[at, 0:1])
        return state + joint + (sums[0] + fade, sums[1] + bonus_grad)

    empty = (blank, blank, blank + NEGATIVE)
    items = lax.fori_loop(0, length - 1, back_scan, empty + empty + (blank, blank))
    first = tuple(item[0:1] for item in items[:3])
    items = back_scan(jnp.int32(length - 1), items)
    heads = items[:3]
    for k in range(3):
        fade_ref[k] = items[3 + k]
    for k in range(2):
        sums_ref[4 + k : 5 + k] = jnp.sum(items[6 + k], axis=0, keepdims=True)
    tile = slice(own, rows)
    direct = own_share[tile] * gw[tile]
    gw[tile] = direct * (value_ref[tile] - wkv[tile])
    own_share[tile] = direct
    sent[3].start()
    sent[4].start()
    nothing = jnp.zeros((1, features), jnp.float32)
    after = back_token(
        (nothing, nothing, nothing + NEGATIVE),
        row(ext, own), row(wkv, own), row(top_log, own), marks_ref[own : own + 1, 0:1],
    )
    for c in range(CHUNKS - 1, -1, -1):
        for k in range(3):
            suffix_ref[k, c : c + 1] = after[k]
        if c > 0:
            old = aged(after, float(length), chunk_ref[c : c + 1, 0:1], rate)
            after = merge(tuple(item[c : c + 1] for item in heads), old)
    last = merge(first, aged(after, float(length - 1), marks_ref[0:1, 3:4], rate))
    summary_ref[...] = jnp.concatenate(last, axis=0)
    for k, (place, count) in enumerate(((at_out, per), (at_key, ff), (at_value, ff), (at_recept, per))):
        await_gradient(store, slot_grad, out_sem.at[k], place, count)
    for copy in sent:
        copy.wait()


def middle_pass(slots, x_rows, grad_rows, vectors, marks, chunk_marks, incoming, opened, pool):
    key, value, recept, states, prefix = opened
    rows, features = x_rows.shape
    own = rows - ROW_TILE
    full = jax.ShapeDtypeStruct((rows, features), jnp.float32)
    low = jax.ShapeDtypeStruct((rows, features), jnp.bfloat16)
    vmem = pl.BlockSpec(memory_space=pltpu.VMEM)
    anywhere = pl.BlockSpec(memory_space=pl.ANY)
    f32 = lambda *shape: pltpu.VMEM(shape, jnp.float32)
    b16 = lambda *shape: pltpu.VMEM(shape, jnp.bfloat16)
    return pl.pallas_call(
        middle_kernel,
        out_shape=(
            jax.ShapeDtypeStruct((3, CHUNKS, features), jnp.float32),
            jax.ShapeDtypeStruct((3, features), jnp.float32),
            jax.ShapeDtypeStruct((6, features), jnp.float32),
            jax.ShapeDtypeStruct((3, CHUNKS, features), jnp.float32),
            jax.ShapeDtypeStruct((own, features), jnp.bfloat16),
            full, full, full, low,
            jax.ShapeDtypeStruct(pool.shape, jnp.bfloat16),
        ),
        in_specs=[pl.BlockSpec(memory_space=pltpu.SMEM)] + [vmem] * 5 + [anywhere] * 7,
        out_specs=(vmem,) * 4 + (anywhere,) * 6,
        scratch_shapes=[
            b16(rows, features),
            b16(rows, features),
            f32(rows, features),
            f32(rows, features),
            f32(rows, features),
            b16(own, features),
            f32(rows, features),
            f32(rows, features),
            f32(rows, features),
            f32(rows, features),
            b16(rows, features),
            f32(own, features),
            f32(own, features),
            f32(own, features),
            b16(rows, features),
            f32(rows + 8, features),
            f32(rows, features),
            f32(rows, 1),
            b16(rows, features),
            b16(rows, features),
            f32(rows, FF),
            b16(rows, FF),
            f32(rows, features),
            f32(rows, features),
            b16(rows, features),
            b16(rows, features),
            b16(rows, FF),
            b16(rows, features),
            f32(rows, features),
            f32(features // LANES, own, LANES),
            b16((2 * EMBED_SIZE + 2 * FF) // BLOCK_ROWS, BLOCK_ROWS, features),
            pltpu.SemaphoreType.DMA((4,)),
            pltpu.SemaphoreType.DMA((4,)),
            pltpu.SemaphoreType.DMA((2,)),
            pltpu.SemaphoreType.DMA((6, PIECES + 1)),
            pltpu.SemaphoreType.DMA((5,)),
        ],
        compiler_params=pltpu.CompilerParams(vmem_limit_bytes=VMEM_BYTES),
        name="middle_pass",
    )(slots, vectors, marks, chunk_marks, incoming, prefix, x_rows, grad_rows, key, value, recept, states, pool)


def tail_shapes(shape):
    rows, features = shape
    own = rows - ROW_TILE
    f32 = lambda *dims: pltpu.VMEM(dims, jnp.float32)
    grads = [f32(rows, features)] * 3
    rest = [
        f32(rows + 8, features),
        f32(rows, features),
        f32(rows, 1),
        f32(rows, features),
        f32(features // LANES, own, LANES),
    ]
    return grads, rest


def tail_steps(x_ref, vec_ref, marks_ref, resid_ref, lows, weights, outs, ext, unit, inverse, carried, wide, input_ref, sums_ref):
    rows, features = x_ref.shape
    own = rows - ROW_TILE
    length = own // CHUNKS
    per = EMBED_SIZE // BLOCK_ROWS

    def back(m):
        def write(cols, piece):
            outs[m][:, cols] = piece

        times_weight_back(lows[m], weights, m * per, per, write)

    def norm(first, size):
        at = pl.ds(first, size)
        out, inv = unit_norm(x_ref[at].astype(jnp.float32))
        unit[at] = out
        inverse[at] = inv
        ext[pl.ds(pl.multiple_of(first + 8, 8), size)] = out * vec_ref[0:1] + vec_ref[1:2]

    def norms():
        for_rows(rows, norm)
        norm(own, ROW_TILE)
        shift_in(ext, own)

    mixes = tuple(vec_ref[k : k + 1] for k in (2, 3, 4))

    def carry_over(first, size):
        at = pl.ds(first, size)
        total = (1.0 - mixes[0]) * outs[0][at] + (1.0 - mixes[1]) * outs[1][at] + (1.0 - mixes[2]) * outs[2][at]
        carried[at] = marks_ref[at, 1:2] * total

    def carry_all():
        for_rows(rows, carry_over)
        carry_over(own, ROW_TILE)
        carried[own : own + 8] = jnp.concatenate([carried[1:8], carried[own : own + 1]], axis=0)

    def back_step(first, size, *sums):
        at = pl.ds(first, size)
        grads = (outs[0][at], outs[1][at], outs[2][at])
        grad = carried[pl.ds(pl.multiple_of(first + 8, 8), size)]
        for weight, piece in zip(mixes, grads):
            grad = grad + weight * piece
        scaled = grad * vec_ref[0:1]
        inner = (
            scaled
            - jnp.mean(scaled, axis=1, keepdims=True)
            - unit[at] * jnp.mean(scaled * unit[at], axis=1, keepdims=True)
        )
        out = resid_ref[at] + inner * inverse[at]
        for k in range(size // CHUNKS):
            put_step(wide, first // CHUNKS + k, length, out[CHUNKS * k : CHUNKS * (k + 1)])
        here, before = normed_pair(ext, marks_ref, first, size)
        spread = here - before
        return (sums[0] + fold(grad * unit[at]), sums[1] + fold(grad)) + tuple(
            s + fold(piece * spread) for s, piece in zip(sums[2:], grads)
        )

    def back_all():
        blank = jnp.zeros((CHUNKS, features), jnp.float32)
        sums = for_rows(rows, back_step, (blank,) * 5)
        for k in range(5):
            sums_ref[k : k + 1] = jnp.sum(sums[k], axis=0, keepdims=True)

    def emit(first, size):
        input_ref[pl.ds(first, size)] = take_rows(wide, pl.ds(first, size))

    return [
        functools.partial(back, 0), functools.partial(back, 1), functools.partial(back, 2),
        norms, carry_all, back_all, lambda: for_rows(rows, emit),
    ]


def tail_kernel(
    vec_ref, marks_ref, x_ref, resid_ref, key_grad, value_grad, recept_grad, weights, rows_ref,
    input_ref, sums_ref, grad_key_in, grad_value_in, grad_recept_in, ext, unit, inverse, carried, wide,
):
    sums_ref[...] = rows_ref[...]
    steps = tail_steps(
        x_ref, vec_ref, marks_ref, resid_ref, (key_grad, value_grad, recept_grad), weights,
        (grad_key_in, grad_value_in, grad_recept_in), ext, unit, inverse, carried, wide, input_ref, sums_ref,
    )
    for step in steps:
        step()


def tail_pass(rows, tail):
    x_rows = tail[2]
    own, features = x_rows.shape[0] - ROW_TILE, x_rows.shape[1]
    grads, rest = tail_shapes(x_rows.shape)
    vmem = pl.BlockSpec(memory_space=pltpu.VMEM)
    return pl.pallas_call(
        tail_kernel,
        out_shape=(jax.ShapeDtypeStruct((own, features), jnp.float32), jax.ShapeDtypeStruct(rows.shape, rows.dtype)),
        in_specs=[vmem] * 9,
        out_specs=(vmem, vmem),
        scratch_shapes=grads + rest,
        compiler_params=pltpu.CompilerParams(vmem_limit_bytes=VMEM_BYTES),
        name="tail_pass",
    )(*tail, rows)


def close_kernel(
    slot_ref, vec_ref, marks_ref, chunk_ref, incoming_ref, suffix_ref, sums_two_ref, fade_ref,
    key_hbm, value_hbm, in_key_hbm, in_value_hbm, in_recept_hbm, key_part_hbm, value_part_hbm, recept_hbm, grads_in,
    key_grad, value_grad, sums_ref, slot_grad,
    key_ref, value_ref, in_key, in_value, in_recept, key_wide, value_wide, recept_grad,
    store, out_sem, in_sem, piece_sem,
):
    rows, features = key_ref.shape
    own = rows - ROW_TILE
    length = own // CHUNKS
    per = EMBED_SIZE // BLOCK_ROWS
    early = [
        pltpu.make_async_copy(src, dst, in_sem.at[k])
        for k, (src, dst) in enumerate(
            ((in_recept_hbm, in_recept), (recept_hbm, recept_grad), (in_key_hbm, in_key), (in_value_hbm, in_value))
        )
    ]
    early[0].start()
    early[1].start()
    pairs = [(key_hbm, key_ref), (value_hbm, value_ref), (key_part_hbm, key_wide), (value_part_hbm, value_wide)]
    start_pieces(pairs, piece_sem, own)
    early[2].start()
    early[3].start()
    early[0].wait()
    early[1].wait()
    weight_gradient(in_recept, recept_grad, own, slot_ref, slot_grad, store, out_sem.at[2], 2 * per, 2 * per)
    rate = jnp.exp(vec_ref[5:6])
    incoming = tuple(incoming_ref[k : k + 1] for k in range(3))
    carry = merge(
        tuple(suffix_ref[k] for k in range(3)),
        aged(tuple(jnp.broadcast_to(v, (CHUNKS, features)) for v in incoming), chunk_ref[:, 5:6], chunk_ref[:, 4:5], rate),
    )
    fade = jnp.exp(carry[2] + fade_ref[2]) * (carry[0] * fade_ref[0] + carry[1] * fade_ref[1])
    sums_ref[0:5] = jnp.zeros((5, features), jnp.float32)
    sums_ref[5:6] = -rate * (sums_two_ref[4:5] + jnp.sum(fade, axis=0, keepdims=True))
    sums_ref[6:7] = sums_two_ref[5:6]
    sums_ref[7:] = sums_two_ref[0:4]

    def spread_back(at, state):
        value = value_ref[at]
        lift = jnp.exp(key_ref[at] + state[2])
        key_grad[at] = (key_wide[at] + lift * (state[0] * value + state[1])).astype(jnp.bfloat16)
        value_grad[at] = (value_wide[at] + lift * state[0]).astype(jnp.bfloat16)

    carry_wide = tuple(jnp.concatenate([item] * (STEP_TILE // CHUNKS), axis=0) for item in carry)
    ramp = lax.broadcasted_iota(jnp.int32, (STEP_TILE, 1), 0) // CHUNKS

    def token(i, c):
        at = rows_at(i, STEP_TILE)
        distance = (length - 1 - i * (STEP_TILE // CHUNKS) - ramp).astype(jnp.float32)
        spread_back(at, aged(carry_wide, distance, marks_ref[at, 3:4], rate))
        return c

    for p in range(PIECES):
        wait_piece(pairs, piece_sem, own, p)
        count = own // STEP_TILE
        lax.fori_loop(p * count // PIECES, (p + 1) * count // PIECES, token, 0)
    wait_piece(pairs, piece_sem, own, PIECES)
    halo = tuple(
        jnp.concatenate([incoming[k], jnp.zeros((ROW_TILE - 1, features), jnp.float32) + (NEGATIVE if k == 2 else 0.0)], axis=0)
        for k in range(3)
    )
    spread_back(slice(own, rows), halo)
    early[2].wait()
    early[3].wait()
    weight_gradient(in_key, key_grad, own, slot_ref, slot_grad, store, out_sem.at[0], 0, 0)
    weight_gradient(in_value, value_grad, own, slot_ref, slot_grad, store, out_sem.at[1], per, per)
    for m in range(3):
        await_gradient(store, slot_grad, out_sem.at[m], m * per, per)


def close_pass(slots, vectors, marks, chunk_marks, incoming, suffix, sums_two, fade, kept, slot_grad):
    rows, features = kept[0].shape
    vmem = pl.BlockSpec(memory_space=pltpu.VMEM)
    anywhere = pl.BlockSpec(memory_space=pl.ANY)
    low = jax.ShapeDtypeStruct((rows, features), jnp.bfloat16)
    operands = (slots, vectors, marks, chunk_marks, incoming, suffix, sums_two, fade) + kept + (slot_grad,)
    return pl.pallas_call(
        close_kernel,
        out_shape=(
            low,
            low,
            jax.ShapeDtypeStruct(vectors.shape, jnp.float32),
            jax.ShapeDtypeStruct(slot_grad.shape, jnp.bfloat16),
        ),
        in_specs=[pl.BlockSpec(memory_space=pltpu.SMEM)] + [vmem] * 7 + [anywhere] * (len(kept) + 1),
        out_specs=(vmem, vmem, vmem, anywhere),
        input_output_aliases={len(operands) - 1: 3},
        scratch_shapes=[pltpu.VMEM(k.shape, k.dtype) for k in kept] + [
            pltpu.VMEM((3 * EMBED_SIZE // BLOCK_ROWS, BLOCK_ROWS, features), jnp.bfloat16),
            pltpu.SemaphoreType.DMA((3,)),
            pltpu.SemaphoreType.DMA((4,)),
            pltpu.SemaphoreType.DMA((4, PIECES + 1)),
        ],
        compiler_params=pltpu.CompilerParams(vmem_limit_bytes=VMEM_BYTES),
        name="close_pass",
    )(*operands)


def chain_kernel(forward, own_ref, vec_ref, link_ref, *refs):
    if forward:
        left_hbm, weights_hbm, out_ref, product_hbm, *refs = refs
        *refs, left, weights, product_ref, work_sem = refs
    else:
        out_ref, *refs = refs
    plane, planes, joint, send_sem, recv_sem, far_send, far_recv = refs
    me, _, _, _, z = grid_place()
    place = lax.rem(me, PLANE)
    base = me - place
    at = 0 if forward else 2
    before = z if forward else PLANES - 1 - z
    step = PLANE if forward else -PLANE
    if forward:
        per = EMBED_SIZE // BLOCK_ROWS
        loads = (
            pltpu.make_async_copy(left_hbm, left, work_sem.at[0]),
            pltpu.make_async_copy(weights_hbm.at[pl.ds(2 * per, per)], weights, work_sem.at[1]),
        )
        for copy in loads:
            copy.start()
    planes[...] = jnp.zeros_like(planes)
    bar = pltpu.get_barrier_semaphore()
    for o in range(1, PLANE):
        peer = base + lax.rem(place + o, PLANE)
        pl.semaphore_signal(bar, inc=1, device_id=(peer,), device_id_type=MESH)
    for o in range(1, PLANES):
        @pl.when(o <= before)
        def _():
            pl.semaphore_signal(bar, inc=1, device_id=(me - step * o,), device_id_type=MESH)
    plane[pl.ds(place, 1)] = own_ref[...][None]
    rate = jnp.exp(vec_ref[5:6])
    pl.semaphore_wait(bar, PLANE - 1 + PLANES - 1 - before)

    def near_copy(o, source, peer):
        return pltpu.make_async_remote_copy(
            src_ref=own_ref, dst_ref=plane.at[source], send_sem=send_sem.at[o], recv_sem=recv_sem.at[o],
            device_id=(peer,), device_id_type=MESH,
        )

    def far_copy(o, source, peer):
        return pltpu.make_async_remote_copy(
            src_ref=joint, dst_ref=planes.at[source], send_sem=far_send.at[o], recv_sem=far_recv.at[o],
            device_id=(peer,), device_id_type=MESH,
        )

    for o in range(PLANE - 1, 0, -1):
        near_copy(o, place, base + lax.rem(place + o, PLANE)).start()
    if forward:
        for copy in loads:
            copy.wait()

        def write(cols, piece):
            product_ref[:, cols] = piece

        times_weight(left, weights, 0, per, write)
        leave = pltpu.make_async_copy(product_ref, product_hbm, work_sem.at[2])
        leave.start()
    for o in range(1, PLANE):
        source = lax.rem(place - o + PLANE, PLANE)
        near_copy(o, source, base + source).wait_recv()

    def gather_states(ref, first, count):
        valid = link_ref[first : first + count, at : at + 1]
        logs = jnp.where(valid > 0.5, ref[:, 2] - link_ref[first : first + count, at + 1 : at + 2] * rate, NEGATIVE)
        top = jnp.max(logs, axis=0, keepdims=True)
        weight = jnp.exp(logs - top)
        return (
            jnp.sum(weight * ref[:, 0], axis=0, keepdims=True),
            jnp.sum(weight * ref[:, 1], axis=0, keepdims=True),
            top,
        )

    joint[...] = jnp.concatenate(gather_states(plane, PLANE, PLANE), axis=0)
    for o in range(PLANES - 1, 0, -1):
        @pl.when(o < PLANES - before)
        def _():
            far_copy(o, z, me + step * o).start()
    near = gather_states(plane, 0, PLANE)
    for o in range(1, PLANES):
        @pl.when(o <= before)
        def _():
            source = z - o if forward else z + o
            far_copy(o, source, me - step * o).wait_recv()
    last = 2 * PLANE + PLANES
    old = gather_states(planes, 2 * PLANE, PLANES)
    old = aged(old, link_ref[last : last + 1, at + 1 : at + 2], link_ref[last : last + 1, at : at + 1], rate)
    out_ref[...] = jnp.concatenate(merge(near, old), axis=0)
    if forward:
        leave.wait()
    for o in range(1, PLANE):
        near_copy(o, place, base + lax.rem(place + o, PLANE)).wait_send()
    for o in range(1, PLANES):
        @pl.when(o < PLANES - before)
        def _():
            far_copy(o, z, me + step * o).wait_send()


def chain_state(rows, vectors, links, forward, cid, work=()):
    devices = lax.axis_size("seq")
    if devices != GRID_DEVICES:
        every = lax.all_gather(rows[None], "seq", axis=0, tiled=True)
        at = 0 if forward else 2
        aged_logs = every[:, 2] - links[:, at + 1 : at + 2] * jnp.exp(vectors[5])
        logs = jnp.where(links[:, at : at + 1] > 0.5, aged_logs, NEGATIVE)
        top = jnp.max(logs, axis=0)
        weight = jnp.exp(logs - top)
        state = jnp.stack([jnp.sum(weight * every[:, 0], axis=0), jnp.sum(weight * every[:, 1], axis=0), top])
        if not forward:
            return state
        left, weights = work
        right = weights[2 * EMBED_SIZE // BLOCK_ROWS :].reshape(EMBED_SIZE, -1)
        return state, jnp.dot(left, right, preferred_element_type=jnp.float32)
    vmem = pl.BlockSpec(memory_space=pltpu.VMEM)
    anywhere = pl.BlockSpec(memory_space=pl.ANY)
    out_shape, out_specs, extra = jax.ShapeDtypeStruct(rows.shape, jnp.float32), vmem, []
    if forward:
        left, weights = work
        wide = jax.ShapeDtypeStruct(left.shape, jnp.float32)
        out_shape, out_specs = (out_shape, wide), (vmem, anywhere)
        extra = [
            pltpu.VMEM(left.shape, left.dtype),
            pltpu.VMEM((EMBED_SIZE // BLOCK_ROWS,) + weights.shape[1:], weights.dtype),
            pltpu.VMEM(left.shape, jnp.float32),
            pltpu.SemaphoreType.DMA((3,)),
        ]
    return pl.pallas_call(
        functools.partial(chain_kernel, forward),
        out_shape=out_shape,
        in_specs=[vmem] * 3 + [anywhere] * len(work),
        out_specs=out_specs,
        scratch_shapes=[
            pltpu.VMEM((PLANE,) + rows.shape, jnp.float32),
            pltpu.VMEM((PLANES,) + rows.shape, jnp.float32),
            pltpu.VMEM(rows.shape, jnp.float32),
            pltpu.SemaphoreType.DMA((PLANE,)),
            pltpu.SemaphoreType.DMA((PLANE,)),
            pltpu.SemaphoreType.DMA((PLANES,)),
            pltpu.SemaphoreType.DMA((PLANES,)),
        ] + extra,
        compiler_params=pltpu.CompilerParams(collective_id=cid, has_side_effects=True, vmem_limit_bytes=VMEM_BYTES),
        name="chain_forward" if forward else "chain_backward",
    )(rows, vectors, links, *work)


def body(
    tokens_in,
    cotangent,
    pad_mask,
    doc_lengths,
    masters,
    moment_one,
    moment_two,
    block_slot,
    vectors,
    vector_one,
    vector_two,
):
    tokens, features = tokens_in.shape
    devices = lax.axis_size("seq")
    device_place = lax.axis_index("seq")
    pad_rows = pad_mask.reshape(-1, LANES)
    if devices == GRID_DEVICES:
        gathered, *prepared = gather_blocks(masters, doc_lengths, tokens_in, cotangent, pad_rows, vectors)
        gathered = gathered.reshape(-1, BLOCK_ROWS, features)
    else:
        gathered = lax.all_gather(masters.astype(jnp.bfloat16), "seq", axis=0, tiled=True)
        head_grad = cotangent[:ROW_TILE] * pad_mask[:ROW_TILE].astype(cotangent.dtype)[:, None]
        halo = [
            shifted(tokens_in[:ROW_TILE], "seq", -1),
            shifted(head_grad, "seq", -1),
            shifted(tokens_in[tokens - ROW_TILE :], "seq", 1),
        ]
        prepared = prepare_pass(devices, doc_lengths, tokens_in, cotangent, pad_rows, halo, vectors)
    x_rows, grad_rows, marks, chunk_marks, links, *lows = prepared
    lows = tuple(lows)
    prefix, summary, key, value, states, weights = open_pass(
        block_slot, vectors, marks, chunk_marks, lows, gathered
    )
    incoming, recept = chain_state(summary, vectors, links, True, 3, (lows[2], weights))
    (
        suffix, back_summary, sums_two, fade,
        layer_out, resid_grad, key_part, value_part, recept_grad, slot_grad,
    ) = middle_pass(
        block_slot, x_rows, grad_rows, vectors, marks, chunk_marks, incoming,
        (key, value, recept, states, prefix), gathered,
    )
    back_incoming = chain_state(back_summary, vectors, links, False, 4)
    key_grad, value_grad, stacked, slot_grad = close_pass(
        block_slot, vectors, marks, chunk_marks, back_incoming, suffix, sums_two, fade,
        (key, value) + lows + (key_part, value_part, recept_grad), slot_grad,
    )
    tail = (vectors, marks, x_rows, resid_grad, key_grad, value_grad, recept_grad, weights)
    own_slots = device_place * masters.shape[0] + jnp.arange(masters.shape[0], dtype=jnp.int32)
    named = jnp.any(own_slots[:, None] == block_slot[None, :], axis=1)
    if devices == GRID_DEVICES:
        owner_grad, vector_grad, input_grad = scatter_blocks(
            slot_grad.reshape((devices,) + masters.shape), stacked, tail
        )
        owner_grad = owner_grad.astype(jnp.float32)
    else:
        input_grad, stacked = tail_pass(stacked, tail)
        owner_grad = lax.psum_scatter(
            slot_grad.astype(jnp.float32), "seq", scatter_dimension=0, tiled=True
        )
        vector_grad = lax.psum(stacked, "seq")
    owner_grad = jnp.where(named[:, None, None], owner_grad, 0.0)
    new_one, new_two, new_master = adam_update(
        masters, moment_one, moment_two, owner_grad, MATRIX_RATE, WEIGHT_DECAY
    )
    vector_rates = jnp.array(VECTOR_RATE, jnp.float32)[:, None]
    vector_first, vector_second, vector_next = adam_update(
        vectors, vector_one, vector_two, vector_grad, vector_rates, 0.0
    )
    return (
        layer_out,
        input_grad,
        new_one,
        new_two,
        new_master,
        vector_first,
        vector_second,
        vector_next,
    )


def solution(mesh):
    placed = (
        P("seq", None),
        P("seq", None),
        P("seq"),
        P(),
        P("seq", None, None),
        P("seq", None, None),
        P("seq", None, None),
        P(),
        P(),
        P(),
        P(),
    )
    return jax.shard_map(
        body,
        mesh=mesh,
        in_specs=placed,
        out_specs=(
            P("seq", None),
            P("seq", None),
            P("seq", None, None),
            P("seq", None, None),
            P("seq", None, None),
            P(),
            P(),
            P(),
        ),
        check_vma=False,
    )
```
